32 devices in a mesh: narrow: 4 (over y, x), wide: 8 (over z, core).
Axes of the slice: x: 2, y: 2, z: 4, core: 2. Of those that a mesh axis runs over, the one named last changes fastest.
Arguments:
- tokens: float32 [2048, 768], P('wide'), may hold values from -6 to 6
- norm1_gain: float32 [768], replicated, may hold values from 0.5 to 1.5
- in_weight: float32 [768, 2, 1536], P(None, None, 'narrow'), may hold values from -0.21875 to 0.21875
- conv_weight: float32 [4, 1536], P(None, 'narrow'), may hold values from -3 to 3
- conv_bias: float32 [1536], P('narrow'), may hold values from -1.5 to 1.5
- xproj_weight: float32 [1536, 80], P('narrow'), may hold values from -0.15625 to 0.15625
- dt_weight: float32 [48, 1536], P(None, 'narrow'), may hold values from -0.875 to 0.875
- dt_bias: float32 [1536], P('narrow'), may hold values from -6 to -2
- decay_log: float32 [16, 1536], P(None, 'narrow'), may hold values from -6 to 2.5
- skip_gain: float32 [1536], P('narrow'), may hold values from 0.5 to 1.5
- out_weight: float32 [1536, 768], P('narrow'), may hold values from -0.15625 to 0.15625
- norm2_gain: float32 [768], replicated, may hold values from 0.5 to 1.5
- router_weight: float32 [768, 8], replicated, may hold values from -0.15625 to 0.15625
- expert_in: float32 [8, 768, 3072], P('wide', None, 'narrow'), may hold values from -0.21875 to 0.21875
- expert_out: float32 [8, 3072, 768], P('wide', 'narrow'), may hold values from -1.5 to 1.5
- segments: int32 [2048], replicated, may hold values from -1 to 24, as said below
- expert_ids: int32 [2048, 1], P('wide'), may hold values from 0 to 7; in each aligned block of 256 rows (0 to 255, 256 to 511, ...) at most 51 rows name the same one
- cotangent: float32 [2048, 768], P('wide'), may hold values from -6 to 6
Outputs:
- output: float32 [2048, 768], P('wide')
- grad_tokens: float32 [2048, 768], P('wide')
- grad_norm1_gain: float32 [768], replicated
- grad_in_weight: float32 [768, 2, 1536], P(None, None, 'narrow')
- grad_conv_weight: float32 [4, 1536], P(None, 'narrow')
- grad_conv_bias: float32 [1536], P('narrow')
- grad_xproj_weight: float32 [1536, 80], P('narrow')
- grad_dt_weight: float32 [48, 1536], P(None, 'narrow')
- grad_dt_bias: float32 [1536], P('narrow')
- grad_decay_log: float32 [16, 1536], P(None, 'narrow')
- grad_skip_gain: float32 [1536], P('narrow')
- grad_out_weight: float32 [1536, 768], P('narrow')
- grad_norm2_gain: float32 [768], replicated
- grad_router_weight: float32 [768, 8], replicated
- grad_expert_in: float32 [8, 768, 3072], P('wide', None, 'narrow')
- grad_expert_out: float32 [8, 3072, 768], P('wide', 'narrow')
The draws below stay inside these ranges and needn't reach their ends.
Inputs may be any that keep to these rules, and one draw needn't show every extreme that they name: `segments`: document numbers never fall; each document's number is one more than the previous document's; -1 marks padding, which forms one run at the end of the stream, after the last document, whose number is the largest. Apart from the first, which begins at token 0, every document and the padding begin at least 32 tokens away from either edge of an aligned block of 256 tokens; every document is shorter than 1024 tokens. `expert_ids`: in each aligned block of 256 rows no expert is named by more than 51 rows.
All inputs are finite; a program needn't handle non-finite values.
Results may differ from the reference program's by a relative error of at most 0.0003.
Values sent between devices are 32-bit elements; how exact they have to be, the bound alone decides.
No kernel may reach another device: no remote copies, remote signals or barrier semaphores. Data moves between devices by JAX's collectives and lax.ppermute only.
A program may use at most 192 MiB of HBM per device.

```python
import math
import jax
import jax.numpy as jnp
import numpy as np
from jax import lax

D = 768
DI = 1536
STATE = 16
DT_RANK = 48
CONV = 4
FF = 3072
TOK_DEV = 256
EXPERTS = 8
TOKENS = 2048
CAP = 40
MOST = 51
N_WIDE = 8


def draw_segments(key, part):
    key = jax.random.fold_in(key, 7)
    keys = jax.random.split(key, 3)
    blocks = TOKENS // TOK_DEV
    block_order = jnp.arange(blocks)
    forced = (block_order % 3 == 0) | (block_order == blocks - 1)
    counts = jnp.where(forced, jax.random.randint(keys[0], (blocks,), 1, 4), jax.random.randint(keys[1], (blocks,), 0, 4))
    places = jax.random.randint(keys[2], (blocks, 3), TOK_DEV // 8, TOK_DEV - TOK_DEV // 8)
    used = jnp.arange(3)[None, :] < counts[:, None]
    inside = jnp.arange(TOK_DEV)
    markers = jnp.any(used[:, :, None] & (places[:, :, None] == inside[None, None, :]), axis=1)
    markers = markers.reshape(TOKENS).at[0].set(True)
    starts_seen = jnp.cumsum(markers.astype(jnp.int32))
    total_marks = starts_seen[-1]
    last_place = jnp.max(jnp.where(used[-1], places[-1], -1))
    pad_from = (blocks - 1) * TOK_DEV + last_place
    positions = jnp.arange(TOKENS)
    labels = 3 * blocks - (total_marks - 1 - starts_seen)
    labels = jnp.where(positions >= pad_from, -1, labels)
    return labels.astype(jnp.int32)


def levels(stream_key, dims, shards, smallest, largest):
    def one(axis_at, parts):
        draws = jax.random.uniform(jax.random.fold_in(jax.random.fold_in(stream_key, 6), axis_at), (parts,), jnp.float32, smallest / len(shards), largest / len(shards))
        return jnp.repeat(jnp.exp(draws), dims[axis_at] // parts).reshape((-1,) + (1,) * (len(dims) - axis_at - 1))

    level = one(*shards[0])
    for cut in shards[1:]:
        level = level * one(*cut)
    return level


def deal_out(own_key, own, number, rows, number_of, top, limit, skew):
    order = jax.random.permutation(own_key, number_of)
    crowded, ordinary = portions_of(number_of, rows * top, limit, skew, True), portions_of(number_of, rows * top, limit, skew, False)
    places = jnp.arange(number_of)

    def named(tallies, offset_by):
        used = int((tallies > 0).sum())
        fixed = max(1, used // 4)
        moved = fixed + (places - fixed + offset_by * (used - fixed)) % max(1, number_of - fixed)
        return jnp.zeros((number_of,), jnp.int32).at[order[jnp.where(places < fixed, places, moved)]].set(jnp.asarray(tallies, jnp.int32))

    tallies = jnp.where(number % 4 == 0, named(crowded, number // 4), named(ordinary, number - number // 4 - 1))
    mixed = jax.random.permutation(jax.random.fold_in(own, 3), number_of)
    donor, sink = mixed[0:number_of // 2 * 2:2], mixed[1:number_of // 2 * 2:2]
    slack = jnp.minimum(tallies[donor] - 1, limit - tallies[sink]) // 2
    slack = jnp.where((donor == order[0]) | (sink == order[0]) | (tallies[sink] == 0), 0, jnp.maximum(slack, 0))
    moved = jax.random.randint(jax.random.fold_in(own, 4), (number_of // 2,), 0, 1 << 20) % (slack + 1)
    tallies = tallies.at[donor].add(-moved).at[sink].add(moved)
    items = jnp.searchsorted(jnp.cumsum(tallies), jnp.arange(rows * top), side="right").astype(jnp.int32)
    grid = items.reshape(top, rows).T
    grid = grid[jax.random.permutation(jax.random.fold_in(own, 1), rows)]
    offset_by = jax.random.randint(jax.random.fold_in(own, 2), (rows, 1), 0, top)
    return jnp.take_along_axis(grid, (jnp.arange(top)[None, :] + offset_by) % top, axis=1)


def portions_of(number_of, total, limit, slope, full):
    loads = [(1 << 20) // math.isqrt(grade ** slope) + 1 for grade in range(1, number_of + 1)]
    largest = limit if full else min(limit, max(-(-total // number_of), total * loads[0] // sum(loads)))
    least = 1 if total - largest >= number_of - 1 else 0
    given, surplus = [largest] + [least] * (number_of - 1), total - largest - least * (number_of - 1)
    while surplus > 0:
        free = [i for i in range(1, number_of) if given[i] < largest] or [i for i in range(1, number_of) if given[i] < limit]
        mass, remaining = sum([loads[i] for i in free]), surplus
        for i in free:
            extra = min(limit - given[i], max(1, remaining * loads[i] // mass), surplus)
            given[i] = given[i] + extra
            surplus = surplus - extra
    return np.array(given)


def gaussian(stream_key, shape, width, bound, cuts=(), held_as=jnp.bfloat16):
    loudness = levels(stream_key, shape, cuts, -0.22, 0.18) if cuts else 1.0
    array = jax.random.normal(stream_key, shape, jnp.float32) * width * loudness
    return jnp.minimum(jnp.maximum(array, -bound), bound).astype(held_as)


def setup_inputs(seed: int = 0) -> dict:
    streams_of = jax.random.split(jax.random.key(seed), 19)
    tokens = gaussian(streams_of[0], (TOKENS, D), 1.0, 6.0, ((0, 8),), jnp.float32)
    norm1_gain = jnp.clip(1.0 + 0.1 * jax.random.normal(streams_of[1], (D,), jnp.float32), 0.5, 1.5)
    in_weight = gaussian(streams_of[2], (D, 2, DI), D ** -0.5, 0.21875, ((2, 4),), jnp.float32)
    conv_weight = gaussian(streams_of[3], (CONV, DI), CONV ** -0.5, 3.0, ((1, 4),), jnp.float32)
    conv_bias = gaussian(streams_of[4], (DI,), 0.3, 1.5, ((0, 4),), jnp.float32)
    xproj_weight = gaussian(streams_of[5], (DI, DT_RANK + 2 * STATE), DI ** -0.5, 0.15625, ((0, 4),), jnp.float32)
    dt_weight = gaussian(streams_of[6], (DT_RANK, DI), DT_RANK ** -0.5, 0.875, ((1, 4),), jnp.float32)
    dt_bias = jnp.clip(-6.0 + 4.0 * jax.random.uniform(streams_of[7], (DI,), jnp.float32) ** levels(streams_of[7], (DI,), ((0, 4),), -0.2, 0.2), -6.0, -2.0)
    decay_log = jnp.clip(-6.0 + 8.5 * jax.random.uniform(streams_of[8], (STATE, DI), jnp.float32) ** levels(streams_of[8], (STATE, DI), ((1, 4),), -0.2, 0.2), -6.0, 2.5)
    skip_gain = jnp.clip(1.0 + 0.1 * jax.random.normal(streams_of[9], (DI,), jnp.float32), 0.5, 1.5)
    out_weight = gaussian(streams_of[10], (DI, D), DI ** -0.5, 0.15625, ((0, 4),), jnp.float32)
    norm2_gain = jnp.clip(1.0 + 0.1 * jax.random.normal(streams_of[11], (D,), jnp.float32), 0.5, 1.5)
    router_weight = gaussian(streams_of[12], (D, EXPERTS), (2 * D) ** -0.5, 0.15625, (), jnp.float32)
    expert_in = gaussian(streams_of[13], (EXPERTS, D, FF), D ** -0.5, 0.21875, ((0, 8), (2, 4)), jnp.float32)
    expert_out = gaussian(streams_of[14], (EXPERTS, FF, D), (max(1, FF // (3 * EXPERTS * EXPERTS))) ** -0.5, 1.5, ((0, 8), (1, 4)), jnp.float32)
    segments = draw_segments(jax.random.fold_in(streams_of[18], 71), 0)
    expert_ids_keys = jax.random.split(jax.random.fold_in(streams_of[16], 1), TOKENS // TOK_DEV)
    expert_ids_turns = jax.random.permutation(jax.random.fold_in(streams_of[16], 3), TOKENS // TOK_DEV)
    expert_ids = jax.vmap(lambda own, number: deal_out(jax.random.fold_in(streams_of[16], 2), own, number, TOK_DEV, EXPERTS, 1, MOST, 1))(expert_ids_keys, expert_ids_turns).reshape((TOKENS, 1))
    cotangent = gaussian(streams_of[17], (TOKENS, D), 1.0, 6.0, ((0, 8),), jnp.float32)
    return dict(tokens=tokens, norm1_gain=norm1_gain, in_weight=in_weight, conv_weight=conv_weight, conv_bias=conv_bias, xproj_weight=xproj_weight, dt_weight=dt_weight, dt_bias=dt_bias, decay_log=decay_log, skip_gain=skip_gain, out_weight=out_weight, norm2_gain=norm2_gain, router_weight=router_weight, expert_in=expert_in, expert_out=expert_out, segments=segments, expert_ids=expert_ids, cotangent=cotangent)


@jax.custom_vjp
def low(v):
    return lax.optimization_barrier(v.astype(jnp.bfloat16)).astype(jnp.float32)

@jax.custom_vjp
def low_back(v):
    return v

def low_keep(v):
    return (low(v), None)

def low_pass(kept, grad):
    return (grad,)

def back_keep(v):
    return (v, None)

def back_low(kept, grad):
    return (low(grad),)
low.defvjp(low_keep, low_pass)
low_back.defvjp(back_keep, back_low)
highest = lax.Precision.HIGHEST
epsilon = 1e-05

def matmul(left, right):
    return jnp.dot(left, right, precision=highest)

def rms_norm(values, gain):
    return values * lax.rsqrt(lax.optimization_barrier(jnp.mean(values * values, axis=-1, keepdims=True)) + epsilon) * gain

def combine_linear(earlier, later):
    return (earlier[0] * later[0], later[0] * earlier[1] + later[1])

def ssm_pass(conv_out, projected, dt_weight, dt_bias, decay_log, keeping, start):
    rank_dt = dt_weight.shape[0]
    state_count = decay_log.shape[0]
    dt_low = projected[:, :rank_dt]
    in_coef = projected[:, rank_dt:rank_dt + state_count]
    out_coef = projected[:, rank_dt + state_count:]
    stepsize = jax.nn.softplus(matmul(dt_low, dt_weight) + dt_bias)
    rates = -jnp.exp(decay_log)
    length = conv_out.shape[0]
    blocksize = math.gcd(length, 128)
    count = length // blocksize
    pieces = (stepsize.reshape(count, blocksize, -1), conv_out.reshape(count, blocksize, -1), in_coef.reshape(count, blocksize, -1), out_coef.reshape(count, blocksize, -1), keeping.reshape(count, blocksize))

    def run_block(carry, piece):
        product, current = carry
        step_rows, input_rows, in_rows, out_rows, keep_rows = piece
        decays = jnp.exp(step_rows[:, None, :] * rates[None]) * keep_rows[:, None, None]
        drives = (step_rows * input_rows)[:, None, :] * in_rows[:, :, None]
        cum_decay, cum_drive = lax.associative_scan(combine_linear, (decays, drives), axis=0)
        states = cum_decay * current[None] + cum_drive
        outputs = lax.optimization_barrier(jnp.sum(out_rows[:, :, None] * states, axis=1))
        return ((product * cum_decay[-1], states[-1]), outputs)
    initial = (jnp.ones_like(start), start)
    (product, final), outputs = lax.scan(jax.checkpoint(run_block), initial, pieces)
    return (outputs.reshape(length, -1), product, final)

def conv_mix(conv_in, prev_rows, same_masks, conv_weight, conv_bias):
    taps = conv_weight.shape[0]
    length = conv_in.shape[0]
    extended = jnp.concatenate([prev_rows, conv_in], axis=0)
    mixed = conv_bias + jnp.zeros_like(conv_in)
    for offset in range(taps):
        first_row = taps - 1 - offset
        mixed = mixed + conv_weight[offset] * extended[first_row:first_row + length] * same_masks[offset][:, None]
    return jax.nn.silu(mixed)

def forward(tokens, norm1_gain, in_weight, conv_weight, conv_bias, xproj_weight, dt_weight, dt_bias, decay_log, skip_gain, out_weight, norm2_gain, router_weight, expert_in, expert_out, same_masks, dispatched, expert_index):
    normed = rms_norm(tokens, norm1_gain)
    inner = jnp.einsum('td,dkc->tkc', normed, in_weight, precision=highest)
    conv_in = inner[:, 0]
    gate_in = inner[:, 1]
    taps = conv_weight.shape[0]
    prev_rows = jnp.zeros((taps - 1, conv_in.shape[1]), conv_in.dtype)
    conv_out = conv_mix(conv_in, prev_rows, same_masks, conv_weight, conv_bias)
    projected = matmul(conv_out, xproj_weight)
    start = jnp.zeros(decay_log.shape, conv_out.dtype)
    ssm_out = ssm_pass(conv_out, projected, dt_weight, dt_bias, decay_log, same_masks[1], start)[0]
    gated = (ssm_out + skip_gain * conv_out) * jax.nn.silu(gate_in)
    hidden = tokens + matmul(gated, out_weight)
    second_normed = rms_norm(hidden, norm2_gain)
    probs = jax.nn.softmax(matmul(second_normed, router_weight), axis=-1)
    choose = (expert_index[:, None] == jnp.arange(router_weight.shape[1])[None]).astype(probs.dtype)
    gate = lax.optimization_barrier(jnp.sum(probs * choose, axis=-1)) * dispatched

    def add_expert(total, piece):
        first_matrix, second_matrix, which = piece
        result = matmul(jax.nn.gelu(matmul(second_normed, first_matrix), approximate=False), second_matrix)
        return (total + choose[:, which][:, None] * result, None)
    indices = jnp.arange(router_weight.shape[1])
    total, _ = lax.scan(jax.checkpoint(add_expert), jnp.zeros_like(hidden), (expert_in, expert_out, indices))
    return hidden + gate[:, None] * total

def reference(tokens, norm1_gain, in_weight, conv_weight, conv_bias, xproj_weight, dt_weight, dt_bias, decay_log, skip_gain, out_weight, norm2_gain, router_weight, expert_in, expert_out, segments, expert_ids, cotangent):
    live = segments >= 0
    expert_index = expert_ids[:, 0]
    taps = conv_weight.shape[0]
    seg_ext = jnp.concatenate([jnp.full((taps - 1,), -2, jnp.int32), segments.astype(jnp.int32)])
    same_masks = jnp.stack([seg_ext[taps - 1 - offset:taps - 1 - offset + TOKENS] == segments for offset in range(taps)]).astype(jnp.float32)
    hits = ((expert_index[:, None] == jnp.arange(EXPERTS)[None]) & live[:, None]).astype(jnp.int32)
    ranks = jnp.cumsum(hits.reshape(N_WIDE, TOK_DEV, EXPERTS), axis=1).reshape(TOKENS, EXPERTS) - 1
    own_rank = lax.optimization_barrier(jnp.sum(ranks * hits, axis=-1))
    dispatched = (live & (own_rank < CAP)).astype(jnp.float32)

    def layer(tokens, norm1_gain, in_weight, conv_weight, conv_bias, xproj_weight, dt_weight, dt_bias, decay_log, skip_gain, out_weight, norm2_gain, router_weight, expert_in, expert_out):
        return forward(tokens, norm1_gain, in_weight, conv_weight, conv_bias, xproj_weight, dt_weight, dt_bias, decay_log, skip_gain, out_weight, norm2_gain, router_weight, expert_in, expert_out, same_masks, dispatched, expert_index)
    output, pullback = jax.vjp(layer, tokens, norm1_gain, in_weight, conv_weight, conv_bias, xproj_weight, dt_weight, dt_bias, decay_log, skip_gain, out_weight, norm2_gain, router_weight, expert_in, expert_out)
    grads = pullback(cotangent)
    return (output, grads[0], grads[1], grads[2], grads[3], grads[4], grads[5], grads[6], grads[7], grads[8], grads[9], grads[10], grads[11], grads[12], grads[13], grads[14])
```

```python
import functools

import jax
import jax.numpy as jnp
from jax import lax
from jax.experimental import pallas as pl
from jax.experimental.pallas import tpu as pltpu
from jax.sharding import PartitionSpec as P

EPSILON = 1e-05
SEGMENTS = 8
LANES = 128
NEVER = 1e30
HIGH = lax.Precision.HIGH
VMEM_LIMIT = 48 * 1024 * 1024


def dot(left, right, contract=(1, 0)):
    return lax.dot_general(
        left, right, (((contract[0],), (contract[1],)), ((), ())), precision=HIGH
    )


def interleave(rows):
    length = rows.shape[0]
    split = rows.reshape((SEGMENTS, length // SEGMENTS) + rows.shape[1:])
    return jnp.swapaxes(split, 0, 1).reshape(rows.shape)


def deinterleave(rows):
    length = rows.shape[0]
    split = rows.reshape((length // SEGMENTS, SEGMENTS) + rows.shape[1:])
    return jnp.swapaxes(split, 0, 1).reshape(rows.shape)


def narrow_swap(value, key):
    return lax.ppermute(value, "narrow", [(i, i ^ key) for i in range(4)])


def core_swap(value):
    count = lax.axis_size("wide")
    return lax.ppermute(value, "wide", [(i, i ^ 1) for i in range(count)])


def chip_swap(value, key):
    count = lax.axis_size("wide")
    return lax.ppermute(value, "wide", [(i, i ^ (2 * key)) for i in range(count)])


def wide_shift(value, distance):
    devices = range(lax.axis_size("wide"))
    route = [(i - distance, i) for i in devices if i - distance in devices]
    return lax.ppermute(value, "wide", route)


def pick(stacked, index):
    return lax.dynamic_index_in_dim(stacked, index, 0, keepdims=False)


def narrow_sum(value):
    far = narrow_swap(value, 3)
    return (value + narrow_swap(value, 1)) + (narrow_swap(value, 2) + far)


def narrow_scatter(slices):
    me = lax.axis_index("narrow")
    far = narrow_swap(pick(slices, me ^ 3), 3)
    one = narrow_swap(pick(slices, me ^ 1), 1)
    two = narrow_swap(pick(slices, me ^ 2), 2)
    return (pick(slices, me) + one) + (two + far)


def narrow_gather(value):
    me = lax.axis_index("narrow")
    parts = [value, narrow_swap(value, 1), narrow_swap(value, 2), narrow_swap(value, 3)]
    stacked = jnp.stack(parts)
    return jnp.stack([pick(stacked, me ^ j) for j in range(4)])


def chip_exchange(blocks):
    chips = blocks.shape[0]
    here = lax.axis_index("wide") // 2
    parts = [pick(blocks, here)] + [
        chip_swap(pick(blocks, here ^ key), key) for key in range(1, chips)
    ]
    stacked = jnp.stack(parts)
    return jnp.stack([pick(stacked, here ^ chip) for chip in range(chips)])


def wide_sum(value):
    wide = lax.axis_size("wide")
    me = lax.axis_index("wide")
    rows, columns = value.shape
    levels = wide.bit_length() - 1
    part = value.reshape((2,) * levels + (rows // wide, columns))
    swaps = [core_swap] + [
        functools.partial(chip_swap, key=1 << level) for level in range(levels - 1)
    ]
    bits = [(me >> level) & 1 for level in range(levels)]
    for swap, bit in zip(swaps, bits):
        part = pick(part, bit) + swap(pick(part, 1 - bit))
    for swap, bit in zip(swaps[::-1], bits[::-1]):
        other = swap(part)
        part = jnp.where(bit == 0, jnp.stack([part, other]), jnp.stack([other, part]))
    return part.reshape(rows, columns)


def rows_at(step):
    return pl.ds(pl.multiple_of(step * SEGMENTS, SEGMENTS), SEGMENTS)


def spread(row):
    return jnp.broadcast_to(row, (SEGMENTS, row.shape[-1]))


def chain_pieces(decay, value, backward):
    place = lax.broadcasted_iota(jnp.int32, decay.shape, 0)
    if backward:
        place = SEGMENTS - 1 - place

    def moved(array, distance):
        return pltpu.roll(array, (SEGMENTS - distance) if backward else distance, 0)

    distance = 1
    while distance < SEGMENTS:
        inside = place >= distance
        value = jnp.where(inside, decay * moved(value, distance) + value, value)
        decay = jnp.where(inside, decay * moved(decay, distance), decay)
        distance *= 2
    first = place == 0
    before = jnp.where(first, 0.0, moved(value, 1))
    factor = jnp.where(first, 1.0, moved(decay, 1))
    return factor, before, value


def totals_kernel(states, rank, stepd, drive, coef, rates, entry, total):
    steps = stepd.shape[0] // SEGMENTS
    rate = [spread(rates[n : n + 1, :]) for n in range(states)]

    def body(step, carry):
        current, sums = carry
        rows = rows_at(step)
        width, push, near = stepd[rows, :], drive[rows, :], coef[rows, :]
        current = tuple(
            jnp.exp(width * rate[n]) * current[n] + push * near[:, rank + n : rank + n + 1]
            for n in range(states)
        )
        return current, sums + width

    zero = jnp.zeros((SEGMENTS, LANES), jnp.float32)
    current, sums = lax.fori_loop(0, steps, body, ((zero,) * states, zero), unroll=2)
    for n in range(states):
        factor, before, last = chain_pieces(jnp.exp(sums * rate[n]), current[n], False)
        entry[0, n] = factor
        entry[1, n] = before
        total[n : n + 1, :] = last[SEGMENTS - 1 :, :]
    total[states : states + 1, :] = jnp.sum(sums, axis=0, keepdims=True)


def states_kernel(states, rank, stepd, drive, coef, rates, entry, start, out, kept):
    steps = stepd.shape[0] // SEGMENTS
    rate = [spread(rates[n : n + 1, :]) for n in range(states)]
    current = tuple(entry[0, n] * start[n : n + 1, :] + entry[1, n] for n in range(states))
    for n in range(states):
        kept[0, n] = current[n]

    def body(step, current):
        rows = rows_at(step)
        width, push, near = stepd[rows, :], drive[rows, :], coef[rows, :]
        current = tuple(
            jnp.exp(width * rate[n]) * current[n] + push * near[:, rank + n : rank + n + 1]
            for n in range(states)
        )
        total = None
        for n in range(states):
            kept[step + 1, n] = current[n]
            column = rank + states + n
            term = near[:, column : column + 1] * current[n]
            total = term if total is None else total + term
        out[rows, :] = total
        return current

    lax.fori_loop(0, steps, body, current, unroll=2)


def leaving_kernel(states, rank, stepd, grad, coef, rates, entry, total):
    steps = stepd.shape[0] // SEGMENTS
    rate = [spread(rates[n : n + 1, :]) for n in range(states)]

    def body(back, carry):
        current, sums = carry
        rows = rows_at(steps - 1 - back)
        width, pull, near = stepd[rows, :], grad[rows, :], coef[rows, :]
        column = rank + states
        current = tuple(
            jnp.exp(width * rate[n])
            * (current[n] + pull * near[:, column + n : column + n + 1])
            for n in range(states)
        )
        return current, sums + width

    zero = jnp.zeros((SEGMENTS, LANES), jnp.float32)
    current, sums = lax.fori_loop(0, steps, body, ((zero,) * states, zero), unroll=2)
    for n in range(states):
        factor, before, last = chain_pieces(jnp.exp(sums * rate[n]), current[n], True)
        entry[0, n] = factor
        entry[1, n] = before
        total[n : n + 1, :] = last[:1, :]


def two_parts(value):
    high = value.astype(jnp.bfloat16)
    return high, (value - high.astype(jnp.float32)).astype(jnp.bfloat16)


def adjoint_kernel(
    states, rank, stepd, drive, grad, coef, rates, entry, final, kept,
    grad_push, grad_width, grad_decay, grad_coef, in_terms, out_terms,
):
    steps = stepd.shape[0] // SEGMENTS
    tile, tiles = pl.program_id(0), pl.num_programs(0)
    rate = [spread(rates[n : n + 1, :]) for n in range(states)]
    current = tuple(entry[0, n] * final[n : n + 1, :] + entry[1, n] for n in range(states))

    @pl.when(tile == 0)
    def _():
        in_terms[...] = jnp.zeros_like(in_terms)
        out_terms[...] = jnp.zeros_like(out_terms)

    def body(back, carry):
        current, slopes = carry
        step = steps - 1 - back
        rows = rows_at(step)
        width, push, pull, near = stepd[rows, :], drive[rows, :], grad[rows, :], coef[rows, :]
        later, slope = [], []
        total, width_total = None, None
        for n in range(states):
            column = rank + states + n
            adjoint = near[:, column : column + 1] * pull + current[n]
            decayed = jnp.exp(width * rate[n]) * adjoint
            through = decayed * kept[step, n]
            term = adjoint * near[:, rank + n : rank + n + 1]
            rated = through * rate[n]
            total = term if total is None else total + term
            width_total = rated if width_total is None else width_total + rated
            slope.append(slopes[n] + rated * width)
            later.append(decayed)
            lanes = slice(n * LANES, (n + 1) * LANES)
            in_terms[rows, lanes] += adjoint * push
            out_terms[rows, lanes] += kept[step + 1, n] * pull
        grad_push[rows, :] = total
        grad_width[rows, :] = width_total
        return tuple(later), tuple(slope)

    zero = jnp.zeros((SEGMENTS, LANES), jnp.float32)
    _, slopes = lax.fori_loop(0, steps, body, (current, (zero,) * states))
    for n in range(states):
        grad_decay[n : n + 1, :] = jnp.sum(slopes[n], axis=0, keepdims=True)

    @pl.when(tile == tiles - 1)
    def _():
        shape = (states * LANES, LANES)
        owner = lax.broadcasted_iota(jnp.int32, shape, 0) // LANES
        lane = lax.broadcasted_iota(jnp.int32, shape, 1)
        total = jnp.zeros(grad_coef.shape, jnp.float32)
        for terms, base in ((in_terms, rank), (out_terms, rank + states)):
            ones = (owner + base == lane).astype(jnp.bfloat16)
            for part in two_parts(terms[...]):
                total += jnp.dot(part, ones, preferred_element_type=jnp.float32)
        grad_coef[...] = total


def row_tile(array):
    return pl.BlockSpec((array.shape[0], LANES), lambda tile: (0, tile))


def whole_rows(array):
    return pl.BlockSpec(array.shape, lambda tile: (0, 0))


def deep_tile(shape):
    return pl.BlockSpec(shape[:-1] + (LANES,), lambda tile: (0,) * (len(shape) - 1) + (tile,))


def shape_of(*shape):
    return jax.ShapeDtypeStruct(shape, jnp.float32)


def scan_call(kernel, tiles, in_specs, out_shapes, out_specs, scratch=()):
    return pl.pallas_call(
        kernel,
        grid=(tiles,),
        in_specs=in_specs,
        out_shape=out_shapes,
        out_specs=out_specs,
        scratch_shapes=scratch,
        compiler_params=pltpu.CompilerParams(vmem_limit_bytes=VMEM_LIMIT),
    )


def segment_totals(stepd, drive, coef, rates, rank):
    states, channels = rates.shape
    entry = shape_of(2, states, SEGMENTS, channels)
    total = shape_of(states + 1, channels)
    return scan_call(
        functools.partial(totals_kernel, states, rank),
        channels // LANES,
        [row_tile(stepd), row_tile(drive), whole_rows(coef), row_tile(rates)],
        [entry, total],
        [deep_tile(entry.shape), row_tile(total)],
    )(stepd, drive, coef, rates)


def run_states(stepd, drive, coef, rates, entry, start, rank):
    states, channels = rates.shape
    length = stepd.shape[0]
    out = shape_of(length, channels)
    kept = shape_of(length // SEGMENTS + 1, states, SEGMENTS, channels)
    return scan_call(
        functools.partial(states_kernel, states, rank),
        channels // LANES,
        [row_tile(stepd), row_tile(drive), whole_rows(coef), row_tile(rates),
         deep_tile(entry.shape), row_tile(start)],
        [out, kept],
        [row_tile(out), deep_tile(kept.shape)],
    )(stepd, drive, coef, rates, entry, start)


def leaving_totals(stepd, grad, coef, rates, rank):
    states, channels = rates.shape
    entry = shape_of(2, states, SEGMENTS, channels)
    total = shape_of(states, channels)
    return scan_call(
        functools.partial(leaving_kernel, states, rank),
        channels // LANES,
        [row_tile(stepd), row_tile(grad), whole_rows(coef), row_tile(rates)],
        [entry, total],
        [deep_tile(entry.shape), row_tile(total)],
    )(stepd, grad, coef, rates)


def run_adjoint(stepd, drive, grad, coef, rates, entry, final, kept, rank):
    states, channels = rates.shape
    length = stepd.shape[0]
    rows, slopes = shape_of(length, channels), shape_of(states, channels)
    coefs = shape_of(length, LANES)
    terms = pltpu.VMEM((length, states * LANES), jnp.float32)
    return scan_call(
        functools.partial(adjoint_kernel, states, rank),
        channels // LANES,
        [row_tile(stepd), row_tile(drive), row_tile(grad), whole_rows(coef), row_tile(rates),
         deep_tile(entry.shape), row_tile(final), deep_tile(kept.shape)],
        [rows, rows, slopes, coefs],
        [row_tile(rows), row_tile(rows), row_tile(slopes), whole_rows(coefs)],
        [terms, terms],
    )(stepd, drive, grad, coef, rates, entry, final, kept)


def gather_chips(value):
    chips = lax.axis_size("wide") // 2
    here = lax.axis_index("wide") // 2
    stacked = jnp.stack([value] + [chip_swap(value, key) for key in range(1, chips)])
    return [pick(stacked, here ^ chip) for chip in range(chips)]


def entering_state(total, rates):
    states = rates.shape[0]
    me = lax.axis_index("wide")
    second = (me & 1) == 1
    here = me // 2
    other = core_swap(total)
    early, late = jnp.where(second, other, total), jnp.where(second, total, other)
    early_state, early_sum = early[:states], early[states:]
    late_state, late_sum = late[:states], late[states:]
    chip = jnp.concatenate(
        [jnp.exp(late_sum * rates) * early_state + late_state, early_sum + late_sum]
    )
    chips = gather_chips(chip)
    state = jnp.zeros_like(early_state)
    sums = []
    for place, value in enumerate(chips):
        grown = jnp.exp(value[states:] * rates) * state + value[:states]
        state = jnp.where(place < here, grown, state)
        sums.append(value[states:])
    inner = jnp.exp(early_sum * rates) * state + early_state
    return jnp.where(second, inner, state), (sums, early_sum, late_sum)


def entering_gradient(total, rates, sums):
    chip_sums, early_sum, late_sum = sums
    me = lax.axis_index("wide")
    second = (me & 1) == 1
    here = me // 2
    other = core_swap(total)
    early, late = jnp.where(second, other, total), jnp.where(second, total, other)
    chips = gather_chips(early + jnp.exp(early_sum * rates) * late)
    state = jnp.zeros_like(early)
    for place in reversed(range(len(chips))):
        grown = chips[place] + jnp.exp(chip_sums[place] * rates) * state
        state = jnp.where(place > here, grown, state)
    inner = late + jnp.exp(late_sum * rates) * state
    return jnp.where(second, state, inner)


def to_experts(rows_slice, dispatch_own, dispatch_other, chips):
    own = dot(dispatch_own, rows_slice, (0, 0))
    other = core_swap(dot(dispatch_other, rows_slice, (0, 0)))
    second = (lax.axis_index("wide") & 1) == 1
    pair = jnp.where(
        second, jnp.concatenate([other, own], axis=1), jnp.concatenate([own, other], axis=1)
    )
    arrived = chip_exchange(pair.reshape((chips, -1) + pair.shape[1:]))
    gathered = narrow_gather(arrived.reshape(pair.shape))
    parts, slots, double = gathered.shape
    whole = gathered.reshape(parts, slots, 2, double // 2).transpose(2, 1, 0, 3)
    return whole.reshape(2 * slots, parts * double // 2)


def from_experts(terms, dispatch_own, dispatch_other, chips):
    rows, width = terms.shape
    cut = terms.reshape(2, rows // 2, 4, width // 4).transpose(2, 1, 0, 3)
    mine = narrow_scatter(cut.reshape(4, rows // 2, width // 2))
    back = chip_exchange(mine.reshape((chips, -1) + mine.shape[1:])).reshape(mine.shape)
    second = (lax.axis_index("wide") & 1) == 1
    half = width // 4
    keep = jnp.where(second, back[:, half:], back[:, :half])
    other = core_swap(jnp.where(second, back[:, :half], back[:, half:]))
    return dot(dispatch_own, keep) + dot(dispatch_other, other)


def slices_of(rows):
    length, width = rows.shape
    cut = rows.reshape(2, length // 2, 4, width // 4).transpose(2, 1, 0, 3)
    return cut.reshape(4, length // 2, width // 2)


def slice_rows(packed):
    half, double = packed.shape
    return packed.reshape(half, 2, double // 2).transpose(1, 0, 2).reshape(2 * half, double // 2)


def pack_rows(rows):
    length, width = rows.shape
    return rows.reshape(2, length // 2, width).transpose(1, 0, 2).reshape(length // 2, 2 * width)


def whole_rows_of(gathered):
    parts, half, double = gathered.shape
    whole = gathered.reshape(parts, half, 2, double // 2).transpose(2, 1, 0, 3)
    return whole.reshape(2 * half, parts * double // 2)


def inverse_rms(rows):
    return lax.rsqrt(jnp.mean(rows * rows, axis=-1, keepdims=True) + EPSILON)


def norm_back(rows, inverse, gain, grad):
    scaled = gain * grad
    mean = jnp.mean(rows * scaled, axis=-1, keepdims=True)
    return inverse * scaled - rows * (inverse * inverse * inverse) * mean


def gelu_parts(value):
    spread_of = 0.5 * (1.0 + lax.erf(value * (0.5**0.5)))
    density = jnp.exp(-0.5 * value * value) * ((2.0 * jnp.pi) ** -0.5)
    return value * spread_of, spread_of + value * density


def token_masks(segments, length, taps):
    start = lax.axis_index("wide") * length
    padded = jnp.concatenate([jnp.full((taps - 1,), -2, segments.dtype), segments])
    window = lax.dynamic_slice_in_dim(padded, start, length + taps - 1)
    own = window[taps - 1 :]
    same = [window[taps - 1 - k : taps - 1 - k + length] == own for k in range(taps)]
    return interleave(own), [interleave(mask) for mask in same]


def local(
    tokens, norm1_gain, in_weight, conv_weight, conv_bias, xproj_weight, dt_weight, dt_bias,
    decay_log, skip_gain, out_weight, norm2_gain, router_weight, expert_in, expert_out,
    segments, expert_ids, cotangent,
):
    length, width = tokens.shape
    taps, channels = conv_weight.shape
    experts = router_weight.shape[1]
    capacity = 5 * length // (4 * experts)
    states = decay_log.shape[0]
    rank = dt_weight.shape[0]
    chips = experts // 2
    steps = length // SEGMENTS
    me_wide, me_narrow = lax.axis_index("wide"), lax.axis_index("narrow")
    core = me_wide & 1
    part = width // 4
    halo = 8

    def own_slice(rows):
        return lax.dynamic_slice_in_dim(rows, me_narrow * part, part, axis=1)

    halo_rows = wide_shift(tokens[length - halo :], 1)

    own_seg, same = token_masks(segments, length, taps)
    same_rows = [mask.astype(jnp.float32)[:, None] for mask in same]

    live = own_seg >= 0
    expert_index = interleave(expert_ids[:, 0])
    hits = ((expert_index[:, None] == jnp.arange(experts)[None]) & live[:, None]).astype(
        jnp.bfloat16
    )
    row = jnp.arange(length)
    place = (row % SEGMENTS) * steps + row // SEGMENTS
    earlier = (place[None, :] < place[:, None]).astype(jnp.bfloat16)
    ranks = jnp.dot(earlier, hits, preferred_element_type=jnp.float32)
    own_rank = jnp.sum(ranks * hits.astype(jnp.float32), axis=-1).astype(jnp.int32)
    kept_rows = live & (own_rank < capacity)
    chip_slot = (expert_index // 2) * capacity + own_rank

    def dispatch_for(which):
        wanted = kept_rows & ((expert_index & 1) == which)
        slot = jnp.arange(chips * capacity)[None]
        return ((chip_slot[:, None] == slot) & wanted[:, None]).astype(jnp.float32)

    dispatch_own, dispatch_other = dispatch_for(core), dispatch_for(1 - core)

    rows_in = interleave(tokens)
    grad_rows = interleave(cotangent)

    in_conv, in_gate = in_weight[:, 0], in_weight[:, 1]
    inverse1 = inverse_rms(rows_in)
    normed = rows_in * inverse1 * norm1_gain
    halo_normed = halo_rows * inverse_rms(halo_rows) * norm1_gain
    conv_in = dot(normed, in_conv)
    gate_in = dot(normed, in_gate)
    halo_conv = dot(halo_normed, in_conv)

    conv_steps = conv_in.reshape(steps, SEGMENTS, channels)
    lead = jnp.concatenate(
        [halo_conv[halo - taps + 1 :, None], conv_steps[steps - taps + 1 :, : SEGMENTS - 1]],
        axis=1,
    )
    extended = jnp.concatenate([lead, conv_steps], axis=0)

    def back_by(offset):
        first = taps - 1 - offset
        return extended[first : first + steps].reshape(length, channels)

    mixed = conv_bias[None]
    for offset in range(taps):
        mixed = mixed + conv_weight[offset][None] * back_by(offset) * same_rows[offset]
    mixed_sigmoid = jax.nn.sigmoid(mixed)
    conv_out = mixed * mixed_sigmoid

    projected_t = narrow_sum(dot(xproj_weight, conv_out, (0, 1)))
    projected = projected_t.T
    coef = jnp.pad(projected, ((0, 0), (0, LANES - projected.shape[1])))
    dt_pre = dot(projected_t[:rank], dt_weight, (0, 0)) + dt_bias[None]
    stepsize = jax.nn.softplus(dt_pre)
    rates = -jnp.exp(decay_log)
    drive = stepsize * conv_out
    stepd = jnp.where(same[1][:, None], stepsize, NEVER)

    entry, total = segment_totals(stepd, drive, coef, rates, rank)
    start, sums = entering_state(total, rates)
    ssm_out, kept = run_states(stepd, drive, coef, rates, entry, start, rank)

    gate_sigmoid = jax.nn.sigmoid(gate_in)
    gate_silu = gate_in * gate_sigmoid
    ssm_skip = ssm_out + skip_gain[None] * conv_out
    gated = ssm_skip * gate_silu
    mixer_slice = slice_rows(narrow_scatter(slices_of(dot(gated, out_weight))))
    hidden_slice = own_slice(rows_in) + mixer_slice

    cot_rows = to_experts(own_slice(grad_rows), dispatch_own, dispatch_other, chips)
    hidden_rows = to_experts(hidden_slice, dispatch_own, dispatch_other, chips)
    first_matrix, second_matrix = expert_in[0], expert_out[0]
    raw = dot(cot_rows, second_matrix, (1, 1))
    inverse2 = inverse_rms(hidden_rows)
    second = hidden_rows * inverse2 * norm2_gain
    probs = jax.nn.softmax(dot(second, router_weight), axis=-1)
    chosen = (jnp.arange(experts) == me_wide).astype(jnp.float32)[None]
    gate = jnp.sum(probs * chosen, axis=-1, keepdims=True)
    pre = dot(second, first_matrix)
    act, slope = gelu_parts(pre)
    grad_gate = jnp.sum(act * raw, axis=-1, keepdims=True)
    grad_pre = gate * raw * slope
    grad_logits = grad_gate * gate * (chosen - probs)
    grad_second = dot(grad_pre, first_matrix, (1, 1)) + dot(grad_logits, router_weight, (1, 1))
    grad_hidden_terms = norm_back(hidden_rows, inverse2, norm2_gain, grad_second)
    grad_norm2 = jnp.sum(hidden_rows * inverse2 * grad_second, axis=0)
    grad_router = dot(second, grad_logits, (0, 0))
    grad_expert_in = dot(second, grad_pre, (0, 0))
    grad_expert_out = dot(act, gate * cot_rows, (0, 0))
    value_terms = gate * dot(act, second_matrix)

    hidden_back = from_experts(grad_hidden_terms, dispatch_own, dispatch_other, chips)
    grad_hidden_slice = own_slice(grad_rows) + hidden_back
    grad_hidden = whole_rows_of(narrow_gather(pack_rows(grad_hidden_slice)))

    output_slice = hidden_slice + from_experts(value_terms, dispatch_own, dispatch_other, chips)
    output = deinterleave(whole_rows_of(narrow_gather(pack_rows(output_slice))))

    grad_gated = dot(grad_hidden, out_weight, (1, 1))
    grad_ssm = grad_gated * gate_silu
    grad_gate_in = grad_gated * ssm_skip * (gate_sigmoid * (1.0 + gate_in * (1.0 - gate_sigmoid)))
    grad_skip = jnp.sum(grad_ssm * conv_out, axis=0)
    grad_out_weight = dot(gated, grad_hidden, (0, 0))

    back_entry, back_total = leaving_totals(stepd, grad_ssm, coef, rates, rank)
    final = entering_gradient(back_total, rates, sums)
    grad_push, grad_width, grad_decay_log, grad_coef = run_adjoint(
        stepd, drive, grad_ssm, coef, rates, back_entry, final, kept, rank
    )
    grad_step = grad_push * conv_out + grad_width
    grad_dt_pre = grad_step * jax.nn.sigmoid(dt_pre)
    grad_dt_bias = jnp.sum(grad_dt_pre, axis=0)
    grad_dt_weight = dot(projected_t[:rank], grad_dt_pre)
    grad_projected_t = narrow_sum(
        jnp.concatenate(
            [dot(dt_weight, grad_dt_pre, (1, 1)), grad_coef[:, rank : rank + 2 * states].T]
        )
    )
    grad_conv_out = (
        grad_push * stepsize
        + skip_gain[None] * grad_ssm
        + dot(grad_projected_t, xproj_weight, (0, 1))
    )
    grad_xproj_t = dot(grad_projected_t, conv_out)
    grad_mixed = grad_conv_out * (mixed_sigmoid * (1.0 + mixed * (1.0 - mixed_sigmoid)))
    grad_conv_bias = jnp.sum(grad_mixed, axis=0)
    grad_taps, grad_extended = [], 0.0
    for offset in range(taps):
        masked = grad_mixed * same_rows[offset]
        grad_taps.append(jnp.sum(masked * back_by(offset), axis=0))
        first = taps - 1 - offset
        moved = (conv_weight[offset][None] * masked).reshape(steps, SEGMENTS, channels)
        grad_extended = grad_extended + jnp.pad(moved, ((first, offset), (0, 0), (0, 0)))
    grad_lead = grad_extended[: taps - 1]
    inside = jnp.pad(
        grad_lead[:, 1:], ((steps - taps + 1, 0), (0, 1), (0, 0))
    )
    grad_conv_steps = grad_extended[taps - 1 :] + inside
    grad_halo = jnp.pad(grad_lead[:, 0], ((halo - taps + 1, 0), (0, 0)))
    from_next = wide_shift(grad_halo, -1)[halo - taps + 1 :]
    grad_conv_in = grad_conv_steps.reshape(length, channels)
    grad_conv_all = (
        grad_conv_steps.at[steps - taps + 1 :, SEGMENTS - 1].add(from_next)
    ).reshape(length, channels)
    grad_in_conv = dot(normed, grad_conv_in, (0, 0)) + dot(halo_normed, grad_halo, (0, 0))
    grad_in_gate = dot(normed, grad_gate_in, (0, 0))
    grad_normed = dot(grad_conv_all, in_conv, (1, 1)) + dot(grad_gate_in, in_gate, (1, 1))
    grad_norm1 = jnp.sum(rows_in * inverse1 * grad_normed, axis=0)
    grad_rows_terms = norm_back(rows_in, inverse1, norm1_gain, grad_normed)
    grad_rows_slice = narrow_scatter(slices_of(grad_rows_terms)) + pack_rows(
        own_slice(grad_hidden)
    )
    grad_tokens = deinterleave(whole_rows_of(narrow_gather(grad_rows_slice)))

    shared = jnp.concatenate(
        [grad_norm1.reshape(-1, channels), grad_norm2.reshape(-1, channels),
         grad_router.T.reshape(-1, channels)]
    )
    shared = narrow_sum(shared)
    small = jnp.concatenate(
        [grad_xproj_t, grad_dt_weight, grad_decay_log, jnp.stack(grad_taps),
         grad_conv_bias[None], grad_dt_bias[None], grad_skip[None], shared]
    )
    grain = 8 * lax.axis_size("wide")
    used = small.shape[0]
    small = wide_sum(jnp.pad(small, ((0, -used % grain), (0, 0))))
    grad_out_weight = wide_sum(grad_out_weight)
    grad_in_gate = wide_sum(grad_in_gate)
    grad_in_conv = wide_sum(grad_in_conv)

    at = [0]

    def take(rows):
        at[0] += rows
        return small[at[0] - rows : at[0]]

    sum_xproj = take(rank + 2 * states).T
    sum_dt_weight = take(rank)
    sum_decay = take(states)
    sum_taps = take(taps)
    sum_conv_bias = take(1)[0]
    sum_dt_bias = take(1)[0]
    sum_skip = take(1)[0]
    per = width // channels
    sum_norm1 = take(per).reshape(width)
    sum_norm2 = take(per).reshape(width)
    sum_router = take(per * experts).reshape(experts, width).T
    return (
        output,
        grad_tokens,
        sum_norm1,
        jnp.stack([grad_in_conv, grad_in_gate], axis=1),
        sum_taps,
        sum_conv_bias,
        sum_xproj,
        sum_dt_weight,
        sum_dt_bias,
        sum_decay,
        sum_skip,
        grad_out_weight,
        sum_norm2,
        sum_router,
        grad_expert_in[None],
        grad_expert_out[None],
    )


def solution(mesh):
    in_specs = (
        P("wide", None),
        P(),
        P(None, None, "narrow"),
        P(None, "narrow"),
        P("narrow"),
        P("narrow", None),
        P(None, "narrow"),
        P("narrow"),
        P(None, "narrow"),
        P("narrow"),
        P("narrow", None),
        P(),
        P(),
        P("wide", None, "narrow"),
        P("wide", "narrow", None),
        P(),
        P("wide", None),
        P("wide", None),
    )
    out_specs = (
        P("wide", None),
        P("wide", None),
        P(),
        P(None, None, "narrow"),
        P(None, "narrow"),
        P("narrow"),
        P("narrow", None),
        P(None, "narrow"),
        P("narrow"),
        P(None, "narrow"),
        P("narrow"),
        P("narrow", None),
        P(),
        P(),
        P("wide", None, "narrow"),
        P("wide", "narrow", None),
    )
    return jax.shard_map(local, mesh=mesh, in_specs=in_specs, out_specs=out_specs, check_vma=False)
```

```python
import functools
import math

import jax
import jax.numpy as jnp
from jax import lax
from jax.experimental import pallas as pl
from jax.experimental.pallas import tpu as pltpu
from jax.sharding import PartitionSpec as P

EPSILON = 1e-05
SEGMENTS = 8
LANES = 128
NEVER = 1e30
VMEM_SPARE = 12 * 1024 * 1024
GROUP = 4
LOG2E = 1.4426950408889634


def shape_of(*shape, dtype=jnp.float32):
    return jax.ShapeDtypeStruct(shape, dtype)


def call(kernel, outs, ids, *arrays, scratch=(), flops=0, after=(), in_place=(), out_place=()):
    in_vmem = pl.BlockSpec(memory_space=pltpu.VMEM)
    anywhere = pl.BlockSpec(memory_space=pl.ANY)
    size = lambda a: math.prod(a.shape) * jnp.dtype(a.dtype).itemsize
    sizes = [size(a) for a in (*arrays, *outs)]
    held = [
        size(a)
        for refs, skipped in ((arrays, in_place), (outs, out_place))
        for i, a in enumerate(refs)
        if i not in skipped
    ]
    held += [size(a) for a in scratch if hasattr(a, "dtype") and hasattr(a, "shape")
             and jnp.issubdtype(a.dtype, jnp.number)]
    given = 1 + len(arrays)

    def run(*refs):
        kernel(*refs[:given], *refs[given + len(after) :])

    return pl.pallas_call(
        run,
        out_shape=outs,
        in_specs=[pl.BlockSpec(memory_space=pltpu.SMEM)]
        + [anywhere if i in in_place else in_vmem for i in range(len(arrays))]
        + [anywhere] * len(after),
        out_specs=[anywhere if i in out_place else in_vmem for i in range(len(outs))],
        scratch_shapes=scratch,
        compiler_params=pltpu.CompilerParams(vmem_limit_bytes=sum(held) + VMEM_SPARE),
        cost_estimate=pl.CostEstimate(flops=flops, bytes_accessed=sum(sizes), transcendentals=0),
    )(ids, *arrays, *after)


def two_parts(value):
    high = value.astype(jnp.bfloat16)
    return high, (value - high.astype(jnp.float32)).astype(jnp.bfloat16)


def once(left, right, contract=(1, 0)):
    return lax.dot_general(
        left,
        right,
        (((contract[0],), (contract[1],)), ((), ())),
        preferred_element_type=jnp.float32,
    )


def product(left, right, contract=(1, 0)):
    left_high, left_low = left if isinstance(left, tuple) else two_parts(left)
    right_high, right_low = right if isinstance(right, tuple) else two_parts(right)
    return once(left_high, right_high, contract) + (
        once(left_high, right_low, contract) + once(left_low, right_high, contract)
    )


def select_rows(chosen, rows, contract=(1, 0)):
    high, low = two_parts(rows)
    return once(chosen, high, contract) + once(chosen, low, contract)


def inverse_rms(rows):
    return lax.rsqrt(jnp.mean(rows * rows, axis=-1, keepdims=True) + EPSILON)


def norm_back(rows, inverse, gain, grad):
    scaled = gain * grad
    mean = jnp.mean(rows * scaled, axis=-1, keepdims=True)
    return inverse * scaled - rows * (inverse * inverse * inverse) * mean


def sigmoid(value):
    return 1.0 / (1.0 + jnp.exp(-value))


def softplus(value):
    return jnp.maximum(value, 0.0) + jnp.log1p(jnp.exp(-jnp.abs(value)))


def gelu_parts(value):
    spread_of = 0.5 * (1.0 + lax.erf(value * (0.5**0.5)))
    density = jnp.exp(-0.5 * value * value) * ((2.0 * jnp.pi) ** -0.5)
    return value * spread_of, spread_of + value * density


def cut_slices(me, whole, out):
    rows, part = whole.shape[0] // 2, whole.shape[1] // 4
    for j in range(4):
        out[me ^ j, :, :part] = whole[:rows, part * j : part * (j + 1)]
        out[me ^ j, :, part:] = whole[rows:, part * j : part * (j + 1)]


def join_slices(me, parts, held, whole):
    rows, part = whole.shape[0] // 2, whole.shape[1] // 4
    for key, value in enumerate(parts):
        held[key] = value[...]
    for j in range(4):
        value = held[me ^ j]
        whole[:rows, part * j : part * (j + 1)] = value[:, :part]
        whole[rows:, part * j : part * (j + 1)] = value[:, part:]


def reversed_bits(value, levels):
    place = 0
    for level in range(levels):
        place = place + (((value >> level) & 1) << (levels - 1 - level))
    return place


def interleave_from(rows, held, out):
    length, width = out.shape
    steps = length // SEGMENTS
    for tile in range(width // LANES):
        lanes = slice(tile * LANES, (tile + 1) * LANES)
        held[tile] = rows[:, lanes]
        for step in range(steps):
            out[step * SEGMENTS : (step + 1) * SEGMENTS, lanes] = held[
                tile, pl.ds(step, SEGMENTS, stride=steps), :
            ]


def deinterleave_to(rows, held, out):
    length, width = rows.shape
    steps = length // SEGMENTS
    for tile in range(width // LANES):
        lanes = slice(tile * LANES, (tile + 1) * LANES)
        for step in range(steps):
            held[tile, pl.ds(step, SEGMENTS, stride=steps), :] = rows[
                step * SEGMENTS : (step + 1) * SEGMENTS, lanes
            ]
        out[:, lanes] = held[tile]


def narrow_swap(value, key):
    return lax.ppermute(value, "narrow", [(i, i ^ key) for i in range(4)])


def core_swap(value):
    count = lax.axis_size("wide")
    return lax.ppermute(value, "wide", [(i, i ^ 1) for i in range(count)])


def chip_swap(value, key):
    count = lax.axis_size("wide")
    return lax.ppermute(value, "wide", [(i, i ^ (2 * key)) for i in range(count)])


def wide_shift(value, distance):
    devices = range(lax.axis_size("wide"))
    route = [(i - distance, i) for i in devices if i - distance in devices]
    return lax.ppermute(value, "wide", route)


def narrow_all(value):
    far = narrow_swap(value, 3)
    return [value, narrow_swap(value, 1), narrow_swap(value, 2), far]


def narrow_each(slices):
    far = narrow_swap(slices[3], 3)
    return [slices[0], narrow_swap(slices[1], 1), narrow_swap(slices[2], 2), far]


def pair_sum(parts):
    while len(parts) > 1:
        parts = [a + b for a, b in zip(parts[::2], parts[1::2])]
    return parts[0]


def chip_each(blocks, chips):
    rows = blocks.shape[0] // chips
    order = sorted(range(1, chips), reverse=True)
    arrived = {k: chip_swap(blocks[k * rows : (k + 1) * rows], k) for k in order}
    arrived[0] = blocks[:rows]
    return jnp.concatenate([arrived[k] for k in range(chips)])


def chip_all(value, chips):
    arrived = {k: chip_swap(value, k) for k in sorted(range(1, chips), reverse=True)}
    arrived[0] = value
    return [arrived[k] for k in range(chips)]


def wide_sum(keep, send):
    levels = lax.axis_size("wide").bit_length() - 1
    swaps = [core_swap] + [
        functools.partial(chip_swap, key=1 << level) for level in range(levels - 1)
    ]
    arrived = [swaps[0](send)]
    for swap in swaps[1:]:
        half = keep.shape[0] // 2
        other = arrived[-1]
        send, keep = keep[half:] + other[half:], keep[:half] + other[:half]
        arrived.append(swap(send))
    part = keep + arrived[-1]
    for swap in swaps[::-1]:
        arrived.append(swap(part))
        part = jnp.concatenate([part, arrived[-1]])
    return part, arrived


def route_kernel(capacity, ids, segments, expert_ids, marks, slots_own, slots_other,
                 rows_own, rows_other):
    wide_at, core, chip = ids[1], ids[2], ids[3]
    experts = segments.shape[0]
    length = segments.shape[1]
    steps = length // SEGMENTS
    own = segments[pl.ds(wide_at, 1), :]
    before = segments[pl.ds(jnp.maximum(wide_at - 1, 0), 1), :]
    lane = lax.broadcasted_iota(jnp.int32, (1, length), 1)
    here = lax.broadcasted_iota(jnp.int32, (SEGMENTS, length), 0)
    table = jnp.ones((SEGMENTS, length), jnp.float32)
    for k in range(1, 4):
        back = jnp.where(lane < k, pltpu.roll(before, k, 1), pltpu.roll(own, k, 1))
        same = (back == own) & ((lane >= k) | (wide_at > 0))
        table = jnp.where(here == k, jnp.where(same, 1.0, 0.0), table)
    live = own >= 0
    expert = expert_ids[...]
    at = lax.broadcasted_iota(jnp.int32, (experts, length), 0)
    hits = jnp.where((at == expert) & live, 1.0, 0.0)
    first = lax.broadcasted_iota(jnp.int32, (length, length), 0)
    second = lax.broadcasted_iota(jnp.int32, (length, length), 1)
    earlier = jnp.where(first < second, 1.0, 0.0).astype(jnp.bfloat16)
    ranks = once(hits.astype(jnp.bfloat16), earlier)
    rank = jnp.sum(ranks * hits, axis=0, keepdims=True).astype(jnp.int32)
    kept = live & (rank < capacity)
    order = jnp.where(
        (first % SEGMENTS) * steps + first // SEGMENTS == second, 1.0, 0.0
    ).astype(jnp.bfloat16)
    marks[...] = once(order, table.astype(jnp.bfloat16), (1, 1))
    slot = jnp.where(kept, ((expert >> 1) ^ chip) * capacity + rank, -1)
    count = slots_own.shape[0]
    slot_at = lax.broadcasted_iota(jnp.int32, (count, length), 0)
    for which, slots, rows in ((core, slots_own, rows_own), (1 - core, slots_other, rows_other)):
        mine = (slot_at == slot) & ((expert & 1) == which)
        chosen = jnp.where(mine, 1.0, 0.0).astype(jnp.bfloat16)
        slots[...] = once(chosen, order, (1, 1)).astype(jnp.bfloat16)
        rows[...] = once(order, chosen, (1, 1)).astype(jnp.bfloat16)


def front_kernel(ids, tokens, gain, weight, rows, normed, conv_in, gate_in,
                 conv_high, conv_low, gate_high, gate_low, held):
    interleave_from(tokens, held, rows)
    value = rows[...]
    scaled = value * inverse_rms(value) * gain[...]
    normed[...] = scaled
    parts = two_parts(scaled)
    for k, (high, low, out) in enumerate(
        ((conv_high, conv_low, conv_in), (gate_high, gate_low, gate_in))
    ):
        high[...], low[...] = two_parts(weight[:, k, :])
        out[...] = product(parts, (high[...], low[...]))


def slices_kernel(ids, rows, cotangent, slots_own, slots_other,
                  rows_slice, cot_slice, own, other, cot_rows, held):
    me, core = ids[0], ids[2]
    interleave_from(cotangent, held, cot_rows)
    half, part = rows.shape[0] // 2, rows.shape[1] // 4
    for source, out in ((rows, rows_slice), (cot_rows, cot_slice)):
        for j in range(4):
            @pl.when(me == j)
            def _():
                out[:, :part] = source[:half, part * j : part * (j + 1)]
                out[:, part:] = source[half:, part * j : part * (j + 1)]
    send_slots(core, cot_slice[...], slots_own[...], slots_other[...], own, other)


def send_slots(core, packed, slots_own, slots_other, own, other):
    half = packed.shape[1] // 2
    lane = lax.broadcasted_iota(jnp.int32, packed.shape, 1)
    left = jnp.where(lane < half, packed, 0.0)
    right = jnp.where(lane < half, 0.0, packed)
    second = core == 1
    top = jnp.where(second, pltpu.roll(left, half, 1), left)
    bottom = jnp.where(second, right, pltpu.roll(right, half, 1))
    placed = jnp.concatenate([top, bottom])
    own[...] = select_rows(slots_own, placed)
    other[...] = select_rows(slots_other, placed)


def conv_kernel(ids, halo, gain, conv_high, conv_low, conv_in, marks, conv_weight, conv_bias,
                xproj_t, mixed, conv_out, partial, extended, halo_normed):
    taps, channels = conv_weight.shape
    length = conv_in.shape[0]
    lead = (taps - 1) * SEGMENTS
    rows = halo[...]
    scaled = rows * inverse_rms(rows) * gain[...]
    halo_normed[...] = scaled
    halo_conv = product(scaled, (conv_high[...], conv_low[...]))
    place = lax.broadcasted_iota(jnp.int32, (SEGMENTS, channels), 0)
    for m in range(taps - 1):
        ends = conv_in[length - lead + m * SEGMENTS : length - lead + (m + 1) * SEGMENTS, :]
        at = SEGMENTS - taps + 1 + m
        extended[m * SEGMENTS : (m + 1) * SEGMENTS, :] = jnp.where(
            place == 0, halo_conv[at : at + 1, :], pltpu.roll(ends, 1, 0)
        )
    extended[lead:, :] = conv_in[...]
    total = jnp.broadcast_to(conv_bias[...], (length, channels))
    for k in range(taps):
        first = (taps - 1 - k) * SEGMENTS
        total += conv_weight[k : k + 1, :] * extended[first : first + length, :] * marks[:, k : k + 1]
    mixed[...] = total
    out = total * sigmoid(total)
    conv_out[...] = out
    partial[...] = product(xproj_t[...], out, (1, 1))


def rows_at(step):
    return pl.ds(pl.multiple_of(step * SEGMENTS, SEGMENTS), SEGMENTS)


def spread(row):
    return jnp.broadcast_to(row, (SEGMENTS, row.shape[-1]))


def column_of(rows, column):
    return jnp.broadcast_to(rows[:, column : column + 1], (SEGMENTS, LANES))


def sweep(count, body, carry):
    return lax.fori_loop(0, count, body, carry, unroll=True)


def add_to(ref, first, rows, lanes, value):
    if first:
        ref[rows, lanes] = value
    else:
        ref[rows, lanes] += value


def chain_pieces(decay, value, backward):
    place = lax.broadcasted_iota(jnp.int32, decay.shape, 0)
    if backward:
        place = SEGMENTS - 1 - place

    def moved(array, distance):
        return pltpu.roll(array, (SEGMENTS - distance) if backward else distance, 0)

    distance = 1
    while distance < SEGMENTS:
        inside = place >= distance
        value = jnp.where(inside, decay * moved(value, distance) + value, value)
        decay = jnp.where(inside, decay * moved(decay, distance), decay)
        distance *= 2
    first = place == 0
    before = jnp.where(first, 0.0, moved(value, 1))
    factor = jnp.where(first, 1.0, moved(decay, 1))
    return factor, before, value


def totals_kernel(ids, p0, p1, p2, p3, dt_weight, dt_bias, decay_log, conv_out, marks,
                  coef, dt_pre, stepsize, drive, stepd, rates, entry, total, padded):
    states, channels = decay_log.shape
    rank = dt_weight.shape[0]
    length = conv_out.shape[0]
    steps = length // SEGMENTS
    projected = (p0[...] + p1[...]) + (p2[...] + p3[...])
    missing = LANES - projected.shape[0]
    coef[...] = jnp.concatenate([projected, jnp.zeros((missing, length), jnp.float32)]).T
    padded[...] = jnp.zeros_like(padded)
    padded[:rank, :] = dt_weight[...]
    pre = product(coef[...], padded[...]) + dt_bias[...]
    dt_pre[...] = pre
    size = softplus(pre)
    stepsize[...] = size
    drive[...] = size * conv_out[...]
    stepd[...] = jnp.where(marks[:, 1:2] > 0.5, size, NEVER)
    rates[...] = -jnp.exp(decay_log[...])
    total[...] = jnp.zeros_like(total)
    zero = jnp.zeros((SEGMENTS, LANES), jnp.float32)
    tiles = [slice(at, at + LANES) for at in range(0, channels, LANES)]
    sums = [zero] * len(tiles)
    for step in range(steps):
        rows = slice(step * SEGMENTS, (step + 1) * SEGMENTS)
        sums = [value + stepd[rows, lanes] for value, lanes in zip(sums, tiles)]
    for value, lanes in zip(sums, tiles):
        total[states : states + 1, lanes] = jnp.sum(value, axis=0, keepdims=True)
    for group in range(0, states, GROUP):
        names = range(group, group + GROUP)
        rate = [[spread(rates[n : n + 1, lanes] * LOG2E) for lanes in tiles] for n in names]

        def body(step, current):
            rows = rows_at(step)
            near = coef[rows, :]
            width = [stepd[rows, lanes] for lanes in tiles]
            push = [drive[rows, lanes] for lanes in tiles]
            later = []
            for at, n in enumerate(names):
                entering = column_of(near, rank + n)
                later.append(tuple(
                    jnp.exp2(width[t] * rate[at][t]) * current[at][t] + push[t] * entering
                    for t in range(len(tiles))
                ))
            return tuple(later)

        current = sweep(steps, body, ((zero,) * len(tiles),) * GROUP)
        for at, n in enumerate(names):
            for t, lanes in enumerate(tiles):
                decay = jnp.exp2(sums[t] * rate[at][t])
                factor, before, last = chain_pieces(decay, current[at][t], False)
                entry[0, n, :, lanes] = factor
                entry[1, n, :, lanes] = before
                total[n : n + 1, lanes] = last[SEGMENTS - 1 :, :]


def states_kernel(rank, ids, stepd, drive, coef, rates, entry, early, conv_out, gate_in, skip,
                  out_weight, *rest):
    chips = len(rest) - 8
    totals = rest[:chips]
    ssm_skip, gated, slices, kept, held, whole, kept_here, sems = rest[chips:]
    me, core, here = ids[0], ids[2], ids[3]
    states, channels = rates.shape
    length = stepd.shape[0]
    steps = length // SEGMENTS
    for key, value in enumerate(totals):
        held[key] = value[...]
    state = jnp.zeros((states, channels), jnp.float32)
    for chip in range(chips):
        value = held[here ^ chip]
        grown = jnp.exp(value[states : states + 1] * rates[...]) * state + value[:states]
        state = jnp.where(chip < here, grown, state)
    inner = jnp.exp(early[states : states + 1, :] * rates[...]) * state + early[:states, :]
    start = jnp.where(core == 1, inner, state)
    tiles = [slice(at, at + LANES) for at in range(0, channels, LANES)]
    copies = []
    for group in range(0, states, GROUP):
        names = range(group, group + GROUP)
        slab = group // GROUP
        rate = [[spread(rates[n : n + 1, lanes] * LOG2E) for lanes in tiles] for n in names]
        current = tuple(
            tuple(
                entry[0, n, :, lanes] * start[n : n + 1, lanes] + entry[1, n, :, lanes]
                for lanes in tiles
            )
            for n in names
        )
        for at in range(GROUP):
            for t, lanes in enumerate(tiles):
                kept_here[slab, 0, at, :, lanes] = current[at][t]

        def body(step, current):
            rows = rows_at(step)
            near = coef[rows, :]
            width = [stepd[rows, lanes] for lanes in tiles]
            push = [drive[rows, lanes] for lanes in tiles]
            later, total = [], [None] * len(tiles)
            for at, n in enumerate(names):
                entering, leaving = column_of(near, rank + n), column_of(near, rank + states + n)
                new = []
                for t, lanes in enumerate(tiles):
                    decay = jnp.exp2(width[t] * rate[at][t])
                    new.append(decay * current[at][t] + push[t] * entering)
                    kept_here[slab, step + 1, at, :, lanes] = new[t]
                    term = leaving * new[t]
                    total[t] = term if total[t] is None else total[t] + term
                later.append(tuple(new))
            for t, lanes in enumerate(tiles):
                add_to(ssm_skip, group == 0, rows, lanes, total[t])
            return tuple(later)

        sweep(steps, body, current)
        copies.append(pltpu.make_async_copy(kept_here.at[slab], kept.at[slab], sems.at[slab]))
        copies[-1].start()
    skipped = ssm_skip[...] + skip[...] * conv_out[...]
    ssm_skip[...] = skipped
    gate = gate_in[...]
    out = skipped * gate * sigmoid(gate)
    gated[...] = out
    whole[...] = product(out, out_weight[...])
    cut_slices(me, whole, slices)
    for copy in copies:
        copy.wait()


def dispatch_kernel(ids, s0, s1, s2, s3, rows_slice, slots_own, slots_other,
                    hidden, own, other):
    packed = (s0[...] + s1[...]) + (s2[...] + s3[...]) + rows_slice[...]
    hidden[...] = packed
    send_slots(ids[2], packed, slots_own[...], slots_other[...], own, other)


def raw_kernel(ids, c0, c1, c2, c3, expert_in, expert_out, raw, cot, in_high, in_low,
               out_high, out_low, held):
    join_slices(ids[0], (c0, c1, c2, c3), held, cot)
    in_high[...], in_low[...] = two_parts(expert_in[...])
    out_high[...], out_low[...] = two_parts(expert_out[...])
    raw[...] = product(cot[...], (out_high[...], out_low[...]), (1, 1))


def expert_kernel(ids, h0, h1, h2, h3, raw, in_high, in_low, norm_gain, router_t,
                  slices, second, act, grad_pre, gates, grad_logits, grad_gain,
                  held, whole):
    me, expert = ids[0], ids[1]
    join_slices(me, (h0, h1, h2, h3), held, whole)
    rows = whole[...]
    inverse = inverse_rms(rows)
    normed = rows * inverse * norm_gain[...]
    second[...] = normed
    normed_parts = two_parts(normed)
    router_parts = two_parts(router_t[...])
    weight = (in_high[...], in_low[...])
    logits = product(normed_parts, router_parts, (1, 1))
    logits = logits - jnp.max(logits, axis=-1, keepdims=True)
    powers = jnp.exp(logits)
    probs = powers / jnp.sum(powers, axis=-1, keepdims=True)
    chosen = jnp.where(
        lax.broadcasted_iota(jnp.int32, logits.shape, 1) == expert, 1.0, 0.0
    )
    gate = jnp.sum(probs * chosen, axis=-1, keepdims=True)
    gates[...] = gate
    hidden_act, slope = gelu_parts(product(normed_parts, weight))
    act[...] = hidden_act
    raws = raw[...]
    grad_gate = jnp.sum(hidden_act * raws, axis=-1, keepdims=True)
    grads = gate * raws * slope
    grad_pre[...] = grads
    logit_grads = grad_gate * gate * (chosen - probs)
    grad_logits[...] = logit_grads
    grad_second = product(grads, weight, (1, 1)) + product(logit_grads, router_parts)
    grad_gain[...] = jnp.sum(rows * inverse * grad_second, axis=0, keepdims=True)
    whole[...] = norm_back(rows, inverse, norm_gain[...], grad_second)
    cut_slices(me, whole, slices)


def expert_rest_kernel(ids, second, act, grad_pre, gates, grad_logits, cot, out_high, out_low,
                       slices, grad_in, grad_out, grad_router, whole):
    gate = gates[...]
    acts = two_parts(act[...])
    normed = two_parts(second[...])
    whole[...] = gate * product(acts, (out_high[...], out_low[...]))
    cut_slices(ids[0], whole, slices)
    grad_out[...] = product(acts, gate * cot[...], (0, 0))
    grad_in[...] = product(normed, grad_pre[...], (0, 0))
    grad_router[...] = product(grad_logits[...], normed, (0, 0))


def home_kernel(ids, own, other, base, rows_own, rows_other, out):
    half = own.shape[1] // 2
    second = ids[2] == 1

    def mine(rows):
        return jnp.where(second, pltpu.roll(rows, half, 1), rows)

    total = select_rows(rows_own[...], mine(own[...])) + select_rows(
        rows_other[...], mine(other[...])
    )
    count = base.shape[0]
    lane = lax.broadcasted_iota(jnp.int32, base.shape, 1)
    out[...] = base[...] + jnp.where(
        lane < half, total[:count], pltpu.roll(total[count:], half, 1)
    )


def whole_kernel(ids, p0, p1, p2, p3, out, held, whole, tiles):
    join_slices(ids[0], (p0, p1, p2, p3), held, whole)
    deinterleave_to(whole, tiles, out)


def leaving_kernel(rank, ids, g0, g1, g2, g3, out_weight, gate_in, ssm_skip, conv_out, stepd,
                   coef, rates, grad_hidden, grad_ssm, grad_gate_in, grad_skip, entry, total,
                   held):
    join_slices(ids[0], (g0, g1, g2, g3), held, grad_hidden)
    states, channels = rates.shape
    length = stepd.shape[0]
    steps = length // SEGMENTS
    grad_gated = product(grad_hidden[...], out_weight[...], (1, 1))
    gate = gate_in[...]
    gate_sigmoid = sigmoid(gate)
    pulled = grad_gated * gate * gate_sigmoid
    grad_ssm[...] = pulled
    grad_gate_in[...] = grad_gated * ssm_skip[...] * (
        gate_sigmoid * (1.0 + gate * (1.0 - gate_sigmoid))
    )
    grad_skip[...] = jnp.sum(pulled * conv_out[...], axis=0, keepdims=True)
    zero = jnp.zeros((SEGMENTS, LANES), jnp.float32)
    tiles = [slice(at, at + LANES) for at in range(0, channels, LANES)]
    sums = [zero] * len(tiles)
    for step in range(steps):
        rows = slice(step * SEGMENTS, (step + 1) * SEGMENTS)
        sums = [value + stepd[rows, lanes] for value, lanes in zip(sums, tiles)]
    for group in range(0, states, GROUP):
        names = range(group, group + GROUP)
        rate = [[spread(rates[n : n + 1, lanes] * LOG2E) for lanes in tiles] for n in names]

        def body(back, current):
            rows = rows_at(steps - 1 - back)
            near = coef[rows, :]
            width = [stepd[rows, lanes] for lanes in tiles]
            pull = [grad_ssm[rows, lanes] for lanes in tiles]
            later = []
            for at, n in enumerate(names):
                leaving = column_of(near, rank + states + n)
                later.append(tuple(
                    jnp.exp2(width[t] * rate[at][t]) * (current[at][t] + pull[t] * leaving)
                    for t in range(len(tiles))
                ))
            return tuple(later)

        current = sweep(steps, body, ((zero,) * len(tiles),) * GROUP)
        for at, n in enumerate(names):
            for t, lanes in enumerate(tiles):
                decay = jnp.exp2(sums[t] * rate[at][t])
                factor, before, last = chain_pieces(decay, current[at][t], True)
                entry[0, n, :, lanes] = factor
                entry[1, n, :, lanes] = before
                total[n : n + 1, lanes] = last[:1, :]


def adjoint_kernel(rank, chips, ids, stepd, drive, grad, coef, rates, entry, kept, early, late,
                   late_total, conv_out, stepsize, dt_pre, skip, dt_weight, *rest):
    sums, totals = rest[:chips], rest[chips : 2 * chips]
    (partial, grad_direct, grad_dt_pre, grad_decay, grad_dt_bias, held_sums, held, kept_here,
     in_terms, out_terms, grad_push, grad_width, sems) = rest[2 * chips :]
    core, here = ids[2], ids[3]
    states, channels = rates.shape
    length = stepd.shape[0]
    steps = length // SEGMENTS
    copies = [
        pltpu.make_async_copy(kept.at[slab], kept_here.at[slab], sems.at[slab])
        for slab in range(states // GROUP)
    ]
    for copy in copies:
        copy.start()
    for key in range(chips):
        held_sums[key] = sums[key][states : states + 1, :]
        held[key] = totals[key][...]
    state = jnp.zeros((states, channels), jnp.float32)
    for chip in reversed(range(chips)):
        grown = held[here ^ chip] + jnp.exp(held_sums[here ^ chip] * rates[...]) * state
        state = jnp.where(chip > here, grown, state)
    inner = late_total[...] + jnp.exp(late[states : states + 1, :] * rates[...]) * state
    final = jnp.where(core == 1, state, inner)
    zero = jnp.zeros((SEGMENTS, LANES), jnp.float32)
    tiles = [slice(at, at + LANES) for at in range(0, channels, LANES)]
    for group in range(0, states, GROUP):
        names = range(group, group + GROUP)
        slab = group // GROUP
        rate = [[spread(rates[n : n + 1, lanes]) for lanes in tiles] for n in names]
        current = tuple(
            tuple(
                entry[0, n, :, lanes] * final[n : n + 1, lanes] + entry[1, n, :, lanes]
                for lanes in tiles
            )
            for n in names
        )
        copies[slab].wait()

        def body(back, carry):
            current, slopes = carry
            step = steps - 1 - back
            rows = rows_at(step)
            near = coef[rows, :]
            width = [stepd[rows, lanes] for lanes in tiles]
            push = [drive[rows, lanes] for lanes in tiles]
            pull = [grad[rows, lanes] for lanes in tiles]
            later, slope = [], []
            total, width_total = [None] * len(tiles), [None] * len(tiles)
            for at, n in enumerate(names):
                entering, leaving = column_of(near, rank + n), column_of(near, rank + states + n)
                new, turned, in_term, out_term = [], [], None, None
                for t, lanes in enumerate(tiles):
                    adjoint = leaving * pull[t] + current[at][t]
                    decayed = jnp.exp2(width[t] * (rate[at][t] * LOG2E)) * adjoint
                    through = decayed * kept_here[slab, step, at, :, lanes]
                    term, rated = adjoint * entering, through * rate[at][t]
                    total[t] = term if total[t] is None else total[t] + term
                    width_total[t] = rated if width_total[t] is None else width_total[t] + rated
                    new.append(decayed)
                    turned.append(slopes[at][t] + through * width[t])
                    term = adjoint * push[t]
                    in_term = term if in_term is None else in_term + term
                    term = kept_here[slab, step + 1, at, :, lanes] * pull[t]
                    out_term = term if out_term is None else out_term + term
                place = slice(n * LANES, (n + 1) * LANES)
                in_terms[rows, place] = in_term
                out_terms[rows, place] = out_term
                later.append(tuple(new))
                slope.append(tuple(turned))
            for t, lanes in enumerate(tiles):
                add_to(grad_push, group == 0, rows, lanes, total[t])
                add_to(grad_width, group == 0, rows, lanes, width_total[t])
            return tuple(later), tuple(slope)

        none = ((zero,) * len(tiles),) * GROUP
        _, slopes = sweep(steps, body, (current, none))
        for at, n in enumerate(names):
            for t, lanes in enumerate(tiles):
                grad_decay[n : n + 1, lanes] = rates[n : n + 1, lanes] * jnp.sum(
                    slopes[at][t], axis=0, keepdims=True
                )
    pushed = grad_push[...]
    grads = (pushed * conv_out[...] + grad_width[...]) * sigmoid(dt_pre[...])
    grad_dt_pre[...] = grads
    grad_dt_bias[...] = jnp.sum(grads, axis=0, keepdims=True)
    grad_direct[...] = pushed * stepsize[...] + skip[...] * grad[...]
    partial[:rank, :] = product(dt_weight[...], grads, (1, 1))
    shape = (2 * states, states * LANES)
    column = lax.broadcasted_iota(jnp.int32, shape, 0)
    owner = lax.broadcasted_iota(jnp.int32, shape, 1) // LANES
    total = None
    for terms, base in ((in_terms, 0), (out_terms, states)):
        ones = jnp.where(owner + base == column, 1.0, 0.0).astype(jnp.bfloat16)
        for part in two_parts(terms[...]):
            term = once(ones, part, (1, 1))
            total = term if total is None else total + term
    partial[rank:, :] = total


def conv_back_kernel(ids, p0, p1, p2, p3, xproj_t, grad_direct, mixed, conv_out, extended, marks,
                     conv_weight, coef, grad_dt_pre, grad_decay, grad_dt_bias, grad_skip,
                     grad_conv, grad_halo, small, grad_extended):
    taps, channels = conv_weight.shape
    cols, states = xproj_t.shape[0], grad_decay.shape[0]
    rank = cols - 2 * states
    length = mixed.shape[0]
    lead = (taps - 1) * SEGMENTS
    projected = two_parts((p0[...] + p1[...]) + (p2[...] + p3[...]))
    grad_out = grad_direct[...] + product(projected, xproj_t[...], (0, 0))
    value = mixed[...]
    value_sigmoid = sigmoid(value)
    grad_mixed = grad_out * (value_sigmoid * (1.0 + value * (1.0 - value_sigmoid)))
    grad_extended[...] = jnp.zeros_like(grad_extended)
    first_tap = cols + rank + states
    small[first_tap:, :] = jnp.zeros((small.shape[0] - first_tap, channels), jnp.float32)
    for k in range(taps):
        first = (taps - 1 - k) * SEGMENTS
        masked = grad_mixed * marks[:, k : k + 1]
        small[first_tap + k : first_tap + k + 1, :] = jnp.sum(
            masked * extended[first : first + length, :], axis=0, keepdims=True
        )
        grad_extended[first : first + length, :] += conv_weight[k : k + 1, :] * masked
    grad_conv[...] = grad_extended[lead:, :]
    grad_halo[...] = jnp.zeros_like(grad_halo)
    place = lax.broadcasted_iota(jnp.int32, (SEGMENTS, channels), 0)
    for m in range(taps - 1):
        rows = grad_extended[m * SEGMENTS : (m + 1) * SEGMENTS, :]
        at = SEGMENTS - taps + 1 + m
        grad_halo[at : at + 1, :] = rows[:1, :]
        inside = jnp.where(place == SEGMENTS - 1, 0.0, pltpu.roll(rows, SEGMENTS - 1, 0))
        ends = slice(length - lead + m * SEGMENTS, length - lead + (m + 1) * SEGMENTS)
        grad_conv[ends, :] += inside
    small[:cols, :] = product(projected, conv_out[...])
    low = product(coef[...], grad_dt_pre[...], (0, 0))
    small[cols : cols + rank, :] = low[:rank, :]
    small[cols + rank : first_tap, :] = grad_decay[...]
    last = first_tap + taps
    small[last : last + 1, :] = jnp.sum(grad_mixed, axis=0, keepdims=True)
    small[last + 1 : last + 2, :] = grad_dt_bias[...]
    small[last + 2 : last + 3, :] = grad_skip[...]


def early_weights_kernel(ids, gated, grad_hidden, normed, grad_gate_in, keep, send,
                         whole, gate):
    channels = gated.shape[1]
    halves = product(gated[...], grad_hidden[...], (0, 0))
    whole[:channels, :] = halves[:, :channels]
    whole[channels:, :] = halves[:, channels:]
    gate[...] = product(normed[...], grad_gate_in[...], (0, 0))
    in_order(ids[1], (whole, gate), keep, send)


def in_order(me, wholes, keep, send):
    count = 2 * keep.shape[0]
    levels = count.bit_length() - 1
    for place in range(count):
        block = reversed_bits(place, levels) ^ me
        out, at = (keep, place) if place < count // 2 else (send, place - count // 2)
        first = 0
        for whole in wholes:
            rows = whole.shape[0] // count
            from_row = pl.multiple_of(block * rows, 8)
            out[at, first : first + rows, :] = whole[pl.ds(from_row, rows), :]
            first += rows


def conv_weights_kernel(ids, normed, grad_conv, halo_normed, grad_halo, small, keep, send,
                        whole):
    whole[...] = product(normed[...], grad_conv[...], (0, 0)) + product(
        halo_normed[...], grad_halo[...], (0, 0)
    )
    in_order(ids[1], (whole, small), keep, send)


def gate_tokens_kernel(ids, grad_gate_in, gate_high, gate_low, out):
    out[...] = product(grad_gate_in[...], (gate_high[...], gate_low[...]), (1, 1))


def tokens_kernel(taps, ids, grad_conv, from_next, conv_high, conv_low, gate_part, rows, gain,
                  slices, grad_gain, held, whole):
    length, channels = grad_conv.shape
    lead = (taps - 1) * SEGMENTS
    held[...] = grad_conv[...]
    for m in range(taps - 1):
        row = length - lead + (m + 1) * SEGMENTS - 1
        at = SEGMENTS - taps + 1 + m
        held[row : row + 1, :] += from_next[at : at + 1, :]
    grad = product(held[...], (conv_high[...], conv_low[...]), (1, 1)) + gate_part[...]
    value = rows[...]
    inverse = inverse_rms(value)
    grad_gain[...] = jnp.sum(value * inverse * grad, axis=0, keepdims=True)
    whole[...] = norm_back(value, inverse, gain[...], grad)
    cut_slices(ids[0], whole, slices)


def early_out_kernel(ids, summed, out_weight):
    count, rows = summed.shape[0], summed.shape[1] // 2
    levels = count.bit_length() - 1
    channels = summed.shape[2]
    for block in range(count):
        value = summed[reversed_bits(block ^ ids[1], levels), :rows, :]
        half, row = divmod(block * rows, channels)
        out_weight[row : row + rows, half * channels : (half + 1) * channels] = value


def weights_out_kernel(ids, early, late, weight, small):
    count, rows = early.shape[0], early.shape[1] // 2
    more = late.shape[1] - rows
    levels = count.bit_length() - 1
    for block in range(count):
        place = reversed_bits(block ^ ids[1], levels)
        small[block * more : (block + 1) * more, :] = late[place, rows:, :]
        weight[block * rows : (block + 1) * rows, 0, :] = late[place, :rows, :]
        weight[block * rows : (block + 1) * rows, 1, :] = early[place, rows:, :]


def local(
    tokens, norm1_gain, in_weight, conv_weight, conv_bias, xproj_weight, dt_weight, dt_bias,
    decay_log, skip_gain, out_weight, norm2_gain, router_weight, expert_in, expert_out,
    segments, expert_ids, cotangent,
):
    length, width = tokens.shape
    taps, channels = conv_weight.shape
    experts = router_weight.shape[1]
    wide = experts
    capacity = 5 * length // (4 * experts)
    states, rank = decay_log.shape[0], dt_weight.shape[0]
    chips = wide // 2
    slots = chips * capacity
    steps = length // SEGMENTS
    me_wide = lax.axis_index("wide")
    ids = jnp.stack([lax.axis_index("narrow"), me_wide, me_wide & 1, me_wide // 2]).astype(jnp.int32)
    half, double = length // 2, width // 2
    bf16 = jnp.bfloat16
    rows_shape, channel_rows = shape_of(length, width), shape_of(length, channels)
    packed, packed_slots = shape_of(half, double), shape_of(slots, double)
    row_of = lambda vector: vector.reshape(1, -1)
    vmem = lambda *shape: pltpu.VMEM(shape, jnp.float32)
    gain1, gain2 = row_of(norm1_gain), row_of(norm2_gain)
    xproj_t, router_t = xproj_weight.T, router_weight.T
    cols = xproj_t.shape[0]
    matmul_flops = lambda *dims: 6 * functools.reduce(lambda a, b: a * b, dims)

    tiled = vmem(width // LANES, length, LANES)

    halo_rows = wide_shift(tokens[length - SEGMENTS :], 1)

    rows, normed, conv_in, gate_in, conv_high, conv_low, gate_high, gate_low = call(
        front_kernel,
        [rows_shape, rows_shape, channel_rows, channel_rows]
        + [shape_of(width, channels, dtype=bf16)] * 4,
        ids, tokens, gain1, in_weight,
        scratch=[tiled], flops=matmul_flops(length, width, 2 * channels),
    )
    marks, slots_own, slots_other, rows_own, rows_other = call(
        functools.partial(route_kernel, capacity),
        [shape_of(length, SEGMENTS)]
        + [shape_of(slots, length, dtype=bf16)] * 2
        + [shape_of(length, slots, dtype=bf16)] * 2,
        ids, segments.reshape(wide, length), expert_ids.reshape(1, length),
    )
    mixed, conv_out, partial, extended, halo_normed = call(
        conv_kernel,
        [channel_rows, channel_rows, shape_of(cols, length),
         shape_of(length + (taps - 1) * SEGMENTS, channels), shape_of(SEGMENTS, width)],
        ids, halo_rows, gain1, conv_high, conv_low, conv_in, marks, conv_weight,
        row_of(conv_bias), xproj_t,
    )
    partials = narrow_all(partial)

    rows_slice, cot_slice, cot_own, cot_other, _ = call(
        slices_kernel,
        [packed, packed, packed_slots, packed_slots, rows_shape],
        ids, rows, cotangent, slots_own, slots_other,
        scratch=[tiled], after=[partial],
    )
    cot_pair = cot_own + core_swap(cot_other)

    entry_shape = shape_of(2, states, SEGMENTS, channels)
    total_rows = -(-(states + 1) // 8) * 8
    coef, dt_pre, stepsize, drive, stepd, rates, entry, total = call(
        totals_kernel,
        [shape_of(length, LANES)] + [channel_rows] * 4
        + [shape_of(states, channels), entry_shape, shape_of(total_rows, channels)],
        ids, *partials, dt_weight, row_of(dt_bias), decay_log, conv_out, marks,
        scratch=[vmem(LANES, channels)], after=[cot_own],
    )
    second_core = (me_wide & 1) == 1
    other_total = core_swap(total)
    early = jnp.where(second_core, other_total, total)
    late = jnp.where(second_core, total, other_total)
    late_sum = late[states : states + 1]
    carried = jnp.exp(late_sum * rates) * early[:states] + late[:states]
    chip_total = jnp.concatenate([carried, early[states:] + late[states:]])
    chip_totals = chip_all(chip_total, chips)
    cot_blocks = chip_each(cot_pair, chips)
    slabs = states // GROUP
    kept_shape = (slabs, steps + 1, GROUP, SEGMENTS, channels)
    ssm_skip, gated, mixer_slices, kept = call(
        functools.partial(states_kernel, rank),
        [channel_rows, channel_rows, shape_of(4, half, double), shape_of(*kept_shape)],
        ids, stepd, drive, coef, rates, entry, early, conv_out, gate_in, row_of(skip_gain),
        out_weight, *chip_totals,
        scratch=[vmem(chips, total_rows, channels), vmem(length, width), vmem(*kept_shape),
                 pltpu.SemaphoreType.DMA((slabs,))],
        out_place=[3],
    )
    hidden_slice, hidden_own, hidden_other = call(
        dispatch_kernel,
        [packed, packed_slots, packed_slots],
        ids, *narrow_each(mixer_slices), rows_slice, slots_own, slots_other,
        after=[cot_blocks],
    )
    cot_parts = narrow_all(cot_blocks)
    hidden_parts = narrow_all(chip_each(hidden_own + core_swap(hidden_other), chips))
    expert_rows, square = shape_of(2 * slots, width), (expert_in.shape[1], expert_in.shape[2])
    hidden_units = square[1]
    raw, cot, in_high, in_low, out_high, out_low = call(
        raw_kernel,
        [shape_of(2 * slots, hidden_units), expert_rows]
        + [shape_of(*square, dtype=bf16)] * 2
        + [shape_of(square[1], square[0], dtype=bf16)] * 2,
        ids, *cot_parts, expert_in[0], expert_out[0],
        scratch=[vmem(4, slots, double)], flops=matmul_flops(2 * slots, *square),
    )
    slices_shape = shape_of(4, slots, double)
    grad_slices, second, act, grad_pre, gates, grad_logits, grad_norm2 = call(
        expert_kernel,
        [slices_shape, expert_rows] + [shape_of(2 * slots, hidden_units)] * 2
        + [shape_of(2 * slots, 1), shape_of(2 * slots, experts), shape_of(1, width)],
        ids, *hidden_parts, raw, in_high, in_low, gain2, router_t,
        scratch=[vmem(4, slots, double), vmem(2 * slots, width)],
        flops=2 * matmul_flops(2 * slots, *square),
    )
    grad_mine = pair_sum(narrow_each(grad_slices))
    value_slices, grad_expert_in, grad_expert_out, grad_router_t = call(
        expert_rest_kernel,
        [slices_shape, shape_of(*square), shape_of(square[1], square[0]),
         shape_of(experts, width)],
        ids, second, act, grad_pre, gates, grad_logits, cot, out_high, out_low,
        scratch=[vmem(2 * slots, width)], flops=3 * matmul_flops(2 * slots, *square),
    )
    grad_back = chip_each(grad_mine, chips)
    value_mine = pair_sum(narrow_each(value_slices))
    grad_slice = call(
        home_kernel, [packed], ids, grad_back, core_swap(grad_back), cot_slice, rows_own,
        rows_other, after=[value_mine],
    )[0]
    grad_parts = narrow_all(grad_slice)
    value_back = chip_each(value_mine, chips)

    def whole_of(parts, after=()):
        return call(
            whole_kernel, [rows_shape], ids, *parts, after=after,
            scratch=[vmem(4, half, double), vmem(length, width), tiled],
        )[0]

    grad_hidden, grad_ssm, grad_gate_in, grad_skip, back_entry, back_total = call(
        functools.partial(leaving_kernel, rank),
        [rows_shape, channel_rows, channel_rows, shape_of(1, channels), entry_shape,
         shape_of(states, channels)],
        ids, *grad_parts, out_weight, gate_in, ssm_skip, conv_out, stepd, coef, rates,
        scratch=[vmem(4, half, double)], after=[value_back],
    )
    other_back = core_swap(back_total)
    back_early = jnp.where(second_core, other_back, back_total)
    back_late = jnp.where(second_core, back_total, other_back)
    back_chip = back_early + jnp.exp(early[states : states + 1] * rates) * back_late
    back_totals = chip_all(back_chip, chips)

    block = width // wide
    half_blocks = shape_of(wide // 2, 2 * block, channels)
    early_keep, early_send = call(
        early_weights_kernel,
        [half_blocks, half_blocks],
        ids, gated, grad_hidden, normed, grad_gate_in,
        scratch=[vmem(width, channels)] * 2, flops=2 * matmul_flops(length, width, channels),
        after=[back_chip],
    )
    early_sum, early_steps = wide_sum(early_keep, early_send)
    gate_part = call(
        gate_tokens_kernel, [rows_shape], ids, grad_gate_in, gate_high, gate_low,
        flops=matmul_flops(length, width, channels), after=[back_chip],
    )[0]
    output_slice = call(
        home_kernel, [packed], ids, value_back, core_swap(value_back), hidden_slice, rows_own,
        rows_other, after=[back_chip],
    )[0]
    output_parts = narrow_all(output_slice)

    partial_back, grad_direct, grad_dt_pre, grad_decay, grad_dt_bias = call(
        functools.partial(adjoint_kernel, rank, chips),
        [shape_of(cols, length), channel_rows, channel_rows, shape_of(states, channels),
         shape_of(1, channels)],
        ids, stepd, drive, grad_ssm, coef, rates, back_entry, kept, early, late, back_late,
        conv_out, stepsize, dt_pre, row_of(skip_gain), dt_weight, *chip_totals, *back_totals,
        scratch=[vmem(chips, 1, channels), vmem(chips, states, channels), vmem(*kept_shape),
                 vmem(length, states * LANES), vmem(length, states * LANES),
                 vmem(length, channels), vmem(length, channels),
                 pltpu.SemaphoreType.DMA((slabs,))],
        in_place=[6], after=[early_steps[0], gate_part, output_slice],
    )
    output = whole_of(output_parts, after=[partial_back])
    grain = 8 * wide
    small_rows = cols + rank + states + taps + 3
    small_rows += -small_rows % grain
    grad_conv, grad_halo, small = call(
        conv_back_kernel,
        [channel_rows, shape_of(SEGMENTS, channels), shape_of(small_rows, channels)],
        ids, *narrow_all(partial_back), xproj_t, grad_direct, mixed, conv_out, extended, marks,
        conv_weight, coef, grad_dt_pre, grad_decay, grad_dt_bias, grad_skip,
        scratch=[vmem(length + (taps - 1) * SEGMENTS, channels)],
        after=[output, early_steps[1]],
    )
    from_next = wide_shift(grad_halo, -1)
    more = small_rows // wide
    half_blocks = shape_of(wide // 2, block + more, channels)
    conv_keep, conv_send = call(
        conv_weights_kernel,
        [half_blocks, half_blocks],
        ids, normed, grad_conv, halo_normed, grad_halo, small,
        scratch=[vmem(width, channels)], flops=matmul_flops(length, width, channels),
    )
    conv_sum, conv_steps = wide_sum(conv_keep, conv_send)

    token_slices, grad_norm1 = call(
        functools.partial(tokens_kernel, taps),
        [shape_of(4, half, double), shape_of(1, width)],
        ids, grad_conv, from_next, conv_high, conv_low, gate_part, rows, gain1,
        scratch=[vmem(length, channels), vmem(length, width)],
        flops=matmul_flops(length, width, channels), after=[early_steps[2], conv_steps[0]],
    )
    token_slice = pair_sum(narrow_each(token_slices)) + grad_slice
    grad_tokens = whole_of(narrow_all(token_slice))

    shared = jnp.concatenate([grad_norm1, grad_norm2, grad_router_t])
    shared = jnp.pad(shared, ((0, -shared.shape[0] % 8), (0, 0)))
    shared = pair_sum(narrow_all(shared))
    shared = shared + core_swap(shared)
    shared = pair_sum(chip_all(shared, chips))

    sum_out_weight = call(early_out_kernel, [shape_of(channels, width)], ids, early_sum)[0]
    weight_sum, small_sum = call(
        weights_out_kernel,
        [shape_of(width, 2, channels), shape_of(small_rows, channels)],
        ids, early_sum, conv_sum,
    )

    at = [0]

    def take(count):
        at[0] += count
        return small_sum[at[0] - count : at[0]]

    sum_xproj = take(cols).T
    sum_dt_weight, sum_decay, sum_taps = take(rank), take(states), take(taps)
    sum_conv_bias, sum_dt_bias, sum_skip = take(1)[0], take(1)[0], take(1)[0]
    return (
        output,
        grad_tokens,
        shared[0],
        weight_sum,
        sum_taps,
        sum_conv_bias,
        sum_xproj,
        sum_dt_weight,
        sum_dt_bias,
        sum_decay,
        sum_skip,
        sum_out_weight,
        shared[1],
        shared[2 : 2 + experts].T,
        grad_expert_in[None],
        grad_expert_out[None],
    )


def solution(mesh):
    in_specs = (
        P("wide", None),
        P(),
        P(None, None, "narrow"),
        P(None, "narrow"),
        P("narrow"),
        P("narrow", None),
        P(None, "narrow"),
        P("narrow"),
        P(None, "narrow"),
        P("narrow"),
        P("narrow", None),
        P(),
        P(),
        P("wide", None, "narrow"),
        P("wide", "narrow", None),
        P(),
        P("wide", None),
        P("wide", None),
    )
    out_specs = (
        P("wide", None),
        P("wide", None),
        P(),
        P(None, None, "narrow"),
        P(None, "narrow"),
        P("narrow"),
        P("narrow", None),
        P(None, "narrow"),
        P("narrow"),
        P(None, "narrow"),
        P("narrow"),
        P("narrow", None),
        P(),
        P(),
        P("wide", None, "narrow"),
        P("wide", "narrow", None),
    )
    return jax.shard_map(local, mesh=mesh, in_specs=in_specs, out_specs=out_specs, check_vma=False)
```

```python
import functools
import math

import jax
import jax.numpy as jnp
from jax import lax
from jax.experimental import pallas as pl
from jax.experimental.pallas import tpu as pltpu
from jax.sharding import PartitionSpec as P

EPSILON = 1e-05
SEGMENTS = 8
LANES = 128
NEVER = 1e30
VMEM_SPARE = 4 * 1024 * 1024
GROUP = 4
LOG2E = 1.4426950408889634


def shape_of(*shape, dtype=jnp.float32):
    return jax.ShapeDtypeStruct(shape, dtype)


def call(kernel, outs, ids, *arrays, scratch=(), after=(), far_in=(), out_place=(), in_place=()):
    in_vmem = pl.BlockSpec(memory_space=pltpu.VMEM)
    anywhere = pl.BlockSpec(memory_space=pl.ANY)
    far = pl.BlockSpec(memory_space=pltpu.HBM)
    arrays = [
        pltpu.with_memory_space_constraint(array, pltpu.HBM) if i in far_in else array
        for i, array in enumerate(arrays)
    ]
    size = lambda a: math.prod(a.shape) * jnp.dtype(a.dtype).itemsize
    held = [
        size(a)
        for refs, skipped in ((arrays, (*in_place, *far_in)), (outs, out_place))
        for i, a in enumerate(refs)
        if i not in skipped
    ]
    held += [size(a) for a in scratch if hasattr(a, "dtype") and hasattr(a, "shape")
             and jnp.issubdtype(a.dtype, jnp.number)]
    given = 1 + len(arrays)

    def run(*refs):
        kernel(*refs[:given], *refs[given + len(after) :])

    return pl.pallas_call(
        run,
        out_shape=outs,
        in_specs=[pl.BlockSpec(memory_space=pltpu.SMEM)]
        + [far if i in far_in else anywhere if i in in_place else in_vmem
           for i in range(len(arrays))]
        + [anywhere] * len(after),
        out_specs=[anywhere if i in out_place else in_vmem for i in range(len(outs))],
        scratch_shapes=scratch,
        compiler_params=pltpu.CompilerParams(vmem_limit_bytes=sum(held) + VMEM_SPARE),
        cost_estimate=pl.CostEstimate(flops=1, bytes_accessed=1, transcendentals=0),
    )(ids, *arrays, *after)


def two_parts(value):
    high = value.astype(jnp.bfloat16)
    return high, (value - high.astype(jnp.float32)).astype(jnp.bfloat16)


def once(left, right, contract=(1, 0)):
    return lax.dot_general(
        left,
        right,
        (((contract[0],), (contract[1],)), ((), ())),
        preferred_element_type=jnp.float32,
    )


def product(left, right, contract=(1, 0)):
    left_high, left_low = left if isinstance(left, tuple) else two_parts(left)
    right_high, right_low = right if isinstance(right, tuple) else two_parts(right)
    return once(left_high, right_high, contract) + (
        once(left_high, right_low, contract) + once(left_low, right_high, contract)
    )


def select_rows(chosen, rows, contract=(1, 0)):
    high, low = two_parts(rows)
    return once(chosen, high, contract) + once(chosen, low, contract)


def inverse_rms(rows):
    return lax.rsqrt(jnp.mean(rows * rows, axis=-1, keepdims=True) + EPSILON)


def norm_back(rows, inverse, gain, grad):
    scaled = gain * grad
    mean = jnp.mean(rows * scaled, axis=-1, keepdims=True)
    return inverse * scaled - rows * (inverse * inverse * inverse) * mean


def sigmoid(value):
    return 1.0 / (1.0 + jnp.exp(-value))


def softplus(value):
    return jnp.maximum(value, 0.0) + jnp.log1p(jnp.exp(-jnp.abs(value)))


def gelu_parts(value):
    spread_of = 0.5 * (1.0 + lax.erf(value * (0.5**0.5)))
    density = jnp.exp(-0.5 * value * value) * ((2.0 * jnp.pi) ** -0.5)
    return value * spread_of, spread_of + value * density


def cut_slices(me, whole, out):
    rows, part = whole.shape[0] // 2, whole.shape[1] // 4
    for j in range(4):
        out[me ^ j, :, :part] = whole[:rows, part * j : part * (j + 1)]
        out[me ^ j, :, part:] = whole[rows:, part * j : part * (j + 1)]


def join_slices(me, parts, held, whole):
    rows, part = whole.shape[0] // 2, whole.shape[1] // 4
    for key, value in enumerate(parts):
        held[key] = value[...]
    for j in range(4):
        value = held[me ^ j]
        whole[:rows, part * j : part * (j + 1)] = value[:, :part]
        whole[rows:, part * j : part * (j + 1)] = value[:, part:]


def reversed_bits(value, levels):
    place = 0
    for level in range(levels):
        place = place + (((value >> level) & 1) << (levels - 1 - level))
    return place


def interleave_from(rows, held, out):
    length, width = out.shape
    steps = length // SEGMENTS
    for tile in range(width // LANES):
        lanes = slice(tile * LANES, (tile + 1) * LANES)
        held[tile] = rows[:, lanes]
        for step in range(steps):
            out[step * SEGMENTS : (step + 1) * SEGMENTS, lanes] = held[
                tile, pl.ds(step, SEGMENTS, stride=steps), :
            ]


def deinterleave_to(rows, held, out):
    length, width = out.shape
    steps = length // SEGMENTS
    for tile in range(width // LANES):
        lanes = slice(tile * LANES, (tile + 1) * LANES)
        for step in range(steps):
            held[tile, pl.ds(step, SEGMENTS, stride=steps), :] = rows[
                step * SEGMENTS : (step + 1) * SEGMENTS, lanes
            ]
        out[:, lanes] = held[tile]


def narrow_swap(value, key):
    return lax.ppermute(value, "narrow", [(i, i ^ key) for i in range(4)])


def core_swap(value):
    count = lax.axis_size("wide")
    return lax.ppermute(value, "wide", [(i, i ^ 1) for i in range(count)])


def chip_swap(value, key):
    count = lax.axis_size("wide")
    return lax.ppermute(value, "wide", [(i, i ^ (2 * key)) for i in range(count)])


def wide_shift(value, distance):
    devices = range(lax.axis_size("wide"))
    route = [(i - distance, i) for i in devices if i - distance in devices]
    return lax.ppermute(value, "wide", route)


def hold(value, *others):
    if not others:
        return value
    return lax.optimization_barrier((value, others))[0]


def narrow_all(value):
    far = narrow_swap(value, 3)
    return [value, narrow_swap(value, 1), narrow_swap(value, 2), far]


def narrow_each(slices):
    far = narrow_swap(slices[3], 3)
    return [slices[0], narrow_swap(slices[1], 1), narrow_swap(slices[2], 2), far]


def pair_sum(parts):
    while len(parts) > 1:
        parts = [a + b for a, b in zip(parts[::2], parts[1::2])]
    return parts[0]


def chip_blocks(blocks, chips):
    rows = blocks.shape[0] // chips
    order = sorted(range(1, chips), reverse=True)
    arrived = {k: chip_swap(blocks[k * rows : (k + 1) * rows], k) for k in order}
    arrived[0] = blocks[:rows]
    return [arrived[k] for k in range(chips)]


def chip_each(blocks, chips):
    return jnp.concatenate(chip_blocks(blocks, chips))


def chip_all(value, chips):
    arrived = {k: chip_swap(value, k) for k in sorted(range(1, chips), reverse=True)}
    arrived[0] = value
    return [arrived[k] for k in range(chips)]


class WideSum:
    def __init__(self, keep, send):
        levels = lax.axis_size("wide").bit_length() - 1
        self.swaps = [core_swap] + [
            functools.partial(chip_swap, key=1 << level) for level in range(levels - 1)
        ]
        self.keep, self.send, self.arrived = keep, send, None
        self.level, self.back = 0, False

    def prepare(self):
        if not self.back and self.level == len(self.swaps):
            self.back = True
        if self.back:
            self.level -= 1
            self.send = self.keep
        return self.send

    def start(self, *others):
        self.prepare()
        self.arrived = self.swaps[self.level](hold(self.send, *others))
        return self.arrived

    def finish(self, *others):
        arrived = hold(self.arrived, *others) if others else self.arrived
        if self.back:
            self.keep = jnp.concatenate([self.keep, arrived])
            return
        self.level += 1
        if self.level == len(self.swaps):
            self.keep = self.keep + arrived
            return
        half = self.keep.shape[0] // 2
        self.send = self.keep[half:] + arrived[half:]
        self.keep = self.keep[:half] + arrived[:half]

    def rest(self):
        while not (self.back and self.level == 0):
            self.start()
            self.finish()
        return self.keep


def start_both(one, two):
    first, second = one.prepare(), two.prepare()
    rows = first.shape[1]
    arrived = one.swaps[one.level](jnp.concatenate([first, second], axis=1))
    one.arrived, two.arrived = arrived[:, :rows], arrived[:, rows:]
    return one.arrived, two.arrived


def route_kernel(capacity, ids, segments, expert_ids, marks, slots_own, slots_other,
                 rows_own, rows_other):
    wide_at, core, chip = ids[1], ids[2], ids[3]
    experts = segments.shape[0]
    length = segments.shape[1]
    steps = length // SEGMENTS
    own = segments[pl.ds(wide_at, 1), :]
    before = segments[pl.ds(jnp.maximum(wide_at - 1, 0), 1), :]
    lane = lax.broadcasted_iota(jnp.int32, (1, length), 1)
    here = lax.broadcasted_iota(jnp.int32, (SEGMENTS, length), 0)
    table = jnp.ones((SEGMENTS, length), jnp.float32)
    for k in range(1, 4):
        back = jnp.where(lane < k, pltpu.roll(before, k, 1), pltpu.roll(own, k, 1))
        same = (back == own) & ((lane >= k) | (wide_at > 0))
        table = jnp.where(here == k, jnp.where(same, 1.0, 0.0), table)
    live = own >= 0
    expert = expert_ids[...]
    at = lax.broadcasted_iota(jnp.int32, (experts, length), 0)
    hits = jnp.where((at == expert) & live, 1.0, 0.0)
    first = lax.broadcasted_iota(jnp.int32, (length, length), 0)
    second = lax.broadcasted_iota(jnp.int32, (length, length), 1)
    earlier = jnp.where(first < second, 1.0, 0.0).astype(jnp.bfloat16)
    ranks = once(hits.astype(jnp.bfloat16), earlier)
    rank = jnp.sum(ranks * hits, axis=0, keepdims=True).astype(jnp.int32)
    kept = live & (rank < capacity)
    order = jnp.where(
        (first % SEGMENTS) * steps + first // SEGMENTS == second, 1.0, 0.0
    ).astype(jnp.bfloat16)
    marks[...] = once(order, table.astype(jnp.bfloat16), (1, 1))
    slot = jnp.where(kept, ((expert >> 1) ^ chip) * capacity + rank, -1)
    count = slots_own.shape[0]
    slot_at = lax.broadcasted_iota(jnp.int32, (count, length), 0)
    for which, slots, rows in ((core, slots_own, rows_own), (1 - core, slots_other, rows_other)):
        mine = (slot_at == slot) & ((expert & 1) == which)
        chosen = jnp.where(mine, 1.0, 0.0).astype(jnp.bfloat16)
        slots[...] = once(chosen, order, (1, 1)).astype(jnp.bfloat16)
        rows[...] = once(order, chosen, (1, 1)).astype(jnp.bfloat16)


def front_kernel(ids, tokens, gain, weight, rows, normed, conv_in, gate_in,
                 conv_high, conv_low, gate_high, gate_low, held, branch):
    interleave_from(tokens, held, rows)
    value = rows[...]
    scaled = value * inverse_rms(value) * gain[...][None]
    normed[...] = scaled
    parts = two_parts(scaled)
    for k, (high, low, out) in enumerate(
        ((conv_high, conv_low, conv_in), (gate_high, gate_low, gate_in))
    ):
        branch[k] = weight[:, k, :]
        high[...], low[...] = two_parts(branch[k])
        out[...] = product(parts, (high[...], low[...]))


def start_kernel(capacity, ids, segments, expert_ids, tokens_far, cotangent_far,
                 marks, slots_own, slots_other, rows_own, rows_other,
                 rows_slice, cot_slice, own, other,
                 tokens, cotangent, rows, held, sems):
    copies = [
        pltpu.make_async_copy(far, near, sems.at[i])
        for i, (far, near) in enumerate(((tokens_far, tokens), (cotangent_far, cotangent)))
    ]
    for copy in copies:
        copy.start()
    route_kernel(capacity, ids, segments, expert_ids, marks, slots_own, slots_other,
                 rows_own, rows_other)
    for copy in copies:
        copy.wait()
    slices_kernel(ids, tokens, cotangent, slots_own, slots_other, rows_slice, cot_slice, own, other,
                  rows, held)


def slices_kernel(ids, tokens, cotangent, slots_own, slots_other,
                  rows_slice, cot_slice, own, other, rows, held):
    me, core = ids[0], ids[2]
    half, part = tokens.shape[0] // 2, tokens.shape[1] // 4
    for source, out in ((tokens, rows_slice), (cotangent, cot_slice)):
        interleave_from(source, held, rows)
        for j in range(4):
            @pl.when(me == j)
            def _():
                out[:, :part] = rows[:half, part * j : part * (j + 1)]
                out[:, part:] = rows[half:, part * j : part * (j + 1)]
    send_slots(core, cot_slice[...], slots_own[...], slots_other[...], own, other)


def send_slots(core, packed, slots_own, slots_other, own, other):
    half = packed.shape[1] // 2
    lane = lax.broadcasted_iota(jnp.int32, packed.shape, 1)
    left = jnp.where(lane < half, packed, 0.0)
    right = jnp.where(lane < half, 0.0, packed)
    second = core == 1
    top = jnp.where(second, pltpu.roll(left, half, 1), left)
    bottom = jnp.where(second, right, pltpu.roll(right, half, 1))
    placed = jnp.concatenate([top, bottom])
    own[...] = select_rows(slots_own, placed)
    other[...] = select_rows(slots_other, placed)


def conv_kernel(ids, halo, gain, conv_high, conv_low, conv_in, marks, conv_weight, conv_bias,
                xproj_t, mixed, conv_out, partial, extended, halo_normed):
    taps, channels = conv_weight.shape
    length = conv_in.shape[0]
    lead = (taps - 1) * SEGMENTS
    rows = halo[...]
    scaled = rows * inverse_rms(rows) * gain[...][None]
    halo_normed[...] = scaled
    halo_conv = product(scaled, (conv_high[...], conv_low[...]))
    place = lax.broadcasted_iota(jnp.int32, (SEGMENTS, channels), 0)
    for m in range(taps - 1):
        ends = conv_in[length - lead + m * SEGMENTS : length - lead + (m + 1) * SEGMENTS, :]
        at = SEGMENTS - taps + 1 + m
        extended[m * SEGMENTS : (m + 1) * SEGMENTS, :] = jnp.where(
            place == 0, halo_conv[at : at + 1, :], pltpu.roll(ends, 1, 0)
        )
    extended[lead:, :] = conv_in[...]
    total = jnp.broadcast_to(conv_bias[...][None], (length, channels))
    for k in range(taps):
        first = (taps - 1 - k) * SEGMENTS
        total += conv_weight[k : k + 1, :] * extended[first : first + length, :] * marks[:, k : k + 1]
    mixed[...] = total
    out = total * sigmoid(total)
    conv_out[...] = out
    partial[...] = product(xproj_t[...], out, (1, 1))


def rows_at(step):
    return pl.ds(pl.multiple_of(step * SEGMENTS, SEGMENTS), SEGMENTS)


def spread(row):
    return jnp.broadcast_to(row, (SEGMENTS, row.shape[-1]))


def column_of(rows, column):
    return jnp.broadcast_to(rows[:, column : column + 1], (SEGMENTS, LANES))


def sweep(count, body, carry):
    return lax.fori_loop(0, count, body, carry, unroll=True)


def add_to(ref, first, rows, lanes, value):
    if first:
        ref[rows, lanes] = value
    else:
        ref[rows, lanes] += value


def chain_pieces(decay, value, backward):
    place = lax.broadcasted_iota(jnp.int32, decay.shape, 0)
    if backward:
        place = SEGMENTS - 1 - place

    def moved(array, distance):
        return pltpu.roll(array, (SEGMENTS - distance) if backward else distance, 0)

    distance = 1
    while distance < SEGMENTS:
        inside = place >= distance
        value = jnp.where(inside, decay * moved(value, distance) + value, value)
        decay = jnp.where(inside, decay * moved(decay, distance), decay)
        distance *= 2
    first = place == 0
    before = jnp.where(first, 0.0, moved(value, 1))
    factor = jnp.where(first, 1.0, moved(decay, 1))
    return factor, before, value


def totals_kernel(ids, p0, p1, p2, p3, dt_weight, dt_bias, decay_log, conv_out, marks,
                  coef, dt_pre, stepsize, drive, stepd, rates, entry, total, padded):
    states, channels = decay_log.shape
    rank = dt_weight.shape[0]
    length = conv_out.shape[0]
    steps = length // SEGMENTS
    projected = (p0[...] + p1[...]) + (p2[...] + p3[...])
    missing = LANES - projected.shape[0]
    coef[...] = jnp.concatenate([projected, jnp.zeros((missing, length), jnp.float32)]).T
    padded[...] = jnp.zeros_like(padded)
    padded[:rank, :] = dt_weight[...]
    pre = product(coef[...], padded[...]) + dt_bias[...][None]
    dt_pre[...] = pre
    size = softplus(pre)
    stepsize[...] = size
    drive[...] = size * conv_out[...]
    stepd[...] = jnp.where(marks[:, 1:2] > 0.5, size, NEVER)
    rates[...] = -jnp.exp(decay_log[...])
    total[...] = jnp.zeros_like(total)
    zero = jnp.zeros((SEGMENTS, LANES), jnp.float32)
    tiles = [slice(at, at + LANES) for at in range(0, channels, LANES)]
    sums = [zero] * len(tiles)
    for step in range(steps):
        rows = slice(step * SEGMENTS, (step + 1) * SEGMENTS)
        sums = [value + stepd[rows, lanes] for value, lanes in zip(sums, tiles)]
    for value, lanes in zip(sums, tiles):
        total[states : states + 1, lanes] = jnp.sum(value, axis=0, keepdims=True)
    for group in range(0, states, GROUP):
        names = range(group, group + GROUP)
        rate = [[spread(rates[n : n + 1, lanes] * LOG2E) for lanes in tiles] for n in names]

        def body(step, current):
            rows = rows_at(step)
            near = coef[rows, :]
            width = [stepd[rows, lanes] for lanes in tiles]
            push = [drive[rows, lanes] for lanes in tiles]
            later = []
            for at, n in enumerate(names):
                entering = column_of(near, rank + n)
                later.append(tuple(
                    jnp.exp2(width[t] * rate[at][t]) * current[at][t] + push[t] * entering
                    for t in range(len(tiles))
                ))
            return tuple(later)

        current = sweep(steps, body, ((zero,) * len(tiles),) * GROUP)
        for at, n in enumerate(names):
            for t, lanes in enumerate(tiles):
                decay = jnp.exp2(sums[t] * rate[at][t])
                factor, before, last = chain_pieces(decay, current[at][t], False)
                entry[0, n, :, lanes] = factor
                entry[1, n, :, lanes] = before
                total[n : n + 1, lanes] = last[SEGMENTS - 1 :, :]


def pair_kernel(ids, total, other, rates, early, late, chip):
    states = rates.shape[0]
    second = ids[2] == 1
    mine, theirs = total[...], other[...]
    first, last = jnp.where(second, theirs, mine), jnp.where(second, mine, theirs)
    early[...] = first
    late[...] = last
    chip[...] = first + last
    chip[:states, :] = (
        jnp.exp(last[states : states + 1] * rates[...]) * first[:states] + last[:states]
    )


def pair_back_kernel(ids, total, other, early, rates, late_total, chip):
    states = rates.shape[0]
    second = ids[2] == 1
    mine, theirs = total[...], other[...]
    first, last = jnp.where(second, theirs, mine), jnp.where(second, mine, theirs)
    late_total[...] = last
    chip[...] = first + jnp.exp(early[states : states + 1, :] * rates[...]) * last


def states_kernel(rank, ids, stepd, drive, coef, rates, entry, early, conv_out, gate_in, skip,
                  out_weight, *rest):
    chips = len(rest) - 8
    totals = rest[:chips]
    ssm_skip, gated, slices, kept, held, whole, kept_here, sems = rest[chips:]
    me, core, here = ids[0], ids[2], ids[3]
    states, channels = rates.shape
    length = stepd.shape[0]
    steps = length // SEGMENTS
    for key, value in enumerate(totals):
        held[key] = value[...]
    state = jnp.zeros((states, channels), jnp.float32)
    for chip in range(chips):
        value = held[here ^ chip]
        grown = jnp.exp(value[states : states + 1] * rates[...]) * state + value[:states]
        state = jnp.where(chip < here, grown, state)
    inner = jnp.exp(early[states : states + 1, :] * rates[...]) * state + early[:states, :]
    start = jnp.where(core == 1, inner, state)
    tiles = [slice(at, at + LANES) for at in range(0, channels, LANES)]
    copies = []
    for group in range(0, states, GROUP):
        names = range(group, group + GROUP)
        slab = group // GROUP
        rate = [[spread(rates[n : n + 1, lanes] * LOG2E) for lanes in tiles] for n in names]
        current = tuple(
            tuple(
                entry[0, n, :, lanes] * start[n : n + 1, lanes] + entry[1, n, :, lanes]
                for lanes in tiles
            )
            for n in names
        )
        for at in range(GROUP):
            for t, lanes in enumerate(tiles):
                kept_here[slab, 0, at, :, lanes] = current[at][t]

        def body(step, current):
            rows = rows_at(step)
            near = coef[rows, :]
            width = [stepd[rows, lanes] for lanes in tiles]
            push = [drive[rows, lanes] for lanes in tiles]
            later, total = [], [None] * len(tiles)
            for at, n in enumerate(names):
                entering, leaving = column_of(near, rank + n), column_of(near, rank + states + n)
                new = []
                for t, lanes in enumerate(tiles):
                    decay = jnp.exp2(width[t] * rate[at][t])
                    new.append(decay * current[at][t] + push[t] * entering)
                    kept_here[slab, step + 1, at, :, lanes] = new[t]
                    term = leaving * new[t]
                    total[t] = term if total[t] is None else total[t] + term
                later.append(tuple(new))
            for t, lanes in enumerate(tiles):
                add_to(ssm_skip, group == 0, rows, lanes, total[t])
            return tuple(later)

        sweep(steps, body, current)
        copies.append(pltpu.make_async_copy(kept_here.at[slab], kept.at[slab], sems.at[slab]))
        copies[-1].start()
    skipped = ssm_skip[...] + skip[...][None] * conv_out[...]
    ssm_skip[...] = skipped
    gate = gate_in[...]
    out = skipped * gate * sigmoid(gate)
    gated[...] = out
    whole[...] = product(out, out_weight[...])
    cut_slices(me, whole, slices)
    for copy in copies:
        copy.wait()


def dispatch_kernel(ids, s0, s1, s2, s3, rows_slice, slots_own, slots_other,
                    hidden, own, other):
    packed = (s0[...] + s1[...]) + (s2[...] + s3[...]) + rows_slice[...]
    hidden[...] = packed
    send_slots(ids[2], packed, slots_own[...], slots_other[...], own, other)


def raw_kernel(ids, c0, c1, c2, c3, expert_in, expert_out, raw, cot, in_high, in_low,
               out_high, out_low, held):
    join_slices(ids[0], (c0, c1, c2, c3), held, cot)
    in_high[...], in_low[...] = two_parts(expert_in[...])
    out_high[...], out_low[...] = two_parts(expert_out[...])
    raw[...] = product(cot[...], (out_high[...], out_low[...]), (1, 1))


def expert_kernel(ids, h0, h1, h2, h3, raw, in_high, in_low, norm_gain, router_t,
                  slices, second, act, grad_pre, gates, grad_logits, grad_gain,
                  held, whole):
    me, expert = ids[0], ids[1]
    join_slices(me, (h0, h1, h2, h3), held, whole)
    rows = whole[...]
    inverse = inverse_rms(rows)
    normed = rows * inverse * norm_gain[...][None]
    second[...] = normed
    normed_parts = two_parts(normed)
    router_parts = two_parts(router_t[...])
    weight = (in_high[...], in_low[...])
    logits = product(normed_parts, router_parts, (1, 1))
    logits = logits - jnp.max(logits, axis=-1, keepdims=True)
    powers = jnp.exp(logits)
    probs = powers / jnp.sum(powers, axis=-1, keepdims=True)
    chosen = jnp.where(
        lax.broadcasted_iota(jnp.int32, logits.shape, 1) == expert, 1.0, 0.0
    )
    gate = jnp.sum(probs * chosen, axis=-1, keepdims=True)
    gates[...] = gate
    hidden_act, slope = gelu_parts(product(normed_parts, weight))
    act[...] = hidden_act
    raws = raw[...]
    grad_gate = jnp.sum(hidden_act * raws, axis=-1, keepdims=True)
    grads = gate * raws * slope
    grad_pre[...] = grads
    logit_grads = grad_gate * gate * (chosen - probs)
    grad_logits[...] = logit_grads
    grad_second = product(grads, weight, (1, 1)) + product(logit_grads, router_parts)
    grad_gain[...] = jnp.sum(rows * inverse * grad_second, axis=0, keepdims=True)
    whole[...] = norm_back(rows, inverse, norm_gain[...][None], grad_second)
    cut_slices(me, whole, slices)


def expert_rest_kernel(ids, second, act, grad_pre, gates, grad_logits, cot, out_high, out_low,
                       slices, grad_in, grad_out, grad_router, whole):
    gate = gates[...]
    acts = two_parts(act[...])
    normed = two_parts(second[...])
    whole[...] = gate * product(acts, (out_high[...], out_low[...]))
    cut_slices(ids[0], whole, slices)
    grad_out[...] = product(acts, gate * cot[...], (0, 0))
    grad_in[...] = product(normed, grad_pre[...], (0, 0))
    grad_router[...] = product(grad_logits[...], normed, (0, 0))


def home_kernel(ids, own, other, base, rows_own, rows_other, out):
    half = own.shape[1] // 2
    second = ids[2] == 1

    def mine(rows):
        return jnp.where(second, pltpu.roll(rows, half, 1), rows)

    total = select_rows(rows_own[...], mine(own[...])) + select_rows(
        rows_other[...], mine(other[...])
    )
    count = base.shape[0]
    lane = lax.broadcasted_iota(jnp.int32, base.shape, 1)
    out[...] = base[...] + jnp.where(
        lane < half, total[:count], pltpu.roll(total[count:], half, 1)
    )


def whole_kernel(ids, p0, p1, p2, p3, out, held, whole, tiles):
    join_slices(ids[0], (p0, p1, p2, p3), held, whole)
    deinterleave_to(whole, tiles, out)


def leaving_kernel(rank, ids, g0, g1, g2, g3, out_weight, gate_in, ssm_skip, conv_out, stepd,
                   coef, rates, grad_hidden, grad_ssm, grad_gate_in, grad_skip, entry, total,
                   held):
    join_slices(ids[0], (g0, g1, g2, g3), held, grad_hidden)
    states, channels = rates.shape
    length = stepd.shape[0]
    steps = length // SEGMENTS
    grad_gated = product(grad_hidden[...], out_weight[...], (1, 1))
    gate = gate_in[...]
    gate_sigmoid = sigmoid(gate)
    pulled = grad_gated * gate * gate_sigmoid
    grad_ssm[...] = pulled
    grad_gate_in[...] = grad_gated * ssm_skip[...] * (
        gate_sigmoid * (1.0 + gate * (1.0 - gate_sigmoid))
    )
    grad_skip[...] = jnp.sum(pulled * conv_out[...], axis=0, keepdims=True)
    zero = jnp.zeros((SEGMENTS, LANES), jnp.float32)
    tiles = [slice(at, at + LANES) for at in range(0, channels, LANES)]
    sums = [zero] * len(tiles)
    for step in range(steps):
        rows = slice(step * SEGMENTS, (step + 1) * SEGMENTS)
        sums = [value + stepd[rows, lanes] for value, lanes in zip(sums, tiles)]
    for group in range(0, states, GROUP):
        names = range(group, group + GROUP)
        rate = [[spread(rates[n : n + 1, lanes] * LOG2E) for lanes in tiles] for n in names]

        def body(back, current):
            rows = rows_at(steps - 1 - back)
            near = coef[rows, :]
            width = [stepd[rows, lanes] for lanes in tiles]
            pull = [grad_ssm[rows, lanes] for lanes in tiles]
            later = []
            for at, n in enumerate(names):
                leaving = column_of(near, rank + states + n)
                later.append(tuple(
                    jnp.exp2(width[t] * rate[at][t]) * (current[at][t] + pull[t] * leaving)
                    for t in range(len(tiles))
                ))
            return tuple(later)

        current = sweep(steps, body, ((zero,) * len(tiles),) * GROUP)
        for at, n in enumerate(names):
            for t, lanes in enumerate(tiles):
                decay = jnp.exp2(sums[t] * rate[at][t])
                factor, before, last = chain_pieces(decay, current[at][t], True)
                entry[0, n, :, lanes] = factor
                entry[1, n, :, lanes] = before
                total[n : n + 1, lanes] = last[:1, :]


def adjoint_kernel(rank, chips, ids, stepd, drive, grad, coef, rates, entry, kept, early, late,
                   late_total, conv_out, stepsize, dt_pre, skip, dt_weight, grad_norm2, grad_router,
                   *rest):
    sums, totals = rest[:chips], rest[chips : 2 * chips]
    (partial, grad_direct, grad_dt_pre, grad_decay, grad_dt_bias, held_sums, held, kept_here,
     in_terms, out_terms, grad_push, grad_width, sems) = rest[2 * chips :]
    core, here = ids[2], ids[3]
    states, channels = rates.shape
    length = stepd.shape[0]
    steps = length // SEGMENTS
    copies = [
        pltpu.make_async_copy(kept.at[slab], kept_here.at[slab], sems.at[slab])
        for slab in range(states // GROUP)
    ]
    for copy in copies:
        copy.start()
    for key in range(chips):
        held_sums[key] = sums[key][states : states + 1, :]
        held[key] = totals[key][...]
    state = jnp.zeros((states, channels), jnp.float32)
    for chip in reversed(range(chips)):
        grown = held[here ^ chip] + jnp.exp(held_sums[here ^ chip] * rates[...]) * state
        state = jnp.where(chip > here, grown, state)
    inner = late_total[...] + jnp.exp(late[states : states + 1, :] * rates[...]) * state
    final = jnp.where(core == 1, state, inner)
    zero = jnp.zeros((SEGMENTS, LANES), jnp.float32)
    tiles = [slice(at, at + LANES) for at in range(0, channels, LANES)]
    for group in range(0, states, GROUP):
        names = range(group, group + GROUP)
        slab = group // GROUP
        rate = [[spread(rates[n : n + 1, lanes]) for lanes in tiles] for n in names]
        current = tuple(
            tuple(
                entry[0, n, :, lanes] * final[n : n + 1, lanes] + entry[1, n, :, lanes]
                for lanes in tiles
            )
            for n in names
        )
        copies[slab].wait()

        def body(back, carry):
            current, slopes = carry
            step = steps - 1 - back
            rows = rows_at(step)
            near = coef[rows, :]
            width = [stepd[rows, lanes] for lanes in tiles]
            push = [drive[rows, lanes] for lanes in tiles]
            pull = [grad[rows, lanes] for lanes in tiles]
            later, slope = [], []
            total, width_total = [None] * len(tiles), [None] * len(tiles)
            for at, n in enumerate(names):
                entering, leaving = column_of(near, rank + n), column_of(near, rank + states + n)
                new, turned, in_term, out_term = [], [], None, None
                for t, lanes in enumerate(tiles):
                    adjoint = leaving * pull[t] + current[at][t]
                    decayed = jnp.exp2(width[t] * (rate[at][t] * LOG2E)) * adjoint
                    through = decayed * kept_here[slab, step, at, :, lanes]
                    term, rated = adjoint * entering, through * rate[at][t]
                    total[t] = term if total[t] is None else total[t] + term
                    width_total[t] = rated if width_total[t] is None else width_total[t] + rated
                    new.append(decayed)
                    turned.append(slopes[at][t] + through * width[t])
                    term = adjoint * push[t]
                    in_term = term if in_term is None else in_term + term
                    term = kept_here[slab, step + 1, at, :, lanes] * pull[t]
                    out_term = term if out_term is None else out_term + term
                place = slice(n * LANES, (n + 1) * LANES)
                in_terms[rows, place] = in_term
                out_terms[rows, place] = out_term
                later.append(tuple(new))
                slope.append(tuple(turned))
            for t, lanes in enumerate(tiles):
                add_to(grad_push, group == 0, rows, lanes, total[t])
                add_to(grad_width, group == 0, rows, lanes, width_total[t])
            return tuple(later), tuple(slope)

        none = ((zero,) * len(tiles),) * GROUP
        _, slopes = sweep(steps, body, (current, none))
        for at, n in enumerate(names):
            for t, lanes in enumerate(tiles):
                grad_decay[n : n + 1, lanes] = rates[n : n + 1, lanes] * jnp.sum(
                    slopes[at][t], axis=0, keepdims=True
                )
    pushed = grad_push[...]
    grads = (pushed * conv_out[...] + grad_width[...]) * sigmoid(dt_pre[...])
    grad_dt_pre[...] = grads
    grad_dt_bias[...] = jnp.sum(grads, axis=0, keepdims=True)
    grad_direct[...] = pushed * stepsize[...] + skip[...][None] * grad[...]
    partial[:rank, :] = product(dt_weight[...], grads, (1, 1))
    shape = (2 * states, states * LANES)
    column = lax.broadcasted_iota(jnp.int32, shape, 0)
    owner = lax.broadcasted_iota(jnp.int32, shape, 1) // LANES
    total = None
    for terms, base in ((in_terms, 0), (out_terms, states)):
        ones = jnp.where(owner + base == column, 1.0, 0.0).astype(jnp.bfloat16)
        for part in two_parts(terms[...]):
            term = once(ones, part, (1, 1))
            total = term if total is None else total + term
    cols = rank + 2 * states
    partial[rank:cols, :] = total
    row = cols
    for shared in (grad_norm2, grad_router):
        for at in range(0, shared.shape[1], length):
            partial[row : row + shared.shape[0], :] = shared[:, at : at + length]
            row += shared.shape[0]
    partial[row:, :] = jnp.zeros((partial.shape[0] - row, length), jnp.float32)


def conv_back_kernel(experts, ids, p0, p1, p2, p3, xproj_t, grad_direct, mixed, conv_out, extended,
                     marks, conv_weight, coef, grad_dt_pre, grad_decay, grad_dt_bias, grad_skip,
                     normed, halo_normed, conv_high, conv_low, gate_part, rows_in, halo_rows,
                     keep, send, slices,
                     grad_conv, grad_halo, small, grad_extended, summed, weights, whole):
    taps, channels = conv_weight.shape
    cols, states = xproj_t.shape[0], grad_decay.shape[0]
    rank = cols - 2 * states
    length = mixed.shape[0]
    lead = (taps - 1) * SEGMENTS
    summed[...] = (p0[...] + p1[...]) + (p2[...] + p3[...])
    projected = two_parts(summed[:cols, :])
    grad_out = grad_direct[...] + product(projected, xproj_t[...], (0, 0))
    value = mixed[...]
    value_sigmoid = sigmoid(value)
    grad_mixed = grad_out * (value_sigmoid * (1.0 + value * (1.0 - value_sigmoid)))
    grad_extended[...] = jnp.zeros_like(grad_extended)
    first_tap = cols + rank + states
    small[first_tap:, :] = jnp.zeros((small.shape[0] - first_tap, channels), jnp.float32)
    for k in range(taps):
        first = (taps - 1 - k) * SEGMENTS
        masked = grad_mixed * marks[:, k : k + 1]
        small[first_tap + k : first_tap + k + 1, :] = jnp.sum(
            masked * extended[first : first + length, :], axis=0, keepdims=True
        )
        grad_extended[first : first + length, :] += conv_weight[k : k + 1, :] * masked
    grad_conv[...] = grad_extended[lead:, :]
    grad_halo[...] = jnp.zeros_like(grad_halo)
    place = lax.broadcasted_iota(jnp.int32, (SEGMENTS, channels), 0)
    for m in range(taps - 1):
        rows = grad_extended[m * SEGMENTS : (m + 1) * SEGMENTS, :]
        at = SEGMENTS - taps + 1 + m
        grad_halo[at : at + 1, :] = rows[:1, :]
        inside = jnp.where(place == SEGMENTS - 1, 0.0, pltpu.roll(rows, SEGMENTS - 1, 0))
        ends = slice(length - lead + m * SEGMENTS, length - lead + (m + 1) * SEGMENTS)
        grad_conv[ends, :] += inside
    small[:cols, :] = product(projected, conv_out[...])
    low = product(coef[...], grad_dt_pre[...], (0, 0))
    small[cols : cols + rank, :] = low[:rank, :]
    small[cols + rank : first_tap, :] = grad_decay[...]
    last = first_tap + taps
    small[last : last + 1, :] = jnp.sum(grad_mixed, axis=0, keepdims=True)
    small[last + 1 : last + 2, :] = grad_dt_bias[...]
    small[last + 2 : last + 3, :] = grad_skip[...]
    first, row = last + 3, cols
    for count in (1, experts):
        for at in range(0, 2 * channels, length):
            value = summed[row : row + count, :]
            end = at + length
            for piece in range(at // channels, -(-end // channels)):
                low, high = max(at, piece * channels), min(end, (piece + 1) * channels)
                target = first + piece * count
                small[target : target + count, low - piece * channels : high - piece * channels] = (
                    value[:, low - at : high - at]
                )
            row += count
        first += 2 * count
    weights[...] = product(normed[...], grad_conv[...], (0, 0)) + product(
        halo_normed[...], grad_halo[...], (0, 0)
    )
    in_order(ids[1], (weights, small), keep, send)
    weight = conv_high[...], conv_low[...]
    grad = product(grad_conv[...], weight, (1, 1)) + gate_part[...]
    before = product(grad_halo[...], weight, (1, 1))
    value, value_before = rows_in[...], halo_rows[...]
    whole[:length, :] = grad
    whole[length:, :] = jnp.zeros((whole.shape[0] - length, whole.shape[1]), jnp.float32)
    whole[length : length + SEGMENTS, :] = before
    whole[length : length + 1, :] = jnp.sum(
        value * inverse_rms(value) * grad, axis=0, keepdims=True
    ) + jnp.sum(value_before * inverse_rms(value_before) * before, axis=0, keepdims=True)
    cut_slices(ids[0], whole, slices)


def early_weights_kernel(ids, gated, grad_hidden, normed, grad_gate_in, keep, send, whole,
                         gate):
    channels = gated.shape[1]
    halves = product(gated[...], grad_hidden[...], (0, 0))
    whole[:channels, :] = halves[:, :channels]
    whole[channels:, :] = halves[:, channels:]
    gate[...] = product(normed[...], grad_gate_in[...], (0, 0))
    in_order(ids[1], (whole, gate), keep, send)


def in_order(me, wholes, keep, send):
    count = 2 * keep.shape[0]
    levels = count.bit_length() - 1
    for place in range(count):
        block = reversed_bits(place, levels) ^ me
        out, at = (keep, place) if place < count // 2 else (send, place - count // 2)
        first = 0
        for whole in wholes:
            rows = whole.shape[0] // count
            from_row = pl.multiple_of(block * rows, 8)
            out[at, first : first + rows, :] = whole[pl.ds(from_row, rows), :]
            first += rows


def gate_tokens_kernel(ids, grad_gate_in, gate_high, gate_low, out):
    out[...] = product(grad_gate_in[...], (gate_high[...], gate_low[...]), (1, 1))


def extra_kernel(ids, p0, p1, p2, p3, out, held, whole):
    join_slices(ids[0], (p0, p1, p2, p3), held, whole)
    out[...] = whole[whole.shape[0] - 2 * SEGMENTS : whole.shape[0] - SEGMENTS, :]


def grad_tokens_kernel(taps, ids, p0, p1, p2, p3, from_next, rows, gain, grad_hidden, out,
                       held, whole, tiles):
    join_slices(ids[0], (p0, p1, p2, p3), held, whole)
    length = rows.shape[0]
    lead = (taps - 1) * SEGMENTS
    for m in range(taps - 1):
        row = length - lead + (m + 1) * SEGMENTS - 1
        at = SEGMENTS - taps + 1 + m
        whole[row : row + 1, :] += from_next[at : at + 1, :]
    value = rows[...]
    whole[:length, :] = (
        norm_back(value, inverse_rms(value), gain[...][None], whole[:length, :]) + grad_hidden[...]
    )
    deinterleave_to(whole, tiles, out)


def early_out_kernel(ids, summed, out_weight):
    count, rows, channels = summed.shape
    levels = count.bit_length() - 1
    for block in range(count):
        value = summed[reversed_bits(block ^ ids[1], levels)]
        half, row = divmod(block * rows, channels)
        out_weight[row : row + rows, half * channels : (half + 1) * channels] = value


def weights_out_kernel(counts, ids, early, late, weight, *rest):
    outs, small = rest[:-1], rest[-1]
    count, rows = early.shape[0], early.shape[1]
    more = late.shape[1] - rows
    levels = count.bit_length() - 1
    for block in range(count):
        place = reversed_bits(block ^ ids[1], levels)
        small[block * more : (block + 1) * more, :] = late[place, rows:, :]
        weight[block * rows : (block + 1) * rows, 0, :] = late[place, :rows, :]
        weight[block * rows : (block + 1) * rows, 1, :] = early[place]
    first = 0
    channels = small.shape[1]
    for out, used in zip(outs, counts):
        per = out.shape[-1] // channels
        each = used // per
        for piece in range(per):
            lanes = slice(piece * channels, (piece + 1) * channels)
            if len(out.shape) == 1:
                out[lanes] = small[first, :]
            else:
                out[:, lanes] = small[first : first + each, :]
            first += each


def local(
    tokens, norm1_gain, in_weight, conv_weight, conv_bias, xproj_weight, dt_weight, dt_bias,
    decay_log, skip_gain, out_weight, norm2_gain, router_weight, expert_in, expert_out,
    segments, expert_ids, cotangent,
):
    length, width = tokens.shape
    taps, channels = conv_weight.shape
    experts = router_weight.shape[1]
    wide = experts
    capacity = 5 * length // (4 * experts)
    states, rank = decay_log.shape[0], dt_weight.shape[0]
    chips = wide // 2
    slots = chips * capacity
    steps = length // SEGMENTS
    me_wide = lax.axis_index("wide")
    ids = jnp.stack([lax.axis_index("narrow"), me_wide, me_wide & 1, me_wide // 2]).astype(jnp.int32)
    half, double = length // 2, width // 2
    bf16 = jnp.bfloat16
    rows_shape, channel_rows = shape_of(length, width), shape_of(length, channels)
    packed, packed_slots = shape_of(half, double), shape_of(slots, double)
    vmem = lambda *shape: pltpu.VMEM(shape, jnp.float32)
    xproj_t, router_t = xproj_weight.T, router_weight.T
    cols = xproj_t.shape[0]

    tiled = vmem(width // LANES, length, LANES)

    halo_rows = wide_shift(tokens[length - SEGMENTS :], 1)

    (marks, slots_own, slots_other, rows_own, rows_other, rows_slice, cot_slice, cot_own,
     cot_other) = call(
        functools.partial(start_kernel, capacity),
        [shape_of(length, SEGMENTS)]
        + [shape_of(slots, length, dtype=bf16)] * 2
        + [shape_of(length, slots, dtype=bf16)] * 2
        + [packed, packed, packed_slots, packed_slots],
        ids, segments.reshape(wide, length), expert_ids.reshape(1, length), tokens, cotangent,
        scratch=[vmem(length, width)] * 3 + [tiled, pltpu.SemaphoreType.DMA((2,))],
        far_in=[2, 3],
    )
    cot_pair = cot_own + core_swap(cot_other)
    rows, normed, conv_in, gate_in, conv_high, conv_low, gate_high, gate_low = call(
        front_kernel,
        [rows_shape, rows_shape, channel_rows, channel_rows]
        + [shape_of(width, channels, dtype=bf16)] * 4,
        ids, tokens, norm1_gain, in_weight,
        scratch=[tiled, vmem(2, width, channels)], after=[cot_own],
    )
    mixed, conv_out, partial, extended, halo_normed = call(
        conv_kernel,
        [channel_rows, channel_rows, shape_of(cols, length),
         shape_of(length + (taps - 1) * SEGMENTS, channels), shape_of(SEGMENTS, width)],
        ids, halo_rows, norm1_gain, conv_high, conv_low, conv_in, marks, conv_weight,
        conv_bias, xproj_t, after=[cot_pair],
    )
    partials = narrow_all(partial)

    partials = narrow_all(partial)

    cot_blocks = chip_each(hold(cot_pair, partial), chips)

    entry_shape = shape_of(2, states, SEGMENTS, channels)
    total_rows = -(-(states + 1) // 8) * 8
    coef, dt_pre, stepsize, drive, stepd, rates, entry, total = call(
        totals_kernel,
        [shape_of(length, LANES)] + [channel_rows] * 4
        + [shape_of(states, channels), entry_shape, shape_of(total_rows, channels)],
        ids, *partials, dt_weight, dt_bias, decay_log, conv_out, marks,
        scratch=[vmem(LANES, channels)],
    )
    total_shape = shape_of(total_rows, channels)
    early, late, chip_total = call(
        pair_kernel, [total_shape] * 3, ids, total, core_swap(total), rates, after=[cot_blocks]
    )
    chip_totals = chip_all(chip_total, chips)
    slabs = states // GROUP
    cot_parts = narrow_all(hold(cot_blocks, chip_total))
    kept_shape = (slabs, steps + 1, GROUP, SEGMENTS, channels)
    ssm_skip, gated, mixer_slices, kept = call(
        functools.partial(states_kernel, rank),
        [channel_rows, channel_rows, shape_of(4, half, double), shape_of(*kept_shape)],
        ids, stepd, drive, coef, rates, entry, early, conv_out, gate_in, skip_gain,
        out_weight, *chip_totals,
        scratch=[vmem(chips, total_rows, channels), vmem(length, width), vmem(*kept_shape),
                 pltpu.SemaphoreType.DMA((slabs,))],
        out_place=[3],
    )
    mixer_slices = hold(mixer_slices, *cot_parts)
    expert_rows, square = shape_of(2 * slots, width), (expert_in.shape[1], expert_in.shape[2])
    hidden_units = square[1]
    raw, cot, in_high, in_low, out_high, out_low = call(
        raw_kernel,
        [shape_of(2 * slots, hidden_units), expert_rows]
        + [shape_of(*square, dtype=bf16)] * 2
        + [shape_of(square[1], square[0], dtype=bf16)] * 2,
        ids, *cot_parts, expert_in[0], expert_out[0],
        scratch=[vmem(4, slots, double)], after=[mixer_slices],
    )
    hidden_slice, hidden_own, hidden_other = call(
        dispatch_kernel,
        [packed, packed_slots, packed_slots],
        ids, *narrow_each(mixer_slices), rows_slice, slots_own, slots_other, after=[raw],
    )
    hidden_parts = narrow_all(chip_each(hidden_own + core_swap(hidden_other), chips))
    slices_shape = shape_of(4, slots, double)
    grad_slices, second, act, grad_pre, gates, grad_logits, grad_norm2 = call(
        expert_kernel,
        [slices_shape, expert_rows] + [shape_of(2 * slots, hidden_units)] * 2
        + [shape_of(2 * slots, 1), shape_of(2 * slots, experts), shape_of(1, width)],
        ids, *hidden_parts, raw, in_high, in_low, norm2_gain, router_t,
        scratch=[vmem(4, slots, double), vmem(2 * slots, width)],
    )
    grad_mine = pair_sum(narrow_each(grad_slices))
    value_slices, grad_expert_in, grad_expert_out, grad_router_t = call(
        expert_rest_kernel,
        [slices_shape, shape_of(*square), shape_of(square[1], square[0]),
         shape_of(experts, width)],
        ids, second, act, grad_pre, gates, grad_logits, cot, out_high, out_low,
        scratch=[vmem(2 * slots, width)],
    )
    grad_back = chip_each(grad_mine, chips)
    value_mine = pair_sum(narrow_each(value_slices))
    grad_slice = call(
        home_kernel, [packed], ids, grad_back, core_swap(grad_back), cot_slice, rows_own,
        rows_other, after=[value_mine],
    )[0]
    grad_parts = narrow_all(grad_slice)
    value_back = chip_each(value_mine, chips)

    def whole_of(parts, after=()):
        return call(
            whole_kernel, [rows_shape], ids, *parts, after=after,
            scratch=[vmem(4, half, double), vmem(length, width), tiled],
        )[0]

    grad_hidden, grad_ssm, grad_gate_in, grad_skip, back_entry, back_total = call(
        functools.partial(leaving_kernel, rank),
        [rows_shape, channel_rows, channel_rows, shape_of(1, channels), entry_shape,
         shape_of(states, channels)],
        ids, *grad_parts, out_weight, gate_in, ssm_skip, conv_out, stepd, coef, rates,
        scratch=[vmem(4, half, double)], after=[value_back],
    )
    other_back = core_swap(back_total)
    block = width // wide
    half_blocks = shape_of(wide // 2, 2 * block, channels)
    early_keep, early_send = call(
        early_weights_kernel,
        [half_blocks, half_blocks],
        ids, gated, grad_hidden, normed, grad_gate_in,
        scratch=[vmem(width, channels)] * 2,
    )
    back_late, back_chip = call(
        pair_back_kernel, [shape_of(states, channels)] * 2,
        ids, back_total, other_back, early, rates, after=[early_keep],
    )
    back_totals = chip_all(back_chip, chips)
    early_arrived = core_swap(hold(early_send, back_chip))
    value_other = core_swap(hold(value_back, back_chip))
    out_sum, gate_sum = (
        WideSum(early_keep[:, rows], early_send[:, rows])
        for rows in (slice(0, block), slice(block, None))
    )
    out_sum.arrived, gate_sum.arrived = early_arrived[:, :block], early_arrived[:, block:]
    out_sum.finish()
    gate_sum.finish()
    first_step = out_sum.start(*back_totals)

    shared_rows = (experts + 1) * (width // length)
    partial_rows = cols + shared_rows + -(cols + shared_rows) % 8
    partial_back, grad_direct, grad_dt_pre, grad_decay, grad_dt_bias = call(
        functools.partial(adjoint_kernel, rank, chips),
        [shape_of(partial_rows, length), channel_rows, channel_rows, shape_of(states, channels),
         shape_of(1, channels)],
        ids, stepd, drive, grad_ssm, coef, rates, back_entry, kept, early, late, back_late,
        conv_out, stepsize, dt_pre, skip_gain, dt_weight, grad_norm2, grad_router_t,
        *chip_totals, *back_totals,
        scratch=[vmem(chips, 1, channels), vmem(chips, states, channels), vmem(*kept_shape),
                 vmem(length, states * LANES), vmem(length, states * LANES),
                 vmem(length, channels), vmem(length, channels),
                 pltpu.SemaphoreType.DMA((slabs,))],
        in_place=[6], after=[out_sum.send, gate_sum.send, value_other],
    )
    partials_back = narrow_all(partial_back)
    (output_slice,) = call(
        home_kernel, [packed], ids, value_back, value_other, hidden_slice, rows_own, rows_other,
        after=[partial_back],
    )
    out_sum.finish(partial_back)
    out_step = out_sum.start()
    gate_step = gate_sum.start(partial_back)
    gate_part = call(
        gate_tokens_kernel, [rows_shape], ids, grad_gate_in, gate_high, gate_low,
        after=[partial_back],
    )[0]
    grain = 8 * wide
    small_rows = cols + rank + states + taps + 3 + (experts + 1) * (width // channels)
    small_rows += -small_rows % grain
    more = small_rows // wide
    half_blocks = shape_of(wide // 2, block + more, channels)
    token_rows = length + 2 * SEGMENTS
    conv_keep, conv_send, token_slices = call(
        functools.partial(conv_back_kernel, experts),
        [half_blocks, half_blocks, shape_of(4, token_rows // 2, double)],
        ids, *partials_back, xproj_t, grad_direct, mixed, conv_out, extended, marks,
        conv_weight, coef, grad_dt_pre, grad_decay, grad_dt_bias, grad_skip,
        normed, halo_normed, conv_high, conv_low, gate_part, rows, halo_rows,
        scratch=[vmem(length, channels), vmem(SEGMENTS, channels), vmem(small_rows, channels),
                 vmem(length + (taps - 1) * SEGMENTS, channels), vmem(partial_rows, length),
                 vmem(width, channels), vmem(token_rows, width)],
        after=[output_slice, out_sum.arrived, gate_sum.arrived],
    )
    out_sum.finish(conv_keep)
    gate_sum.finish(conv_keep)
    conv_sum = WideSum(conv_keep, conv_send)
    conv_sum.start()
    conv_sum.finish()
    levels = len(conv_sum.swaps)

    def extra_of(parts):
        return call(
            extra_kernel, [shape_of(SEGMENTS, width)], ids, *parts,
            scratch=[vmem(4, token_rows // 2, double), vmem(token_rows, width)],
        )[0]

    def grad_tokens_of(parts, from_next):
        return call(
            functools.partial(grad_tokens_kernel, taps),
            [rows_shape],
            ids, *parts, from_next, rows, norm1_gain, grad_hidden,
            scratch=[vmem(4, token_rows // 2, double), vmem(token_rows, width), tiled],
        )[0]

    def out_weight_of(total, *others):
        return call(
            early_out_kernel, [shape_of(channels, width)], ids, total, after=others
        )[0]

    if levels == 3:
        sums = conv_sum, gate_sum, out_sum
        joint = [conv_sum.start(), *start_both(gate_sum, out_sum)]
        token_each = narrow_each(token_slices)
        for part in sums:
            part.finish(*joint, *token_each)
        joint = [*start_both(conv_sum, gate_sum), out_sum.start()]
        token_parts = narrow_all(pair_sum(token_each))
        for part in sums:
            part.finish(*joint, *token_parts)
        joint = [conv_sum.start(), gate_sum.start(), out_sum.start()]
        extra = extra_of(token_parts)
        from_next = wide_shift(extra, -1)
        norm1_other = core_swap(extra)
        for part in sums:
            part.finish(*joint, from_next, norm1_other)
        joint = [conv_sum.start(), gate_sum.start()]
        output_parts = narrow_all(hold(output_slice, from_next))
        grad_tokens = grad_tokens_of(token_parts, from_next)
        sum_out_weight = out_weight_of(out_sum.keep, from_next)
        for part in sums[:2]:
            part.finish(*joint, *output_parts, grad_tokens, sum_out_weight)
        norm1_parts = chip_all(hold(extra + norm1_other, grad_tokens), chips)
        sum_norm1 = pair_sum(norm1_parts)
        conv_sum.start()
        output = whole_of(output_parts, after=[conv_sum.send])
        conv_sum.finish(output, sum_norm1)
    else:
        token_parts = narrow_all(pair_sum(narrow_each(token_slices)))
        extra = extra_of(token_parts)
        grad_tokens = grad_tokens_of(token_parts, wide_shift(extra, -1))
        output = whole_of(narrow_all(output_slice))
        sum_out_weight = out_weight_of(out_sum.rest())
        sum_norm1 = pair_sum(chip_all(extra + core_swap(extra), chips))
    per = width // channels
    counts = (cols, rank, states, taps, 1, 1, 1, per, per * experts)
    (weight_sum, sum_xproj_t, sum_dt_weight, sum_decay, sum_taps, sum_conv_bias, sum_dt_bias,
     sum_skip, sum_norm2, sum_router_t) = call(
        functools.partial(weights_out_kernel, counts),
        [shape_of(width, 2, channels)]
        + [shape_of(rows, channels) for rows in (cols, rank, states, taps)]
        + [shape_of(channels)] * 3 + [shape_of(width), shape_of(experts, width)],
        ids, gate_sum.rest(), conv_sum.rest(), scratch=[vmem(small_rows, channels)],
    )
    return (
        output,
        grad_tokens,
        sum_norm1[0],
        weight_sum,
        sum_taps,
        sum_conv_bias,
        sum_xproj_t.T,
        sum_dt_weight,
        sum_dt_bias,
        sum_decay,
        sum_skip,
        sum_out_weight,
        sum_norm2,
        sum_router_t.T,
        grad_expert_in[None],
        grad_expert_out[None],
    )


def solution(mesh):
    in_specs = (
        P("wide", None),
        P(),
        P(None, None, "narrow"),
        P(None, "narrow"),
        P("narrow"),
        P("narrow", None),
        P(None, "narrow"),
        P("narrow"),
        P(None, "narrow"),
        P("narrow"),
        P("narrow", None),
        P(),
        P(),
        P("wide", None, "narrow"),
        P("wide", "narrow", None),
        P(),
        P("wide", None),
        P("wide", None),
    )
    out_specs = (
        P("wide", None),
        P("wide", None),
        P(),
        P(None, None, "narrow"),
        P(None, "narrow"),
        P("narrow"),
        P("narrow", None),
        P(None, "narrow"),
        P("narrow"),
        P(None, "narrow"),
        P("narrow"),
        P("narrow", None),
        P(),
        P(),
        P("wide", None, "narrow"),
        P("wide", "narrow", None),
    )
    return jax.shard_map(local, mesh=mesh, in_specs=in_specs, out_specs=out_specs, check_vma=False)
```

```python
import functools
import math

import jax
import jax.numpy as jnp
from jax import lax
from jax.experimental import pallas as pl
from jax.experimental.pallas import tpu as pltpu
from jax.sharding import PartitionSpec as P

EPSILON = 1e-05
SEGMENTS = 8
LANES = 128
NEVER = 1e30
VMEM_SPARE = 4 * 1024 * 1024
GROUP = 4
LOG2E = 1.4426950408889634


def shape_of(*shape, dtype=jnp.float32):
    return jax.ShapeDtypeStruct(shape, dtype)


def call(kernel, outs, ids, *arrays, scratch=(), after=(), far_in=(), out_place=(), in_place=()):
    in_vmem = pl.BlockSpec(memory_space=pltpu.VMEM)
    anywhere = pl.BlockSpec(memory_space=pl.ANY)
    far = pl.BlockSpec(memory_space=pltpu.HBM)
    arrays = [
        pltpu.with_memory_space_constraint(array, pltpu.HBM) if i in far_in else array
        for i, array in enumerate(arrays)
    ]
    size = lambda a: math.prod(a.shape) * jnp.dtype(a.dtype).itemsize
    held = [
        size(a)
        for refs, skipped in ((arrays, (*in_place, *far_in)), (outs, out_place))
        for i, a in enumerate(refs)
        if i not in skipped
    ]
    held += [size(a) for a in scratch if hasattr(a, "dtype") and hasattr(a, "shape")
             and jnp.issubdtype(a.dtype, jnp.number)]
    given = 1 + len(arrays)

    def run(*refs):
        kernel(*refs[:given], *refs[given + len(after) :])

    return pl.pallas_call(
        run,
        out_shape=outs,
        in_specs=[pl.BlockSpec(memory_space=pltpu.SMEM)]
        + [far if i in far_in else anywhere if i in in_place else in_vmem
           for i in range(len(arrays))]
        + [anywhere] * len(after),
        out_specs=[anywhere if i in out_place else in_vmem for i in range(len(outs))],
        scratch_shapes=scratch,
        compiler_params=pltpu.CompilerParams(vmem_limit_bytes=sum(held) + VMEM_SPARE),
        cost_estimate=pl.CostEstimate(flops=1, bytes_accessed=1, transcendentals=0),
    )(ids, *arrays, *after)


def two_parts(value):
    high = value.astype(jnp.bfloat16)
    return high, (value - high.astype(jnp.float32)).astype(jnp.bfloat16)


def once(left, right, contract=(1, 0)):
    return lax.dot_general(
        left,
        right,
        (((contract[0],), (contract[1],)), ((), ())),
        preferred_element_type=jnp.float32,
    )


def product(left, right, contract=(1, 0)):
    left_high, left_low = left if isinstance(left, tuple) else two_parts(left)
    right_high, right_low = right if isinstance(right, tuple) else two_parts(right)
    free = 1 - contract[0]
    size = left_high.shape[free]
    if size % (16, LANES)[free]:
        return once(left_high, right_high, contract) + (
            once(left_high, right_low, contract) + once(left_low, right_high, contract)
        )
    both = once(jnp.concatenate([left_high, left_low], axis=free), right_high, contract)
    return both[:size] + (both[size:] + once(left_high, right_low, contract))


def select_rows(chosen, rows, contract=(1, 0)):
    high, low = two_parts(rows)
    return once(chosen, high, contract) + once(chosen, low, contract)


def inverse_rms(rows):
    return lax.rsqrt(jnp.mean(rows * rows, axis=-1, keepdims=True) + EPSILON)


def norm_back(rows, inverse, gain, grad):
    scaled = gain * grad
    mean = jnp.mean(rows * scaled, axis=-1, keepdims=True)
    return inverse * scaled - rows * (inverse * inverse * inverse) * mean


def sigmoid(value):
    return 1.0 / (1.0 + jnp.exp(-value))


def softplus(value):
    return jnp.maximum(value, 0.0) + jnp.log1p(jnp.exp(-jnp.abs(value)))


def gelu_parts(value):
    spread_of = 0.5 * (1.0 + lax.erf(value * (0.5**0.5)))
    density = jnp.exp(-0.5 * value * value) * ((2.0 * jnp.pi) ** -0.5)
    return value * spread_of, spread_of + value * density


def cut_slices(me, whole, out):
    rows, part = whole.shape[0] // 2, whole.shape[1] // 4
    for j in range(4):
        out[me ^ j, :, :part] = whole[:rows, part * j : part * (j + 1)]
        out[me ^ j, :, part:] = whole[rows:, part * j : part * (j + 1)]


def join_slices(me, parts, held, whole):
    rows, part = whole.shape[0] // 2, whole.shape[1] // 4
    for key, value in enumerate(parts):
        held[key] = value[...]
    for j in range(4):
        value = held[me ^ j]
        whole[:rows, part * j : part * (j + 1)] = value[:, :part]
        whole[rows:, part * j : part * (j + 1)] = value[:, part:]


def reversed_bits(value, levels):
    place = 0
    for level in range(levels):
        place = place + (((value >> level) & 1) << (levels - 1 - level))
    return place


def interleave_from(rows, held, out):
    length, width = out.shape
    steps = length // SEGMENTS
    for tile in range(width // LANES):
        lanes = slice(tile * LANES, (tile + 1) * LANES)
        held[tile] = rows[:, lanes]
        for step in range(steps):
            out[step * SEGMENTS : (step + 1) * SEGMENTS, lanes] = held[
                tile, pl.ds(step, SEGMENTS, stride=steps), :
            ]


def deinterleave_to(rows, held, out):
    length, width = out.shape
    steps = length // SEGMENTS
    for tile in range(width // LANES):
        lanes = slice(tile * LANES, (tile + 1) * LANES)
        for step in range(steps):
            held[tile, pl.ds(step, SEGMENTS, stride=steps), :] = rows[
                step * SEGMENTS : (step + 1) * SEGMENTS, lanes
            ]
        out[:, lanes] = held[tile]


def narrow_swap(value, key):
    return lax.ppermute(value, "narrow", [(i, i ^ key) for i in range(4)])


def core_swap(value):
    count = lax.axis_size("wide")
    return lax.ppermute(value, "wide", [(i, i ^ 1) for i in range(count)])


def chip_swap(value, key):
    count = lax.axis_size("wide")
    return lax.ppermute(value, "wide", [(i, i ^ (2 * key)) for i in range(count)])


def wide_shift(value, distance):
    devices = range(lax.axis_size("wide"))
    route = [(i - distance, i) for i in devices if i - distance in devices]
    return lax.ppermute(value, "wide", route)


def hold(value, *others):
    if not others:
        return value
    return lax.optimization_barrier((value, others))[0]


def narrow_all(value):
    far = narrow_swap(value, 3)
    return [value, narrow_swap(value, 1), narrow_swap(value, 2), far]


def narrow_each(slices):
    far = narrow_swap(slices[3], 3)
    return [slices[0], narrow_swap(slices[1], 1), narrow_swap(slices[2], 2), far]


def pair_sum(parts):
    while len(parts) > 1:
        parts = [a + b for a, b in zip(parts[::2], parts[1::2])]
    return parts[0]


def chip_blocks(blocks, chips):
    rows = blocks.shape[0] // chips
    order = sorted(range(1, chips), reverse=True)
    arrived = {k: chip_swap(blocks[k * rows : (k + 1) * rows], k) for k in order}
    arrived[0] = blocks[:rows]
    return [arrived[k] for k in range(chips)]


def chip_each(blocks, chips):
    return jnp.concatenate(chip_blocks(blocks, chips))


def chip_all(value, chips):
    arrived = {k: chip_swap(value, k) for k in sorted(range(1, chips), reverse=True)}
    arrived[0] = value
    return [arrived[k] for k in range(chips)]


class WideSum:
    def __init__(self, keep, send):
        levels = lax.axis_size("wide").bit_length() - 1
        self.swaps = [core_swap] + [
            functools.partial(chip_swap, key=1 << level) for level in range(levels - 1)
        ]
        self.keep, self.send, self.arrived = keep, send, None
        self.level, self.back = 0, False

    def prepare(self):
        if not self.back and self.level == len(self.swaps):
            self.back = True
        if self.back:
            self.level -= 1
            self.send = self.keep
        return self.send

    def start(self, *others):
        self.prepare()
        self.arrived = self.swaps[self.level](hold(self.send, *others))
        return self.arrived

    def start_with(self, rider):
        sent = self.prepare()
        joined = jnp.concatenate([sent.reshape(1, -1, sent.shape[2]), rider], axis=1)
        arrived = self.swaps[self.level](joined)
        rows = rider.shape[1]
        self.arrived = arrived[:, :-rows].reshape(sent.shape)
        return self.arrived, arrived[:, -rows:]

    def finish(self, *others):
        arrived = hold(self.arrived, *others) if others else self.arrived
        if self.back:
            self.keep = jnp.concatenate([self.keep, arrived])
            return
        self.level += 1
        if self.level == len(self.swaps):
            self.keep = self.keep + arrived
            return
        half = self.keep.shape[0] // 2
        self.send = self.keep[half:] + arrived[half:]
        self.keep = self.keep[:half] + arrived[:half]

    def rest(self):
        while not (self.back and self.level == 0):
            self.start()
            self.finish()
        return self.keep


def start_both(one, two):
    first, second = one.prepare(), two.prepare()
    rows = first.shape[1]
    arrived = one.swaps[one.level](jnp.concatenate([first, second], axis=1))
    one.arrived, two.arrived = arrived[:, :rows], arrived[:, rows:]
    return one.arrived, two.arrived


def route_kernel(capacity, ids, segments, expert_ids, marks, slots_own, slots_other,
                 rows_own, rows_other):
    wide_at, core, chip = ids[1], ids[2], ids[3]
    length = expert_ids.shape[1]
    per = length // LANES
    experts = segments.shape[0] // per
    steps = length // SEGMENTS

    def block(at):
        return jnp.concatenate([segments[pl.ds(at * per + i, 1), :] for i in range(per)], axis=1)

    own, before = block(wide_at), block(jnp.maximum(wide_at - 1, 0))
    lane = lax.broadcasted_iota(jnp.int32, (1, length), 1)
    here = lax.broadcasted_iota(jnp.int32, (SEGMENTS, length), 0)
    table = jnp.ones((SEGMENTS, length), jnp.float32)
    for k in range(1, 4):
        back = jnp.where(lane < k, pltpu.roll(before, k, 1), pltpu.roll(own, k, 1))
        same = (back == own) & ((lane >= k) | (wide_at > 0))
        table = jnp.where(here == k, jnp.where(same, 1.0, 0.0), table)
    live = own >= 0
    expert = expert_ids[...]
    at = lax.broadcasted_iota(jnp.int32, (experts, length), 0)
    hits = jnp.where((at == expert) & live, 1.0, 0.0)
    first = lax.broadcasted_iota(jnp.int32, (length, length), 0)
    second = lax.broadcasted_iota(jnp.int32, (length, length), 1)
    earlier = jnp.where(first < second, 1.0, 0.0).astype(jnp.bfloat16)
    ranks = once(hits.astype(jnp.bfloat16), earlier)
    rank = jnp.sum(ranks * hits, axis=0, keepdims=True).astype(jnp.int32)
    kept = live & (rank < capacity)
    order = jnp.where(
        (first % SEGMENTS) * steps + first // SEGMENTS == second, 1.0, 0.0
    ).astype(jnp.bfloat16)
    marks[...] = once(order, table.astype(jnp.bfloat16), (1, 1))
    slot = jnp.where(kept, ((expert >> 1) ^ chip) * capacity + rank, -1)
    count = slots_own.shape[0]
    slot_at = lax.broadcasted_iota(jnp.int32, (count, length), 0)
    for which, slots, rows in ((core, slots_own, rows_own), (1 - core, slots_other, rows_other)):
        mine = (slot_at == slot) & ((expert & 1) == which)
        chosen = jnp.where(mine, 1.0, 0.0).astype(jnp.bfloat16)
        slots[...] = once(chosen, order, (1, 1)).astype(jnp.bfloat16)
        rows[...] = once(order, chosen, (1, 1)).astype(jnp.bfloat16)


def front_kernel(ids, tokens, gain, conv_high, conv_low, gate_high, gate_low,
                 rows, normed, conv_in, gate_in, held):
    interleave_from(tokens, held, rows)
    value = rows[...]
    scaled = value * inverse_rms(value) * gain[...][None]
    normed[...] = scaled
    parts = two_parts(scaled)
    conv_in[...] = product(parts, (conv_high[...], conv_low[...]))
    gate_in[...] = product(parts, (gate_high[...], gate_low[...]))


def start_kernel(capacity, ids, segments_far, expert_ids_far, tokens_far, cotangent_far, weight_far,
                 marks, slots_own, slots_other, rows_own, rows_other,
                 rows_slice, cot_slice, own, other, conv_high, conv_low, gate_high, gate_low,
                 segments, expert_ids, tokens, cotangent, weight, rows, held, branch,
                 sems):
    pairs = (
        (segments_far, segments),
        (expert_ids_far, expert_ids),
        (tokens_far, tokens),
        (cotangent_far, cotangent),
        (weight_far, weight),
    )
    copies = [
        pltpu.make_async_copy(far, near, sems.at[i]) for i, (far, near) in enumerate(pairs)
    ]
    for copy in copies:
        copy.start()
    copies[0].wait()
    copies[1].wait()
    route_kernel(capacity, ids, segments, expert_ids, marks, slots_own, slots_other,
                 rows_own, rows_other)
    copies[2].wait()
    copies[3].wait()
    slices_kernel(ids, tokens, cotangent, slots_own, slots_other, rows_slice, cot_slice, own, other,
                  rows, held)
    copies[4].wait()
    for k, (high, low) in enumerate(((conv_high, conv_low), (gate_high, gate_low))):
        branch[k] = weight[:, k, :]
        high[...], low[...] = two_parts(branch[k])


def slices_kernel(ids, tokens, cotangent, slots_own, slots_other,
                  rows_slice, cot_slice, own, other, rows, held):
    me, core = ids[0], ids[2]
    half, part = tokens.shape[0] // 2, tokens.shape[1] // 4
    for source, out in ((tokens, rows_slice), (cotangent, cot_slice)):
        interleave_from(source, held, rows)
        for j in range(4):
            @pl.when(me == j)
            def _():
                out[:, :part] = rows[:half, part * j : part * (j + 1)]
                out[:, part:] = rows[half:, part * j : part * (j + 1)]
    send_slots(core, cot_slice[...], slots_own[...], slots_other[...], own, other)


def send_slots(core, packed, slots_own, slots_other, own, other):
    half = packed.shape[1] // 2
    lane = lax.broadcasted_iota(jnp.int32, packed.shape, 1)
    left = jnp.where(lane < half, packed, 0.0)
    right = jnp.where(lane < half, 0.0, packed)
    second = core == 1
    top = jnp.where(second, pltpu.roll(left, half, 1), left)
    bottom = jnp.where(second, right, pltpu.roll(right, half, 1))
    placed = jnp.concatenate([top, bottom])
    own[...] = select_rows(slots_own, placed)
    other[...] = select_rows(slots_other, placed)


def conv_kernel(ids, halo, gain, conv_high, conv_low, conv_in, marks, conv_weight, conv_bias,
                xproj_t, mixed, conv_out, partial, extended, halo_normed):
    taps, channels = conv_weight.shape
    length = conv_in.shape[0]
    lead = (taps - 1) * SEGMENTS
    rows = halo[...]
    scaled = rows * inverse_rms(rows) * gain[...][None]
    halo_normed[...] = scaled
    halo_conv = product(scaled, (conv_high[...], conv_low[...]))
    place = lax.broadcasted_iota(jnp.int32, (SEGMENTS, channels), 0)
    for m in range(taps - 1):
        ends = conv_in[length - lead + m * SEGMENTS : length - lead + (m + 1) * SEGMENTS, :]
        at = SEGMENTS - taps + 1 + m
        extended[m * SEGMENTS : (m + 1) * SEGMENTS, :] = jnp.where(
            place == 0, halo_conv[at : at + 1, :], pltpu.roll(ends, 1, 0)
        )
    extended[lead:, :] = conv_in[...]
    total = jnp.broadcast_to(conv_bias[...][None], (length, channels))
    for k in range(taps):
        first = (taps - 1 - k) * SEGMENTS
        total += conv_weight[k : k + 1, :] * extended[first : first + length, :] * marks[:, k : k + 1]
    mixed[...] = total
    out = total * sigmoid(total)
    conv_out[...] = out
    partial[...] = product(xproj_t[...], out, (1, 1))


def rows_at(step):
    return pl.ds(pl.multiple_of(step * SEGMENTS, SEGMENTS), SEGMENTS)


def spread(row):
    return jnp.broadcast_to(row, (SEGMENTS, row.shape[-1]))


def column_of(rows, column):
    return jnp.broadcast_to(rows[:, column : column + 1], (SEGMENTS, LANES))


def sweep(count, body, carry):
    return lax.fori_loop(0, count, body, carry, unroll=True)


def add_to(ref, first, rows, lanes, value):
    if first:
        ref[rows, lanes] = value
    else:
        ref[rows, lanes] += value


def chain_pieces(decay, value, backward):
    place = lax.broadcasted_iota(jnp.int32, decay.shape, 0)
    if backward:
        place = SEGMENTS - 1 - place

    def moved(array, distance):
        return pltpu.roll(array, (SEGMENTS - distance) if backward else distance, 0)

    distance = 1
    while distance < SEGMENTS:
        inside = place >= distance
        value = jnp.where(inside, decay * moved(value, distance) + value, value)
        decay = jnp.where(inside, decay * moved(decay, distance), decay)
        distance *= 2
    first = place == 0
    before = jnp.where(first, 0.0, moved(value, 1))
    factor = jnp.where(first, 1.0, moved(decay, 1))
    return factor, before, value


def totals_kernel(ids, p0, p1, p2, p3, dt_weight, dt_bias, decay_log, conv_out, marks,
                  coef, dt_pre, stepsize, drive, stepd, rates, entry, total, padded):
    states, channels = decay_log.shape
    rank = dt_weight.shape[0]
    length = conv_out.shape[0]
    steps = length // SEGMENTS
    projected = (p0[...] + p1[...]) + (p2[...] + p3[...])
    missing = LANES - projected.shape[0]
    coef[...] = jnp.concatenate([projected, jnp.zeros((missing, length), jnp.float32)]).T
    padded[...] = jnp.zeros_like(padded)
    padded[:rank, :] = dt_weight[...]
    pre = product(coef[...], padded[...]) + dt_bias[...][None]
    dt_pre[...] = pre
    size = softplus(pre)
    stepsize[...] = size
    drive[...] = size * conv_out[...]
    stepd[...] = jnp.where(marks[:, 1:2] > 0.5, size, NEVER)
    rates[...] = -jnp.exp(decay_log[...])
    total[...] = jnp.zeros_like(total)
    zero = jnp.zeros((SEGMENTS, LANES), jnp.float32)
    tiles = [slice(at, at + LANES) for at in range(0, channels, LANES)]
    sums = [zero] * len(tiles)
    for step in range(steps):
        rows = slice(step * SEGMENTS, (step + 1) * SEGMENTS)
        sums = [value + stepd[rows, lanes] for value, lanes in zip(sums, tiles)]
    for value, lanes in zip(sums, tiles):
        total[states : states + 1, lanes] = jnp.sum(value, axis=0, keepdims=True)
    for group in range(0, states, GROUP):
        names = range(group, group + GROUP)
        rate = [[spread(rates[n : n + 1, lanes] * LOG2E) for lanes in tiles] for n in names]

        def body(step, current):
            rows = rows_at(step)
            near = coef[rows, :]
            width = [stepd[rows, lanes] for lanes in tiles]
            push = [drive[rows, lanes] for lanes in tiles]
            later = []
            for at, n in enumerate(names):
                entering = column_of(near, rank + n)
                later.append(tuple(
                    jnp.exp2(width[t] * rate[at][t]) * current[at][t] + push[t] * entering
                    for t in range(len(tiles))
                ))
            return tuple(later)

        current = sweep(steps, body, ((zero,) * len(tiles),) * GROUP)
        for at, n in enumerate(names):
            for t, lanes in enumerate(tiles):
                decay = jnp.exp2(sums[t] * rate[at][t])
                factor, before, last = chain_pieces(decay, current[at][t], False)
                entry[0, n, :, lanes] = factor
                entry[1, n, :, lanes] = before
                total[n : n + 1, lanes] = last[SEGMENTS - 1 :, :]


def pair_kernel(ids, total, other, rates, early, late, chip):
    states = rates.shape[0]
    second = ids[2] == 1
    mine, theirs = total[...], other[...]
    first, last = jnp.where(second, theirs, mine), jnp.where(second, mine, theirs)
    early[...] = first
    late[...] = last
    chip[...] = first + last
    chip[:states, :] = (
        jnp.exp(last[states : states + 1] * rates[...]) * first[:states] + last[:states]
    )


def pair_back_kernel(ids, total, other, early, rates, late_total, chip):
    states = rates.shape[0]
    second = ids[2] == 1
    mine, theirs = total[...], other[...]
    first, last = jnp.where(second, theirs, mine), jnp.where(second, mine, theirs)
    late_total[...] = last
    chip[...] = first + jnp.exp(early[states : states + 1, :] * rates[...]) * last


def states_kernel(rank, ids, stepd, drive, coef, rates, entry, early, conv_out, gate_in, skip,
                  out_weight, *rest):
    chips = len(rest) - 8
    totals = rest[:chips]
    ssm_skip, gated, slices, kept, held, whole, kept_here, sems = rest[chips:]
    me, core, here = ids[0], ids[2], ids[3]
    states, channels = rates.shape
    length = stepd.shape[0]
    steps = length // SEGMENTS
    for key, value in enumerate(totals):
        held[key] = value[...]
    state = jnp.zeros((states, channels), jnp.float32)
    for chip in range(chips):
        value = held[here ^ chip]
        grown = jnp.exp(value[states : states + 1] * rates[...]) * state + value[:states]
        state = jnp.where(chip < here, grown, state)
    inner = jnp.exp(early[states : states + 1, :] * rates[...]) * state + early[:states, :]
    start = jnp.where(core == 1, inner, state)
    tiles = [slice(at, at + LANES) for at in range(0, channels, LANES)]
    copies = []
    for group in range(0, states, GROUP):
        names = range(group, group + GROUP)
        slab = group // GROUP
        rate = [[spread(rates[n : n + 1, lanes] * LOG2E) for lanes in tiles] for n in names]
        current = tuple(
            tuple(
                entry[0, n, :, lanes] * start[n : n + 1, lanes] + entry[1, n, :, lanes]
                for lanes in tiles
            )
            for n in names
        )
        for at in range(GROUP):
            for t, lanes in enumerate(tiles):
                kept_here[slab, 0, at, :, lanes] = current[at][t]

        def body(step, current):
            rows = rows_at(step)
            near = coef[rows, :]
            width = [stepd[rows, lanes] for lanes in tiles]
            push = [drive[rows, lanes] for lanes in tiles]
            later, total = [], [None] * len(tiles)
            for at, n in enumerate(names):
                entering, leaving = column_of(near, rank + n), column_of(near, rank + states + n)
                new = []
                for t, lanes in enumerate(tiles):
                    decay = jnp.exp2(width[t] * rate[at][t])
                    new.append(decay * current[at][t] + push[t] * entering)
                    kept_here[slab, step + 1, at, :, lanes] = new[t]
                    term = leaving * new[t]
                    total[t] = term if total[t] is None else total[t] + term
                later.append(tuple(new))
            for t, lanes in enumerate(tiles):
                add_to(ssm_skip, group == 0, rows, lanes, total[t])
            return tuple(later)

        sweep(steps, body, current)
        copies.append(pltpu.make_async_copy(kept_here.at[slab], kept.at[slab], sems.at[slab]))
        copies[-1].start()
    skipped = ssm_skip[...] + skip[...][None] * conv_out[...]
    ssm_skip[...] = skipped
    gate = gate_in[...]
    out = skipped * gate * sigmoid(gate)
    gated[...] = out
    whole[...] = product(out, out_weight[...])
    cut_slices(me, whole, slices)
    for copy in copies:
        copy.wait()


def dispatch_kernel(ids, s0, s1, s2, s3, rows_slice, slots_own, slots_other,
                    hidden, own, other):
    packed = (s0[...] + s1[...]) + (s2[...] + s3[...]) + rows_slice[...]
    hidden[...] = packed
    send_slots(ids[2], packed, slots_own[...], slots_other[...], own, other)


def raw_kernel(ids, c0, c1, c2, c3, expert_in, expert_out, raw, cot, in_high, in_low,
               out_high, out_low, held):
    join_slices(ids[0], (c0, c1, c2, c3), held, cot)
    in_high[...], in_low[...] = two_parts(expert_in[...])
    out_high[...], out_low[...] = two_parts(expert_out[...])
    raw[...] = product(cot[...], (out_high[...], out_low[...]), (1, 1))


def expert_kernel(ids, h0, h1, h2, h3, raw, in_high, in_low, norm_gain, router_t,
                  slices, second, act, grad_pre, gates, grad_logits, grad_gain,
                  held, whole):
    me, expert = ids[0], ids[1]
    join_slices(me, (h0, h1, h2, h3), held, whole)
    rows = whole[...]
    inverse = inverse_rms(rows)
    normed = rows * inverse * norm_gain[...][None]
    second[...] = normed
    normed_parts = two_parts(normed)
    router_parts = two_parts(router_t[...])
    weight = (in_high[...], in_low[...])
    logits = product(normed_parts, router_parts, (1, 1))
    logits = logits - jnp.max(logits, axis=-1, keepdims=True)
    powers = jnp.exp(logits)
    probs = powers / jnp.sum(powers, axis=-1, keepdims=True)
    chosen = jnp.where(
        lax.broadcasted_iota(jnp.int32, logits.shape, 1) == expert, 1.0, 0.0
    )
    gate = jnp.sum(probs * chosen, axis=-1, keepdims=True)
    gates[...] = gate
    hidden_act, slope = gelu_parts(product(normed_parts, weight))
    act[...] = hidden_act
    raws = raw[...]
    grad_gate = jnp.sum(hidden_act * raws, axis=-1, keepdims=True)
    grads = gate * raws * slope
    grad_pre[...] = grads
    logit_grads = grad_gate * gate * (chosen - probs)
    grad_logits[...] = logit_grads
    grad_second = product(grads, weight, (1, 1)) + product(logit_grads, router_parts)
    grad_gain[...] = jnp.sum(rows * inverse * grad_second, axis=0, keepdims=True)
    whole[...] = norm_back(rows, inverse, norm_gain[...][None], grad_second)
    cut_slices(me, whole, slices)


def expert_rest_kernel(ids, second, act, grad_pre, gates, grad_logits, cot, out_high, out_low,
                       slices, grad_in, grad_out, grad_router, whole):
    gate = gates[...]
    acts = two_parts(act[...])
    normed = two_parts(second[...])
    whole[...] = gate * product(acts, (out_high[...], out_low[...]))
    cut_slices(ids[0], whole, slices)
    grad_out[...] = product(acts, gate * cot[...], (0, 0))
    grad_in[...] = product(normed, grad_pre[...], (0, 0))
    grad_router[...] = product(grad_logits[...], normed, (0, 0))


def home_kernel(ids, own, other, base, rows_own, rows_other, out):
    half = own.shape[1] // 2
    second = ids[2] == 1

    def mine(rows):
        return jnp.where(second, pltpu.roll(rows, half, 1), rows)

    total = select_rows(rows_own[...], mine(own[...])) + select_rows(
        rows_other[...], mine(other[...])
    )
    count = base.shape[0]
    lane = lax.broadcasted_iota(jnp.int32, base.shape, 1)
    out[...] = base[...] + jnp.where(
        lane < half, total[:count], pltpu.roll(total[count:], half, 1)
    )


def whole_kernel(ids, p0, p1, p2, p3, out, held, whole, tiles):
    join_slices(ids[0], (p0, p1, p2, p3), held, whole)
    deinterleave_to(whole, tiles, out)


def leaving_kernel(rank, ids, g0, g1, g2, g3, out_weight, gate_in, ssm_skip, conv_out, stepd,
                   coef, rates, grad_hidden, grad_ssm, grad_gate_in, grad_skip, entry, total,
                   held):
    join_slices(ids[0], (g0, g1, g2, g3), held, grad_hidden)
    states, channels = rates.shape
    length = stepd.shape[0]
    steps = length // SEGMENTS
    grad_gated = product(grad_hidden[...], out_weight[...], (1, 1))
    gate = gate_in[...]
    gate_sigmoid = sigmoid(gate)
    pulled = grad_gated * gate * gate_sigmoid
    grad_ssm[...] = pulled
    grad_gate_in[...] = grad_gated * ssm_skip[...] * (
        gate_sigmoid * (1.0 + gate * (1.0 - gate_sigmoid))
    )
    grad_skip[...] = jnp.sum(pulled * conv_out[...], axis=0, keepdims=True)
    zero = jnp.zeros((SEGMENTS, LANES), jnp.float32)
    tiles = [slice(at, at + LANES) for at in range(0, channels, LANES)]
    sums = [zero] * len(tiles)
    for step in range(steps):
        rows = slice(step * SEGMENTS, (step + 1) * SEGMENTS)
        sums = [value + stepd[rows, lanes] for value, lanes in zip(sums, tiles)]
    for group in range(0, states, GROUP):
        names = range(group, group + GROUP)
        rate = [[spread(rates[n : n + 1, lanes] * LOG2E) for lanes in tiles] for n in names]

        def body(back, current):
            rows = rows_at(steps - 1 - back)
            near = coef[rows, :]
            width = [stepd[rows, lanes] for lanes in tiles]
            pull = [grad_ssm[rows, lanes] for lanes in tiles]
            later = []
            for at, n in enumerate(names):
                leaving = column_of(near, rank + states + n)
                later.append(tuple(
                    jnp.exp2(width[t] * rate[at][t]) * (current[at][t] + pull[t] * leaving)
                    for t in range(len(tiles))
                ))
            return tuple(later)

        current = sweep(steps, body, ((zero,) * len(tiles),) * GROUP)
        for at, n in enumerate(names):
            for t, lanes in enumerate(tiles):
                decay = jnp.exp2(sums[t] * rate[at][t])
                factor, before, last = chain_pieces(decay, current[at][t], True)
                entry[0, n, :, lanes] = factor
                entry[1, n, :, lanes] = before
                total[n : n + 1, lanes] = last[:1, :]


def adjoint_kernel(rank, chips, ids, stepd, drive, grad, coef, rates, entry, kept, early, late,
                   late_total, conv_out, stepsize, dt_pre, skip, dt_weight, grad_norm2, grad_router,
                   *rest):
    sums, totals = rest[:chips], rest[chips : 2 * chips]
    (partial, grad_direct, grad_dt_pre, grad_decay, grad_dt_bias, held_sums, held, kept_here,
     in_terms, out_terms, grad_push, grad_width, sems) = rest[2 * chips :]
    core, here = ids[2], ids[3]
    states, channels = rates.shape
    length = stepd.shape[0]
    steps = length // SEGMENTS
    copies = [
        pltpu.make_async_copy(kept.at[slab], kept_here.at[slab], sems.at[slab])
        for slab in range(states // GROUP)
    ]
    for copy in copies:
        copy.start()
    for key in range(chips):
        held_sums[key] = sums[key][states : states + 1, :]
        held[key] = totals[key][...]
    state = jnp.zeros((states, channels), jnp.float32)
    for chip in reversed(range(chips)):
        grown = held[here ^ chip] + jnp.exp(held_sums[here ^ chip] * rates[...]) * state
        state = jnp.where(chip > here, grown, state)
    inner = late_total[...] + jnp.exp(late[states : states + 1, :] * rates[...]) * state
    final = jnp.where(core == 1, state, inner)
    zero = jnp.zeros((SEGMENTS, LANES), jnp.float32)
    tiles = [slice(at, at + LANES) for at in range(0, channels, LANES)]
    for group in range(0, states, GROUP):
        names = range(group, group + GROUP)
        slab = group // GROUP
        rate = [[spread(rates[n : n + 1, lanes]) for lanes in tiles] for n in names]
        current = tuple(
            tuple(
                entry[0, n, :, lanes] * final[n : n + 1, lanes] + entry[1, n, :, lanes]
                for lanes in tiles
            )
            for n in names
        )
        copies[slab].wait()

        def body(back, carry):
            current, slopes = carry
            step = steps - 1 - back
            rows = rows_at(step)
            near = coef[rows, :]
            width = [stepd[rows, lanes] for lanes in tiles]
            push = [drive[rows, lanes] for lanes in tiles]
            pull = [grad[rows, lanes] for lanes in tiles]
            later, slope = [], []
            total, width_total = [None] * len(tiles), [None] * len(tiles)
            for at, n in enumerate(names):
                entering, leaving = column_of(near, rank + n), column_of(near, rank + states + n)
                new, turned, in_term, out_term = [], [], None, None
                for t, lanes in enumerate(tiles):
                    adjoint = leaving * pull[t] + current[at][t]
                    decayed = jnp.exp2(width[t] * (rate[at][t] * LOG2E)) * adjoint
                    through = decayed * kept_here[slab, step, at, :, lanes]
                    term, rated = adjoint * entering, through * rate[at][t]
                    total[t] = term if total[t] is None else total[t] + term
                    width_total[t] = rated if width_total[t] is None else width_total[t] + rated
                    new.append(decayed)
                    turned.append(slopes[at][t] + through * width[t])
                    term = adjoint * push[t]
                    in_term = term if in_term is None else in_term + term
                    term = kept_here[slab, step + 1, at, :, lanes] * pull[t]
                    out_term = term if out_term is None else out_term + term
                place = slice(n * LANES, (n + 1) * LANES)
                in_terms[rows, place] = in_term
                out_terms[rows, place] = out_term
                later.append(tuple(new))
                slope.append(tuple(turned))
            for t, lanes in enumerate(tiles):
                add_to(grad_push, group == 0, rows, lanes, total[t])
                add_to(grad_width, group == 0, rows, lanes, width_total[t])
            return tuple(later), tuple(slope)

        none = ((zero,) * len(tiles),) * GROUP
        _, slopes = sweep(steps, body, (current, none))
        for at, n in enumerate(names):
            for t, lanes in enumerate(tiles):
                grad_decay[n : n + 1, lanes] = rates[n : n + 1, lanes] * jnp.sum(
                    slopes[at][t], axis=0, keepdims=True
                )
    pushed = grad_push[...]
    grads = (pushed * conv_out[...] + grad_width[...]) * sigmoid(dt_pre[...])
    grad_dt_pre[...] = grads
    grad_dt_bias[...] = jnp.sum(grads, axis=0, keepdims=True)
    grad_direct[...] = pushed * stepsize[...] + skip[...][None] * grad[...]
    partial[:rank, :] = product(dt_weight[...], grads, (1, 1))
    shape = (2 * states, states * LANES)
    column = lax.broadcasted_iota(jnp.int32, shape, 0)
    owner = lax.broadcasted_iota(jnp.int32, shape, 1) // LANES
    total = None
    for terms, base in ((in_terms, 0), (out_terms, states)):
        ones = jnp.where(owner + base == column, 1.0, 0.0).astype(jnp.bfloat16)
        for part in two_parts(terms[...]):
            term = once(ones, part, (1, 1))
            total = term if total is None else total + term
    cols = rank + 2 * states
    partial[rank:cols, :] = total
    row = cols
    for shared in (grad_norm2, grad_router):
        for at in range(0, shared.shape[1], length):
            partial[row : row + shared.shape[0], :] = shared[:, at : at + length]
            row += shared.shape[0]
    partial[row:, :] = jnp.zeros((partial.shape[0] - row, length), jnp.float32)


def conv_back_kernel(experts, ids, p0, p1, p2, p3, xproj_t, grad_direct, mixed, conv_out, extended,
                     marks, conv_weight, coef, grad_dt_pre, grad_decay, grad_dt_bias, grad_skip,
                     normed, halo_normed, keep, send, grad_conv, grad_halo,
                     small, grad_extended, summed, weights):
    taps, channels = conv_weight.shape
    cols, states = xproj_t.shape[0], grad_decay.shape[0]
    rank = cols - 2 * states
    length = mixed.shape[0]
    lead = (taps - 1) * SEGMENTS
    summed[...] = (p0[...] + p1[...]) + (p2[...] + p3[...])
    projected = two_parts(summed[:cols, :])
    grad_out = grad_direct[...] + product(projected, xproj_t[...], (0, 0))
    value = mixed[...]
    value_sigmoid = sigmoid(value)
    grad_mixed = grad_out * (value_sigmoid * (1.0 + value * (1.0 - value_sigmoid)))
    grad_extended[...] = jnp.zeros_like(grad_extended)
    first_tap = cols + rank + states
    small[first_tap:, :] = jnp.zeros((small.shape[0] - first_tap, channels), jnp.float32)
    for k in range(taps):
        first = (taps - 1 - k) * SEGMENTS
        masked = grad_mixed * marks[:, k : k + 1]
        small[first_tap + k : first_tap + k + 1, :] = jnp.sum(
            masked * extended[first : first + length, :], axis=0, keepdims=True
        )
        grad_extended[first : first + length, :] += conv_weight[k : k + 1, :] * masked
    grad_conv[...] = grad_extended[lead:, :]
    grad_halo[...] = jnp.zeros_like(grad_halo)
    place = lax.broadcasted_iota(jnp.int32, (SEGMENTS, channels), 0)
    for m in range(taps - 1):
        rows = grad_extended[m * SEGMENTS : (m + 1) * SEGMENTS, :]
        at = SEGMENTS - taps + 1 + m
        grad_halo[at : at + 1, :] = rows[:1, :]
        inside = jnp.where(place == SEGMENTS - 1, 0.0, pltpu.roll(rows, SEGMENTS - 1, 0))
        ends = slice(length - lead + m * SEGMENTS, length - lead + (m + 1) * SEGMENTS)
        grad_conv[ends, :] += inside
    small[:cols, :] = product(projected, conv_out[...])
    low = product(coef[...], grad_dt_pre[...], (0, 0))
    small[cols : cols + rank, :] = low[:rank, :]
    small[cols + rank : first_tap, :] = grad_decay[...]
    last = first_tap + taps
    small[last : last + 1, :] = jnp.sum(grad_mixed, axis=0, keepdims=True)
    small[last + 1 : last + 2, :] = grad_dt_bias[...]
    small[last + 2 : last + 3, :] = grad_skip[...]
    first, row = last + 3, cols
    for count in (1, experts):
        for at in range(0, 2 * channels, length):
            value = summed[row : row + count, :]
            end = at + length
            for piece in range(at // channels, -(-end // channels)):
                low, high = max(at, piece * channels), min(end, (piece + 1) * channels)
                target = first + piece * count
                small[target : target + count, low - piece * channels : high - piece * channels] = (
                    value[:, low - at : high - at]
                )
            row += count
        first += 2 * count
    weights[...] = product(normed[...], grad_conv[...], (0, 0)) + product(
        halo_normed[...], grad_halo[...], (0, 0)
    )
    in_order(ids[1], (weights, small), keep, send)


def tokens_kernel(ids, grad_conv, grad_halo, conv_high, conv_low, gate_part, rows, halo_rows,
                  slices, whole):
    weight = conv_high[...], conv_low[...]
    length = grad_conv.shape[0]
    grad = product(grad_conv[...], weight, (1, 1)) + gate_part[...]
    before = product(grad_halo[...], weight, (1, 1))
    value, value_before = rows[...], halo_rows[...]
    whole[:length, :] = grad
    whole[length:, :] = jnp.zeros((whole.shape[0] - length, whole.shape[1]), jnp.float32)
    whole[length : length + SEGMENTS, :] = before
    whole[length : length + 1, :] = jnp.sum(
        value * inverse_rms(value) * grad, axis=0, keepdims=True
    ) + jnp.sum(value_before * inverse_rms(value_before) * before, axis=0, keepdims=True)
    cut_slices(ids[0], whole, slices)


def early_weights_kernel(ids, gated, grad_hidden, normed, grad_gate_in, keep, send, whole,
                         gate):
    channels = gated.shape[1]
    halves = product(gated[...], grad_hidden[...], (0, 0))
    whole[:channels, :] = halves[:, :channels]
    whole[channels:, :] = halves[:, channels:]
    gate[...] = product(normed[...], grad_gate_in[...], (0, 0))
    in_order(ids[1], (whole, gate), keep, send)


def in_order(me, wholes, keep, send):
    count = 2 * keep.shape[0]
    levels = count.bit_length() - 1
    for place in range(count):
        block = reversed_bits(place, levels) ^ me
        out, at = (keep, place) if place < count // 2 else (send, place - count // 2)
        first = 0
        for whole in wholes:
            rows = whole.shape[0] // count
            from_row = pl.multiple_of(block * rows, 8)
            out[at, first : first + rows, :] = whole[pl.ds(from_row, rows), :]
            first += rows


def gate_tokens_kernel(ids, grad_gate_in, gate_high, gate_low, out):
    out[...] = product(grad_gate_in[...], (gate_high[...], gate_low[...]), (1, 1))


def extra_kernel(ids, p0, p1, p2, p3, extra, norm1, held, whole):
    join_slices(ids[0], (p0, p1, p2, p3), held, whole)
    row = whole.shape[0] - 2 * SEGMENTS
    channels = norm1.shape[2]
    extra[...] = whole[row : row + SEGMENTS, :]
    norm1[...] = jnp.zeros_like(norm1)
    for piece in range(whole.shape[1] // channels):
        lanes = slice(piece * channels, (piece + 1) * channels)
        norm1[0, piece : piece + 1, :] = whole[row : row + 1, lanes]


def grad_tokens_kernel(taps, ids, p0, p1, p2, p3, from_next, rows, gain, grad_hidden, out,
                       held, whole, tiles):
    join_slices(ids[0], (p0, p1, p2, p3), held, whole)
    length = rows.shape[0]
    lead = (taps - 1) * SEGMENTS
    for m in range(taps - 1):
        row = length - lead + (m + 1) * SEGMENTS - 1
        at = SEGMENTS - taps + 1 + m
        whole[row : row + 1, :] += from_next[at : at + 1, :]
    value = rows[...]
    whole[:length, :] = (
        norm_back(value, inverse_rms(value), gain[...][None], whole[:length, :]) + grad_hidden[...]
    )
    deinterleave_to(whole, tiles, out)


def early_out_kernel(ids, summed, out_weight):
    count, rows, channels = summed.shape
    levels = count.bit_length() - 1
    for block in range(count):
        value = summed[reversed_bits(block ^ ids[1], levels)]
        half, row = divmod(block * rows, channels)
        out_weight[row : row + rows, half * channels : (half + 1) * channels] = value


def weights_out_kernel(counts, ids, early, late, norm1, weight, *rest):
    *outs, sum_norm1, small = rest
    count, rows = early.shape[0], early.shape[1]
    more = late.shape[1] - rows
    levels = count.bit_length() - 1
    for block in range(count):
        place = reversed_bits(block ^ ids[1], levels)
        small[block * more : (block + 1) * more, :] = late[place, rows:, :]
        weight[block * rows : (block + 1) * rows, 0, :] = late[place, :rows, :]
        weight[block * rows : (block + 1) * rows, 1, :] = early[place]
    first = 0
    channels = small.shape[1]
    for out, used in zip(outs, counts):
        per = out.shape[-1] // channels
        each = used // per
        for piece in range(per):
            lanes = slice(piece * channels, (piece + 1) * channels)
            if len(out.shape) == 1:
                out[lanes] = small[first, :]
            else:
                out[:, lanes] = small[first : first + each, :]
            first += each
    for piece in range(sum_norm1.shape[0] // channels):
        sum_norm1[piece * channels : (piece + 1) * channels] = norm1[0, piece, :]


def local(
    tokens, norm1_gain, in_weight, conv_weight, conv_bias, xproj_weight, dt_weight, dt_bias,
    decay_log, skip_gain, out_weight, norm2_gain, router_weight, expert_in, expert_out,
    segments, expert_ids, cotangent,
):
    length, width = tokens.shape
    taps, channels = conv_weight.shape
    experts = router_weight.shape[1]
    wide = experts
    capacity = 5 * length // (4 * experts)
    states, rank = decay_log.shape[0], dt_weight.shape[0]
    chips = wide // 2
    slots = chips * capacity
    steps = length // SEGMENTS
    me_wide = lax.axis_index("wide")
    ids = jnp.stack([lax.axis_index("narrow"), me_wide, me_wide & 1, me_wide // 2]).astype(jnp.int32)
    half, double = length // 2, width // 2
    bf16 = jnp.bfloat16
    rows_shape, channel_rows = shape_of(length, width), shape_of(length, channels)
    packed, packed_slots = shape_of(half, double), shape_of(slots, double)
    vmem = lambda *shape: pltpu.VMEM(shape, jnp.float32)
    xproj_t, router_t = xproj_weight.T, router_weight.T
    cols = xproj_t.shape[0]

    tiled = vmem(width // LANES, length, LANES)

    halo_rows = wide_shift(tokens[length - SEGMENTS :], 1)

    (marks, slots_own, slots_other, rows_own, rows_other, rows_slice, cot_slice, cot_own,
     cot_other, conv_high, conv_low, gate_high, gate_low) = call(
        functools.partial(start_kernel, capacity),
        [shape_of(length, SEGMENTS)]
        + [shape_of(slots, length, dtype=bf16)] * 2
        + [shape_of(length, slots, dtype=bf16)] * 2
        + [packed, packed, packed_slots, packed_slots]
        + [shape_of(width, channels, dtype=bf16)] * 4,
        ids, segments.reshape(-1, LANES), expert_ids.reshape(1, length), tokens, cotangent,
        in_weight,
        scratch=[pltpu.VMEM((segments.shape[0] // LANES, LANES), jnp.int32),
                 pltpu.VMEM((1, length), jnp.int32)] + [vmem(length, width)] * 2
        + [vmem(width, 2, channels), vmem(length, width), tiled, vmem(2, width, channels),
           pltpu.SemaphoreType.DMA((5,))],
        far_in=[0, 1, 2, 3, 4],
    )
    cot_pair = cot_own + core_swap(cot_other)
    rows, normed, conv_in, gate_in = call(
        front_kernel,
        [rows_shape, rows_shape, channel_rows, channel_rows],
        ids, tokens, norm1_gain, conv_high, conv_low, gate_high, gate_low,
        scratch=[tiled],
    )
    mixed, conv_out, partial, extended, halo_normed = call(
        conv_kernel,
        [channel_rows, channel_rows, shape_of(cols, length),
         shape_of(length + (taps - 1) * SEGMENTS, channels), shape_of(SEGMENTS, width)],
        ids, halo_rows, norm1_gain, conv_high, conv_low, conv_in, marks, conv_weight,
        conv_bias, xproj_t, after=[cot_pair],
    )
    partials = narrow_all(partial)

    partials = narrow_all(partial)

    cot_blocks = chip_each(hold(cot_pair, partial), chips)

    entry_shape = shape_of(2, states, SEGMENTS, channels)
    total_rows = -(-(states + 1) // 8) * 8
    coef, dt_pre, stepsize, drive, stepd, rates, entry, total = call(
        totals_kernel,
        [shape_of(length, LANES)] + [channel_rows] * 4
        + [shape_of(states, channels), entry_shape, shape_of(total_rows, channels)],
        ids, *partials, dt_weight, dt_bias, decay_log, conv_out, marks,
        scratch=[vmem(LANES, channels)],
    )
    total_shape = shape_of(total_rows, channels)
    early, late, chip_total = call(
        pair_kernel, [total_shape] * 3, ids, total, core_swap(total), rates, after=[cot_blocks]
    )
    chip_totals = chip_all(chip_total, chips)
    slabs = states // GROUP
    cot_parts = narrow_all(hold(cot_blocks, chip_total))
    kept_shape = (slabs, steps + 1, GROUP, SEGMENTS, channels)
    ssm_skip, gated, mixer_slices, kept = call(
        functools.partial(states_kernel, rank),
        [channel_rows, channel_rows, shape_of(4, half, double), shape_of(*kept_shape)],
        ids, stepd, drive, coef, rates, entry, early, conv_out, gate_in, skip_gain,
        out_weight, *chip_totals,
        scratch=[vmem(chips, total_rows, channels), vmem(length, width), vmem(*kept_shape),
                 pltpu.SemaphoreType.DMA((slabs,))],
        out_place=[3],
    )
    mixer_slices = hold(mixer_slices, *cot_parts)
    expert_rows, square = shape_of(2 * slots, width), (expert_in.shape[1], expert_in.shape[2])
    hidden_units = square[1]
    raw, cot, in_high, in_low, out_high, out_low = call(
        raw_kernel,
        [shape_of(2 * slots, hidden_units), expert_rows]
        + [shape_of(*square, dtype=bf16)] * 2
        + [shape_of(square[1], square[0], dtype=bf16)] * 2,
        ids, *cot_parts, expert_in[0], expert_out[0],
        scratch=[vmem(4, slots, double)], after=[mixer_slices],
    )
    hidden_slice, hidden_own, hidden_other = call(
        dispatch_kernel,
        [packed, packed_slots, packed_slots],
        ids, *narrow_each(mixer_slices), rows_slice, slots_own, slots_other, after=[raw],
    )
    hidden_parts = narrow_all(chip_each(hidden_own + core_swap(hidden_other), chips))
    slices_shape = shape_of(4, slots, double)
    grad_slices, second, act, grad_pre, gates, grad_logits, grad_norm2 = call(
        expert_kernel,
        [slices_shape, expert_rows] + [shape_of(2 * slots, hidden_units)] * 2
        + [shape_of(2 * slots, 1), shape_of(2 * slots, experts), shape_of(1, width)],
        ids, *hidden_parts, raw, in_high, in_low, norm2_gain, router_t,
        scratch=[vmem(4, slots, double), vmem(2 * slots, width)],
    )
    grad_mine = pair_sum(narrow_each(grad_slices))
    value_slices, grad_expert_in, grad_expert_out, grad_router_t = call(
        expert_rest_kernel,
        [slices_shape, shape_of(*square), shape_of(square[1], square[0]),
         shape_of(experts, width)],
        ids, second, act, grad_pre, gates, grad_logits, cot, out_high, out_low,
        scratch=[vmem(2 * slots, width)],
    )
    grad_back = chip_each(grad_mine, chips)
    value_mine = pair_sum(narrow_each(value_slices))
    grad_slice = call(
        home_kernel, [packed], ids, grad_back, core_swap(grad_back), cot_slice, rows_own,
        rows_other, after=[value_mine],
    )[0]
    grad_parts = narrow_all(grad_slice)
    value_back = chip_each(value_mine, chips)

    def whole_of(parts, after=()):
        return call(
            whole_kernel, [rows_shape], ids, *parts, after=after,
            scratch=[vmem(4, half, double), vmem(length, width), tiled],
        )[0]

    grad_hidden, grad_ssm, grad_gate_in, grad_skip, back_entry, back_total = call(
        functools.partial(leaving_kernel, rank),
        [rows_shape, channel_rows, channel_rows, shape_of(1, channels), entry_shape,
         shape_of(states, channels)],
        ids, *grad_parts, out_weight, gate_in, ssm_skip, conv_out, stepd, coef, rates,
        scratch=[vmem(4, half, double)], after=[value_back],
    )
    other_back = core_swap(back_total)
    block = width // wide
    half_blocks = shape_of(wide // 2, 2 * block, channels)
    early_keep, early_send = call(
        early_weights_kernel,
        [half_blocks, half_blocks],
        ids, gated, grad_hidden, normed, grad_gate_in,
        scratch=[vmem(width, channels)] * 2,
    )
    back_late, back_chip = call(
        pair_back_kernel, [shape_of(states, channels)] * 2,
        ids, back_total, other_back, early, rates, after=[early_keep],
    )
    back_totals = chip_all(back_chip, chips)
    early_arrived = core_swap(hold(early_send, back_chip))
    out_sum, gate_sum = (
        WideSum(early_keep[:, rows], early_send[:, rows])
        for rows in (slice(0, block), slice(block, None))
    )
    out_sum.arrived, gate_sum.arrived = early_arrived[:, :block], early_arrived[:, block:]
    out_sum.finish()
    gate_sum.finish()
    first_step = out_sum.start(*back_totals)

    shared_rows = (experts + 1) * (width // length)
    partial_rows = cols + shared_rows + -(cols + shared_rows) % 8
    partial_back, grad_direct, grad_dt_pre, grad_decay, grad_dt_bias = call(
        functools.partial(adjoint_kernel, rank, chips),
        [shape_of(partial_rows, length), channel_rows, channel_rows, shape_of(states, channels),
         shape_of(1, channels)],
        ids, stepd, drive, grad_ssm, coef, rates, back_entry, kept, early, late, back_late,
        conv_out, stepsize, dt_pre, skip_gain, dt_weight, grad_norm2, grad_router_t,
        *chip_totals, *back_totals,
        scratch=[vmem(chips, 1, channels), vmem(chips, states, channels), vmem(*kept_shape),
                 vmem(length, states * LANES), vmem(length, states * LANES),
                 vmem(length, channels), vmem(length, channels),
                 pltpu.SemaphoreType.DMA((slabs,))],
        in_place=[6], after=[out_sum.send, gate_sum.send],
    )
    partials_back = narrow_all(partial_back)
    gate_part = call(
        gate_tokens_kernel, [rows_shape], ids, grad_gate_in, gate_high, gate_low,
        after=[partial_back],
    )[0]
    out_sum.finish(partial_back)
    out_sum.start()
    gate_sum.start(partial_back)
    grain = 8 * wide
    small_rows = cols + rank + states + taps + 3 + (experts + 1) * (width // channels)
    small_rows += -small_rows % grain
    more = small_rows // wide
    half_blocks = shape_of(wide // 2, block + more, channels)
    token_rows = length + 2 * SEGMENTS
    conv_keep, conv_send, grad_conv, grad_halo = call(
        functools.partial(conv_back_kernel, experts),
        [half_blocks, half_blocks, channel_rows, shape_of(SEGMENTS, channels)],
        ids, *partials_back, xproj_t, grad_direct, mixed, conv_out, extended, marks,
        conv_weight, coef, grad_dt_pre, grad_decay, grad_dt_bias, grad_skip,
        normed, halo_normed,
        scratch=[vmem(small_rows, channels),
                 vmem(length + (taps - 1) * SEGMENTS, channels), vmem(partial_rows, length),
                 vmem(width, channels)],
        after=[gate_sum.arrived, out_sum.arrived],
    )
    (token_slices,) = call(
        tokens_kernel, [shape_of(4, token_rows // 2, double)],
        ids, grad_conv, grad_halo, conv_high, conv_low, gate_part, rows, halo_rows,
        scratch=[vmem(token_rows, width)],
    )
    out_sum.finish()
    gate_sum.finish()
    conv_sum = WideSum(conv_keep, conv_send)
    conv_sum.start()
    conv_sum.finish()
    (output_slice,) = call(
        home_kernel, [packed], ids, value_back, core_swap(hold(value_back, conv_keep)),
        hidden_slice, rows_own, rows_other,
    )
    levels = len(conv_sum.swaps)

    def extra_of(parts):
        return call(
            extra_kernel,
            [shape_of(SEGMENTS, width), shape_of(1, SEGMENTS, channels)],
            ids, *parts,
            scratch=[vmem(4, token_rows // 2, double), vmem(token_rows, width)],
        )

    def grad_tokens_of(parts, from_next):
        return call(
            functools.partial(grad_tokens_kernel, taps),
            [rows_shape], ids, *parts, from_next, rows, norm1_gain, grad_hidden,
            scratch=[vmem(4, token_rows // 2, double), vmem(token_rows, width), tiled],
        )[0]

    def out_weight_of(total, *others):
        return call(
            early_out_kernel, [shape_of(channels, width)], ids, total, after=others
        )[0]

    if levels == 3:
        sums = conv_sum, gate_sum, out_sum
        joint = [conv_sum.start(), *start_both(gate_sum, out_sum)]
        token_each = narrow_each(token_slices)
        for part in sums:
            part.finish(*joint, *token_each, output_slice)
        joint = [*start_both(conv_sum, gate_sum), out_sum.start()]
        token_parts = narrow_all(pair_sum(token_each))
        extra, norm1 = extra_of(token_parts)
        from_next = wide_shift(extra, -1)
        for part in sums:
            part.finish(*joint, norm1, from_next)
        arrived, norm1_other = conv_sum.start_with(norm1)
        joint = [arrived, gate_sum.start()]
        output_parts = narrow_all(hold(output_slice, norm1))
        for part in sums[:2]:
            part.finish(*joint, *output_parts)
        norm1 = norm1 + norm1_other
        arrived, norm1_other = conv_sum.start_with(norm1)
        joint = [arrived, *start_both(gate_sum, out_sum)]
        grad_tokens = grad_tokens_of(token_parts, from_next)
        output = whole_of(output_parts, after=[conv_sum.send])
        for part in sums:
            part.finish(*joint, output, grad_tokens)
        norm1 = norm1 + norm1_other
        arrived, norm1_other = conv_sum.start_with(norm1)
        sum_out_weight = out_weight_of(out_sum.keep, conv_sum.send)
        conv_sum.finish(sum_out_weight)
        norm1 = norm1 + norm1_other
    else:
        token_parts = narrow_all(pair_sum(narrow_each(token_slices)))
        extra, norm1 = extra_of(token_parts)
        grad_tokens = grad_tokens_of(token_parts, wide_shift(extra, -1))
        output = whole_of(narrow_all(output_slice))
        sum_out_weight = out_weight_of(out_sum.rest())
        norm1 = norm1 + core_swap(norm1)
        norm1 = pair_sum(chip_all(norm1, chips))
    per = width // channels
    counts = (cols, rank, states, taps, 1, 1, 1, per, per * experts)
    (weight_sum, sum_xproj_t, sum_dt_weight, sum_decay, sum_taps, sum_conv_bias, sum_dt_bias,
     sum_skip, sum_norm2, sum_router_t, sum_norm1) = call(
        functools.partial(weights_out_kernel, counts),
        [shape_of(width, 2, channels)]
        + [shape_of(rows, channels) for rows in (cols, rank, states, taps)]
        + [shape_of(channels)] * 3
        + [shape_of(width), shape_of(experts, width), shape_of(width)],
        ids, gate_sum.rest(), conv_sum.rest(), norm1, scratch=[vmem(small_rows, channels)],
    )
    return (
        output,
        grad_tokens,
        sum_norm1,
        weight_sum,
        sum_taps,
        sum_conv_bias,
        sum_xproj_t.T,
        sum_dt_weight,
        sum_dt_bias,
        sum_decay,
        sum_skip,
        sum_out_weight,
        sum_norm2,
        sum_router_t.T,
        grad_expert_in[None],
        grad_expert_out[None],
    )


def solution(mesh):
    in_specs = (
        P("wide", None),
        P(),
        P(None, None, "narrow"),
        P(None, "narrow"),
        P("narrow"),
        P("narrow", None),
        P(None, "narrow"),
        P("narrow"),
        P(None, "narrow"),
        P("narrow"),
        P("narrow", None),
        P(),
        P(),
        P("wide", None, "narrow"),
        P("wide", "narrow", None),
        P(),
        P("wide", None),
        P("wide", None),
    )
    out_specs = (
        P("wide", None),
        P("wide", None),
        P(),
        P(None, None, "narrow"),
        P(None, "narrow"),
        P("narrow"),
        P("narrow", None),
        P(None, "narrow"),
        P("narrow"),
        P(None, "narrow"),
        P("narrow"),
        P("narrow", None),
        P(),
        P(),
        P("wide", None, "narrow"),
        P("wide", "narrow", None),
    )
    return jax.shard_map(local, mesh=mesh, in_specs=in_specs, out_specs=out_specs, check_vma=False)
```

```python
import functools
import math

import jax
import jax.numpy as jnp
from jax import lax
from jax.experimental import pallas as pl
from jax.experimental.pallas import tpu as pltpu
from jax.sharding import PartitionSpec as P

EPSILON = 1e-05
SEGMENTS = 8
LANES = 128
NEVER = 1e30
VMEM_SPARE = 4 * 1024 * 1024
GROUP = 4
LOG2E = 1.4426950408889634


def shape_of(*shape, dtype=jnp.float32):
    return jax.ShapeDtypeStruct(shape, dtype)


def call(kernel, outs, ids, *arrays, scratch=(), after=(), far_in=(), out_place=(), in_place=()):
    in_vmem = pl.BlockSpec(memory_space=pltpu.VMEM)
    anywhere = pl.BlockSpec(memory_space=pl.ANY)
    far = pl.BlockSpec(memory_space=pltpu.HBM)
    arrays = [
        pltpu.with_memory_space_constraint(array, pltpu.HBM) if i in far_in else array
        for i, array in enumerate(arrays)
    ]
    size = lambda a: math.prod(a.shape) * jnp.dtype(a.dtype).itemsize
    held = [
        size(a)
        for refs, skipped in ((arrays, (*in_place, *far_in)), (outs, out_place))
        for i, a in enumerate(refs)
        if i not in skipped
    ]
    held += [size(a) for a in scratch if hasattr(a, "dtype") and hasattr(a, "shape")
             and jnp.issubdtype(a.dtype, jnp.number)]
    given = 1 + len(arrays)

    def run(*refs):
        kernel(*refs[:given], *refs[given + len(after) :])

    return pl.pallas_call(
        run,
        out_shape=outs,
        in_specs=[pl.BlockSpec(memory_space=pltpu.SMEM)]
        + [far if i in far_in else anywhere if i in in_place else in_vmem
           for i in range(len(arrays))]
        + [anywhere] * len(after),
        out_specs=[anywhere if i in out_place else in_vmem for i in range(len(outs))],
        scratch_shapes=scratch,
        compiler_params=pltpu.CompilerParams(vmem_limit_bytes=sum(held) + VMEM_SPARE),
        cost_estimate=pl.CostEstimate(flops=1, bytes_accessed=1, transcendentals=0),
    )(ids, *arrays, *after)


def two_parts(value):
    high = value.astype(jnp.bfloat16)
    return high, (value - high.astype(jnp.float32)).astype(jnp.bfloat16)


def once(left, right, contract=(1, 0)):
    return lax.dot_general(
        left,
        right,
        (((contract[0],), (contract[1],)), ((), ())),
        preferred_element_type=jnp.float32,
    )


def product(left, right, contract=(1, 0)):
    left_high, left_low = left if isinstance(left, tuple) else two_parts(left)
    right_high, right_low = right if isinstance(right, tuple) else two_parts(right)
    free = 1 - contract[0]
    size = left_high.shape[free]
    if size % (16, LANES)[free]:
        return once(left_high, right_high, contract) + (
            once(left_high, right_low, contract) + once(left_low, right_high, contract)
        )
    both = once(jnp.concatenate([left_high, left_low], axis=free), right_high, contract)
    return both[:size] + (both[size:] + once(left_high, right_low, contract))


def select_rows(chosen, rows, contract=(1, 0)):
    high, low = two_parts(rows)
    return once(chosen, high, contract) + once(chosen, low, contract)


def inverse_rms(rows):
    return lax.rsqrt(jnp.mean(rows * rows, axis=-1, keepdims=True) + EPSILON)


def norm_back(rows, inverse, gain, grad):
    scaled = gain * grad
    mean = jnp.mean(rows * scaled, axis=-1, keepdims=True)
    return inverse * scaled - rows * (inverse * inverse * inverse) * mean


def sigmoid(value):
    return 1.0 / (1.0 + jnp.exp(-value))


def softplus(value):
    return jnp.maximum(value, 0.0) + jnp.log1p(jnp.exp(-jnp.abs(value)))


def gelu_parts(value):
    spread_of = 0.5 * (1.0 + lax.erf(value * (0.5**0.5)))
    density = jnp.exp(-0.5 * value * value) * ((2.0 * jnp.pi) ** -0.5)
    return value * spread_of, spread_of + value * density


def cut_slices(me, whole, out):
    rows, part = whole.shape[0] // 2, whole.shape[1] // 4
    for j in range(4):
        out[me ^ j, :, :part] = whole[:rows, part * j : part * (j + 1)]
        out[me ^ j, :, part:] = whole[rows:, part * j : part * (j + 1)]


def join_slices(me, parts, held, whole):
    rows, part = whole.shape[0] // 2, whole.shape[1] // 4
    for key, value in enumerate(parts):
        held[key] = value[...]
    for j in range(4):
        value = held[me ^ j]
        whole[:rows, part * j : part * (j + 1)] = value[:, :part]
        whole[rows:, part * j : part * (j + 1)] = value[:, part:]


def reversed_bits(value, levels):
    place = 0
    for level in range(levels):
        place = place + (((value >> level) & 1) << (levels - 1 - level))
    return place


def interleave_from(rows, held, out):
    length, width = out.shape
    steps = length // SEGMENTS
    for tile in range(width // LANES):
        lanes = slice(tile * LANES, (tile + 1) * LANES)
        held[tile] = rows[:, lanes]
        for step in range(steps):
            out[step * SEGMENTS : (step + 1) * SEGMENTS, lanes] = held[
                tile, pl.ds(step, SEGMENTS, stride=steps), :
            ]


def deinterleave_to(rows, held, out):
    length, width = out.shape
    steps = length // SEGMENTS
    for tile in range(width // LANES):
        lanes = slice(tile * LANES, (tile + 1) * LANES)
        for step in range(steps):
            held[tile, pl.ds(step, SEGMENTS, stride=steps), :] = rows[
                step * SEGMENTS : (step + 1) * SEGMENTS, lanes
            ]
        out[:, lanes] = held[tile]


def narrow_swap(value, key):
    return lax.ppermute(value, "narrow", [(i, i ^ key) for i in range(4)])


def core_swap(value):
    count = lax.axis_size("wide")
    return lax.ppermute(value, "wide", [(i, i ^ 1) for i in range(count)])


def chip_swap(value, key):
    count = lax.axis_size("wide")
    return lax.ppermute(value, "wide", [(i, i ^ (2 * key)) for i in range(count)])


def wide_shift(value, distance):
    devices = range(lax.axis_size("wide"))
    route = [(i - distance, i) for i in devices if i - distance in devices]
    return lax.ppermute(value, "wide", route)


def hold(value, *others):
    if not others:
        return value
    return lax.optimization_barrier((value, others))[0]


def narrow_all(value):
    far = narrow_swap(value, 3)
    return [value, narrow_swap(value, 1), narrow_swap(value, 2), far]


def narrow_each(slices):
    far = narrow_swap(slices[3], 3)
    return [slices[0], narrow_swap(slices[1], 1), narrow_swap(slices[2], 2), far]


def pair_sum(parts):
    while len(parts) > 1:
        parts = [a + b for a, b in zip(parts[::2], parts[1::2])]
    return parts[0]


def chip_blocks(blocks, chips):
    rows = blocks.shape[0] // chips
    order = sorted(range(1, chips), reverse=True)
    arrived = {k: chip_swap(blocks[k * rows : (k + 1) * rows], k) for k in order}
    arrived[0] = blocks[:rows]
    return [arrived[k] for k in range(chips)]


def chip_each(blocks, chips):
    return jnp.concatenate(chip_blocks(blocks, chips))


def chip_all(value, chips):
    arrived = {k: chip_swap(value, k) for k in sorted(range(1, chips), reverse=True)}
    arrived[0] = value
    return [arrived[k] for k in range(chips)]


class WideSum:
    def __init__(self, keep, send):
        levels = lax.axis_size("wide").bit_length() - 1
        self.swaps = [core_swap] + [
            functools.partial(chip_swap, key=1 << level) for level in range(levels - 1)
        ]
        self.keep, self.send, self.arrived = keep, send, None
        self.level, self.back = 0, False

    def prepare(self):
        if not self.back and self.level == len(self.swaps):
            self.back = True
        if self.back:
            self.level -= 1
            self.send = self.keep
        return self.send

    def start(self, *others):
        self.prepare()
        self.arrived = self.swaps[self.level](hold(self.send, *others))
        return self.arrived

    def start_with(self, rider):
        sent = self.prepare()
        joined = jnp.concatenate([sent.reshape(1, -1, sent.shape[2]), rider], axis=1)
        arrived = self.swaps[self.level](joined)
        rows = rider.shape[1]
        self.arrived = arrived[:, :-rows].reshape(sent.shape)
        return self.arrived, arrived[:, -rows:]

    def finish(self, *others):
        arrived = hold(self.arrived, *others) if others else self.arrived
        if self.back:
            self.keep = jnp.concatenate([self.keep, arrived])
            return
        self.level += 1
        if self.level == len(self.swaps):
            self.keep = self.keep + arrived
            return
        half = self.keep.shape[0] // 2
        self.send = self.keep[half:] + arrived[half:]
        self.keep = self.keep[:half] + arrived[:half]

    def rest(self):
        while not (self.back and self.level == 0):
            self.start()
            self.finish()
        return self.keep


def start_both(one, two, *others):
    first, second = one.prepare(), two.prepare()
    rows = first.shape[1]
    arrived = one.swaps[one.level](hold(jnp.concatenate([first, second], axis=1), *others))
    one.arrived, two.arrived = arrived[:, :rows], arrived[:, rows:]
    return one.arrived, two.arrived


def route_kernel(capacity, ids, segments, expert_ids, marks, slots_own, slots_other,
                 rows_own, rows_other):
    wide_at, core, chip = ids[1], ids[2], ids[3]
    length = expert_ids.shape[1]
    per = length // LANES
    experts = segments.shape[0] // per
    steps = length // SEGMENTS

    def block(at):
        return jnp.concatenate([segments[pl.ds(at * per + i, 1), :] for i in range(per)], axis=1)

    own, before = block(wide_at), block(jnp.maximum(wide_at - 1, 0))
    lane = lax.broadcasted_iota(jnp.int32, (1, length), 1)
    here = lax.broadcasted_iota(jnp.int32, (SEGMENTS, length), 0)
    table = jnp.ones((SEGMENTS, length), jnp.float32)
    for k in range(1, 4):
        back = jnp.where(lane < k, pltpu.roll(before, k, 1), pltpu.roll(own, k, 1))
        same = (back == own) & ((lane >= k) | (wide_at > 0))
        table = jnp.where(here == k, jnp.where(same, 1.0, 0.0), table)
    live = own >= 0
    expert = expert_ids[...]
    at = lax.broadcasted_iota(jnp.int32, (experts, length), 0)
    hits = jnp.where((at == expert) & live, 1.0, 0.0)
    first = lax.broadcasted_iota(jnp.int32, (length, length), 0)
    second = lax.broadcasted_iota(jnp.int32, (length, length), 1)
    earlier = jnp.where(first < second, 1.0, 0.0).astype(jnp.bfloat16)
    ranks = once(hits.astype(jnp.bfloat16), earlier)
    rank = jnp.sum(ranks * hits, axis=0, keepdims=True).astype(jnp.int32)
    kept = live & (rank < capacity)
    order = jnp.where(
        (first % SEGMENTS) * steps + first // SEGMENTS == second, 1.0, 0.0
    ).astype(jnp.bfloat16)
    marks[...] = once(order, table.astype(jnp.bfloat16), (1, 1))
    slot = jnp.where(kept, ((expert >> 1) ^ chip) * capacity + rank, -1)
    count = slots_own.shape[0]
    slot_at = lax.broadcasted_iota(jnp.int32, (count, length), 0)
    for which, slots, rows in ((core, slots_own, rows_own), (1 - core, slots_other, rows_other)):
        mine = (slot_at == slot) & ((expert & 1) == which)
        chosen = jnp.where(mine, 1.0, 0.0).astype(jnp.bfloat16)
        slots[...] = once(chosen, order, (1, 1)).astype(jnp.bfloat16)
        rows[...] = once(order, chosen, (1, 1)).astype(jnp.bfloat16)


def front_kernel(ids, tokens, gain, conv_high, conv_low, gate_high, gate_low,
                 rows, normed, conv_in, gate_in, held):
    interleave_from(tokens, held, rows)
    value = rows[...]
    scaled = value * inverse_rms(value) * gain[...][None]
    normed[...] = scaled
    parts = two_parts(scaled)
    conv_in[...] = product(parts, (conv_high[...], conv_low[...]))
    gate_in[...] = product(parts, (gate_high[...], gate_low[...]))


def start_kernel(capacity, ids, segments_far, expert_ids_far, tokens_far, cotangent_far, weight_far,
                 marks, slots_own, slots_other, rows_own, rows_other,
                 rows_slice, cot_slice, own, other, conv_high, conv_low, gate_high, gate_low,
                 segments, expert_ids, tokens, cotangent, weight, rows, held, branch,
                 sems):
    pairs = (
        (segments_far, segments),
        (expert_ids_far, expert_ids),
        (tokens_far, tokens),
        (cotangent_far, cotangent),
        (weight_far, weight),
    )
    copies = [
        pltpu.make_async_copy(far, near, sems.at[i]) for i, (far, near) in enumerate(pairs)
    ]
    for copy in copies:
        copy.start()
    copies[0].wait()
    copies[1].wait()
    route_kernel(capacity, ids, segments, expert_ids, marks, slots_own, slots_other,
                 rows_own, rows_other)
    copies[2].wait()
    copies[3].wait()
    slices_kernel(ids, tokens, cotangent, slots_own, slots_other, rows_slice, cot_slice, own, other,
                  rows, held)
    copies[4].wait()
    for k, (high, low) in enumerate(((conv_high, conv_low), (gate_high, gate_low))):
        branch[k] = weight[:, k, :]
        high[...], low[...] = two_parts(branch[k])


def slices_kernel(ids, tokens, cotangent, slots_own, slots_other,
                  rows_slice, cot_slice, own, other, rows, held):
    me, core = ids[0], ids[2]
    half, part = tokens.shape[0] // 2, tokens.shape[1] // 4
    for source, out in ((tokens, rows_slice), (cotangent, cot_slice)):
        interleave_from(source, held, rows)
        for j in range(4):
            @pl.when(me == j)
            def _():
                out[:, :part] = rows[:half, part * j : part * (j + 1)]
                out[:, part:] = rows[half:, part * j : part * (j + 1)]
    send_slots(core, cot_slice[...], slots_own[...], slots_other[...], own, other)


def send_slots(core, packed, slots_own, slots_other, own, other):
    half = packed.shape[1] // 2
    lane = lax.broadcasted_iota(jnp.int32, packed.shape, 1)
    left = jnp.where(lane < half, packed, 0.0)
    right = jnp.where(lane < half, 0.0, packed)
    second = core == 1
    top = jnp.where(second, pltpu.roll(left, half, 1), left)
    bottom = jnp.where(second, right, pltpu.roll(right, half, 1))
    placed = jnp.concatenate([top, bottom])
    own[...] = select_rows(slots_own, placed)
    other[...] = select_rows(slots_other, placed)


def conv_kernel(ids, halo, gain, conv_high, conv_low, conv_in, marks, conv_weight, conv_bias,
                xproj_t, mixed, conv_out, partial, extended, halo_normed):
    taps, channels = conv_weight.shape
    length = conv_in.shape[0]
    lead = (taps - 1) * SEGMENTS
    rows = halo[...]
    scaled = rows * inverse_rms(rows) * gain[...][None]
    halo_normed[...] = scaled
    halo_conv = product(scaled, (conv_high[...], conv_low[...]))
    place = lax.broadcasted_iota(jnp.int32, (SEGMENTS, channels), 0)
    for m in range(taps - 1):
        ends = conv_in[length - lead + m * SEGMENTS : length - lead + (m + 1) * SEGMENTS, :]
        at = SEGMENTS - taps + 1 + m
        extended[m * SEGMENTS : (m + 1) * SEGMENTS, :] = jnp.where(
            place == 0, halo_conv[at : at + 1, :], pltpu.roll(ends, 1, 0)
        )
    extended[lead:, :] = conv_in[...]
    total = jnp.broadcast_to(conv_bias[...][None], (length, channels))
    for k in range(taps):
        first = (taps - 1 - k) * SEGMENTS
        total += conv_weight[k : k + 1, :] * extended[first : first + length, :] * marks[:, k : k + 1]
    mixed[...] = total
    out = total * sigmoid(total)
    conv_out[...] = out
    partial[...] = product(xproj_t[...], out, (1, 1))


def rows_at(step):
    return pl.ds(pl.multiple_of(step * SEGMENTS, SEGMENTS), SEGMENTS)


def spread(row):
    return jnp.broadcast_to(row, (SEGMENTS, row.shape[-1]))


def column_of(rows, column):
    return jnp.broadcast_to(rows[:, column : column + 1], (SEGMENTS, LANES))


def sweep(count, body, carry):
    return lax.fori_loop(0, count, body, carry, unroll=True)


def add_to(ref, first, rows, lanes, value):
    if first:
        ref[rows, lanes] = value
    else:
        ref[rows, lanes] += value


def chain_pieces(decay, value, backward):
    place = lax.broadcasted_iota(jnp.int32, decay.shape, 0)
    if backward:
        place = SEGMENTS - 1 - place

    def moved(array, distance):
        return pltpu.roll(array, (SEGMENTS - distance) if backward else distance, 0)

    distance = 1
    while distance < SEGMENTS:
        inside = place >= distance
        value = jnp.where(inside, decay * moved(value, distance) + value, value)
        decay = jnp.where(inside, decay * moved(decay, distance), decay)
        distance *= 2
    first = place == 0
    before = jnp.where(first, 0.0, moved(value, 1))
    factor = jnp.where(first, 1.0, moved(decay, 1))
    return factor, before, value


def totals_kernel(ids, p0, p1, p2, p3, dt_weight, dt_bias, decay_log, conv_out, marks,
                  coef, dt_pre, stepsize, drive, stepd, rates, entry, total, padded):
    states, channels = decay_log.shape
    rank = dt_weight.shape[0]
    length = conv_out.shape[0]
    steps = length // SEGMENTS
    projected = (p0[...] + p1[...]) + (p2[...] + p3[...])
    missing = LANES - projected.shape[0]
    coef[...] = jnp.concatenate([projected, jnp.zeros((missing, length), jnp.float32)]).T
    padded[...] = jnp.zeros_like(padded)
    padded[:rank, :] = dt_weight[...]
    pre = product(coef[...], padded[...]) + dt_bias[...][None]
    dt_pre[...] = pre
    size = softplus(pre)
    stepsize[...] = size
    drive[...] = size * conv_out[...]
    stepd[...] = jnp.where(marks[:, 1:2] > 0.5, size, NEVER)
    rates[...] = -jnp.exp(decay_log[...])
    total[...] = jnp.zeros_like(total)
    zero = jnp.zeros((SEGMENTS, LANES), jnp.float32)
    tiles = [slice(at, at + LANES) for at in range(0, channels, LANES)]
    sums = [zero] * len(tiles)
    for step in range(steps):
        rows = slice(step * SEGMENTS, (step + 1) * SEGMENTS)
        sums = [value + stepd[rows, lanes] for value, lanes in zip(sums, tiles)]
    for value, lanes in zip(sums, tiles):
        total[states : states + 1, lanes] = jnp.sum(value, axis=0, keepdims=True)
    for group in range(0, states, GROUP):
        names = range(group, group + GROUP)
        rate = [[spread(rates[n : n + 1, lanes] * LOG2E) for lanes in tiles] for n in names]

        def body(step, current):
            rows = rows_at(step)
            near = coef[rows, :]
            width = [stepd[rows, lanes] for lanes in tiles]
            push = [drive[rows, lanes] for lanes in tiles]
            later = []
            for at, n in enumerate(names):
                entering = column_of(near, rank + n)
                later.append(tuple(
                    jnp.exp2(width[t] * rate[at][t]) * current[at][t] + push[t] * entering
                    for t in range(len(tiles))
                ))
            return tuple(later)

        current = sweep(steps, body, ((zero,) * len(tiles),) * GROUP)
        for at, n in enumerate(names):
            for t, lanes in enumerate(tiles):
                decay = jnp.exp2(sums[t] * rate[at][t])
                factor, before, last = chain_pieces(decay, current[at][t], False)
                entry[0, n, :, lanes] = factor
                entry[1, n, :, lanes] = before
                total[n : n + 1, lanes] = last[SEGMENTS - 1 :, :]


def pair_kernel(ids, total, other, rates, early, late, chip):
    states = rates.shape[0]
    second = ids[2] == 1
    mine, theirs = total[...], other[...]
    first, last = jnp.where(second, theirs, mine), jnp.where(second, mine, theirs)
    early[...] = first
    late[...] = last
    chip[...] = first + last
    chip[:states, :] = (
        jnp.exp(last[states : states + 1] * rates[...]) * first[:states] + last[:states]
    )


def pair_back_kernel(ids, total, other, early, rates, late_total, chip):
    states = rates.shape[0]
    second = ids[2] == 1
    mine, theirs = total[...], other[...]
    first, last = jnp.where(second, theirs, mine), jnp.where(second, mine, theirs)
    late_total[...] = last
    chip[...] = first + jnp.exp(early[states : states + 1, :] * rates[...]) * last


def states_kernel(rank, ids, stepd, drive, coef, rates, entry, early, conv_out, gate_in, skip,
                  out_weight, *rest):
    chips = len(rest) - 8
    totals = rest[:chips]
    ssm_skip, gated, slices, kept, held, whole, kept_here, sems = rest[chips:]
    me, core, here = ids[0], ids[2], ids[3]
    states, channels = rates.shape
    length = stepd.shape[0]
    steps = length // SEGMENTS
    for key, value in enumerate(totals):
        held[key] = value[...]
    state = jnp.zeros((states, channels), jnp.float32)
    for chip in range(chips):
        value = held[here ^ chip]
        grown = jnp.exp(value[states : states + 1] * rates[...]) * state + value[:states]
        state = jnp.where(chip < here, grown, state)
    inner = jnp.exp(early[states : states + 1, :] * rates[...]) * state + early[:states, :]
    start = jnp.where(core == 1, inner, state)
    tiles = [slice(at, at + LANES) for at in range(0, channels, LANES)]
    copies = []
    for group in range(0, states, GROUP):
        names = range(group, group + GROUP)
        slab = group // GROUP
        rate = [[spread(rates[n : n + 1, lanes] * LOG2E) for lanes in tiles] for n in names]
        current = tuple(
            tuple(
                entry[0, n, :, lanes] * start[n : n + 1, lanes] + entry[1, n, :, lanes]
                for lanes in tiles
            )
            for n in names
        )
        for at in range(GROUP):
            for t, lanes in enumerate(tiles):
                kept_here[slab, 0, at, :, lanes] = current[at][t]

        def body(step, current):
            rows = rows_at(step)
            near = coef[rows, :]
            width = [stepd[rows, lanes] for lanes in tiles]
            push = [drive[rows, lanes] for lanes in tiles]
            later, total = [], [None] * len(tiles)
            for at, n in enumerate(names):
                entering, leaving = column_of(near, rank + n), column_of(near, rank + states + n)
                new = []
                for t, lanes in enumerate(tiles):
                    decay = jnp.exp2(width[t] * rate[at][t])
                    new.append(decay * current[at][t] + push[t] * entering)
                    kept_here[slab, step + 1, at, :, lanes] = new[t]
                    term = leaving * new[t]
                    total[t] = term if total[t] is None else total[t] + term
                later.append(tuple(new))
            for t, lanes in enumerate(tiles):
                add_to(ssm_skip, group == 0, rows, lanes, total[t])
            return tuple(later)

        sweep(steps, body, current)
        copies.append(pltpu.make_async_copy(kept_here.at[slab], kept.at[slab], sems.at[slab]))
        copies[-1].start()
    skipped = ssm_skip[...] + skip[...][None] * conv_out[...]
    ssm_skip[...] = skipped
    gate = gate_in[...]
    out = skipped * gate * sigmoid(gate)
    gated[...] = out
    whole[...] = product(out, out_weight[...])
    cut_slices(me, whole, slices)
    for copy in copies:
        copy.wait()


def dispatch_kernel(ids, s0, s1, s2, s3, rows_slice, slots_own, slots_other,
                    hidden, own, other):
    packed = (s0[...] + s1[...]) + (s2[...] + s3[...]) + rows_slice[...]
    hidden[...] = packed
    send_slots(ids[2], packed, slots_own[...], slots_other[...], own, other)


def raw_kernel(ids, c0, c1, c2, c3, expert_in, expert_out, raw, cot, in_high, in_low,
               out_high, out_low, held):
    join_slices(ids[0], (c0, c1, c2, c3), held, cot)
    in_high[...], in_low[...] = two_parts(expert_in[...])
    out_high[...], out_low[...] = two_parts(expert_out[...])
    raw[...] = product(cot[...], (out_high[...], out_low[...]), (1, 1))


def expert_kernel(ids, h0, h1, h2, h3, raw, in_high, in_low, norm_gain, router_t,
                  slices, second, act, grad_pre, gates, grad_logits, grad_gain,
                  held, whole):
    me, expert = ids[0], ids[1]
    join_slices(me, (h0, h1, h2, h3), held, whole)
    rows = whole[...]
    inverse = inverse_rms(rows)
    normed = rows * inverse * norm_gain[...][None]
    second[...] = normed
    normed_parts = two_parts(normed)
    router_parts = two_parts(router_t[...])
    weight = (in_high[...], in_low[...])
    logits = product(normed_parts, router_parts, (1, 1))
    logits = logits - jnp.max(logits, axis=-1, keepdims=True)
    powers = jnp.exp(logits)
    probs = powers / jnp.sum(powers, axis=-1, keepdims=True)
    chosen = jnp.where(
        lax.broadcasted_iota(jnp.int32, logits.shape, 1) == expert, 1.0, 0.0
    )
    gate = jnp.sum(probs * chosen, axis=-1, keepdims=True)
    gates[...] = gate
    hidden_act, slope = gelu_parts(product(normed_parts, weight))
    act[...] = hidden_act
    raws = raw[...]
    grad_gate = jnp.sum(hidden_act * raws, axis=-1, keepdims=True)
    grads = gate * raws * slope
    grad_pre[...] = grads
    logit_grads = grad_gate * gate * (chosen - probs)
    grad_logits[...] = logit_grads
    grad_second = product(grads, weight, (1, 1)) + product(logit_grads, router_parts)
    grad_gain[...] = jnp.sum(rows * inverse * grad_second, axis=0, keepdims=True)
    whole[...] = norm_back(rows, inverse, norm_gain[...][None], grad_second)
    cut_slices(me, whole, slices)


def expert_rest_kernel(ids, second, act, grad_pre, gates, grad_logits, cot, out_high, out_low,
                       slices, grad_in, grad_out, grad_router, whole):
    gate = gates[...]
    acts = two_parts(act[...])
    normed = two_parts(second[...])
    whole[...] = gate * product(acts, (out_high[...], out_low[...]))
    cut_slices(ids[0], whole, slices)
    grad_out[...] = product(acts, gate * cot[...], (0, 0))
    grad_in[...] = product(normed, grad_pre[...], (0, 0))
    grad_router[...] = product(grad_logits[...], normed, (0, 0))


def home_kernel(ids, own, other, base, rows_own, rows_other, out):
    half = own.shape[1] // 2
    second = ids[2] == 1

    def mine(rows):
        return jnp.where(second, pltpu.roll(rows, half, 1), rows)

    total = select_rows(rows_own[...], mine(own[...])) + select_rows(
        rows_other[...], mine(other[...])
    )
    count = base.shape[0]
    lane = lax.broadcasted_iota(jnp.int32, base.shape, 1)
    out[...] = base[...] + jnp.where(
        lane < half, total[:count], pltpu.roll(total[count:], half, 1)
    )


def whole_kernel(ids, p0, p1, p2, p3, out, held, whole, tiles):
    join_slices(ids[0], (p0, p1, p2, p3), held, whole)
    deinterleave_to(whole, tiles, out)


def leaving_kernel(rank, ids, g0, g1, g2, g3, out_weight, gate_in, ssm_skip, conv_out, stepd,
                   coef, rates, grad_hidden, grad_ssm, grad_gate_in, grad_skip, entry, total,
                   held):
    join_slices(ids[0], (g0, g1, g2, g3), held, grad_hidden)
    states, channels = rates.shape
    length = stepd.shape[0]
    steps = length // SEGMENTS
    grad_gated = product(grad_hidden[...], out_weight[...], (1, 1))
    gate = gate_in[...]
    gate_sigmoid = sigmoid(gate)
    pulled = grad_gated * gate * gate_sigmoid
    grad_ssm[...] = pulled
    grad_gate_in[...] = grad_gated * ssm_skip[...] * (
        gate_sigmoid * (1.0 + gate * (1.0 - gate_sigmoid))
    )
    grad_skip[...] = jnp.sum(pulled * conv_out[...], axis=0, keepdims=True)
    zero = jnp.zeros((SEGMENTS, LANES), jnp.float32)
    tiles = [slice(at, at + LANES) for at in range(0, channels, LANES)]
    sums = [zero] * len(tiles)
    for step in range(steps):
        rows = slice(step * SEGMENTS, (step + 1) * SEGMENTS)
        sums = [value + stepd[rows, lanes] for value, lanes in zip(sums, tiles)]
    for group in range(0, states, GROUP):
        names = range(group, group + GROUP)
        rate = [[spread(rates[n : n + 1, lanes] * LOG2E) for lanes in tiles] for n in names]

        def body(back, current):
            rows = rows_at(steps - 1 - back)
            near = coef[rows, :]
            width = [stepd[rows, lanes] for lanes in tiles]
            pull = [grad_ssm[rows, lanes] for lanes in tiles]
            later = []
            for at, n in enumerate(names):
                leaving = column_of(near, rank + states + n)
                later.append(tuple(
                    jnp.exp2(width[t] * rate[at][t]) * (current[at][t] + pull[t] * leaving)
                    for t in range(len(tiles))
                ))
            return tuple(later)

        current = sweep(steps, body, ((zero,) * len(tiles),) * GROUP)
        for at, n in enumerate(names):
            for t, lanes in enumerate(tiles):
                decay = jnp.exp2(sums[t] * rate[at][t])
                factor, before, last = chain_pieces(decay, current[at][t], True)
                entry[0, n, :, lanes] = factor
                entry[1, n, :, lanes] = before
                total[n : n + 1, lanes] = last[:1, :]


def adjoint_kernel(rank, chips, ids, stepd, drive, grad, coef, rates, entry, kept, early, late,
                   late_total, conv_out, stepsize, dt_pre, skip, dt_weight, grad_norm2, grad_router,
                   *rest):
    sums, totals = rest[:chips], rest[chips : 2 * chips]
    (partial, grad_direct, grad_dt_pre, grad_decay, grad_dt_bias, held_sums, held, kept_here,
     in_terms, out_terms, grad_push, grad_width, sems) = rest[2 * chips :]
    core, here = ids[2], ids[3]
    states, channels = rates.shape
    length = stepd.shape[0]
    steps = length // SEGMENTS
    copies = [
        pltpu.make_async_copy(kept.at[slab], kept_here.at[slab], sems.at[slab])
        for slab in range(states // GROUP)
    ]
    for copy in copies:
        copy.start()
    for key in range(chips):
        held_sums[key] = sums[key][states : states + 1, :]
        held[key] = totals[key][...]
    state = jnp.zeros((states, channels), jnp.float32)
    for chip in reversed(range(chips)):
        grown = held[here ^ chip] + jnp.exp(held_sums[here ^ chip] * rates[...]) * state
        state = jnp.where(chip > here, grown, state)
    inner = late_total[...] + jnp.exp(late[states : states + 1, :] * rates[...]) * state
    final = jnp.where(core == 1, state, inner)
    zero = jnp.zeros((SEGMENTS, LANES), jnp.float32)
    tiles = [slice(at, at + LANES) for at in range(0, channels, LANES)]
    for group in range(0, states, GROUP):
        names = range(group, group + GROUP)
        slab = group // GROUP
        rate = [[spread(rates[n : n + 1, lanes]) for lanes in tiles] for n in names]
        current = tuple(
            tuple(
                entry[0, n, :, lanes] * final[n : n + 1, lanes] + entry[1, n, :, lanes]
                for lanes in tiles
            )
            for n in names
        )
        copies[slab].wait()

        def body(back, carry):
            current, slopes = carry
            step = steps - 1 - back
            rows = rows_at(step)
            near = coef[rows, :]
            width = [stepd[rows, lanes] for lanes in tiles]
            push = [drive[rows, lanes] for lanes in tiles]
            pull = [grad[rows, lanes] for lanes in tiles]
            later, slope = [], []
            total, width_total = [None] * len(tiles), [None] * len(tiles)
            for at, n in enumerate(names):
                entering, leaving = column_of(near, rank + n), column_of(near, rank + states + n)
                new, turned, in_term, out_term = [], [], None, None
                for t, lanes in enumerate(tiles):
                    adjoint = leaving * pull[t] + current[at][t]
                    decayed = jnp.exp2(width[t] * (rate[at][t] * LOG2E)) * adjoint
                    through = decayed * kept_here[slab, step, at, :, lanes]
                    term, rated = adjoint * entering, through * rate[at][t]
                    total[t] = term if total[t] is None else total[t] + term
                    width_total[t] = rated if width_total[t] is None else width_total[t] + rated
                    new.append(decayed)
                    turned.append(slopes[at][t] + through * width[t])
                    term = adjoint * push[t]
                    in_term = term if in_term is None else in_term + term
                    term = kept_here[slab, step + 1, at, :, lanes] * pull[t]
                    out_term = term if out_term is None else out_term + term
                place = slice(n * LANES, (n + 1) * LANES)
                in_terms[rows, place] = in_term
                out_terms[rows, place] = out_term
                later.append(tuple(new))
                slope.append(tuple(turned))
            for t, lanes in enumerate(tiles):
                add_to(grad_push, group == 0, rows, lanes, total[t])
                add_to(grad_width, group == 0, rows, lanes, width_total[t])
            return tuple(later), tuple(slope)

        none = ((zero,) * len(tiles),) * GROUP
        _, slopes = sweep(steps, body, (current, none))
        for at, n in enumerate(names):
            for t, lanes in enumerate(tiles):
                grad_decay[n : n + 1, lanes] = rates[n : n + 1, lanes] * jnp.sum(
                    slopes[at][t], axis=0, keepdims=True
                )
    pushed = grad_push[...]
    grads = (pushed * conv_out[...] + grad_width[...]) * sigmoid(dt_pre[...])
    grad_dt_pre[...] = grads
    grad_dt_bias[...] = jnp.sum(grads, axis=0, keepdims=True)
    grad_direct[...] = pushed * stepsize[...] + skip[...][None] * grad[...]
    partial[:rank, :] = product(dt_weight[...], grads, (1, 1))
    shape = (2 * states, states * LANES)
    column = lax.broadcasted_iota(jnp.int32, shape, 0)
    owner = lax.broadcasted_iota(jnp.int32, shape, 1) // LANES
    total = None
    for terms, base in ((in_terms, 0), (out_terms, states)):
        ones = jnp.where(owner + base == column, 1.0, 0.0).astype(jnp.bfloat16)
        for part in two_parts(terms[...]):
            term = once(ones, part, (1, 1))
            total = term if total is None else total + term
    cols = rank + 2 * states
    partial[rank:cols, :] = total
    row = cols
    for shared in (grad_norm2, grad_router):
        for at in range(0, shared.shape[1], length):
            partial[row : row + shared.shape[0], :] = shared[:, at : at + length]
            row += shared.shape[0]
    partial[row:, :] = jnp.zeros((partial.shape[0] - row, length), jnp.float32)


def conv_back_kernel(experts, ids, p0, p1, p2, p3, xproj_t, grad_direct, mixed, conv_out, extended,
                     marks, conv_weight, coef, grad_dt_pre, grad_decay, grad_dt_bias, grad_skip,
                     normed, halo_normed, keep, send, grad_conv, grad_halo,
                     small, grad_extended, summed, weights):
    taps, channels = conv_weight.shape
    cols, states = xproj_t.shape[0], grad_decay.shape[0]
    rank = cols - 2 * states
    length = mixed.shape[0]
    lead = (taps - 1) * SEGMENTS
    summed[...] = (p0[...] + p1[...]) + (p2[...] + p3[...])
    projected = two_parts(summed[:cols, :])
    grad_out = grad_direct[...] + product(projected, xproj_t[...], (0, 0))
    value = mixed[...]
    value_sigmoid = sigmoid(value)
    grad_mixed = grad_out * (value_sigmoid * (1.0 + value * (1.0 - value_sigmoid)))
    grad_extended[...] = jnp.zeros_like(grad_extended)
    first_tap = cols + rank + states
    small[first_tap:, :] = jnp.zeros((small.shape[0] - first_tap, channels), jnp.float32)
    for k in range(taps):
        first = (taps - 1 - k) * SEGMENTS
        masked = grad_mixed * marks[:, k : k + 1]
        small[first_tap + k : first_tap + k + 1, :] = jnp.sum(
            masked * extended[first : first + length, :], axis=0, keepdims=True
        )
        grad_extended[first : first + length, :] += conv_weight[k : k + 1, :] * masked
    grad_conv[...] = grad_extended[lead:, :]
    grad_halo[...] = jnp.zeros_like(grad_halo)
    place = lax.broadcasted_iota(jnp.int32, (SEGMENTS, channels), 0)
    for m in range(taps - 1):
        rows = grad_extended[m * SEGMENTS : (m + 1) * SEGMENTS, :]
        at = SEGMENTS - taps + 1 + m
        grad_halo[at : at + 1, :] = rows[:1, :]
        inside = jnp.where(place == SEGMENTS - 1, 0.0, pltpu.roll(rows, SEGMENTS - 1, 0))
        ends = slice(length - lead + m * SEGMENTS, length - lead + (m + 1) * SEGMENTS)
        grad_conv[ends, :] += inside
    small[:cols, :] = product(projected, conv_out[...])
    low = product(coef[...], grad_dt_pre[...], (0, 0))
    small[cols : cols + rank, :] = low[:rank, :]
    small[cols + rank : first_tap, :] = grad_decay[...]
    last = first_tap + taps
    small[last : last + 1, :] = jnp.sum(grad_mixed, axis=0, keepdims=True)
    small[last + 1 : last + 2, :] = grad_dt_bias[...]
    small[last + 2 : last + 3, :] = grad_skip[...]
    first, row = last + 3, cols
    for count in (1, experts):
        for at in range(0, 2 * channels, length):
            value = summed[row : row + count, :]
            end = at + length
            for piece in range(at // channels, -(-end // channels)):
                low, high = max(at, piece * channels), min(end, (piece + 1) * channels)
                target = first + piece * count
                small[target : target + count, low - piece * channels : high - piece * channels] = (
                    value[:, low - at : high - at]
                )
            row += count
        first += 2 * count
    weights[...] = product(normed[...], grad_conv[...], (0, 0)) + product(
        halo_normed[...], grad_halo[...], (0, 0)
    )
    in_order(ids[1], (weights, small), keep, send)


def tokens_kernel(ids, grad_conv, grad_halo, conv_high, conv_low, gate_part, rows, halo_rows,
                  slices, whole):
    weight = conv_high[...], conv_low[...]
    length = grad_conv.shape[0]
    grad = product(grad_conv[...], weight, (1, 1)) + gate_part[...]
    before = product(grad_halo[...], weight, (1, 1))
    value, value_before = rows[...], halo_rows[...]
    whole[:length, :] = grad
    whole[length:, :] = jnp.zeros((whole.shape[0] - length, whole.shape[1]), jnp.float32)
    whole[length : length + SEGMENTS, :] = before
    whole[length : length + 1, :] = jnp.sum(
        value * inverse_rms(value) * grad, axis=0, keepdims=True
    ) + jnp.sum(value_before * inverse_rms(value_before) * before, axis=0, keepdims=True)
    cut_slices(ids[0], whole, slices)


def early_weights_kernel(ids, gated, grad_hidden, normed, grad_gate_in, keep, send, whole,
                         gate):
    channels = gated.shape[1]
    halves = product(gated[...], grad_hidden[...], (0, 0))
    whole[:channels, :] = halves[:, :channels]
    whole[channels:, :] = halves[:, channels:]
    gate[...] = product(normed[...], grad_gate_in[...], (0, 0))
    in_order(ids[1], (whole, gate), keep, send)


def in_order(me, wholes, keep, send):
    count = 2 * keep.shape[0]
    levels = count.bit_length() - 1
    for place in range(count):
        block = reversed_bits(place, levels) ^ me
        out, at = (keep, place) if place < count // 2 else (send, place - count // 2)
        first = 0
        for whole in wholes:
            rows = whole.shape[0] // count
            from_row = pl.multiple_of(block * rows, 8)
            out[at, first : first + rows, :] = whole[pl.ds(from_row, rows), :]
            first += rows


def gate_tokens_kernel(ids, grad_gate_in, gate_high, gate_low, out):
    out[...] = product(grad_gate_in[...], (gate_high[...], gate_low[...]), (1, 1))


def extra_kernel(ids, p0, p1, p2, p3, extra, norm1, held, whole):
    join_slices(ids[0], (p0, p1, p2, p3), held, whole)
    row = whole.shape[0] - 2 * SEGMENTS
    channels = norm1.shape[2]
    extra[...] = whole[row : row + SEGMENTS, :]
    norm1[...] = jnp.zeros_like(norm1)
    for piece in range(whole.shape[1] // channels):
        lanes = slice(piece * channels, (piece + 1) * channels)
        norm1[0, piece : piece + 1, :] = whole[row : row + 1, lanes]


def grad_tokens_kernel(taps, ids, p0, p1, p2, p3, from_next, rows, gain, grad_hidden, out,
                       held, whole, tiles):
    join_slices(ids[0], (p0, p1, p2, p3), held, whole)
    length = rows.shape[0]
    lead = (taps - 1) * SEGMENTS
    for m in range(taps - 1):
        row = length - lead + (m + 1) * SEGMENTS - 1
        at = SEGMENTS - taps + 1 + m
        whole[row : row + 1, :] += from_next[at : at + 1, :]
    value = rows[...]
    whole[:length, :] = (
        norm_back(value, inverse_rms(value), gain[...][None], whole[:length, :]) + grad_hidden[...]
    )
    deinterleave_to(whole, tiles, out)


def early_out_kernel(ids, summed, out_weight):
    count, rows, channels = summed.shape
    levels = count.bit_length() - 1
    for block in range(count):
        value = summed[reversed_bits(block ^ ids[1], levels)]
        half, row = divmod(block * rows, channels)
        out_weight[row : row + rows, half * channels : (half + 1) * channels] = value


def weights_out_kernel(counts, ids, early, late, norm1, weight, *rest):
    *outs, sum_norm1, small = rest
    count, rows = early.shape[0], early.shape[1]
    more = late.shape[1] - rows
    levels = count.bit_length() - 1
    for block in range(count):
        place = reversed_bits(block ^ ids[1], levels)
        small[block * more : (block + 1) * more, :] = late[place, rows:, :]
        weight[block * rows : (block + 1) * rows, 0, :] = late[place, :rows, :]
        weight[block * rows : (block + 1) * rows, 1, :] = early[place]
    first = 0
    channels = small.shape[1]
    for out, used in zip(outs, counts):
        per = out.shape[-1] // channels
        each = used // per
        for piece in range(per):
            lanes = slice(piece * channels, (piece + 1) * channels)
            if len(out.shape) == 1:
                out[lanes] = small[first, :]
            else:
                out[:, lanes] = small[first : first + each, :]
            first += each
    for piece in range(sum_norm1.shape[0] // channels):
        sum_norm1[piece * channels : (piece + 1) * channels] = norm1[0, piece, :]


def local(
    tokens, norm1_gain, in_weight, conv_weight, conv_bias, xproj_weight, dt_weight, dt_bias,
    decay_log, skip_gain, out_weight, norm2_gain, router_weight, expert_in, expert_out,
    segments, expert_ids, cotangent,
):
    length, width = tokens.shape
    taps, channels = conv_weight.shape
    experts = router_weight.shape[1]
    wide = experts
    capacity = 5 * length // (4 * experts)
    states, rank = decay_log.shape[0], dt_weight.shape[0]
    chips = wide // 2
    slots = chips * capacity
    steps = length // SEGMENTS
    me_wide = lax.axis_index("wide")
    ids = jnp.stack([lax.axis_index("narrow"), me_wide, me_wide & 1, me_wide // 2]).astype(jnp.int32)
    half, double = length // 2, width // 2
    bf16 = jnp.bfloat16
    rows_shape, channel_rows = shape_of(length, width), shape_of(length, channels)
    packed, packed_slots = shape_of(half, double), shape_of(slots, double)
    vmem = lambda *shape: pltpu.VMEM(shape, jnp.float32)
    xproj_t, router_t = xproj_weight.T, router_weight.T
    cols = xproj_t.shape[0]

    tiled = vmem(width // LANES, length, LANES)

    halo_rows = wide_shift(tokens[length - SEGMENTS :], 1)

    (marks, slots_own, slots_other, rows_own, rows_other, rows_slice, cot_slice, cot_own,
     cot_other, conv_high, conv_low, gate_high, gate_low) = call(
        functools.partial(start_kernel, capacity),
        [shape_of(length, SEGMENTS)]
        + [shape_of(slots, length, dtype=bf16)] * 2
        + [shape_of(length, slots, dtype=bf16)] * 2
        + [packed, packed, packed_slots, packed_slots]
        + [shape_of(width, channels, dtype=bf16)] * 4,
        ids, segments.reshape(-1, LANES), expert_ids.reshape(1, length), tokens, cotangent,
        in_weight,
        scratch=[pltpu.VMEM((segments.shape[0] // LANES, LANES), jnp.int32),
                 pltpu.VMEM((1, length), jnp.int32)] + [vmem(length, width)] * 2
        + [vmem(width, 2, channels), vmem(length, width), tiled, vmem(2, width, channels),
           pltpu.SemaphoreType.DMA((5,))],
        far_in=[0, 1, 2, 3, 4],
    )
    cot_pair = cot_own + core_swap(cot_other)
    rows, normed, conv_in, gate_in = call(
        front_kernel,
        [rows_shape, rows_shape, channel_rows, channel_rows],
        ids, tokens, norm1_gain, conv_high, conv_low, gate_high, gate_low,
        scratch=[tiled],
    )
    mixed, conv_out, partial, extended, halo_normed = call(
        conv_kernel,
        [channel_rows, channel_rows, shape_of(cols, length),
         shape_of(length + (taps - 1) * SEGMENTS, channels), shape_of(SEGMENTS, width)],
        ids, halo_rows, norm1_gain, conv_high, conv_low, conv_in, marks, conv_weight,
        conv_bias, xproj_t, after=[cot_pair],
    )
    partials = narrow_all(partial)

    partials = narrow_all(partial)

    cot_blocks = chip_each(hold(cot_pair, partial), chips)

    entry_shape = shape_of(2, states, SEGMENTS, channels)
    total_rows = -(-(states + 1) // 8) * 8
    coef, dt_pre, stepsize, drive, stepd, rates, entry, total = call(
        totals_kernel,
        [shape_of(length, LANES)] + [channel_rows] * 4
        + [shape_of(states, channels), entry_shape, shape_of(total_rows, channels)],
        ids, *partials, dt_weight, dt_bias, decay_log, conv_out, marks,
        scratch=[vmem(LANES, channels)],
    )
    total_shape = shape_of(total_rows, channels)
    early, late, chip_total = call(
        pair_kernel, [total_shape] * 3, ids, total, core_swap(total), rates, after=[cot_blocks]
    )
    chip_totals = chip_all(chip_total, chips)
    slabs = states // GROUP
    cot_held = hold(cot_blocks, chip_total)
    cot_one, cot_two = narrow_swap(cot_held, 1), narrow_swap(cot_held, 2)
    kept_shape = (slabs, steps + 1, GROUP, SEGMENTS, channels)
    ssm_skip, gated, mixer_slices, kept = call(
        functools.partial(states_kernel, rank),
        [channel_rows, channel_rows, shape_of(4, half, double), shape_of(*kept_shape)],
        ids, stepd, drive, coef, rates, entry, early, conv_out, gate_in, skip_gain,
        out_weight, *chip_totals,
        scratch=[vmem(chips, total_rows, channels), vmem(length, width), vmem(*kept_shape),
                 pltpu.SemaphoreType.DMA((slabs,))],
        out_place=[3],
    )
    mixer_slices = hold(mixer_slices, cot_one, cot_two)
    expert_rows, square = shape_of(2 * slots, width), (expert_in.shape[1], expert_in.shape[2])
    hidden_units = square[1]
    hidden_slice, hidden_own, hidden_other = call(
        dispatch_kernel,
        [packed, packed_slots, packed_slots],
        ids, *narrow_each(mixer_slices), rows_slice, slots_own, slots_other,
    )
    hidden_blocks = chip_each(hidden_own + core_swap(hidden_other), chips)
    cot_three = narrow_swap(hold(cot_one, hidden_own), 2)
    raw, cot, in_high, in_low, out_high, out_low = call(
        raw_kernel,
        [shape_of(2 * slots, hidden_units), expert_rows]
        + [shape_of(*square, dtype=bf16)] * 2
        + [shape_of(square[1], square[0], dtype=bf16)] * 2,
        ids, cot_blocks, cot_one, cot_two, cot_three, expert_in[0], expert_out[0],
        scratch=[vmem(4, slots, double)],
    )
    hidden_parts = narrow_all(hold(hidden_blocks, raw))
    slices_shape = shape_of(4, slots, double)
    grad_slices, second, act, grad_pre, gates, grad_logits, grad_norm2 = call(
        expert_kernel,
        [slices_shape, expert_rows] + [shape_of(2 * slots, hidden_units)] * 2
        + [shape_of(2 * slots, 1), shape_of(2 * slots, experts), shape_of(1, width)],
        ids, *hidden_parts, raw, in_high, in_low, norm2_gain, router_t,
        scratch=[vmem(4, slots, double), vmem(2 * slots, width)],
    )
    grad_mine = pair_sum(narrow_each(grad_slices))
    value_slices, grad_expert_in, grad_expert_out, grad_router_t = call(
        expert_rest_kernel,
        [slices_shape, shape_of(*square), shape_of(square[1], square[0]),
         shape_of(experts, width)],
        ids, second, act, grad_pre, gates, grad_logits, cot, out_high, out_low,
        scratch=[vmem(2 * slots, width)],
    )
    grad_back = chip_each(grad_mine, chips)
    value_mine = pair_sum(narrow_each(value_slices))
    grad_slice = call(
        home_kernel, [packed], ids, grad_back, core_swap(grad_back), cot_slice, rows_own,
        rows_other, after=[value_mine],
    )[0]
    grad_parts = narrow_all(grad_slice)
    value_back = chip_each(value_mine, chips)

    def whole_of(parts, after=()):
        return call(
            whole_kernel, [rows_shape], ids, *parts, after=after,
            scratch=[vmem(4, half, double), vmem(length, width), tiled],
        )[0]

    grad_hidden, grad_ssm, grad_gate_in, grad_skip, back_entry, back_total = call(
        functools.partial(leaving_kernel, rank),
        [rows_shape, channel_rows, channel_rows, shape_of(1, channels), entry_shape,
         shape_of(states, channels)],
        ids, *grad_parts, out_weight, gate_in, ssm_skip, conv_out, stepd, coef, rates,
        scratch=[vmem(4, half, double)], after=[value_back],
    )
    other_back = core_swap(back_total)
    block = width // wide
    half_blocks = shape_of(wide // 2, 2 * block, channels)
    early_keep, early_send = call(
        early_weights_kernel,
        [half_blocks, half_blocks],
        ids, gated, grad_hidden, normed, grad_gate_in,
        scratch=[vmem(width, channels)] * 2,
    )
    back_late, back_chip = call(
        pair_back_kernel, [shape_of(states, channels)] * 2,
        ids, back_total, other_back, early, rates, after=[early_keep],
    )
    back_totals = chip_all(back_chip, chips)
    early_arrived = core_swap(hold(early_send, back_chip))
    out_sum, gate_sum = (
        WideSum(early_keep[:, rows], early_send[:, rows])
        for rows in (slice(0, block), slice(block, None))
    )
    out_sum.arrived, gate_sum.arrived = early_arrived[:, :block], early_arrived[:, block:]
    out_sum.finish()
    gate_sum.finish()
    first_step = out_sum.start(*back_totals)

    shared_rows = (experts + 1) * (width // length)
    partial_rows = cols + shared_rows + -(cols + shared_rows) % 8
    partial_back, grad_direct, grad_dt_pre, grad_decay, grad_dt_bias = call(
        functools.partial(adjoint_kernel, rank, chips),
        [shape_of(partial_rows, length), channel_rows, channel_rows, shape_of(states, channels),
         shape_of(1, channels)],
        ids, stepd, drive, grad_ssm, coef, rates, back_entry, kept, early, late, back_late,
        conv_out, stepsize, dt_pre, skip_gain, dt_weight, grad_norm2, grad_router_t,
        *chip_totals, *back_totals,
        scratch=[vmem(chips, 1, channels), vmem(chips, states, channels), vmem(*kept_shape),
                 vmem(length, states * LANES), vmem(length, states * LANES),
                 vmem(length, channels), vmem(length, channels),
                 pltpu.SemaphoreType.DMA((slabs,))],
        in_place=[6], after=[out_sum.send, gate_sum.send],
    )
    partials_back = narrow_all(partial_back)
    gate_part = call(
        gate_tokens_kernel, [rows_shape], ids, grad_gate_in, gate_high, gate_low,
        after=[partial_back],
    )[0]
    out_sum.finish(partial_back)
    out_sum.start()
    gate_sum.start(partial_back)
    grain = 8 * wide
    small_rows = cols + rank + states + taps + 3 + (experts + 1) * (width // channels)
    small_rows += -small_rows % grain
    more = small_rows // wide
    half_blocks = shape_of(wide // 2, block + more, channels)
    token_rows = length + 2 * SEGMENTS
    conv_keep, conv_send, grad_conv, grad_halo = call(
        functools.partial(conv_back_kernel, experts),
        [half_blocks, half_blocks, channel_rows, shape_of(SEGMENTS, channels)],
        ids, *partials_back, xproj_t, grad_direct, mixed, conv_out, extended, marks,
        conv_weight, coef, grad_dt_pre, grad_decay, grad_dt_bias, grad_skip,
        normed, halo_normed,
        scratch=[vmem(small_rows, channels),
                 vmem(length + (taps - 1) * SEGMENTS, channels), vmem(partial_rows, length),
                 vmem(width, channels)],
        after=[gate_sum.arrived, out_sum.arrived],
    )
    (token_slices,) = call(
        tokens_kernel, [shape_of(4, token_rows // 2, double)],
        ids, grad_conv, grad_halo, conv_high, conv_low, gate_part, rows, halo_rows,
        scratch=[vmem(token_rows, width)],
    )
    out_sum.finish()
    gate_sum.finish()
    conv_sum = WideSum(conv_keep, conv_send)
    conv_sum.start()
    conv_sum.finish()
    (output_slice,) = call(
        home_kernel, [packed], ids, value_back, core_swap(hold(value_back, conv_keep)),
        hidden_slice, rows_own, rows_other,
    )
    levels = len(conv_sum.swaps)

    def extra_of(parts):
        return call(
            extra_kernel,
            [shape_of(SEGMENTS, width), shape_of(1, SEGMENTS, channels)],
            ids, *parts,
            scratch=[vmem(4, token_rows // 2, double), vmem(token_rows, width)],
        )

    def grad_tokens_of(parts, from_next):
        return call(
            functools.partial(grad_tokens_kernel, taps),
            [rows_shape], ids, *parts, from_next, rows, norm1_gain, grad_hidden,
            scratch=[vmem(4, token_rows // 2, double), vmem(token_rows, width), tiled],
        )[0]

    def out_weight_of(total, *others):
        return call(
            early_out_kernel, [shape_of(channels, width)], ids, total, after=others
        )[0]

    if levels == 3:
        sums = conv_sum, gate_sum, out_sum
        joint = [conv_sum.start(), *start_both(gate_sum, out_sum)]
        token_each = narrow_each(token_slices)
        for part in sums:
            part.finish(*joint, *token_each, output_slice)
        joint = [*start_both(conv_sum, gate_sum), out_sum.start()]
        token_parts = narrow_all(pair_sum(token_each))
        extra, norm1 = extra_of(token_parts)
        from_next = wide_shift(extra, -1)
        for part in sums:
            part.finish(*joint, norm1, from_next)
        arrived, norm1_other = conv_sum.start_with(norm1)
        joint = [arrived, gate_sum.start()]
        output_parts = narrow_all(hold(output_slice, norm1))
        for part in sums[:2]:
            part.finish(*joint, *output_parts)
        norm1 = norm1 + norm1_other
        arrived, norm1_other = conv_sum.start_with(norm1)
        grad_tokens = grad_tokens_of(token_parts, from_next)
        joint = [arrived, *start_both(gate_sum, out_sum, grad_tokens)]
        output = whole_of(output_parts, after=[conv_sum.send])
        for part in sums:
            part.finish(*joint, output, grad_tokens)
        norm1 = norm1 + norm1_other
        arrived, norm1_other = conv_sum.start_with(norm1)
        sum_out_weight = out_weight_of(out_sum.keep, conv_sum.send)
        conv_sum.finish(sum_out_weight)
        norm1 = norm1 + norm1_other
    else:
        token_parts = narrow_all(pair_sum(narrow_each(token_slices)))
        extra, norm1 = extra_of(token_parts)
        grad_tokens = grad_tokens_of(token_parts, wide_shift(extra, -1))
        output = whole_of(narrow_all(output_slice))
        sum_out_weight = out_weight_of(out_sum.rest())
        norm1 = norm1 + core_swap(norm1)
        norm1 = pair_sum(chip_all(norm1, chips))
    per = width // channels
    counts = (cols, rank, states, taps, 1, 1, 1, per, per * experts)
    (weight_sum, sum_xproj_t, sum_dt_weight, sum_decay, sum_taps, sum_conv_bias, sum_dt_bias,
     sum_skip, sum_norm2, sum_router_t, sum_norm1) = call(
        functools.partial(weights_out_kernel, counts),
        [shape_of(width, 2, channels)]
        + [shape_of(rows, channels) for rows in (cols, rank, states, taps)]
        + [shape_of(channels)] * 3
        + [shape_of(width), shape_of(experts, width), shape_of(width)],
        ids, gate_sum.rest(), conv_sum.rest(), norm1, scratch=[vmem(small_rows, channels)],
    )
    return (
        output,
        grad_tokens,
        sum_norm1,
        weight_sum,
        sum_taps,
        sum_conv_bias,
        sum_xproj_t.T,
        sum_dt_weight,
        sum_dt_bias,
        sum_decay,
        sum_skip,
        sum_out_weight,
        sum_norm2,
        sum_router_t.T,
        grad_expert_in[None],
        grad_expert_out[None],
    )


def solution(mesh):
    in_specs = (
        P("wide", None),
        P(),
        P(None, None, "narrow"),
        P(None, "narrow"),
        P("narrow"),
        P("narrow", None),
        P(None, "narrow"),
        P("narrow"),
        P(None, "narrow"),
        P("narrow"),
        P("narrow", None),
        P(),
        P(),
        P("wide", None, "narrow"),
        P("wide", "narrow", None),
        P(),
        P("wide", None),
        P("wide", None),
    )
    out_specs = (
        P("wide", None),
        P("wide", None),
        P(),
        P(None, None, "narrow"),
        P(None, "narrow"),
        P("narrow"),
        P("narrow", None),
        P(None, "narrow"),
        P("narrow"),
        P(None, "narrow"),
        P("narrow"),
        P("narrow", None),
        P(),
        P(),
        P("wide", None, "narrow"),
        P("wide", "narrow", None),
    )
    return jax.shard_map(local, mesh=mesh, in_specs=in_specs, out_specs=out_specs, check_vma=False)
```

```python
import functools
import math

import jax
import jax.numpy as jnp
from jax import lax
from jax.experimental import pallas as pl
from jax.experimental.pallas import tpu as pltpu
from jax.sharding import PartitionSpec as P

EPSILON = 1e-05
SEGMENTS = 8
LANES = 128
NEVER = 1e30
VMEM_SPARE = 4 * 1024 * 1024
GROUP = 4
LOG2E = 1.4426950408889634


def shape_of(*shape, dtype=jnp.float32):
    return jax.ShapeDtypeStruct(shape, dtype)


def call(kernel, outs, ids, *arrays, scratch=(), after=(), far_in=(), out_place=(), in_place=()):
    in_vmem = pl.BlockSpec(memory_space=pltpu.VMEM)
    anywhere = pl.BlockSpec(memory_space=pl.ANY)
    far = pl.BlockSpec(memory_space=pltpu.HBM)
    arrays = [
        pltpu.with_memory_space_constraint(array, pltpu.HBM) if i in far_in else array
        for i, array in enumerate(arrays)
    ]
    size = lambda a: math.prod(a.shape) * jnp.dtype(a.dtype).itemsize
    held = [
        size(a)
        for refs, skipped in ((arrays, (*in_place, *far_in)), (outs, out_place))
        for i, a in enumerate(refs)
        if i not in skipped
    ]
    held += [size(a) for a in scratch if hasattr(a, "dtype") and hasattr(a, "shape")
             and jnp.issubdtype(a.dtype, jnp.number)]
    given = 1 + len(arrays)

    def run(*refs):
        kernel(*refs[:given], *refs[given + len(after) :])

    return pl.pallas_call(
        run,
        out_shape=outs,
        in_specs=[pl.BlockSpec(memory_space=pltpu.SMEM)]
        + [far if i in far_in else anywhere if i in in_place else in_vmem
           for i in range(len(arrays))]
        + [anywhere] * len(after),
        out_specs=[anywhere if i in out_place else in_vmem for i in range(len(outs))],
        scratch_shapes=scratch,
        compiler_params=pltpu.CompilerParams(vmem_limit_bytes=sum(held) + VMEM_SPARE),
        cost_estimate=pl.CostEstimate(flops=1, bytes_accessed=1, transcendentals=0),
    )(ids, *arrays, *after)


def two_parts(value):
    high = value.astype(jnp.bfloat16)
    return high, (value - high.astype(jnp.float32)).astype(jnp.bfloat16)


def once(left, right, contract=(1, 0)):
    return lax.dot_general(
        left,
        right,
        (((contract[0],), (contract[1],)), ((), ())),
        preferred_element_type=jnp.float32,
    )


def product(left, right, contract=(1, 0)):
    left_high, left_low = left if isinstance(left, tuple) else two_parts(left)
    right_high, right_low = right if isinstance(right, tuple) else two_parts(right)
    free = 1 - contract[0]
    size = left_high.shape[free]
    if size % (16, LANES)[free]:
        return once(left_high, right_high, contract) + (
            once(left_high, right_low, contract) + once(left_low, right_high, contract)
        )
    both = once(jnp.concatenate([left_high, left_low], axis=free), right_high, contract)
    return both[:size] + (both[size:] + once(left_high, right_low, contract))


def select_rows(chosen, rows, contract=(1, 0)):
    high, low = two_parts(rows)
    return once(chosen, high, contract) + once(chosen, low, contract)


def inverse_rms(rows):
    return lax.rsqrt(jnp.mean(rows * rows, axis=-1, keepdims=True) + EPSILON)


def norm_back(rows, inverse, gain, grad):
    scaled = gain * grad
    mean = jnp.mean(rows * scaled, axis=-1, keepdims=True)
    return inverse * scaled - rows * (inverse * inverse * inverse) * mean


def sigmoid(value):
    return 1.0 / (1.0 + jnp.exp(-value))


def softplus(value):
    return jnp.maximum(value, 0.0) + jnp.log1p(jnp.exp(-jnp.abs(value)))


def gelu_parts(value):
    spread_of = 0.5 * (1.0 + lax.erf(value * (0.5**0.5)))
    density = jnp.exp(-0.5 * value * value) * ((2.0 * jnp.pi) ** -0.5)
    return value * spread_of, spread_of + value * density


def cut_slices(me, whole, out):
    rows, part = whole.shape[0] // 2, whole.shape[1] // 4
    for j in range(4):
        out[me ^ j, :, :part] = whole[:rows, part * j : part * (j + 1)]
        out[me ^ j, :, part:] = whole[rows:, part * j : part * (j + 1)]


def join_slices(me, parts, held, whole):
    rows, part = whole.shape[0] // 2, whole.shape[1] // 4
    for key, value in enumerate(parts):
        held[key] = value[...]
    for j in range(4):
        value = held[me ^ j]
        whole[:rows, part * j : part * (j + 1)] = value[:, :part]
        whole[rows:, part * j : part * (j + 1)] = value[:, part:]


def reversed_bits(value, levels):
    place = 0
    for level in range(levels):
        place = place + (((value >> level) & 1) << (levels - 1 - level))
    return place


def interleave_from(rows, held, out):
    length, width = out.shape
    steps = length // SEGMENTS
    for tile in range(width // LANES):
        lanes = slice(tile * LANES, (tile + 1) * LANES)
        held[tile] = rows[:, lanes]
        for step in range(steps):
            out[step * SEGMENTS : (step + 1) * SEGMENTS, lanes] = held[
                tile, pl.ds(step, SEGMENTS, stride=steps), :
            ]


def deinterleave_to(rows, held, out):
    length, width = out.shape
    steps = length // SEGMENTS
    for tile in range(width // LANES):
        lanes = slice(tile * LANES, (tile + 1) * LANES)
        for step in range(steps):
            held[tile, pl.ds(step, SEGMENTS, stride=steps), :] = rows[
                step * SEGMENTS : (step + 1) * SEGMENTS, lanes
            ]
        out[:, lanes] = held[tile]


def narrow_swap(value, key):
    return lax.ppermute(value, "narrow", [(i, i ^ key) for i in range(4)])


def core_swap(value):
    count = lax.axis_size("wide")
    return lax.ppermute(value, "wide", [(i, i ^ 1) for i in range(count)])


def chip_swap(value, key):
    count = lax.axis_size("wide")
    return lax.ppermute(value, "wide", [(i, i ^ (2 * key)) for i in range(count)])


def wide_shift(value, distance):
    devices = range(lax.axis_size("wide"))
    route = [(i - distance, i) for i in devices if i - distance in devices]
    return lax.ppermute(value, "wide", route)


def hold(value, *others):
    if not others:
        return value
    return lax.optimization_barrier((value, others))[0]


def narrow_all(value):
    far = narrow_swap(value, 3)
    return [value, narrow_swap(value, 1), narrow_swap(value, 2), far]


def narrow_each(slices):
    far = narrow_swap(slices[3], 3)
    return [slices[0], narrow_swap(slices[1], 1), narrow_swap(slices[2], 2), far]


def pair_sum(parts):
    while len(parts) > 1:
        parts = [a + b for a, b in zip(parts[::2], parts[1::2])]
    return parts[0]


def chip_blocks(blocks, chips):
    rows = blocks.shape[0] // chips
    order = sorted(range(1, chips), reverse=True)
    arrived = {k: chip_swap(blocks[k * rows : (k + 1) * rows], k) for k in order}
    arrived[0] = blocks[:rows]
    return [arrived[k] for k in range(chips)]


def chip_each(blocks, chips):
    return jnp.concatenate(chip_blocks(blocks, chips))


def chip_all(value, chips):
    arrived = {k: chip_swap(value, k) for k in sorted(range(1, chips), reverse=True)}
    arrived[0] = value
    return [arrived[k] for k in range(chips)]


class WideSum:
    def __init__(self, keep, send):
        levels = lax.axis_size("wide").bit_length() - 1
        self.swaps = [core_swap] + [
            functools.partial(chip_swap, key=1 << level) for level in range(levels - 1)
        ]
        self.keep, self.send, self.arrived = keep, send, None
        self.level, self.back = 0, False

    def prepare(self):
        if not self.back and self.level == len(self.swaps):
            self.back = True
        if self.back:
            self.level -= 1
            self.send = self.keep
        return self.send

    def start(self, *others):
        self.prepare()
        self.arrived = self.swaps[self.level](hold(self.send, *others))
        return self.arrived

    def start_with(self, rider):
        sent = self.prepare()
        joined = jnp.concatenate([sent.reshape(1, -1, sent.shape[2]), rider], axis=1)
        arrived = self.swaps[self.level](joined)
        rows = rider.shape[1]
        self.arrived = arrived[:, :-rows].reshape(sent.shape)
        return self.arrived, arrived[:, -rows:]

    def finish(self, *others):
        arrived = hold(self.arrived, *others) if others else self.arrived
        if self.back:
            self.keep = jnp.concatenate([self.keep, arrived])
            return
        self.level += 1
        if self.level == len(self.swaps):
            self.keep = self.keep + arrived
            return
        half = self.keep.shape[0] // 2
        self.send = self.keep[half:] + arrived[half:]
        self.keep = self.keep[:half] + arrived[:half]

    def rest(self):
        while not (self.back and self.level == 0):
            self.start()
            self.finish()
        return self.keep


def start_both(one, two, *others):
    first, second = one.prepare(), two.prepare()
    rows = first.shape[1]
    arrived = one.swaps[one.level](hold(jnp.concatenate([first, second], axis=1), *others))
    one.arrived, two.arrived = arrived[:, :rows], arrived[:, rows:]
    return one.arrived, two.arrived


def route_kernel(capacity, ids, segments, expert_ids, marks, slots_own, slots_other,
                 rows_own, rows_other):
    wide_at, core, chip = ids[1], ids[2], ids[3]
    length = expert_ids.shape[1]
    per = length // LANES
    experts = segments.shape[0] // per
    steps = length // SEGMENTS

    def block(at):
        return jnp.concatenate([segments[pl.ds(at * per + i, 1), :] for i in range(per)], axis=1)

    own, before = block(wide_at), block(jnp.maximum(wide_at - 1, 0))
    lane = lax.broadcasted_iota(jnp.int32, (1, length), 1)
    here = lax.broadcasted_iota(jnp.int32, (SEGMENTS, length), 0)
    table = jnp.ones((SEGMENTS, length), jnp.float32)
    for k in range(1, 4):
        back = jnp.where(lane < k, pltpu.roll(before, k, 1), pltpu.roll(own, k, 1))
        same = (back == own) & ((lane >= k) | (wide_at > 0))
        table = jnp.where(here == k, jnp.where(same, 1.0, 0.0), table)
    live = own >= 0
    expert = expert_ids[...]
    at = lax.broadcasted_iota(jnp.int32, (experts, length), 0)
    hits = jnp.where((at == expert) & live, 1.0, 0.0)
    first = lax.broadcasted_iota(jnp.int32, (length, length), 0)
    second = lax.broadcasted_iota(jnp.int32, (length, length), 1)
    earlier = jnp.where(first < second, 1.0, 0.0).astype(jnp.bfloat16)
    ranks = once(hits.astype(jnp.bfloat16), earlier)
    rank = jnp.sum(ranks * hits, axis=0, keepdims=True).astype(jnp.int32)
    kept = live & (rank < capacity)
    order = jnp.where(
        (first % SEGMENTS) * steps + first // SEGMENTS == second, 1.0, 0.0
    ).astype(jnp.bfloat16)
    marks[...] = once(order, table.astype(jnp.bfloat16), (1, 1))
    slot = jnp.where(kept, ((expert >> 1) ^ chip) * capacity + rank, -1)
    count = slots_own.shape[0]
    slot_at = lax.broadcasted_iota(jnp.int32, (count, length), 0)
    for which, slots, rows in ((core, slots_own, rows_own), (1 - core, slots_other, rows_other)):
        mine = (slot_at == slot) & ((expert & 1) == which)
        chosen = jnp.where(mine, 1.0, 0.0).astype(jnp.bfloat16)
        slots[...] = once(chosen, order, (1, 1)).astype(jnp.bfloat16)
        rows[...] = once(order, chosen, (1, 1)).astype(jnp.bfloat16)


def front_kernel(ids, tokens, gain, conv_high, conv_low, gate_high, gate_low,
                 rows, normed, conv_in, gate_in, held):
    interleave_from(tokens, held, rows)
    value = rows[...]
    scaled = value * inverse_rms(value) * gain[...][None]
    normed[...] = scaled
    parts = two_parts(scaled)
    conv_in[...] = product(parts, (conv_high[...], conv_low[...]))
    gate_in[...] = product(parts, (gate_high[...], gate_low[...]))


def start_kernel(capacity, ids, segments_far, expert_ids_far, tokens_far, cotangent_far, weight_far,
                 marks, slots_own, slots_other, rows_own, rows_other,
                 rows_slice, cot_slice, own, other, conv_high, conv_low, gate_high, gate_low,
                 segments, expert_ids, tokens, cotangent, weight, rows, held, branch,
                 sems):
    pairs = (
        (segments_far, segments),
        (expert_ids_far, expert_ids),
        (tokens_far, tokens),
        (cotangent_far, cotangent),
        (weight_far, weight),
    )
    copies = [
        pltpu.make_async_copy(far, near, sems.at[i]) for i, (far, near) in enumerate(pairs)
    ]
    for copy in copies:
        copy.start()
    copies[0].wait()
    copies[1].wait()
    route_kernel(capacity, ids, segments, expert_ids, marks, slots_own, slots_other,
                 rows_own, rows_other)
    copies[2].wait()
    copies[3].wait()
    slices_kernel(ids, tokens, cotangent, slots_own, slots_other, rows_slice, cot_slice, own, other,
                  rows, held)
    copies[4].wait()
    for k, (high, low) in enumerate(((conv_high, conv_low), (gate_high, gate_low))):
        branch[k] = weight[:, k, :]
        high[...], low[...] = two_parts(branch[k])


def slices_kernel(ids, tokens, cotangent, slots_own, slots_other,
                  rows_slice, cot_slice, own, other, rows, held):
    me, core = ids[0], ids[2]
    half, part = tokens.shape[0] // 2, tokens.shape[1] // 4
    for source, out in ((tokens, rows_slice), (cotangent, cot_slice)):
        interleave_from(source, held, rows)
        for j in range(4):
            @pl.when(me == j)
            def _():
                out[:, :part] = rows[:half, part * j : part * (j + 1)]
                out[:, part:] = rows[half:, part * j : part * (j + 1)]
    send_slots(core, cot_slice[...], slots_own[...], slots_other[...], own, other)


def send_slots(core, packed, slots_own, slots_other, own, other):
    half = packed.shape[1] // 2
    lane = lax.broadcasted_iota(jnp.int32, packed.shape, 1)
    left = jnp.where(lane < half, packed, 0.0)
    right = jnp.where(lane < half, 0.0, packed)
    second = core == 1
    top = jnp.where(second, pltpu.roll(left, half, 1), left)
    bottom = jnp.where(second, right, pltpu.roll(right, half, 1))
    placed = jnp.concatenate([top, bottom])
    own[...] = select_rows(slots_own, placed)
    other[...] = select_rows(slots_other, placed)


def conv_kernel(ids, halo, gain, conv_high, conv_low, conv_in, marks, conv_weight, conv_bias,
                xproj_t, mixed, conv_out, partial, extended, halo_normed):
    taps, channels = conv_weight.shape
    length = conv_in.shape[0]
    lead = (taps - 1) * SEGMENTS
    rows = halo[...]
    scaled = rows * inverse_rms(rows) * gain[...][None]
    halo_normed[...] = scaled
    halo_conv = product(scaled, (conv_high[...], conv_low[...]))
    place = lax.broadcasted_iota(jnp.int32, (SEGMENTS, channels), 0)
    for m in range(taps - 1):
        ends = conv_in[length - lead + m * SEGMENTS : length - lead + (m + 1) * SEGMENTS, :]
        at = SEGMENTS - taps + 1 + m
        extended[m * SEGMENTS : (m + 1) * SEGMENTS, :] = jnp.where(
            place == 0, halo_conv[at : at + 1, :], pltpu.roll(ends, 1, 0)
        )
    extended[lead:, :] = conv_in[...]
    total = jnp.broadcast_to(conv_bias[...][None], (length, channels))
    for k in range(taps):
        first = (taps - 1 - k) * SEGMENTS
        total += conv_weight[k : k + 1, :] * extended[first : first + length, :] * marks[:, k : k + 1]
    mixed[...] = total
    out = total * sigmoid(total)
    conv_out[...] = out
    partial[...] = product(xproj_t[...], out, (1, 1))


def rows_at(step):
    return pl.ds(pl.multiple_of(step * SEGMENTS, SEGMENTS), SEGMENTS)


def spread(row):
    return jnp.broadcast_to(row, (SEGMENTS, row.shape[-1]))


def column_of(rows, column):
    return jnp.broadcast_to(rows[:, column : column + 1], (SEGMENTS, LANES))


def sweep(count, body, carry):
    return lax.fori_loop(0, count, body, carry, unroll=True)


def add_to(ref, first, rows, lanes, value):
    if first:
        ref[rows, lanes] = value
    else:
        ref[rows, lanes] += value


def chain_pieces(decay, value, backward):
    place = lax.broadcasted_iota(jnp.int32, decay.shape, 0)
    if backward:
        place = SEGMENTS - 1 - place

    def moved(array, distance):
        return pltpu.roll(array, (SEGMENTS - distance) if backward else distance, 0)

    distance = 1
    while distance < SEGMENTS:
        inside = place >= distance
        value = jnp.where(inside, decay * moved(value, distance) + value, value)
        decay = jnp.where(inside, decay * moved(decay, distance), decay)
        distance *= 2
    first = place == 0
    before = jnp.where(first, 0.0, moved(value, 1))
    factor = jnp.where(first, 1.0, moved(decay, 1))
    return factor, before, value


def totals_kernel(ids, p0, p1, p2, p3, dt_weight, dt_bias, decay_log, conv_out, marks,
                  coef, dt_pre, stepsize, drive, stepd, rates, entry, total, padded):
    states, channels = decay_log.shape
    rank = dt_weight.shape[0]
    length = conv_out.shape[0]
    steps = length // SEGMENTS
    projected = (p0[...] + p1[...]) + (p2[...] + p3[...])
    missing = LANES - projected.shape[0]
    coef[...] = jnp.concatenate([projected, jnp.zeros((missing, length), jnp.float32)]).T
    padded[...] = jnp.zeros_like(padded)
    padded[:rank, :] = dt_weight[...]
    pre = product(coef[...], padded[...]) + dt_bias[...][None]
    dt_pre[...] = pre
    size = softplus(pre)
    stepsize[...] = size
    drive[...] = size * conv_out[...]
    stepd[...] = jnp.where(marks[:, 1:2] > 0.5, size, NEVER)
    rates[...] = -jnp.exp(decay_log[...])
    total[...] = jnp.zeros_like(total)
    zero = jnp.zeros((SEGMENTS, LANES), jnp.float32)
    tiles = [slice(at, at + LANES) for at in range(0, channels, LANES)]
    sums = [zero] * len(tiles)
    for step in range(steps):
        rows = slice(step * SEGMENTS, (step + 1) * SEGMENTS)
        sums = [value + stepd[rows, lanes] for value, lanes in zip(sums, tiles)]
    for value, lanes in zip(sums, tiles):
        total[states : states + 1, lanes] = jnp.sum(value, axis=0, keepdims=True)
    for group in range(0, states, GROUP):
        names = range(group, group + GROUP)
        rate = [[spread(rates[n : n + 1, lanes] * LOG2E) for lanes in tiles] for n in names]

        def body(step, current):
            rows = rows_at(step)
            near = coef[rows, :]
            width = [stepd[rows, lanes] for lanes in tiles]
            push = [drive[rows, lanes] for lanes in tiles]
            later = []
            for at, n in enumerate(names):
                entering = column_of(near, rank + n)
                later.append(tuple(
                    jnp.exp2(width[t] * rate[at][t]) * current[at][t] + push[t] * entering
                    for t in range(len(tiles))
                ))
            return tuple(later)

        current = sweep(steps, body, ((zero,) * len(tiles),) * GROUP)
        for at, n in enumerate(names):
            for t, lanes in enumerate(tiles):
                decay = jnp.exp2(sums[t] * rate[at][t])
                factor, before, last = chain_pieces(decay, current[at][t], False)
                entry[0, n, :, lanes] = factor
                entry[1, n, :, lanes] = before
                total[n : n + 1, lanes] = last[SEGMENTS - 1 :, :]


def pair_kernel(ids, total, other, rates, early, late, chip):
    states = rates.shape[0]
    second = ids[2] == 1
    mine, theirs = total[...], other[...]
    first, last = jnp.where(second, theirs, mine), jnp.where(second, mine, theirs)
    early[...] = first
    late[...] = last
    chip[...] = first + last
    chip[:states, :] = (
        jnp.exp(last[states : states + 1] * rates[...]) * first[:states] + last[:states]
    )


def pair_back_kernel(ids, total, other, early, rates, late_total, chip):
    states = rates.shape[0]
    second = ids[2] == 1
    mine, theirs = total[...], other[...]
    first, last = jnp.where(second, theirs, mine), jnp.where(second, mine, theirs)
    late_total[...] = last
    chip[...] = first + jnp.exp(early[states : states + 1, :] * rates[...]) * last


def states_kernel(rank, ids, stepd, drive, coef, rates, entry, early, conv_out, gate_in, skip,
                  out_weight, *rest):
    chips = len(rest) - 8
    totals = rest[:chips]
    ssm_skip, gated, slices, kept, held, whole, kept_here, sems = rest[chips:]
    me, core, here = ids[0], ids[2], ids[3]
    states, channels = rates.shape
    length = stepd.shape[0]
    steps = length // SEGMENTS
    for key, value in enumerate(totals):
        held[key] = value[...]
    state = jnp.zeros((states, channels), jnp.float32)
    for chip in range(chips):
        value = held[here ^ chip]
        grown = jnp.exp(value[states : states + 1] * rates[...]) * state + value[:states]
        state = jnp.where(chip < here, grown, state)
    inner = jnp.exp(early[states : states + 1, :] * rates[...]) * state + early[:states, :]
    start = jnp.where(core == 1, inner, state)
    tiles = [slice(at, at + LANES) for at in range(0, channels, LANES)]
    copies = []
    for group in range(0, states, GROUP):
        names = range(group, group + GROUP)
        slab = group // GROUP
        rate = [[spread(rates[n : n + 1, lanes] * LOG2E) for lanes in tiles] for n in names]
        current = tuple(
            tuple(
                entry[0, n, :, lanes] * start[n : n + 1, lanes] + entry[1, n, :, lanes]
                for lanes in tiles
            )
            for n in names
        )
        for at in range(GROUP):
            for t, lanes in enumerate(tiles):
                kept_here[slab, 0, at, :, lanes] = current[at][t]

        def body(step, current):
            rows = rows_at(step)
            near = coef[rows, :]
            width = [stepd[rows, lanes] for lanes in tiles]
            push = [drive[rows, lanes] for lanes in tiles]
            later, total = [], [None] * len(tiles)
            for at, n in enumerate(names):
                entering, leaving = column_of(near, rank + n), column_of(near, rank + states + n)
                new = []
                for t, lanes in enumerate(tiles):
                    decay = jnp.exp2(width[t] * rate[at][t])
                    new.append(decay * current[at][t] + push[t] * entering)
                    kept_here[slab, step + 1, at, :, lanes] = new[t]
                    term = leaving * new[t]
                    total[t] = term if total[t] is None else total[t] + term
                later.append(tuple(new))
            for t, lanes in enumerate(tiles):
                add_to(ssm_skip, group == 0, rows, lanes, total[t])
            return tuple(later)

        sweep(steps, body, current)
        copies.append(pltpu.make_async_copy(kept_here.at[slab], kept.at[slab], sems.at[slab]))
        copies[-1].start()
    skipped = ssm_skip[...] + skip[...][None] * conv_out[...]
    ssm_skip[...] = skipped
    gate = gate_in[...]
    out = skipped * gate * sigmoid(gate)
    gated[...] = out
    whole[...] = product(out, out_weight[...])
    cut_slices(me, whole, slices)
    for copy in copies:
        copy.wait()


def dispatch_kernel(ids, s0, s1, s2, s3, rows_slice, slots_own, slots_other,
                    hidden, own, other):
    packed = (s0[...] + s1[...]) + (s2[...] + s3[...]) + rows_slice[...]
    hidden[...] = packed
    send_slots(ids[2], packed, slots_own[...], slots_other[...], own, other)


def raw_kernel(ids, c0, c1, c2, c3, expert_in, expert_out, raw, cot, in_high, in_low,
               out_high, out_low, held):
    join_slices(ids[0], (c0, c1, c2, c3), held, cot)
    in_high[...], in_low[...] = two_parts(expert_in[...])
    out_high[...], out_low[...] = two_parts(expert_out[...])
    raw[...] = product(cot[...], (out_high[...], out_low[...]), (1, 1))


def expert_kernel(ids, parts, raw, in_high, in_low, norm_gain, router_t,
                  slices, second, act, grad_pre, gates, grad_logits, grad_gain,
                  whole):
    me, expert = ids[0], ids[1]
    count, part = whole.shape[0] // 2, whole.shape[1] // 4
    for j in range(4):
        whole[:count, part * j : part * (j + 1)] = parts[j, :, :part]
        whole[count:, part * j : part * (j + 1)] = parts[j, :, part:]
    rows = whole[...]
    inverse = inverse_rms(rows)
    normed = rows * inverse * norm_gain[...][None]
    second[...] = normed
    normed_parts = two_parts(normed)
    router_parts = two_parts(router_t[...])
    weight = (in_high[...], in_low[...])
    logits = product(normed_parts, router_parts, (1, 1))
    logits = logits - jnp.max(logits, axis=-1, keepdims=True)
    powers = jnp.exp(logits)
    probs = powers / jnp.sum(powers, axis=-1, keepdims=True)
    chosen = jnp.where(
        lax.broadcasted_iota(jnp.int32, logits.shape, 1) == expert, 1.0, 0.0
    )
    gate = jnp.sum(probs * chosen, axis=-1, keepdims=True)
    gates[...] = gate
    hidden_act, slope = gelu_parts(product(normed_parts, weight))
    act[...] = hidden_act
    raws = raw[...]
    grad_gate = jnp.sum(hidden_act * raws, axis=-1, keepdims=True)
    grads = gate * raws * slope
    grad_pre[...] = grads
    logit_grads = grad_gate * gate * (chosen - probs)
    grad_logits[...] = logit_grads
    grad_second = product(grads, weight, (1, 1)) + product(logit_grads, router_parts)
    grad_gain[...] = jnp.sum(rows * inverse * grad_second, axis=0, keepdims=True)
    whole[...] = norm_back(rows, inverse, norm_gain[...][None], grad_second)
    cut_slices(me, whole, slices)


def expert_rest_kernel(ids, second, act, grad_pre, gates, grad_logits, cot, out_high, out_low,
                       slices, grad_in, grad_out, grad_router, whole):
    gate = gates[...]
    acts = two_parts(act[...])
    normed = two_parts(second[...])
    whole[...] = gate * product(acts, (out_high[...], out_low[...]))
    cut_slices(ids[0], whole, slices)
    grad_out[...] = product(acts, gate * cot[...], (0, 0))
    grad_in[...] = product(normed, grad_pre[...], (0, 0))
    grad_router[...] = product(grad_logits[...], normed, (0, 0))


def home_kernel(ids, own, other, base, rows_own, rows_other, out):
    half = own.shape[1] // 2
    second = ids[2] == 1

    def mine(rows):
        return jnp.where(second, pltpu.roll(rows, half, 1), rows)

    total = select_rows(rows_own[...], mine(own[...])) + select_rows(
        rows_other[...], mine(other[...])
    )
    count = base.shape[0]
    lane = lax.broadcasted_iota(jnp.int32, base.shape, 1)
    out[...] = base[...] + jnp.where(
        lane < half, total[:count], pltpu.roll(total[count:], half, 1)
    )


def whole_kernel(ids, p0, p1, p2, p3, out, held, whole, tiles):
    join_slices(ids[0], (p0, p1, p2, p3), held, whole)
    deinterleave_to(whole, tiles, out)


def leaving_kernel(rank, ids, g0, g1, g2, g3, out_weight, gate_in, ssm_skip, conv_out, stepd,
                   coef, rates, grad_hidden, grad_ssm, grad_gate_in, grad_skip, entry, total,
                   held):
    join_slices(ids[0], (g0, g1, g2, g3), held, grad_hidden)
    states, channels = rates.shape
    length = stepd.shape[0]
    steps = length // SEGMENTS
    grad_gated = product(grad_hidden[...], out_weight[...], (1, 1))
    gate = gate_in[...]
    gate_sigmoid = sigmoid(gate)
    pulled = grad_gated * gate * gate_sigmoid
    grad_ssm[...] = pulled
    grad_gate_in[...] = grad_gated * ssm_skip[...] * (
        gate_sigmoid * (1.0 + gate * (1.0 - gate_sigmoid))
    )
    grad_skip[...] = jnp.sum(pulled * conv_out[...], axis=0, keepdims=True)
    zero = jnp.zeros((SEGMENTS, LANES), jnp.float32)
    tiles = [slice(at, at + LANES) for at in range(0, channels, LANES)]
    sums = [zero] * len(tiles)
    for step in range(steps):
        rows = slice(step * SEGMENTS, (step + 1) * SEGMENTS)
        sums = [value + stepd[rows, lanes] for value, lanes in zip(sums, tiles)]
    for group in range(0, states, GROUP):
        names = range(group, group + GROUP)
        rate = [[spread(rates[n : n + 1, lanes] * LOG2E) for lanes in tiles] for n in names]

        def body(back, current):
            rows = rows_at(steps - 1 - back)
            near = coef[rows, :]
            width = [stepd[rows, lanes] for lanes in tiles]
            pull = [grad_ssm[rows, lanes] for lanes in tiles]
            later = []
            for at, n in enumerate(names):
                leaving = column_of(near, rank + states + n)
                later.append(tuple(
                    jnp.exp2(width[t] * rate[at][t]) * (current[at][t] + pull[t] * leaving)
                    for t in range(len(tiles))
                ))
            return tuple(later)

        current = sweep(steps, body, ((zero,) * len(tiles),) * GROUP)
        for at, n in enumerate(names):
            for t, lanes in enumerate(tiles):
                decay = jnp.exp2(sums[t] * rate[at][t])
                factor, before, last = chain_pieces(decay, current[at][t], True)
                entry[0, n, :, lanes] = factor
                entry[1, n, :, lanes] = before
                total[n : n + 1, lanes] = last[:1, :]


def adjoint_kernel(rank, chips, ids, stepd, drive, grad, coef, rates, entry, kept, early, late,
                   late_total, conv_out, stepsize, dt_pre, skip, dt_weight, grad_norm2, grad_router,
                   *rest):
    sums, totals = rest[:chips], rest[chips : 2 * chips]
    (partial, grad_direct, grad_dt_pre, grad_decay, grad_dt_bias, held_sums, held, kept_here,
     in_terms, out_terms, grad_push, grad_width, sems) = rest[2 * chips :]
    core, here = ids[2], ids[3]
    states, channels = rates.shape
    length = stepd.shape[0]
    steps = length // SEGMENTS
    copies = [
        pltpu.make_async_copy(kept.at[slab], kept_here.at[slab], sems.at[slab])
        for slab in range(states // GROUP)
    ]
    for copy in copies:
        copy.start()
    for key in range(chips):
        held_sums[key] = sums[key][states : states + 1, :]
        held[key] = totals[key][...]
    state = jnp.zeros((states, channels), jnp.float32)
    for chip in reversed(range(chips)):
        grown = held[here ^ chip] + jnp.exp(held_sums[here ^ chip] * rates[...]) * state
        state = jnp.where(chip > here, grown, state)
    inner = late_total[...] + jnp.exp(late[states : states + 1, :] * rates[...]) * state
    final = jnp.where(core == 1, state, inner)
    zero = jnp.zeros((SEGMENTS, LANES), jnp.float32)
    tiles = [slice(at, at + LANES) for at in range(0, channels, LANES)]
    for group in range(0, states, GROUP):
        names = range(group, group + GROUP)
        slab = group // GROUP
        rate = [[spread(rates[n : n + 1, lanes]) for lanes in tiles] for n in names]
        current = tuple(
            tuple(
                entry[0, n, :, lanes] * final[n : n + 1, lanes] + entry[1, n, :, lanes]
                for lanes in tiles
            )
            for n in names
        )
        copies[slab].wait()

        def body(back, carry):
            current, slopes = carry
            step = steps - 1 - back
            rows = rows_at(step)
            near = coef[rows, :]
            width = [stepd[rows, lanes] for lanes in tiles]
            push = [drive[rows, lanes] for lanes in tiles]
            pull = [grad[rows, lanes] for lanes in tiles]
            later, slope = [], []
            total, width_total = [None] * len(tiles), [None] * len(tiles)
            for at, n in enumerate(names):
                entering, leaving = column_of(near, rank + n), column_of(near, rank + states + n)
                new, turned, in_term, out_term = [], [], None, None
                for t, lanes in enumerate(tiles):
                    adjoint = leaving * pull[t] + current[at][t]
                    decayed = jnp.exp2(width[t] * (rate[at][t] * LOG2E)) * adjoint
                    through = decayed * kept_here[slab, step, at, :, lanes]
                    term, rated = adjoint * entering, through * rate[at][t]
                    total[t] = term if total[t] is None else total[t] + term
                    width_total[t] = rated if width_total[t] is None else width_total[t] + rated
                    new.append(decayed)
                    turned.append(slopes[at][t] + through * width[t])
                    term = adjoint * push[t]
                    in_term = term if in_term is None else in_term + term
                    term = kept_here[slab, step + 1, at, :, lanes] * pull[t]
                    out_term = term if out_term is None else out_term + term
                place = slice(n * LANES, (n + 1) * LANES)
                in_terms[rows, place] = in_term
                out_terms[rows, place] = out_term
                later.append(tuple(new))
                slope.append(tuple(turned))
            for t, lanes in enumerate(tiles):
                add_to(grad_push, group == 0, rows, lanes, total[t])
                add_to(grad_width, group == 0, rows, lanes, width_total[t])
            return tuple(later), tuple(slope)

        none = ((zero,) * len(tiles),) * GROUP
        _, slopes = sweep(steps, body, (current, none))
        for at, n in enumerate(names):
            for t, lanes in enumerate(tiles):
                grad_decay[n : n + 1, lanes] = rates[n : n + 1, lanes] * jnp.sum(
                    slopes[at][t], axis=0, keepdims=True
                )
    pushed = grad_push[...]
    grads = (pushed * conv_out[...] + grad_width[...]) * sigmoid(dt_pre[...])
    grad_dt_pre[...] = grads
    grad_dt_bias[...] = jnp.sum(grads, axis=0, keepdims=True)
    grad_direct[...] = pushed * stepsize[...] + skip[...][None] * grad[...]
    partial[:rank, :] = product(dt_weight[...], grads, (1, 1))
    shape = (2 * states, states * LANES)
    column = lax.broadcasted_iota(jnp.int32, shape, 0)
    owner = lax.broadcasted_iota(jnp.int32, shape, 1) // LANES
    total = None
    for terms, base in ((in_terms, 0), (out_terms, states)):
        ones = jnp.where(owner + base == column, 1.0, 0.0).astype(jnp.bfloat16)
        for part in two_parts(terms[...]):
            term = once(ones, part, (1, 1))
            total = term if total is None else total + term
    cols = rank + 2 * states
    partial[rank:cols, :] = total
    row = cols
    for shared in (grad_norm2, grad_router):
        for at in range(0, shared.shape[1], length):
            partial[row : row + shared.shape[0], :] = shared[:, at : at + length]
            row += shared.shape[0]
    partial[row:, :] = jnp.zeros((partial.shape[0] - row, length), jnp.float32)


def conv_back_kernel(experts, ids, p0, p1, p2, p3, xproj_t, grad_direct, mixed, conv_out, extended,
                     marks, conv_weight, coef, grad_dt_pre, grad_decay, grad_dt_bias, grad_skip,
                     normed, halo_normed, keep, send, grad_conv, grad_halo,
                     small, grad_extended, summed, weights):
    taps, channels = conv_weight.shape
    cols, states = xproj_t.shape[0], grad_decay.shape[0]
    rank = cols - 2 * states
    length = mixed.shape[0]
    lead = (taps - 1) * SEGMENTS
    summed[...] = (p0[...] + p1[...]) + (p2[...] + p3[...])
    projected = two_parts(summed[:cols, :])
    grad_out = grad_direct[...] + product(projected, xproj_t[...], (0, 0))
    value = mixed[...]
    value_sigmoid = sigmoid(value)
    grad_mixed = grad_out * (value_sigmoid * (1.0 + value * (1.0 - value_sigmoid)))
    grad_extended[...] = jnp.zeros_like(grad_extended)
    first_tap = cols + rank + states
    small[first_tap:, :] = jnp.zeros((small.shape[0] - first_tap, channels), jnp.float32)
    for k in range(taps):
        first = (taps - 1 - k) * SEGMENTS
        masked = grad_mixed * marks[:, k : k + 1]
        small[first_tap + k : first_tap + k + 1, :] = jnp.sum(
            masked * extended[first : first + length, :], axis=0, keepdims=True
        )
        grad_extended[first : first + length, :] += conv_weight[k : k + 1, :] * masked
    grad_conv[...] = grad_extended[lead:, :]
    grad_halo[...] = jnp.zeros_like(grad_halo)
    place = lax.broadcasted_iota(jnp.int32, (SEGMENTS, channels), 0)
    for m in range(taps - 1):
        rows = grad_extended[m * SEGMENTS : (m + 1) * SEGMENTS, :]
        at = SEGMENTS - taps + 1 + m
        grad_halo[at : at + 1, :] = rows[:1, :]
        inside = jnp.where(place == SEGMENTS - 1, 0.0, pltpu.roll(rows, SEGMENTS - 1, 0))
        ends = slice(length - lead + m * SEGMENTS, length - lead + (m + 1) * SEGMENTS)
        grad_conv[ends, :] += inside
    small[:cols, :] = product(projected, conv_out[...])
    low = product(coef[...], grad_dt_pre[...], (0, 0))
    small[cols : cols + rank, :] = low[:rank, :]
    small[cols + rank : first_tap, :] = grad_decay[...]
    last = first_tap + taps
    small[last : last + 1, :] = jnp.sum(grad_mixed, axis=0, keepdims=True)
    small[last + 1 : last + 2, :] = grad_dt_bias[...]
    small[last + 2 : last + 3, :] = grad_skip[...]
    first, row = last + 3, cols
    for count in (1, experts):
        for at in range(0, 2 * channels, length):
            value = summed[row : row + count, :]
            end = at + length
            for piece in range(at // channels, -(-end // channels)):
                low, high = max(at, piece * channels), min(end, (piece + 1) * channels)
                target = first + piece * count
                small[target : target + count, low - piece * channels : high - piece * channels] = (
                    value[:, low - at : high - at]
                )
            row += count
        first += 2 * count
    weights[...] = product(normed[...], grad_conv[...], (0, 0)) + product(
        halo_normed[...], grad_halo[...], (0, 0)
    )
    in_order(ids[1], (weights, small), keep, send)


def tokens_kernel(ids, grad_conv, grad_halo, conv_high, conv_low, gate_part, rows, halo_rows,
                  slices, whole):
    weight = conv_high[...], conv_low[...]
    length = grad_conv.shape[0]
    grad = product(grad_conv[...], weight, (1, 1)) + gate_part[...]
    before = product(grad_halo[...], weight, (1, 1))
    value, value_before = rows[...], halo_rows[...]
    whole[:length, :] = grad
    whole[length:, :] = jnp.zeros((whole.shape[0] - length, whole.shape[1]), jnp.float32)
    whole[length : length + SEGMENTS, :] = before
    whole[length : length + 1, :] = jnp.sum(
        value * inverse_rms(value) * grad, axis=0, keepdims=True
    ) + jnp.sum(value_before * inverse_rms(value_before) * before, axis=0, keepdims=True)
    cut_slices(ids[0], whole, slices)


def early_weights_kernel(ids, gated, grad_hidden, normed, grad_gate_in, keep, send, whole,
                         gate):
    channels = gated.shape[1]
    halves = product(gated[...], grad_hidden[...], (0, 0))
    whole[:channels, :] = halves[:, :channels]
    whole[channels:, :] = halves[:, channels:]
    gate[...] = product(normed[...], grad_gate_in[...], (0, 0))
    in_order(ids[1], (whole, gate), keep, send)


def in_order(me, wholes, keep, send):
    count = 2 * keep.shape[0]
    levels = count.bit_length() - 1
    for place in range(count):
        block = reversed_bits(place, levels) ^ me
        out, at = (keep, place) if place < count // 2 else (send, place - count // 2)
        first = 0
        for whole in wholes:
            rows = whole.shape[0] // count
            from_row = pl.multiple_of(block * rows, 8)
            out[at, first : first + rows, :] = whole[pl.ds(from_row, rows), :]
            first += rows


def gate_tokens_kernel(ids, grad_gate_in, gate_high, gate_low, out):
    out[...] = product(grad_gate_in[...], (gate_high[...], gate_low[...]), (1, 1))


def extra_kernel(ids, p0, p1, p2, p3, extra, norm1, held, whole):
    join_slices(ids[0], (p0, p1, p2, p3), held, whole)
    row = whole.shape[0] - 2 * SEGMENTS
    channels = norm1.shape[2]
    extra[...] = whole[row : row + SEGMENTS, :]
    norm1[...] = jnp.zeros_like(norm1)
    for piece in range(whole.shape[1] // channels):
        lanes = slice(piece * channels, (piece + 1) * channels)
        norm1[0, piece : piece + 1, :] = whole[row : row + 1, lanes]


def grad_tokens_kernel(taps, ids, p0, p1, p2, p3, from_next, rows, gain, grad_hidden, out,
                       held, whole, tiles):
    join_slices(ids[0], (p0, p1, p2, p3), held, whole)
    length = rows.shape[0]
    lead = (taps - 1) * SEGMENTS
    for m in range(taps - 1):
        row = length - lead + (m + 1) * SEGMENTS - 1
        at = SEGMENTS - taps + 1 + m
        whole[row : row + 1, :] += from_next[at : at + 1, :]
    value = rows[...]
    whole[:length, :] = (
        norm_back(value, inverse_rms(value), gain[...][None], whole[:length, :]) + grad_hidden[...]
    )
    deinterleave_to(whole, tiles, out)


def early_out_kernel(ids, summed, out_weight):
    count, rows, channels = summed.shape
    levels = count.bit_length() - 1
    for block in range(count):
        value = summed[reversed_bits(block ^ ids[1], levels)]
        half, row = divmod(block * rows, channels)
        out_weight[row : row + rows, half * channels : (half + 1) * channels] = value


def weights_out_kernel(counts, ids, early, late, norm1, weight, *rest):
    *outs, sum_norm1, small = rest
    count, rows = early.shape[0], early.shape[1]
    more = late.shape[1] - rows
    levels = count.bit_length() - 1
    for block in range(count):
        place = reversed_bits(block ^ ids[1], levels)
        small[block * more : (block + 1) * more, :] = late[place, rows:, :]
        weight[block * rows : (block + 1) * rows, 0, :] = late[place, :rows, :]
        weight[block * rows : (block + 1) * rows, 1, :] = early[place]
    first = 0
    channels = small.shape[1]
    for out, used in zip(outs, counts):
        per = out.shape[-1] // channels
        each = used // per
        for piece in range(per):
            lanes = slice(piece * channels, (piece + 1) * channels)
            if len(out.shape) == 1:
                out[lanes] = small[first, :]
            else:
                out[:, lanes] = small[first : first + each, :]
            first += each
    for piece in range(sum_norm1.shape[0] // channels):
        sum_norm1[piece * channels : (piece + 1) * channels] = norm1[0, piece, :]


def local(
    tokens, norm1_gain, in_weight, conv_weight, conv_bias, xproj_weight, dt_weight, dt_bias,
    decay_log, skip_gain, out_weight, norm2_gain, router_weight, expert_in, expert_out,
    segments, expert_ids, cotangent,
):
    length, width = tokens.shape
    taps, channels = conv_weight.shape
    experts = router_weight.shape[1]
    wide = experts
    capacity = 5 * length // (4 * experts)
    states, rank = decay_log.shape[0], dt_weight.shape[0]
    chips = wide // 2
    slots = chips * capacity
    steps = length // SEGMENTS
    me_wide = lax.axis_index("wide")
    ids = jnp.stack([lax.axis_index("narrow"), me_wide, me_wide & 1, me_wide // 2]).astype(jnp.int32)
    half, double = length // 2, width // 2
    bf16 = jnp.bfloat16
    rows_shape, channel_rows = shape_of(length, width), shape_of(length, channels)
    packed, packed_slots = shape_of(half, double), shape_of(slots, double)
    vmem = lambda *shape: pltpu.VMEM(shape, jnp.float32)
    xproj_t, router_t = xproj_weight.T, router_weight.T
    cols = xproj_t.shape[0]

    tiled = vmem(width // LANES, length, LANES)

    halo_rows = wide_shift(tokens[length - SEGMENTS :], 1)

    (marks, slots_own, slots_other, rows_own, rows_other, rows_slice, cot_slice, cot_own,
     cot_other, conv_high, conv_low, gate_high, gate_low) = call(
        functools.partial(start_kernel, capacity),
        [shape_of(length, SEGMENTS)]
        + [shape_of(slots, length, dtype=bf16)] * 2
        + [shape_of(length, slots, dtype=bf16)] * 2
        + [packed, packed, packed_slots, packed_slots]
        + [shape_of(width, channels, dtype=bf16)] * 4,
        ids, segments.reshape(-1, LANES), expert_ids.reshape(1, length), tokens, cotangent,
        in_weight,
        scratch=[pltpu.VMEM((segments.shape[0] // LANES, LANES), jnp.int32),
                 pltpu.VMEM((1, length), jnp.int32)] + [vmem(length, width)] * 2
        + [vmem(width, 2, channels), vmem(length, width), tiled, vmem(2, width, channels),
           pltpu.SemaphoreType.DMA((5,))],
        far_in=[0, 1, 2, 3, 4],
    )
    cot_pair = cot_own + core_swap(cot_other)
    rows, normed, conv_in, gate_in = call(
        front_kernel,
        [rows_shape, rows_shape, channel_rows, channel_rows],
        ids, tokens, norm1_gain, conv_high, conv_low, gate_high, gate_low,
        scratch=[tiled],
    )
    mixed, conv_out, partial, extended, halo_normed = call(
        conv_kernel,
        [channel_rows, channel_rows, shape_of(cols, length),
         shape_of(length + (taps - 1) * SEGMENTS, channels), shape_of(SEGMENTS, width)],
        ids, halo_rows, norm1_gain, conv_high, conv_low, conv_in, marks, conv_weight,
        conv_bias, xproj_t, after=[cot_pair],
    )
    partials = narrow_all(partial)

    partials = narrow_all(partial)

    cot_blocks = chip_each(hold(cot_pair, partial), chips)

    entry_shape = shape_of(2, states, SEGMENTS, channels)
    total_rows = -(-(states + 1) // 8) * 8
    coef, dt_pre, stepsize, drive, stepd, rates, entry, total = call(
        totals_kernel,
        [shape_of(length, LANES)] + [channel_rows] * 4
        + [shape_of(states, channels), entry_shape, shape_of(total_rows, channels)],
        ids, *partials, dt_weight, dt_bias, decay_log, conv_out, marks,
        scratch=[vmem(LANES, channels)],
    )
    total_shape = shape_of(total_rows, channels)
    early, late, chip_total = call(
        pair_kernel, [total_shape] * 3, ids, total, core_swap(total), rates, after=[cot_blocks]
    )
    chip_totals = chip_all(chip_total, chips)
    slabs = states // GROUP
    cot_held = hold(cot_blocks, chip_total)
    cot_one, cot_two = narrow_swap(cot_held, 1), narrow_swap(cot_held, 2)
    kept_shape = (slabs, steps + 1, GROUP, SEGMENTS, channels)
    ssm_skip, gated, mixer_slices, kept = call(
        functools.partial(states_kernel, rank),
        [channel_rows, channel_rows, shape_of(4, half, double), shape_of(*kept_shape)],
        ids, stepd, drive, coef, rates, entry, early, conv_out, gate_in, skip_gain,
        out_weight, *chip_totals,
        scratch=[vmem(chips, total_rows, channels), vmem(length, width), vmem(*kept_shape),
                 pltpu.SemaphoreType.DMA((slabs,))],
        out_place=[3],
    )
    mixer_slices = hold(mixer_slices, cot_one, cot_two)
    expert_rows, square = shape_of(2 * slots, width), (expert_in.shape[1], expert_in.shape[2])
    hidden_units = square[1]
    hidden_slice, hidden_own, hidden_other = call(
        dispatch_kernel,
        [packed, packed_slots, packed_slots],
        ids, *narrow_each(mixer_slices), rows_slice, slots_own, slots_other,
    )
    hidden_blocks = chip_each(hidden_own + core_swap(hidden_other), chips)
    upper, lower = hold(cot_one[: slots // 2], hidden_own), hold(cot_two[slots // 2 :], hidden_own)
    cot_three = jnp.concatenate([narrow_swap(upper, 2), narrow_swap(lower, 1)])
    raw, cot, in_high, in_low, out_high, out_low = call(
        raw_kernel,
        [shape_of(2 * slots, hidden_units), expert_rows]
        + [shape_of(*square, dtype=bf16)] * 2
        + [shape_of(square[1], square[0], dtype=bf16)] * 2,
        ids, cot_blocks, cot_one, cot_two, cot_three, expert_in[0], expert_out[0],
        scratch=[vmem(4, slots, double)],
    )
    hidden_parts = lax.all_gather(hold(hidden_blocks, raw), "narrow")
    slices_shape = shape_of(4, slots, double)
    grad_slices, second, act, grad_pre, gates, grad_logits, grad_norm2 = call(
        expert_kernel,
        [slices_shape, expert_rows] + [shape_of(2 * slots, hidden_units)] * 2
        + [shape_of(2 * slots, 1), shape_of(2 * slots, experts), shape_of(1, width)],
        ids, hidden_parts, raw, in_high, in_low, norm2_gain, router_t,
        scratch=[vmem(2 * slots, width)],
    )
    grad_mine = pair_sum(narrow_each(grad_slices))
    value_slices, grad_expert_in, grad_expert_out, grad_router_t = call(
        expert_rest_kernel,
        [slices_shape, shape_of(*square), shape_of(square[1], square[0]),
         shape_of(experts, width)],
        ids, second, act, grad_pre, gates, grad_logits, cot, out_high, out_low,
        scratch=[vmem(2 * slots, width)],
    )
    grad_back = chip_each(grad_mine, chips)
    value_mine = pair_sum(narrow_each(value_slices))
    grad_slice = call(
        home_kernel, [packed], ids, grad_back, core_swap(grad_back), cot_slice, rows_own,
        rows_other, after=[value_mine],
    )[0]
    grad_parts = narrow_all(grad_slice)
    value_back = chip_each(value_mine, chips)

    def whole_of(parts, after=()):
        return call(
            whole_kernel, [rows_shape], ids, *parts, after=after,
            scratch=[vmem(4, half, double), vmem(length, width), tiled],
        )[0]

    grad_hidden, grad_ssm, grad_gate_in, grad_skip, back_entry, back_total = call(
        functools.partial(leaving_kernel, rank),
        [rows_shape, channel_rows, channel_rows, shape_of(1, channels), entry_shape,
         shape_of(states, channels)],
        ids, *grad_parts, out_weight, gate_in, ssm_skip, conv_out, stepd, coef, rates,
        scratch=[vmem(4, half, double)], after=[value_back],
    )
    other_back = core_swap(back_total)
    block = width // wide
    half_blocks = shape_of(wide // 2, 2 * block, channels)
    early_keep, early_send = call(
        early_weights_kernel,
        [half_blocks, half_blocks],
        ids, gated, grad_hidden, normed, grad_gate_in,
        scratch=[vmem(width, channels)] * 2,
    )
    back_late, back_chip = call(
        pair_back_kernel, [shape_of(states, channels)] * 2,
        ids, back_total, other_back, early, rates, after=[early_keep],
    )
    back_totals = chip_all(back_chip, chips)
    early_arrived = core_swap(hold(early_send, back_chip))
    out_sum, gate_sum = (
        WideSum(early_keep[:, rows], early_send[:, rows])
        for rows in (slice(0, block), slice(block, None))
    )
    out_sum.arrived, gate_sum.arrived = early_arrived[:, :block], early_arrived[:, block:]
    out_sum.finish()
    gate_sum.finish()
    first_step = out_sum.start(*back_totals)

    shared_rows = (experts + 1) * (width // length)
    partial_rows = cols + shared_rows + -(cols + shared_rows) % 8
    partial_back, grad_direct, grad_dt_pre, grad_decay, grad_dt_bias = call(
        functools.partial(adjoint_kernel, rank, chips),
        [shape_of(partial_rows, length), channel_rows, channel_rows, shape_of(states, channels),
         shape_of(1, channels)],
        ids, stepd, drive, grad_ssm, coef, rates, back_entry, kept, early, late, back_late,
        conv_out, stepsize, dt_pre, skip_gain, dt_weight, grad_norm2, grad_router_t,
        *chip_totals, *back_totals,
        scratch=[vmem(chips, 1, channels), vmem(chips, states, channels), vmem(*kept_shape),
                 vmem(length, states * LANES), vmem(length, states * LANES),
                 vmem(length, channels), vmem(length, channels),
                 pltpu.SemaphoreType.DMA((slabs,))],
        in_place=[6], after=[out_sum.send, gate_sum.send],
    )
    partials_back = narrow_all(partial_back)
    gate_part = call(
        gate_tokens_kernel, [rows_shape], ids, grad_gate_in, gate_high, gate_low,
        after=[partial_back],
    )[0]
    out_sum.finish(partial_back)
    out_sum.start()
    gate_sum.start(partial_back)
    grain = 8 * wide
    small_rows = cols + rank + states + taps + 3 + (experts + 1) * (width // channels)
    small_rows += -small_rows % grain
    more = small_rows // wide
    half_blocks = shape_of(wide // 2, block + more, channels)
    token_rows = length + 2 * SEGMENTS
    conv_keep, conv_send, grad_conv, grad_halo = call(
        functools.partial(conv_back_kernel, experts),
        [half_blocks, half_blocks, channel_rows, shape_of(SEGMENTS, channels)],
        ids, *partials_back, xproj_t, grad_direct, mixed, conv_out, extended, marks,
        conv_weight, coef, grad_dt_pre, grad_decay, grad_dt_bias, grad_skip,
        normed, halo_normed,
        scratch=[vmem(small_rows, channels),
                 vmem(length + (taps - 1) * SEGMENTS, channels), vmem(partial_rows, length),
                 vmem(width, channels)],
        after=[gate_sum.arrived, out_sum.arrived],
    )
    (token_slices,) = call(
        tokens_kernel, [shape_of(4, token_rows // 2, double)],
        ids, grad_conv, grad_halo, conv_high, conv_low, gate_part, rows, halo_rows,
        scratch=[vmem(token_rows, width)],
    )
    out_sum.finish()
    gate_sum.finish()
    conv_sum = WideSum(conv_keep, conv_send)
    conv_sum.start()
    conv_sum.finish()
    (output_slice,) = call(
        home_kernel, [packed], ids, value_back, core_swap(hold(value_back, conv_keep)),
        hidden_slice, rows_own, rows_other,
    )
    levels = len(conv_sum.swaps)

    def extra_of(parts):
        return call(
            extra_kernel,
            [shape_of(SEGMENTS, width), shape_of(1, SEGMENTS, channels)],
            ids, *parts,
            scratch=[vmem(4, token_rows // 2, double), vmem(token_rows, width)],
        )

    def grad_tokens_of(parts, from_next):
        return call(
            functools.partial(grad_tokens_kernel, taps),
            [rows_shape], ids, *parts, from_next, rows, norm1_gain, grad_hidden,
            scratch=[vmem(4, token_rows // 2, double), vmem(token_rows, width), tiled],
        )[0]

    def out_weight_of(total, *others):
        return call(
            early_out_kernel, [shape_of(channels, width)], ids, total, after=others
        )[0]

    if levels == 3:
        sums = conv_sum, gate_sum, out_sum
        joint = [conv_sum.start(), *start_both(gate_sum, out_sum)]
        token_each = narrow_each(token_slices)
        for part in sums:
            part.finish(*joint, *token_each, output_slice)
        joint = [*start_both(conv_sum, gate_sum), out_sum.start()]
        token_parts = narrow_all(pair_sum(token_each))
        extra, norm1 = extra_of(token_parts)
        from_next = wide_shift(extra, -1)
        for part in sums:
            part.finish(*joint, norm1, from_next)
        arrived, norm1_other = conv_sum.start_with(norm1)
        joint = [arrived, gate_sum.start()]
        output_parts = narrow_all(hold(output_slice, norm1))
        for part in sums[:2]:
            part.finish(*joint, *output_parts)
        norm1 = norm1 + norm1_other
        arrived, norm1_other = conv_sum.start_with(norm1)
        grad_tokens = grad_tokens_of(token_parts, from_next)
        joint = [arrived, *start_both(gate_sum, out_sum, grad_tokens)]
        output = whole_of(output_parts, after=[conv_sum.send])
        for part in sums:
            part.finish(*joint, output, grad_tokens)
        norm1 = norm1 + norm1_other
        arrived, norm1_other = conv_sum.start_with(norm1)
        sum_out_weight = out_weight_of(out_sum.keep, conv_sum.send)
        conv_sum.finish(sum_out_weight)
        norm1 = norm1 + norm1_other
    else:
        token_parts = narrow_all(pair_sum(narrow_each(token_slices)))
        extra, norm1 = extra_of(token_parts)
        grad_tokens = grad_tokens_of(token_parts, wide_shift(extra, -1))
        output = whole_of(narrow_all(output_slice))
        sum_out_weight = out_weight_of(out_sum.rest())
        norm1 = norm1 + core_swap(norm1)
        norm1 = pair_sum(chip_all(norm1, chips))
    per = width // channels
    counts = (cols, rank, states, taps, 1, 1, 1, per, per * experts)
    (weight_sum, sum_xproj_t, sum_dt_weight, sum_decay, sum_taps, sum_conv_bias, sum_dt_bias,
     sum_skip, sum_norm2, sum_router_t, sum_norm1) = call(
        functools.partial(weights_out_kernel, counts),
        [shape_of(width, 2, channels)]
        + [shape_of(rows, channels) for rows in (cols, rank, states, taps)]
        + [shape_of(channels)] * 3
        + [shape_of(width), shape_of(experts, width), shape_of(width)],
        ids, gate_sum.rest(), conv_sum.rest(), norm1, scratch=[vmem(small_rows, channels)],
    )
    return (
        output,
        grad_tokens,
        sum_norm1,
        weight_sum,
        sum_taps,
        sum_conv_bias,
        sum_xproj_t.T,
        sum_dt_weight,
        sum_dt_bias,
        sum_decay,
        sum_skip,
        sum_out_weight,
        sum_norm2,
        sum_router_t.T,
        grad_expert_in[None],
        grad_expert_out[None],
    )


def solution(mesh):
    in_specs = (
        P("wide", None),
        P(),
        P(None, None, "narrow"),
        P(None, "narrow"),
        P("narrow"),
        P("narrow", None),
        P(None, "narrow"),
        P("narrow"),
        P(None, "narrow"),
        P("narrow"),
        P("narrow", None),
        P(),
        P(),
        P("wide", None, "narrow"),
        P("wide", "narrow", None),
        P(),
        P("wide", None),
        P("wide", None),
    )
    out_specs = (
        P("wide", None),
        P("wide", None),
        P(),
        P(None, None, "narrow"),
        P(None, "narrow"),
        P("narrow"),
        P("narrow", None),
        P(None, "narrow"),
        P("narrow"),
        P(None, "narrow"),
        P("narrow"),
        P("narrow", None),
        P(),
        P(),
        P("wide", None, "narrow"),
        P("wide", "narrow", None),
    )
    return jax.shard_map(local, mesh=mesh, in_specs=in_specs, out_specs=out_specs, check_vma=False)
```

```python
import functools
import math

import jax
import jax.numpy as jnp
from jax import lax
from jax.experimental import pallas as pl
from jax.experimental.pallas import tpu as pltpu
from jax.sharding import PartitionSpec as P

EPSILON = 1e-05
SEGMENTS = 8
LANES = 128
NEVER = 1e30
VMEM_SPARE = 4 * 1024 * 1024
GROUP = 4
LOG2E = 1.4426950408889634


def shape_of(*shape, dtype=jnp.float32):
    return jax.ShapeDtypeStruct(shape, dtype)


def call(kernel, outs, ids, *arrays, scratch=(), after=(), far_in=(), out_place=(), in_place=()):
    in_vmem = pl.BlockSpec(memory_space=pltpu.VMEM)
    anywhere = pl.BlockSpec(memory_space=pl.ANY)
    far = pl.BlockSpec(memory_space=pltpu.HBM)
    arrays = [
        pltpu.with_memory_space_constraint(array, pltpu.HBM) if i in far_in else array
        for i, array in enumerate(arrays)
    ]
    size = lambda a: math.prod(a.shape) * jnp.dtype(a.dtype).itemsize
    held = [
        size(a)
        for refs, skipped in ((arrays, (*in_place, *far_in)), (outs, out_place))
        for i, a in enumerate(refs)
        if i not in skipped
    ]
    held += [size(a) for a in scratch if hasattr(a, "dtype") and hasattr(a, "shape")
             and jnp.issubdtype(a.dtype, jnp.number)]
    given = 1 + len(arrays)

    def run(*refs):
        kernel(*refs[:given], *refs[given + len(after) :])

    return pl.pallas_call(
        run,
        out_shape=outs,
        in_specs=[pl.BlockSpec(memory_space=pltpu.SMEM)]
        + [far if i in far_in else anywhere if i in in_place else in_vmem
           for i in range(len(arrays))]
        + [anywhere] * len(after),
        out_specs=[anywhere if i in out_place else in_vmem for i in range(len(outs))],
        scratch_shapes=scratch,
        compiler_params=pltpu.CompilerParams(vmem_limit_bytes=sum(held) + VMEM_SPARE),
        cost_estimate=pl.CostEstimate(flops=1, bytes_accessed=1, transcendentals=0),
    )(ids, *arrays, *after)


def two_parts(value):
    high = value.astype(jnp.bfloat16)
    return high, (value - high.astype(jnp.float32)).astype(jnp.bfloat16)


def once(left, right, contract=(1, 0)):
    return lax.dot_general(
        left,
        right,
        (((contract[0],), (contract[1],)), ((), ())),
        preferred_element_type=jnp.float32,
    )


def product(left, right, contract=(1, 0)):
    left_high, left_low = left if isinstance(left, tuple) else two_parts(left)
    right_high, right_low = right if isinstance(right, tuple) else two_parts(right)
    free = 1 - contract[0]
    size = left_high.shape[free]
    if size % (16, LANES)[free]:
        return once(left_high, right_high, contract) + (
            once(left_high, right_low, contract) + once(left_low, right_high, contract)
        )
    both = once(jnp.concatenate([left_high, left_low], axis=free), right_high, contract)
    return both[:size] + (both[size:] + once(left_high, right_low, contract))


def select_rows(chosen, rows, contract=(1, 0)):
    high, low = two_parts(rows)
    return once(chosen, high, contract) + once(chosen, low, contract)


def inverse_rms(rows):
    return lax.rsqrt(jnp.mean(rows * rows, axis=-1, keepdims=True) + EPSILON)


def norm_back(rows, inverse, gain, grad):
    scaled = gain * grad
    mean = jnp.mean(rows * scaled, axis=-1, keepdims=True)
    return inverse * scaled - rows * (inverse * inverse * inverse) * mean


def sigmoid(value):
    return 1.0 / (1.0 + jnp.exp(-value))


def softplus(value):
    return jnp.maximum(value, 0.0) + jnp.log1p(jnp.exp(-jnp.abs(value)))


def gelu_parts(value):
    spread_of = 0.5 * (1.0 + lax.erf(value * (0.5**0.5)))
    density = jnp.exp(-0.5 * value * value) * ((2.0 * jnp.pi) ** -0.5)
    return value * spread_of, spread_of + value * density


def cut_slices(me, whole, out):
    rows, part = whole.shape[0] // 2, whole.shape[1] // 4
    for j in range(4):
        out[me ^ j, :, :part] = whole[:rows, part * j : part * (j + 1)]
        out[me ^ j, :, part:] = whole[rows:, part * j : part * (j + 1)]


def join_slices(me, parts, held, whole):
    rows, part = whole.shape[0] // 2, whole.shape[1] // 4
    for key, value in enumerate(parts):
        held[key] = value[...]
    for j in range(4):
        value = held[me ^ j]
        whole[:rows, part * j : part * (j + 1)] = value[:, :part]
        whole[rows:, part * j : part * (j + 1)] = value[:, part:]


def reversed_bits(value, levels):
    place = 0
    for level in range(levels):
        place = place + (((value >> level) & 1) << (levels - 1 - level))
    return place


def interleave_from(rows, held, out):
    length, width = out.shape
    steps = length // SEGMENTS
    for tile in range(width // LANES):
        lanes = slice(tile * LANES, (tile + 1) * LANES)
        held[tile] = rows[:, lanes]
        for step in range(steps):
            out[step * SEGMENTS : (step + 1) * SEGMENTS, lanes] = held[
                tile, pl.ds(step, SEGMENTS, stride=steps), :
            ]


def deinterleave_to(rows, held, out):
    length, width = out.shape
    steps = length // SEGMENTS
    for tile in range(width // LANES):
        lanes = slice(tile * LANES, (tile + 1) * LANES)
        for step in range(steps):
            held[tile, pl.ds(step, SEGMENTS, stride=steps), :] = rows[
                step * SEGMENTS : (step + 1) * SEGMENTS, lanes
            ]
        out[:, lanes] = held[tile]


def narrow_swap(value, key):
    return lax.ppermute(value, "narrow", [(i, i ^ key) for i in range(4)])


def core_swap(value):
    count = lax.axis_size("wide")
    return lax.ppermute(value, "wide", [(i, i ^ 1) for i in range(count)])


def chip_swap(value, key):
    count = lax.axis_size("wide")
    return lax.ppermute(value, "wide", [(i, i ^ (2 * key)) for i in range(count)])


def wide_shift(value, distance):
    devices = range(lax.axis_size("wide"))
    route = [(i - distance, i) for i in devices if i - distance in devices]
    return lax.ppermute(value, "wide", route)


def hold(value, *others):
    if not others:
        return value
    return lax.optimization_barrier((value, others))[0]


def narrow_all(value):
    far = narrow_swap(value, 3)
    return [value, narrow_swap(value, 1), narrow_swap(value, 2), far]


def narrow_each(slices):
    far = narrow_swap(slices[3], 3)
    return [slices[0], narrow_swap(slices[1], 1), narrow_swap(slices[2], 2), far]


def pair_sum(parts):
    while len(parts) > 1:
        parts = [a + b for a, b in zip(parts[::2], parts[1::2])]
    return parts[0]


def chip_blocks(blocks, chips):
    rows = blocks.shape[0] // chips
    order = sorted(range(1, chips), reverse=True)
    arrived = {k: chip_swap(blocks[k * rows : (k + 1) * rows], k) for k in order}
    arrived[0] = blocks[:rows]
    return [arrived[k] for k in range(chips)]


def chip_each(blocks, chips):
    return jnp.concatenate(chip_blocks(blocks, chips))


def chip_all(value, chips):
    arrived = {k: chip_swap(value, k) for k in sorted(range(1, chips), reverse=True)}
    arrived[0] = value
    return [arrived[k] for k in range(chips)]


class WideSum:
    def __init__(self, keep, send):
        levels = lax.axis_size("wide").bit_length() - 1
        self.swaps = [core_swap] + [
            functools.partial(chip_swap, key=1 << level) for level in range(levels - 1)
        ]
        self.keep, self.send, self.arrived = keep, send, None
        self.level, self.back = 0, False

    def prepare(self):
        if not self.back and self.level == len(self.swaps):
            self.back = True
        if self.back:
            self.level -= 1
            self.send = self.keep
        return self.send

    def start(self, *others):
        self.prepare()
        self.arrived = self.swaps[self.level](hold(self.send, *others))
        return self.arrived

    def start_with(self, rider):
        sent = self.prepare()
        joined = jnp.concatenate([sent.reshape(1, -1, sent.shape[2]), rider], axis=1)
        arrived = self.swaps[self.level](joined)
        rows = rider.shape[1]
        self.arrived = arrived[:, :-rows].reshape(sent.shape)
        return self.arrived, arrived[:, -rows:]

    def finish(self, *others):
        arrived = hold(self.arrived, *others) if others else self.arrived
        if self.back:
            self.keep = jnp.concatenate([self.keep, arrived])
            return
        self.level += 1
        if self.level == len(self.swaps):
            self.keep = self.keep + arrived
            return
        half = self.keep.shape[0] // 2
        self.send = self.keep[half:] + arrived[half:]
        self.keep = self.keep[:half] + arrived[:half]

    def rest(self):
        while not (self.back and self.level == 0):
            self.start()
            self.finish()
        return self.keep


def start_both(one, two, *others):
    first, second = one.prepare(), two.prepare()
    rows = first.shape[1]
    arrived = one.swaps[one.level](hold(jnp.concatenate([first, second], axis=1), *others))
    one.arrived, two.arrived = arrived[:, :rows], arrived[:, rows:]
    return one.arrived, two.arrived


def route_kernel(capacity, ids, segments, expert_ids, marks, slots_own, slots_other,
                 rows_own, rows_other):
    wide_at, core, chip = ids[1], ids[2], ids[3]
    length = expert_ids.shape[1]
    per = length // LANES
    experts = segments.shape[0] // per
    steps = length // SEGMENTS

    def block(at):
        return jnp.concatenate([segments[pl.ds(at * per + i, 1), :] for i in range(per)], axis=1)

    own, before = block(wide_at), block(jnp.maximum(wide_at - 1, 0))
    lane = lax.broadcasted_iota(jnp.int32, (1, length), 1)
    here = lax.broadcasted_iota(jnp.int32, (SEGMENTS, length), 0)
    table = jnp.ones((SEGMENTS, length), jnp.float32)
    for k in range(1, 4):
        back = jnp.where(lane < k, pltpu.roll(before, k, 1), pltpu.roll(own, k, 1))
        same = (back == own) & ((lane >= k) | (wide_at > 0))
        table = jnp.where(here == k, jnp.where(same, 1.0, 0.0), table)
    live = own >= 0
    expert = expert_ids[...]
    at = lax.broadcasted_iota(jnp.int32, (experts, length), 0)
    hits = jnp.where((at == expert) & live, 1.0, 0.0)
    first = lax.broadcasted_iota(jnp.int32, (length, length), 0)
    second = lax.broadcasted_iota(jnp.int32, (length, length), 1)
    earlier = jnp.where(first < second, 1.0, 0.0).astype(jnp.bfloat16)
    ranks = once(hits.astype(jnp.bfloat16), earlier)
    rank = jnp.sum(ranks * hits, axis=0, keepdims=True).astype(jnp.int32)
    kept = live & (rank < capacity)
    order = jnp.where(
        (first % SEGMENTS) * steps + first // SEGMENTS == second, 1.0, 0.0
    ).astype(jnp.bfloat16)
    marks[...] = once(order, table.astype(jnp.bfloat16), (1, 1))
    slot = jnp.where(kept, ((expert >> 1) ^ chip) * capacity + rank, -1)
    count = slots_own.shape[0]
    slot_at = lax.broadcasted_iota(jnp.int32, (count, length), 0)
    for which, slots, rows in ((core, slots_own, rows_own), (1 - core, slots_other, rows_other)):
        mine = (slot_at == slot) & ((expert & 1) == which)
        chosen = jnp.where(mine, 1.0, 0.0).astype(jnp.bfloat16)
        slots[...] = once(chosen, order, (1, 1)).astype(jnp.bfloat16)
        rows[...] = once(order, chosen, (1, 1)).astype(jnp.bfloat16)


def front_kernel(ids, tokens, gain, conv_high, conv_low, gate_high, gate_low,
                 rows, normed, conv_in, gate_in, held):
    interleave_from(tokens, held, rows)
    value = rows[...]
    scaled = value * inverse_rms(value) * gain[...][None]
    normed[...] = scaled
    parts = two_parts(scaled)
    conv_in[...] = product(parts, (conv_high[...], conv_low[...]))
    gate_in[...] = product(parts, (gate_high[...], gate_low[...]))


def start_kernel(capacity, ids, segments_far, expert_ids_far, cotangent_far, weight_far,
                 marks, slots_own, slots_other, rows_own, rows_other,
                 cot_slice, own, other, conv_high, conv_low, gate_high, gate_low,
                 segments, expert_ids, cotangent, weight, rows, held, branch,
                 sems):
    pairs = (
        (segments_far, segments),
        (expert_ids_far, expert_ids),
        (cotangent_far, cotangent),
        (weight_far, weight),
    )
    copies = [
        pltpu.make_async_copy(far, near, sems.at[i]) for i, (far, near) in enumerate(pairs)
    ]
    for copy in copies:
        copy.start()
    copies[0].wait()
    copies[1].wait()
    route_kernel(capacity, ids, segments, expert_ids, marks, slots_own, slots_other,
                 rows_own, rows_other)
    copies[2].wait()
    interleave_from(cotangent, held, rows)
    own_slice(ids[0], rows, cot_slice)
    send_slots(ids[2], cot_slice[...], slots_own[...], slots_other[...], own, other)
    copies[3].wait()
    for k, (high, low) in enumerate(((conv_high, conv_low), (gate_high, gate_low))):
        branch[k] = weight[:, k, :]
        high[...], low[...] = two_parts(branch[k])


def own_slice(me, rows, out):
    half, part = rows.shape[0] // 2, rows.shape[1] // 4
    for j in range(4):
        @pl.when(me == j)
        def _():
            out[:, :part] = rows[:half, part * j : part * (j + 1)]
            out[:, part:] = rows[half:, part * j : part * (j + 1)]


def own_slice_kernel(ids, rows, out):
    own_slice(ids[0], rows, out)


def send_slots(core, packed, slots_own, slots_other, own, other):
    half = packed.shape[1] // 2
    rows = jnp.concatenate([packed[:, :half], packed[:, half:]])
    for slots, out in ((slots_own, own), (slots_other, other)):
        sent = select_rows(slots, rows)
        for side in range(2):
            @pl.when(core == side)
            def _():
                out[:, side * half : (side + 1) * half] = sent
                out[:, (1 - side) * half : (2 - side) * half] = jnp.zeros_like(sent)


def conv_kernel(ids, halo, gain, conv_high, conv_low, conv_in, marks, conv_weight, conv_bias,
                xproj_t, mixed, conv_out, partial, extended, halo_normed):
    taps, channels = conv_weight.shape
    length = conv_in.shape[0]
    lead = (taps - 1) * SEGMENTS
    rows = halo[...]
    scaled = rows * inverse_rms(rows) * gain[...][None]
    halo_normed[...] = scaled
    halo_conv = product(scaled, (conv_high[...], conv_low[...]))
    place = lax.broadcasted_iota(jnp.int32, (SEGMENTS, channels), 0)
    for m in range(taps - 1):
        ends = conv_in[length - lead + m * SEGMENTS : length - lead + (m + 1) * SEGMENTS, :]
        at = SEGMENTS - taps + 1 + m
        extended[m * SEGMENTS : (m + 1) * SEGMENTS, :] = jnp.where(
            place == 0, halo_conv[at : at + 1, :], pltpu.roll(ends, 1, 0)
        )
    extended[lead:, :] = conv_in[...]
    total = jnp.broadcast_to(conv_bias[...][None], (length, channels))
    for k in range(taps):
        first = (taps - 1 - k) * SEGMENTS
        total += conv_weight[k : k + 1, :] * extended[first : first + length, :] * marks[:, k : k + 1]
    mixed[...] = total
    out = total * sigmoid(total)
    conv_out[...] = out
    partial[...] = product(xproj_t[...], out, (1, 1))


def rows_at(step):
    return pl.ds(pl.multiple_of(step * SEGMENTS, SEGMENTS), SEGMENTS)


def spread(row):
    return jnp.broadcast_to(row, (SEGMENTS, row.shape[-1]))


def column_of(rows, column):
    return jnp.broadcast_to(rows[:, column : column + 1], (SEGMENTS, LANES))


def sweep(count, body, carry):
    return lax.fori_loop(0, count, body, carry, unroll=True)


def add_to(ref, first, rows, lanes, value):
    if first:
        ref[rows, lanes] = value
    else:
        ref[rows, lanes] += value


def chain_pieces(decay, value, backward):
    place = lax.broadcasted_iota(jnp.int32, decay.shape, 0)
    if backward:
        place = SEGMENTS - 1 - place

    def moved(array, distance):
        return pltpu.roll(array, (SEGMENTS - distance) if backward else distance, 0)

    distance = 1
    while distance < SEGMENTS:
        inside = place >= distance
        value = jnp.where(inside, decay * moved(value, distance) + value, value)
        decay = jnp.where(inside, decay * moved(decay, distance), decay)
        distance *= 2
    first = place == 0
    before = jnp.where(first, 0.0, moved(value, 1))
    factor = jnp.where(first, 1.0, moved(decay, 1))
    return factor, before, value


def totals_kernel(ids, p0, p1, p2, p3, dt_weight, dt_bias, decay_log, conv_out, marks,
                  coef, dt_pre, stepsize, drive, stepd, rates, entry, total, padded):
    states, channels = decay_log.shape
    rank = dt_weight.shape[0]
    length = conv_out.shape[0]
    steps = length // SEGMENTS
    projected = (p0[...] + p1[...]) + (p2[...] + p3[...])
    missing = LANES - projected.shape[0]
    coef[...] = jnp.concatenate([projected, jnp.zeros((missing, length), jnp.float32)]).T
    padded[...] = jnp.zeros_like(padded)
    padded[:rank, :] = dt_weight[...]
    pre = product(coef[...], padded[...]) + dt_bias[...][None]
    dt_pre[...] = pre
    size = softplus(pre)
    stepsize[...] = size
    drive[...] = size * conv_out[...]
    stepd[...] = jnp.where(marks[:, 1:2] > 0.5, size, NEVER)
    rates[...] = -jnp.exp(decay_log[...])
    total[...] = jnp.zeros_like(total)
    zero = jnp.zeros((SEGMENTS, LANES), jnp.float32)
    tiles = [slice(at, at + LANES) for at in range(0, channels, LANES)]
    sums = [zero] * len(tiles)
    for step in range(steps):
        rows = slice(step * SEGMENTS, (step + 1) * SEGMENTS)
        sums = [value + stepd[rows, lanes] for value, lanes in zip(sums, tiles)]
    for value, lanes in zip(sums, tiles):
        total[states : states + 1, lanes] = jnp.sum(value, axis=0, keepdims=True)
    for group in range(0, states, GROUP):
        names = range(group, group + GROUP)
        rate = [[spread(rates[n : n + 1, lanes] * LOG2E) for lanes in tiles] for n in names]

        def body(step, current):
            rows = rows_at(step)
            near = coef[rows, :]
            width = [stepd[rows, lanes] for lanes in tiles]
            push = [drive[rows, lanes] for lanes in tiles]
            later = []
            for at, n in enumerate(names):
                entering = column_of(near, rank + n)
                later.append(tuple(
                    jnp.exp2(width[t] * rate[at][t]) * current[at][t] + push[t] * entering
                    for t in range(len(tiles))
                ))
            return tuple(later)

        current = sweep(steps, body, ((zero,) * len(tiles),) * GROUP)
        for at, n in enumerate(names):
            for t, lanes in enumerate(tiles):
                decay = jnp.exp2(sums[t] * rate[at][t])
                factor, before, last = chain_pieces(decay, current[at][t], False)
                entry[0, n, :, lanes] = factor
                entry[1, n, :, lanes] = before
                total[n : n + 1, lanes] = last[SEGMENTS - 1 :, :]


def pair_kernel(ids, total, other, rates, early, late, chip):
    states = rates.shape[0]
    second = ids[2] == 1
    mine, theirs = total[...], other[...]
    first, last = jnp.where(second, theirs, mine), jnp.where(second, mine, theirs)
    early[...] = first
    late[...] = last
    chip[...] = first + last
    chip[:states, :] = (
        jnp.exp(last[states : states + 1] * rates[...]) * first[:states] + last[:states]
    )


def pair_back_kernel(ids, total, other, early, rates, late_total, chip):
    states = rates.shape[0]
    second = ids[2] == 1
    mine, theirs = total[...], other[...]
    first, last = jnp.where(second, theirs, mine), jnp.where(second, mine, theirs)
    late_total[...] = last
    chip[...] = first + jnp.exp(early[states : states + 1, :] * rates[...]) * last


def states_kernel(rank, ids, stepd, drive, coef, rates, entry, early, conv_out, gate_in, skip,
                  out_weight, *rest):
    chips = len(rest) - 8
    totals = rest[:chips]
    ssm_skip, gated, slices, kept, held, whole, kept_here, sems = rest[chips:]
    me, core, here = ids[0], ids[2], ids[3]
    states, channels = rates.shape
    length = stepd.shape[0]
    steps = length // SEGMENTS
    for key, value in enumerate(totals):
        held[key] = value[...]
    state = jnp.zeros((states, channels), jnp.float32)
    for chip in range(chips):
        value = held[here ^ chip]
        grown = jnp.exp(value[states : states + 1] * rates[...]) * state + value[:states]
        state = jnp.where(chip < here, grown, state)
    inner = jnp.exp(early[states : states + 1, :] * rates[...]) * state + early[:states, :]
    start = jnp.where(core == 1, inner, state)
    tiles = [slice(at, at + LANES) for at in range(0, channels, LANES)]
    copies = []
    for group in range(0, states, GROUP):
        names = range(group, group + GROUP)
        slab = group // GROUP
        rate = [[spread(rates[n : n + 1, lanes] * LOG2E) for lanes in tiles] for n in names]
        current = tuple(
            tuple(
                entry[0, n, :, lanes] * start[n : n + 1, lanes] + entry[1, n, :, lanes]
                for lanes in tiles
            )
            for n in names
        )
        for at in range(GROUP):
            for t, lanes in enumerate(tiles):
                kept_here[slab, 0, at, :, lanes] = current[at][t]

        def body(step, current):
            rows = rows_at(step)
            near = coef[rows, :]
            width = [stepd[rows, lanes] for lanes in tiles]
            push = [drive[rows, lanes] for lanes in tiles]
            later, total = [], [None] * len(tiles)
            for at, n in enumerate(names):
                entering, leaving = column_of(near, rank + n), column_of(near, rank + states + n)
                new = []
                for t, lanes in enumerate(tiles):
                    decay = jnp.exp2(width[t] * rate[at][t])
                    new.append(decay * current[at][t] + push[t] * entering)
                    kept_here[slab, step + 1, at, :, lanes] = new[t]
                    term = leaving * new[t]
                    total[t] = term if total[t] is None else total[t] + term
                later.append(tuple(new))
            for t, lanes in enumerate(tiles):
                add_to(ssm_skip, group == 0, rows, lanes, total[t])
            return tuple(later)

        sweep(steps, body, current)
        copies.append(pltpu.make_async_copy(kept_here.at[slab], kept.at[slab], sems.at[slab]))
        copies[-1].start()
    skipped = ssm_skip[...] + skip[...][None] * conv_out[...]
    ssm_skip[...] = skipped
    gate = gate_in[...]
    out = skipped * gate * sigmoid(gate)
    gated[...] = out
    whole[...] = product(out, out_weight[...])
    cut_slices(me, whole, slices)
    for copy in copies:
        copy.wait()


def dispatch_kernel(ids, s0, s1, s2, s3, rows_slice, slots_own, slots_other,
                    hidden, own, other):
    packed = (s0[...] + s1[...]) + (s2[...] + s3[...]) + rows_slice[...]
    hidden[...] = packed
    send_slots(ids[2], packed, slots_own[...], slots_other[...], own, other)


def raw_kernel(ids, c0, c1, c2, c3, expert_in, expert_out, raw, cot, in_high, in_low,
               out_high, out_low, held):
    join_slices(ids[0], (c0, c1, c2, c3), held, cot)
    in_high[...], in_low[...] = two_parts(expert_in[...])
    out_high[...], out_low[...] = two_parts(expert_out[...])
    raw[...] = product(cot[...], (out_high[...], out_low[...]), (1, 1))


def expert_kernel(ids, parts, raw, in_high, in_low, norm_gain, router_t,
                  slices, second, act, grad_pre, gates, grad_logits, grad_gain,
                  whole):
    me, expert = ids[0], ids[1]
    count, part = whole.shape[0] // 2, whole.shape[1] // 4
    for j in range(4):
        whole[:count, part * j : part * (j + 1)] = parts[j, :, :part]
        whole[count:, part * j : part * (j + 1)] = parts[j, :, part:]
    rows = whole[...]
    inverse = inverse_rms(rows)
    normed = rows * inverse * norm_gain[...][None]
    second[...] = normed
    normed_parts = two_parts(normed)
    router_parts = two_parts(router_t[...])
    weight = (in_high[...], in_low[...])
    logits = product(normed_parts, router_parts, (1, 1))
    logits = logits - jnp.max(logits, axis=-1, keepdims=True)
    powers = jnp.exp(logits)
    probs = powers / jnp.sum(powers, axis=-1, keepdims=True)
    chosen = jnp.where(
        lax.broadcasted_iota(jnp.int32, logits.shape, 1) == expert, 1.0, 0.0
    )
    gate = jnp.sum(probs * chosen, axis=-1, keepdims=True)
    gates[...] = gate
    hidden_act, slope = gelu_parts(product(normed_parts, weight))
    act[...] = hidden_act
    raws = raw[...]
    grad_gate = jnp.sum(hidden_act * raws, axis=-1, keepdims=True)
    grads = gate * raws * slope
    grad_pre[...] = grads
    logit_grads = grad_gate * gate * (chosen - probs)
    grad_logits[...] = logit_grads
    grad_second = product(grads, weight, (1, 1)) + product(logit_grads, router_parts)
    grad_gain[...] = jnp.sum(rows * inverse * grad_second, axis=0, keepdims=True)
    whole[...] = norm_back(rows, inverse, norm_gain[...][None], grad_second)
    cut_slices(me, whole, slices)


def expert_rest_kernel(ids, second, act, grad_pre, gates, grad_logits, cot, out_high, out_low,
                       slices, grad_in, grad_out, grad_router, whole):
    gate = gates[...]
    acts = two_parts(act[...])
    normed = two_parts(second[...])
    whole[...] = gate * product(acts, (out_high[...], out_low[...]))
    cut_slices(ids[0], whole, slices)
    grad_out[...] = product(acts, gate * cot[...], (0, 0))
    grad_in[...] = product(normed, grad_pre[...], (0, 0))
    grad_router[...] = product(grad_logits[...], normed, (0, 0))


def home_kernel(ids, own, other, base, rows_own, rows_other, out):
    half = own.shape[1] // 2
    second = ids[2] == 1

    def mine(rows):
        return jnp.where(second, rows[:, half:], rows[:, :half])

    total = select_rows(rows_own[...], mine(own[...])) + select_rows(
        rows_other[...], mine(other[...])
    )
    count = base.shape[0]
    out[:, :half] = base[:, :half] + total[:count]
    out[:, half:] = base[:, half:] + total[count:]


def whole_kernel(ids, p0, p1, p2, p3, out, held, whole, tiles):
    join_slices(ids[0], (p0, p1, p2, p3), held, whole)
    deinterleave_to(whole, tiles, out)


def leaving_kernel(rank, ids, g0, g1, g2, g3, out_weight, gate_in, ssm_skip, conv_out, stepd,
                   coef, rates, grad_hidden, grad_ssm, grad_gate_in, grad_skip, entry, total,
                   held):
    join_slices(ids[0], (g0, g1, g2, g3), held, grad_hidden)
    states, channels = rates.shape
    length = stepd.shape[0]
    steps = length // SEGMENTS
    grad_gated = product(grad_hidden[...], out_weight[...], (1, 1))
    gate = gate_in[...]
    gate_sigmoid = sigmoid(gate)
    pulled = grad_gated * gate * gate_sigmoid
    grad_ssm[...] = pulled
    grad_gate_in[...] = grad_gated * ssm_skip[...] * (
        gate_sigmoid * (1.0 + gate * (1.0 - gate_sigmoid))
    )
    grad_skip[...] = jnp.sum(pulled * conv_out[...], axis=0, keepdims=True)
    zero = jnp.zeros((SEGMENTS, LANES), jnp.float32)
    tiles = [slice(at, at + LANES) for at in range(0, channels, LANES)]
    sums = [zero] * len(tiles)
    for step in range(steps):
        rows = slice(step * SEGMENTS, (step + 1) * SEGMENTS)
        sums = [value + stepd[rows, lanes] for value, lanes in zip(sums, tiles)]
    for group in range(0, states, GROUP):
        names = range(group, group + GROUP)
        rate = [[spread(rates[n : n + 1, lanes] * LOG2E) for lanes in tiles] for n in names]

        def body(back, current):
            rows = rows_at(steps - 1 - back)
            near = coef[rows, :]
            width = [stepd[rows, lanes] for lanes in tiles]
            pull = [grad_ssm[rows, lanes] for lanes in tiles]
            later = []
            for at, n in enumerate(names):
                leaving = column_of(near, rank + states + n)
                later.append(tuple(
                    jnp.exp2(width[t] * rate[at][t]) * (current[at][t] + pull[t] * leaving)
                    for t in range(len(tiles))
                ))
            return tuple(later)

        current = sweep(steps, body, ((zero,) * len(tiles),) * GROUP)
        for at, n in enumerate(names):
            for t, lanes in enumerate(tiles):
                decay = jnp.exp2(sums[t] * rate[at][t])
                factor, before, last = chain_pieces(decay, current[at][t], True)
                entry[0, n, :, lanes] = factor
                entry[1, n, :, lanes] = before
                total[n : n + 1, lanes] = last[:1, :]


def adjoint_kernel(rank, chips, ids, stepd, drive, grad, coef, rates, entry, kept, early, late,
                   late_total, conv_out, stepsize, dt_pre, skip, dt_weight, grad_norm2, grad_router,
                   *rest):
    sums, totals = rest[:chips], rest[chips : 2 * chips]
    (partial, grad_direct, grad_dt_pre, grad_decay, grad_dt_bias, held_sums, held, kept_here,
     in_terms, out_terms, grad_push, grad_width, sems) = rest[2 * chips :]
    core, here = ids[2], ids[3]
    states, channels = rates.shape
    length = stepd.shape[0]
    steps = length // SEGMENTS
    copies = [
        pltpu.make_async_copy(kept.at[slab], kept_here.at[slab], sems.at[slab])
        for slab in range(states // GROUP)
    ]
    for copy in copies:
        copy.start()
    for key in range(chips):
        held_sums[key] = sums[key][states : states + 1, :]
        held[key] = totals[key][...]
    state = jnp.zeros((states, channels), jnp.float32)
    for chip in reversed(range(chips)):
        grown = held[here ^ chip] + jnp.exp(held_sums[here ^ chip] * rates[...]) * state
        state = jnp.where(chip > here, grown, state)
    inner = late_total[...] + jnp.exp(late[states : states + 1, :] * rates[...]) * state
    final = jnp.where(core == 1, state, inner)
    zero = jnp.zeros((SEGMENTS, LANES), jnp.float32)
    tiles = [slice(at, at + LANES) for at in range(0, channels, LANES)]
    for group in range(0, states, GROUP):
        names = range(group, group + GROUP)
        slab = group // GROUP
        rate = [[spread(rates[n : n + 1, lanes]) for lanes in tiles] for n in names]
        current = tuple(
            tuple(
                entry[0, n, :, lanes] * final[n : n + 1, lanes] + entry[1, n, :, lanes]
                for lanes in tiles
            )
            for n in names
        )
        copies[slab].wait()

        def body(back, carry):
            current, slopes = carry
            step = steps - 1 - back
            rows = rows_at(step)
            near = coef[rows, :]
            width = [stepd[rows, lanes] for lanes in tiles]
            push = [drive[rows, lanes] for lanes in tiles]
            pull = [grad[rows, lanes] for lanes in tiles]
            later, slope = [], []
            total, width_total = [None] * len(tiles), [None] * len(tiles)
            for at, n in enumerate(names):
                entering, leaving = column_of(near, rank + n), column_of(near, rank + states + n)
                new, turned, in_term, out_term = [], [], None, None
                for t, lanes in enumerate(tiles):
                    adjoint = leaving * pull[t] + current[at][t]
                    decayed = jnp.exp2(width[t] * (rate[at][t] * LOG2E)) * adjoint
                    through = decayed * kept_here[slab, step, at, :, lanes]
                    term, rated = adjoint * entering, through * rate[at][t]
                    total[t] = term if total[t] is None else total[t] + term
                    width_total[t] = rated if width_total[t] is None else width_total[t] + rated
                    new.append(decayed)
                    turned.append(slopes[at][t] + through * width[t])
                    term = adjoint * push[t]
                    in_term = term if in_term is None else in_term + term
                    term = kept_here[slab, step + 1, at, :, lanes] * pull[t]
                    out_term = term if out_term is None else out_term + term
                place = slice(n * LANES, (n + 1) * LANES)
                in_terms[rows, place] = in_term
                out_terms[rows, place] = out_term
                later.append(tuple(new))
                slope.append(tuple(turned))
            for t, lanes in enumerate(tiles):
                add_to(grad_push, group == 0, rows, lanes, total[t])
                add_to(grad_width, group == 0, rows, lanes, width_total[t])
            return tuple(later), tuple(slope)

        none = ((zero,) * len(tiles),) * GROUP
        _, slopes = sweep(steps, body, (current, none))
        for at, n in enumerate(names):
            for t, lanes in enumerate(tiles):
                grad_decay[n : n + 1, lanes] = rates[n : n + 1, lanes] * jnp.sum(
                    slopes[at][t], axis=0, keepdims=True
                )
    pushed = grad_push[...]
    grads = (pushed * conv_out[...] + grad_width[...]) * sigmoid(dt_pre[...])
    grad_dt_pre[...] = grads
    grad_dt_bias[...] = jnp.sum(grads, axis=0, keepdims=True)
    grad_direct[...] = pushed * stepsize[...] + skip[...][None] * grad[...]
    partial[:rank, :] = product(dt_weight[...], grads, (1, 1))
    shape = (2 * states, states * LANES)
    column = lax.broadcasted_iota(jnp.int32, shape, 0)
    owner = lax.broadcasted_iota(jnp.int32, shape, 1) // LANES
    total = None
    for terms, base in ((in_terms, 0), (out_terms, states)):
        ones = jnp.where(owner + base == column, 1.0, 0.0).astype(jnp.bfloat16)
        for part in two_parts(terms[...]):
            term = once(ones, part, (1, 1))
            total = term if total is None else total + term
    cols = rank + 2 * states
    partial[rank:cols, :] = total
    row = cols
    for shared in (grad_norm2, grad_router):
        for at in range(0, shared.shape[1], length):
            partial[row : row + shared.shape[0], :] = shared[:, at : at + length]
            row += shared.shape[0]
    partial[row:, :] = jnp.zeros((partial.shape[0] - row, length), jnp.float32)


def conv_back_kernel(experts, ids, p0, p1, p2, p3, xproj_t, grad_direct, mixed, conv_out, extended,
                     marks, conv_weight, coef, grad_dt_pre, grad_decay, grad_dt_bias, grad_skip,
                     normed, halo_normed, keep, send, grad_conv, grad_halo,
                     small, grad_extended, summed, weights):
    taps, channels = conv_weight.shape
    cols, states = xproj_t.shape[0], grad_decay.shape[0]
    rank = cols - 2 * states
    length = mixed.shape[0]
    lead = (taps - 1) * SEGMENTS
    summed[...] = (p0[...] + p1[...]) + (p2[...] + p3[...])
    projected = two_parts(summed[:cols, :])
    grad_out = grad_direct[...] + product(projected, xproj_t[...], (0, 0))
    value = mixed[...]
    value_sigmoid = sigmoid(value)
    grad_mixed = grad_out * (value_sigmoid * (1.0 + value * (1.0 - value_sigmoid)))
    grad_extended[...] = jnp.zeros_like(grad_extended)
    first_tap = cols + rank + states
    small[first_tap:, :] = jnp.zeros((small.shape[0] - first_tap, channels), jnp.float32)
    for k in range(taps):
        first = (taps - 1 - k) * SEGMENTS
        masked = grad_mixed * marks[:, k : k + 1]
        small[first_tap + k : first_tap + k + 1, :] = jnp.sum(
            masked * extended[first : first + length, :], axis=0, keepdims=True
        )
        grad_extended[first : first + length, :] += conv_weight[k : k + 1, :] * masked
    grad_conv[...] = grad_extended[lead:, :]
    grad_halo[...] = jnp.zeros_like(grad_halo)
    place = lax.broadcasted_iota(jnp.int32, (SEGMENTS, channels), 0)
    for m in range(taps - 1):
        rows = grad_extended[m * SEGMENTS : (m + 1) * SEGMENTS, :]
        at = SEGMENTS - taps + 1 + m
        grad_halo[at : at + 1, :] = rows[:1, :]
        inside = jnp.where(place == SEGMENTS - 1, 0.0, pltpu.roll(rows, SEGMENTS - 1, 0))
        ends = slice(length - lead + m * SEGMENTS, length - lead + (m + 1) * SEGMENTS)
        grad_conv[ends, :] += inside
    small[:cols, :] = product(projected, conv_out[...])
    low = product(coef[...], grad_dt_pre[...], (0, 0))
    small[cols : cols + rank, :] = low[:rank, :]
    small[cols + rank : first_tap, :] = grad_decay[...]
    last = first_tap + taps
    small[last : last + 1, :] = jnp.sum(grad_mixed, axis=0, keepdims=True)
    small[last + 1 : last + 2, :] = grad_dt_bias[...]
    small[last + 2 : last + 3, :] = grad_skip[...]
    first, row = last + 3, cols
    for count in (1, experts):
        for at in range(0, 2 * channels, length):
            value = summed[row : row + count, :]
            end = at + length
            for piece in range(at // channels, -(-end // channels)):
                low, high = max(at, piece * channels), min(end, (piece + 1) * channels)
                target = first + piece * count
                small[target : target + count, low - piece * channels : high - piece * channels] = (
                    value[:, low - at : high - at]
                )
            row += count
        first += 2 * count
    weights[...] = product(normed[...], grad_conv[...], (0, 0)) + product(
        halo_normed[...], grad_halo[...], (0, 0)
    )
    in_order(ids[1], (weights, small), keep, send)


def tokens_kernel(ids, grad_conv, grad_halo, conv_high, conv_low, gate_part, rows, halo_rows,
                  slices, whole):
    weight = conv_high[...], conv_low[...]
    length = grad_conv.shape[0]
    grad = product(grad_conv[...], weight, (1, 1)) + gate_part[...]
    before = product(grad_halo[...], weight, (1, 1))
    value, value_before = rows[...], halo_rows[...]
    whole[:length, :] = grad
    whole[length:, :] = jnp.zeros((whole.shape[0] - length, whole.shape[1]), jnp.float32)
    whole[length : length + SEGMENTS, :] = before
    whole[length : length + 1, :] = jnp.sum(
        value * inverse_rms(value) * grad, axis=0, keepdims=True
    ) + jnp.sum(value_before * inverse_rms(value_before) * before, axis=0, keepdims=True)
    cut_slices(ids[0], whole, slices)


def early_weights_kernel(ids, gated, grad_hidden, normed, grad_gate_in, keep, send, whole,
                         gate):
    channels = gated.shape[1]
    halves = product(gated[...], grad_hidden[...], (0, 0))
    whole[:channels, :] = halves[:, :channels]
    whole[channels:, :] = halves[:, channels:]
    gate[...] = product(normed[...], grad_gate_in[...], (0, 0))
    in_order(ids[1], (whole, gate), keep, send)


def in_order(me, wholes, keep, send):
    count = 2 * keep.shape[0]
    levels = count.bit_length() - 1
    for place in range(count):
        block = reversed_bits(place, levels) ^ me
        out, at = (keep, place) if place < count // 2 else (send, place - count // 2)
        first = 0
        for whole in wholes:
            rows = whole.shape[0] // count
            from_row = pl.multiple_of(block * rows, 8)
            out[at, first : first + rows, :] = whole[pl.ds(from_row, rows), :]
            first += rows


def gate_tokens_kernel(ids, grad_gate_in, gate_high, gate_low, out):
    out[...] = product(grad_gate_in[...], (gate_high[...], gate_low[...]), (1, 1))


def extra_kernel(ids, p0, p1, p2, p3, extra, norm1, held, whole):
    join_slices(ids[0], (p0, p1, p2, p3), held, whole)
    row = whole.shape[0] - 2 * SEGMENTS
    channels = norm1.shape[2]
    extra[...] = whole[row : row + SEGMENTS, :]
    norm1[...] = jnp.zeros_like(norm1)
    for piece in range(whole.shape[1] // channels):
        lanes = slice(piece * channels, (piece + 1) * channels)
        norm1[0, piece : piece + 1, :] = whole[row : row + 1, lanes]


def grad_tokens_kernel(taps, ids, p0, p1, p2, p3, from_next, rows, gain, grad_hidden, out,
                       held, whole, tiles):
    join_slices(ids[0], (p0, p1, p2, p3), held, whole)
    length = rows.shape[0]
    lead = (taps - 1) * SEGMENTS
    for m in range(taps - 1):
        row = length - lead + (m + 1) * SEGMENTS - 1
        at = SEGMENTS - taps + 1 + m
        whole[row : row + 1, :] += from_next[at : at + 1, :]
    value = rows[...]
    whole[:length, :] = (
        norm_back(value, inverse_rms(value), gain[...][None], whole[:length, :]) + grad_hidden[...]
    )
    deinterleave_to(whole, tiles, out)


def early_out_kernel(ids, summed, out_weight):
    count, rows, channels = summed.shape
    levels = count.bit_length() - 1
    for block in range(count):
        value = summed[reversed_bits(block ^ ids[1], levels)]
        half, row = divmod(block * rows, channels)
        out_weight[row : row + rows, half * channels : (half + 1) * channels] = value


def weights_out_kernel(counts, ids, early, late, norm1, weight, *rest):
    *outs, sum_norm1, small = rest
    count, rows = early.shape[0], early.shape[1]
    more = late.shape[1] - rows
    levels = count.bit_length() - 1
    for block in range(count):
        place = reversed_bits(block ^ ids[1], levels)
        small[block * more : (block + 1) * more, :] = late[place, rows:, :]
        weight[block * rows : (block + 1) * rows, 0, :] = late[place, :rows, :]
        weight[block * rows : (block + 1) * rows, 1, :] = early[place]
    first = 0
    channels = small.shape[1]
    for out, used in zip(outs, counts):
        per = out.shape[-1] // channels
        each = used // per
        for piece in range(per):
            lanes = slice(piece * channels, (piece + 1) * channels)
            if len(out.shape) == 1:
                out[lanes] = small[first, :]
            else:
                out[:, lanes] = small[first : first + each, :]
            first += each
    for piece in range(sum_norm1.shape[0] // channels):
        sum_norm1[piece * channels : (piece + 1) * channels] = norm1[0, piece, :]


def local(
    tokens, norm1_gain, in_weight, conv_weight, conv_bias, xproj_weight, dt_weight, dt_bias,
    decay_log, skip_gain, out_weight, norm2_gain, router_weight, expert_in, expert_out,
    segments, expert_ids, cotangent,
):
    length, width = tokens.shape
    taps, channels = conv_weight.shape
    experts = router_weight.shape[1]
    wide = experts
    capacity = 5 * length // (4 * experts)
    states, rank = decay_log.shape[0], dt_weight.shape[0]
    chips = wide // 2
    slots = chips * capacity
    steps = length // SEGMENTS
    me_wide = lax.axis_index("wide")
    ids = jnp.stack([lax.axis_index("narrow"), me_wide, me_wide & 1, me_wide // 2]).astype(jnp.int32)
    half, double = length // 2, width // 2
    bf16 = jnp.bfloat16
    rows_shape, channel_rows = shape_of(length, width), shape_of(length, channels)
    packed, packed_slots = shape_of(half, double), shape_of(slots, double)
    vmem = lambda *shape: pltpu.VMEM(shape, jnp.float32)
    xproj_t, router_t = xproj_weight.T, router_weight.T
    cols = xproj_t.shape[0]

    tiled = vmem(width // LANES, length, LANES)

    halo_rows = wide_shift(tokens[length - SEGMENTS :], 1)

    (marks, slots_own, slots_other, rows_own, rows_other, cot_slice, cot_own, cot_other,
     conv_high, conv_low, gate_high, gate_low) = call(
        functools.partial(start_kernel, capacity),
        [shape_of(length, SEGMENTS)]
        + [shape_of(slots, length, dtype=bf16)] * 2
        + [shape_of(length, slots, dtype=bf16)] * 2
        + [packed, packed_slots, packed_slots]
        + [shape_of(width, channels, dtype=bf16)] * 4,
        ids, segments.reshape(-1, LANES), expert_ids.reshape(1, length), cotangent, in_weight,
        scratch=[pltpu.VMEM((segments.shape[0] // LANES, LANES), jnp.int32),
                 pltpu.VMEM((1, length), jnp.int32)] + [vmem(length, width)]
        + [vmem(width, 2, channels), vmem(length, width), tiled, vmem(2, width, channels),
           pltpu.SemaphoreType.DMA((4,))],
        far_in=[0, 1, 2, 3],
    )
    cot_pair = cot_own + core_swap(cot_other)
    rows, normed, conv_in, gate_in = call(
        front_kernel,
        [rows_shape, rows_shape, channel_rows, channel_rows],
        ids, tokens, norm1_gain, conv_high, conv_low, gate_high, gate_low,
        scratch=[tiled],
    )
    mixed, conv_out, partial, extended, halo_normed = call(
        conv_kernel,
        [channel_rows, channel_rows, shape_of(cols, length),
         shape_of(length + (taps - 1) * SEGMENTS, channels), shape_of(SEGMENTS, width)],
        ids, halo_rows, norm1_gain, conv_high, conv_low, conv_in, marks, conv_weight,
        conv_bias, xproj_t, after=[cot_pair],
    )
    partials = narrow_all(partial)

    partials = narrow_all(partial)

    cot_blocks = chip_each(hold(cot_pair, partial), chips)

    entry_shape = shape_of(2, states, SEGMENTS, channels)
    total_rows = -(-(states + 1) // 8) * 8
    coef, dt_pre, stepsize, drive, stepd, rates, entry, total = call(
        totals_kernel,
        [shape_of(length, LANES)] + [channel_rows] * 4
        + [shape_of(states, channels), entry_shape, shape_of(total_rows, channels)],
        ids, *partials, dt_weight, dt_bias, decay_log, conv_out, marks,
        scratch=[vmem(LANES, channels)],
    )
    total_shape = shape_of(total_rows, channels)
    early, late, chip_total = call(
        pair_kernel, [total_shape] * 3, ids, total, core_swap(total), rates, after=[cot_blocks]
    )
    chip_totals = chip_all(chip_total, chips)
    slabs = states // GROUP
    cot_held = hold(cot_blocks, chip_total)
    cot_one, cot_two = narrow_swap(cot_held, 1), narrow_swap(cot_held, 2)
    kept_shape = (slabs, steps + 1, GROUP, SEGMENTS, channels)
    ssm_skip, gated, mixer_slices, kept = call(
        functools.partial(states_kernel, rank),
        [channel_rows, channel_rows, shape_of(4, half, double), shape_of(*kept_shape)],
        ids, stepd, drive, coef, rates, entry, early, conv_out, gate_in, skip_gain,
        out_weight, *chip_totals,
        scratch=[vmem(chips, total_rows, channels), vmem(length, width), vmem(*kept_shape),
                 pltpu.SemaphoreType.DMA((slabs,))],
        out_place=[3],
    )
    mixer_slices = hold(mixer_slices, cot_one, cot_two)
    (rows_slice,) = call(own_slice_kernel, [packed], ids, rows, after=[mixer_slices])
    expert_rows, square = shape_of(2 * slots, width), (expert_in.shape[1], expert_in.shape[2])
    hidden_units = square[1]
    hidden_slice, hidden_own, hidden_other = call(
        dispatch_kernel,
        [packed, packed_slots, packed_slots],
        ids, *narrow_each(mixer_slices), rows_slice, slots_own, slots_other,
    )
    hidden_blocks = chip_each(hidden_own + core_swap(hidden_other), chips)
    upper, lower = hold(cot_one[: slots // 2], hidden_own), hold(cot_two[slots // 2 :], hidden_own)
    cot_three = jnp.concatenate([narrow_swap(upper, 2), narrow_swap(lower, 1)])
    raw, cot, in_high, in_low, out_high, out_low = call(
        raw_kernel,
        [shape_of(2 * slots, hidden_units), expert_rows]
        + [shape_of(*square, dtype=bf16)] * 2
        + [shape_of(square[1], square[0], dtype=bf16)] * 2,
        ids, cot_blocks, cot_one, cot_two, cot_three, expert_in[0], expert_out[0],
        scratch=[vmem(4, slots, double)],
    )
    hidden_parts = lax.all_gather(hold(hidden_blocks, raw), "narrow")
    slices_shape = shape_of(4, slots, double)
    grad_slices, second, act, grad_pre, gates, grad_logits, grad_norm2 = call(
        expert_kernel,
        [slices_shape, expert_rows] + [shape_of(2 * slots, hidden_units)] * 2
        + [shape_of(2 * slots, 1), shape_of(2 * slots, experts), shape_of(1, width)],
        ids, hidden_parts, raw, in_high, in_low, norm2_gain, router_t,
        scratch=[vmem(2 * slots, width)],
    )
    grad_mine = pair_sum(narrow_each(grad_slices))
    value_slices, grad_expert_in, grad_expert_out, grad_router_t = call(
        expert_rest_kernel,
        [slices_shape, shape_of(*square), shape_of(square[1], square[0]),
         shape_of(experts, width)],
        ids, second, act, grad_pre, gates, grad_logits, cot, out_high, out_low,
        scratch=[vmem(2 * slots, width)],
    )
    grad_back = chip_each(grad_mine, chips)
    value_mine = pair_sum(narrow_each(value_slices))
    grad_slice = call(
        home_kernel, [packed], ids, grad_back, core_swap(grad_back), cot_slice, rows_own,
        rows_other, after=[value_mine],
    )[0]
    grad_parts = narrow_all(grad_slice)
    value_back = chip_each(value_mine, chips)

    def whole_of(parts, after=()):
        return call(
            whole_kernel, [rows_shape], ids, *parts, after=after,
            scratch=[vmem(4, half, double), vmem(length, width), tiled],
        )[0]

    grad_hidden, grad_ssm, grad_gate_in, grad_skip, back_entry, back_total = call(
        functools.partial(leaving_kernel, rank),
        [rows_shape, channel_rows, channel_rows, shape_of(1, channels), entry_shape,
         shape_of(states, channels)],
        ids, *grad_parts, out_weight, gate_in, ssm_skip, conv_out, stepd, coef, rates,
        scratch=[vmem(4, half, double)], after=[value_back],
    )
    other_back = core_swap(back_total)
    block = width // wide
    half_blocks = shape_of(wide // 2, 2 * block, channels)
    early_keep, early_send = call(
        early_weights_kernel,
        [half_blocks, half_blocks],
        ids, gated, grad_hidden, normed, grad_gate_in,
        scratch=[vmem(width, channels)] * 2,
    )
    back_late, back_chip = call(
        pair_back_kernel, [shape_of(states, channels)] * 2,
        ids, back_total, other_back, early, rates, after=[early_keep],
    )
    back_totals = chip_all(back_chip, chips)
    early_arrived = core_swap(hold(early_send, back_chip))
    out_sum, gate_sum = (
        WideSum(early_keep[:, rows], early_send[:, rows])
        for rows in (slice(0, block), slice(block, None))
    )
    out_sum.arrived, gate_sum.arrived = early_arrived[:, :block], early_arrived[:, block:]
    out_sum.finish()
    gate_sum.finish()
    first_step = out_sum.start(*back_totals)

    shared_rows = (experts + 1) * (width // length)
    partial_rows = cols + shared_rows + -(cols + shared_rows) % 8
    partial_back, grad_direct, grad_dt_pre, grad_decay, grad_dt_bias = call(
        functools.partial(adjoint_kernel, rank, chips),
        [shape_of(partial_rows, length), channel_rows, channel_rows, shape_of(states, channels),
         shape_of(1, channels)],
        ids, stepd, drive, grad_ssm, coef, rates, back_entry, kept, early, late, back_late,
        conv_out, stepsize, dt_pre, skip_gain, dt_weight, grad_norm2, grad_router_t,
        *chip_totals, *back_totals,
        scratch=[vmem(chips, 1, channels), vmem(chips, states, channels), vmem(*kept_shape),
                 vmem(length, states * LANES), vmem(length, states * LANES),
                 vmem(length, channels), vmem(length, channels),
                 pltpu.SemaphoreType.DMA((slabs,))],
        in_place=[6], after=[out_sum.send, gate_sum.send],
    )
    partials_back = narrow_all(partial_back)
    gate_part = call(
        gate_tokens_kernel, [rows_shape], ids, grad_gate_in, gate_high, gate_low,
        after=[partial_back],
    )[0]
    out_sum.finish(partial_back)
    out_sum.start()
    gate_sum.start(partial_back)
    grain = 8 * wide
    small_rows = cols + rank + states + taps + 3 + (experts + 1) * (width // channels)
    small_rows += -small_rows % grain
    more = small_rows // wide
    half_blocks = shape_of(wide // 2, block + more, channels)
    token_rows = length + 2 * SEGMENTS
    conv_keep, conv_send, grad_conv, grad_halo = call(
        functools.partial(conv_back_kernel, experts),
        [half_blocks, half_blocks, channel_rows, shape_of(SEGMENTS, channels)],
        ids, *partials_back, xproj_t, grad_direct, mixed, conv_out, extended, marks,
        conv_weight, coef, grad_dt_pre, grad_decay, grad_dt_bias, grad_skip,
        normed, halo_normed,
        scratch=[vmem(small_rows, channels),
                 vmem(length + (taps - 1) * SEGMENTS, channels), vmem(partial_rows, length),
                 vmem(width, channels)],
        after=[gate_sum.arrived, out_sum.arrived],
    )
    (token_slices,) = call(
        tokens_kernel, [shape_of(4, token_rows // 2, double)],
        ids, grad_conv, grad_halo, conv_high, conv_low, gate_part, rows, halo_rows,
        scratch=[vmem(token_rows, width)],
    )
    out_sum.finish()
    gate_sum.finish()
    conv_sum = WideSum(conv_keep, conv_send)
    conv_sum.start()
    conv_sum.finish()
    (output_slice,) = call(
        home_kernel, [packed], ids, value_back, core_swap(hold(value_back, conv_keep)),
        hidden_slice, rows_own, rows_other,
    )
    levels = len(conv_sum.swaps)

    def extra_of(parts):
        return call(
            extra_kernel,
            [shape_of(SEGMENTS, width), shape_of(1, SEGMENTS, channels)],
            ids, *parts,
            scratch=[vmem(4, token_rows // 2, double), vmem(token_rows, width)],
        )

    def grad_tokens_of(parts, from_next):
        return call(
            functools.partial(grad_tokens_kernel, taps),
            [rows_shape], ids, *parts, from_next, rows, norm1_gain, grad_hidden,
            scratch=[vmem(4, token_rows // 2, double), vmem(token_rows, width), tiled],
        )[0]

    def out_weight_of(total, *others):
        return call(
            early_out_kernel, [shape_of(channels, width)], ids, total, after=others
        )[0]

    if levels == 3:
        sums = conv_sum, gate_sum, out_sum
        joint = [conv_sum.start(), *start_both(gate_sum, out_sum)]
        token_each = narrow_each(token_slices)
        for part in sums:
            part.finish(*joint, *token_each, output_slice)
        joint = [*start_both(conv_sum, gate_sum), out_sum.start()]
        token_parts = narrow_all(pair_sum(token_each))
        extra, norm1 = extra_of(token_parts)
        from_next = wide_shift(extra, -1)
        for part in sums:
            part.finish(*joint, norm1, from_next)
        arrived, norm1_other = conv_sum.start_with(norm1)
        joint = [arrived, gate_sum.start()]
        output_parts = narrow_all(hold(output_slice, norm1))
        for part in sums[:2]:
            part.finish(*joint, *output_parts)
        norm1 = norm1 + norm1_other
        arrived, norm1_other = conv_sum.start_with(norm1)
        grad_tokens = grad_tokens_of(token_parts, from_next)
        joint = [arrived, *start_both(gate_sum, out_sum, grad_tokens)]
        output = whole_of(output_parts, after=[conv_sum.send])
        for part in sums:
            part.finish(*joint, output, grad_tokens)
        norm1 = norm1 + norm1_other
        arrived, norm1_other = conv_sum.start_with(norm1)
        sum_out_weight = out_weight_of(out_sum.keep, conv_sum.send)
        conv_sum.finish(sum_out_weight)
        norm1 = norm1 + norm1_other
    else:
        token_parts = narrow_all(pair_sum(narrow_each(token_slices)))
        extra, norm1 = extra_of(token_parts)
        grad_tokens = grad_tokens_of(token_parts, wide_shift(extra, -1))
        output = whole_of(narrow_all(output_slice))
        sum_out_weight = out_weight_of(out_sum.rest())
        norm1 = norm1 + core_swap(norm1)
        norm1 = pair_sum(chip_all(norm1, chips))
    per = width // channels
    counts = (cols, rank, states, taps, 1, 1, 1, per, per * experts)
    (weight_sum, sum_xproj_t, sum_dt_weight, sum_decay, sum_taps, sum_conv_bias, sum_dt_bias,
     sum_skip, sum_norm2, sum_router_t, sum_norm1) = call(
        functools.partial(weights_out_kernel, counts),
        [shape_of(width, 2, channels)]
        + [shape_of(rows, channels) for rows in (cols, rank, states, taps)]
        + [shape_of(channels)] * 3
        + [shape_of(width), shape_of(experts, width), shape_of(width)],
        ids, gate_sum.rest(), conv_sum.rest(), norm1, scratch=[vmem(small_rows, channels)],
    )
    return (
        output,
        grad_tokens,
        sum_norm1,
        weight_sum,
        sum_taps,
        sum_conv_bias,
        sum_xproj_t.T,
        sum_dt_weight,
        sum_dt_bias,
        sum_decay,
        sum_skip,
        sum_out_weight,
        sum_norm2,
        sum_router_t.T,
        grad_expert_in[None],
        grad_expert_out[None],
    )


def solution(mesh):
    in_specs = (
        P("wide", None),
        P(),
        P(None, None, "narrow"),
        P(None, "narrow"),
        P("narrow"),
        P("narrow", None),
        P(None, "narrow"),
        P("narrow"),
        P(None, "narrow"),
        P("narrow"),
        P("narrow", None),
        P(),
        P(),
        P("wide", None, "narrow"),
        P("wide", "narrow", None),
        P(),
        P("wide", None),
        P("wide", None),
    )
    out_specs = (
        P("wide", None),
        P("wide", None),
        P(),
        P(None, None, "narrow"),
        P(None, "narrow"),
        P("narrow"),
        P("narrow", None),
        P(None, "narrow"),
        P("narrow"),
        P(None, "narrow"),
        P("narrow"),
        P("narrow", None),
        P(),
        P(),
        P("wide", None, "narrow"),
        P("wide", "narrow", None),
    )
    return jax.shard_map(local, mesh=mesh, in_specs=in_specs, out_specs=out_specs, check_vma=False)
```

```python
import functools
import math

import jax
import jax.numpy as jnp
from jax import lax
from jax.experimental import pallas as pl
from jax.experimental.pallas import tpu as pltpu
from jax.sharding import PartitionSpec as P

EPSILON = 1e-05
SEGMENTS = 8
LANES = 128
NEVER = 1e30
VMEM_SPARE = 4 * 1024 * 1024
GROUP = 4
LOG2E = 1.4426950408889634


def shape_of(*shape, dtype=jnp.float32):
    return jax.ShapeDtypeStruct(shape, dtype)


def call(kernel, outs, ids, *arrays, scratch=(), after=(), far_in=(), out_place=(), in_place=()):
    in_vmem = pl.BlockSpec(memory_space=pltpu.VMEM)
    anywhere = pl.BlockSpec(memory_space=pl.ANY)
    far = pl.BlockSpec(memory_space=pltpu.HBM)
    arrays = [
        pltpu.with_memory_space_constraint(array, pltpu.HBM) if i in far_in else array
        for i, array in enumerate(arrays)
    ]
    size = lambda a: math.prod(a.shape) * jnp.dtype(a.dtype).itemsize
    held = [
        size(a)
        for refs, skipped in ((arrays, (*in_place, *far_in)), (outs, out_place))
        for i, a in enumerate(refs)
        if i not in skipped
    ]
    held += [size(a) for a in scratch if hasattr(a, "dtype") and hasattr(a, "shape")
             and jnp.issubdtype(a.dtype, jnp.number)]
    given = 1 + len(arrays)

    def run(*refs):
        kernel(*refs[:given], *refs[given + len(after) :])

    return pl.pallas_call(
        run,
        out_shape=outs,
        in_specs=[pl.BlockSpec(memory_space=pltpu.SMEM)]
        + [far if i in far_in else anywhere if i in in_place else in_vmem
           for i in range(len(arrays))]
        + [anywhere] * len(after),
        out_specs=[anywhere if i in out_place else in_vmem for i in range(len(outs))],
        scratch_shapes=scratch,
        compiler_params=pltpu.CompilerParams(vmem_limit_bytes=sum(held) + VMEM_SPARE),
        cost_estimate=pl.CostEstimate(flops=1, bytes_accessed=1, transcendentals=0),
    )(ids, *arrays, *after)


def two_parts(value):
    high = value.astype(jnp.bfloat16)
    return high, (value - high.astype(jnp.float32)).astype(jnp.bfloat16)


def once(left, right, contract=(1, 0)):
    return lax.dot_general(
        left,
        right,
        (((contract[0],), (contract[1],)), ((), ())),
        preferred_element_type=jnp.float32,
    )


def product(left, right, contract=(1, 0)):
    left_high, left_low = left if isinstance(left, tuple) else two_parts(left)
    right_high, right_low = right if isinstance(right, tuple) else two_parts(right)
    free = 1 - contract[0]
    size = left_high.shape[free]
    if size % (16, LANES)[free]:
        return once(left_high, right_high, contract) + (
            once(left_high, right_low, contract) + once(left_low, right_high, contract)
        )
    both = once(jnp.concatenate([left_high, left_low], axis=free), right_high, contract)
    return both[:size] + (both[size:] + once(left_high, right_low, contract))


def select_rows(chosen, rows, contract=(1, 0)):
    high, low = two_parts(rows)
    return once(chosen, high, contract) + once(chosen, low, contract)


def inverse_rms(rows):
    return lax.rsqrt(jnp.mean(rows * rows, axis=-1, keepdims=True) + EPSILON)


def norm_back(rows, inverse, gain, grad):
    scaled = gain * grad
    mean = jnp.mean(rows * scaled, axis=-1, keepdims=True)
    return inverse * scaled - rows * (inverse * inverse * inverse) * mean


def sigmoid(value):
    return 1.0 / (1.0 + jnp.exp(-value))


def softplus(value):
    return jnp.maximum(value, 0.0) + jnp.log1p(jnp.exp(-jnp.abs(value)))


def gelu_parts(value):
    spread_of = 0.5 * (1.0 + lax.erf(value * (0.5**0.5)))
    density = jnp.exp(-0.5 * value * value) * ((2.0 * jnp.pi) ** -0.5)
    return value * spread_of, spread_of + value * density


def cut_slices(me, whole, out):
    rows, part = whole.shape[0] // 2, whole.shape[1] // 4
    for j in range(4):
        out[me ^ j, :, :part] = whole[:rows, part * j : part * (j + 1)]
        out[me ^ j, :, part:] = whole[rows:, part * j : part * (j + 1)]


def join_slices(me, parts, held, whole):
    rows, part = whole.shape[0] // 2, whole.shape[1] // 4
    for key, value in enumerate(parts):
        held[key] = value[...]
    for j in range(4):
        value = held[me ^ j]
        whole[:rows, part * j : part * (j + 1)] = value[:, :part]
        whole[rows:, part * j : part * (j + 1)] = value[:, part:]


def reversed_bits(value, levels):
    place = 0
    for level in range(levels):
        place = place + (((value >> level) & 1) << (levels - 1 - level))
    return place


def interleave_from(rows, held, out):
    length, width = out.shape
    steps = length // SEGMENTS
    for tile in range(width // LANES):
        lanes = slice(tile * LANES, (tile + 1) * LANES)
        held[tile] = rows[:, lanes]
        for step in range(steps):
            out[step * SEGMENTS : (step + 1) * SEGMENTS, lanes] = held[
                tile, pl.ds(step, SEGMENTS, stride=steps), :
            ]


def deinterleave_to(rows, held, out):
    length, width = out.shape
    steps = length // SEGMENTS
    for tile in range(width // LANES):
        lanes = slice(tile * LANES, (tile + 1) * LANES)
        for step in range(steps):
            held[tile, pl.ds(step, SEGMENTS, stride=steps), :] = rows[
                step * SEGMENTS : (step + 1) * SEGMENTS, lanes
            ]
        out[:, lanes] = held[tile]


def narrow_swap(value, key):
    return lax.ppermute(value, "narrow", [(i, i ^ key) for i in range(4)])


def core_swap(value):
    count = lax.axis_size("wide")
    return lax.ppermute(value, "wide", [(i, i ^ 1) for i in range(count)])


def chip_swap(value, key):
    count = lax.axis_size("wide")
    return lax.ppermute(value, "wide", [(i, i ^ (2 * key)) for i in range(count)])


def wide_shift(value, distance):
    devices = range(lax.axis_size("wide"))
    route = [(i - distance, i) for i in devices if i - distance in devices]
    return lax.ppermute(value, "wide", route)


def hold(value, *others):
    if not others:
        return value
    return lax.optimization_barrier((value, others))[0]


def narrow_all(value):
    far = narrow_swap(value, 3)
    return [value, narrow_swap(value, 1), narrow_swap(value, 2), far]


def narrow_each(slices):
    far = narrow_swap(slices[3], 3)
    return [slices[0], narrow_swap(slices[1], 1), narrow_swap(slices[2], 2), far]


def pair_sum(parts):
    while len(parts) > 1:
        parts = [a + b for a, b in zip(parts[::2], parts[1::2])]
    return parts[0]


def chip_blocks(blocks, chips):
    rows = blocks.shape[0] // chips
    order = sorted(range(1, chips), reverse=True)
    arrived = {k: chip_swap(blocks[k * rows : (k + 1) * rows], k) for k in order}
    arrived[0] = blocks[:rows]
    return [arrived[k] for k in range(chips)]


def chip_each(blocks, chips):
    return jnp.concatenate(chip_blocks(blocks, chips))


def chip_all(value, chips):
    arrived = {k: chip_swap(value, k) for k in sorted(range(1, chips), reverse=True)}
    arrived[0] = value
    return [arrived[k] for k in range(chips)]


class WideSum:
    def __init__(self, keep, send):
        levels = lax.axis_size("wide").bit_length() - 1
        self.swaps = [core_swap] + [
            functools.partial(chip_swap, key=1 << level) for level in range(levels - 1)
        ]
        self.keep, self.send, self.arrived = keep, send, None
        self.level, self.back = 0, False

    def prepare(self):
        if not self.back and self.level == len(self.swaps):
            self.back = True
        if self.back:
            self.level -= 1
            self.send = self.keep
        return self.send

    def start(self, *others):
        self.prepare()
        self.arrived = self.swaps[self.level](hold(self.send, *others))
        return self.arrived

    def start_with(self, rider):
        sent = self.prepare()
        joined = jnp.concatenate([sent.reshape(1, -1, sent.shape[2]), rider], axis=1)
        arrived = self.swaps[self.level](joined)
        rows = rider.shape[1]
        self.arrived = arrived[:, :-rows].reshape(sent.shape)
        return self.arrived, arrived[:, -rows:]

    def finish(self, *others):
        arrived = hold(self.arrived, *others) if others else self.arrived
        if self.back:
            self.keep = jnp.concatenate([self.keep, arrived])
            return
        self.level += 1
        if self.level == len(self.swaps):
            self.keep = self.keep + arrived
            return
        half = self.keep.shape[0] // 2
        self.send = self.keep[half:] + arrived[half:]
        self.keep = self.keep[:half] + arrived[:half]

    def rest(self):
        while not (self.back and self.level == 0):
            self.start()
            self.finish()
        return self.keep


def start_both(one, two, *others):
    first, second = one.prepare(), two.prepare()
    rows = first.shape[1]
    arrived = one.swaps[one.level](hold(jnp.concatenate([first, second], axis=1), *others))
    one.arrived, two.arrived = arrived[:, :rows], arrived[:, rows:]
    return one.arrived, two.arrived


def route_kernel(capacity, ids, segments, expert_ids, marks, slots_own, slots_other,
                 rows_own, rows_other):
    wide_at, core, chip = ids[1], ids[2], ids[3]
    length = expert_ids.shape[1]
    per = length // LANES
    experts = segments.shape[0] // per
    steps = length // SEGMENTS

    def block(at):
        return jnp.concatenate([segments[pl.ds(at * per + i, 1), :] for i in range(per)], axis=1)

    own, before = block(wide_at), block(jnp.maximum(wide_at - 1, 0))
    lane = lax.broadcasted_iota(jnp.int32, (1, length), 1)
    here = lax.broadcasted_iota(jnp.int32, (SEGMENTS, length), 0)
    table = jnp.ones((SEGMENTS, length), jnp.float32)
    for k in range(1, 4):
        back = jnp.where(lane < k, pltpu.roll(before, k, 1), pltpu.roll(own, k, 1))
        same = (back == own) & ((lane >= k) | (wide_at > 0))
        table = jnp.where(here == k, jnp.where(same, 1.0, 0.0), table)
    live = own >= 0
    expert = expert_ids[...]
    at = lax.broadcasted_iota(jnp.int32, (experts, length), 0)
    hits = jnp.where((at == expert) & live, 1.0, 0.0)
    first = lax.broadcasted_iota(jnp.int32, (length, length), 0)
    second = lax.broadcasted_iota(jnp.int32, (length, length), 1)
    earlier = jnp.where(first < second, 1.0, 0.0).astype(jnp.bfloat16)
    ranks = once(hits.astype(jnp.bfloat16), earlier)
    rank = jnp.sum(ranks * hits, axis=0, keepdims=True).astype(jnp.int32)
    kept = live & (rank < capacity)
    order = jnp.where(
        (first % SEGMENTS) * steps + first // SEGMENTS == second, 1.0, 0.0
    ).astype(jnp.bfloat16)
    marks[...] = once(order, table.astype(jnp.bfloat16), (1, 1))
    slot = jnp.where(kept, ((expert >> 1) ^ chip) * capacity + rank, -1)
    count = slots_own.shape[0]
    slot_at = lax.broadcasted_iota(jnp.int32, (count, length), 0)
    for which, slots, rows in ((core, slots_own, rows_own), (1 - core, slots_other, rows_other)):
        mine = (slot_at == slot) & ((expert & 1) == which)
        chosen = jnp.where(mine, 1.0, 0.0).astype(jnp.bfloat16)
        slots[...] = once(chosen, order, (1, 1)).astype(jnp.bfloat16)
        rows[...] = once(order, chosen, (1, 1)).astype(jnp.bfloat16)


def front_kernel(ids, tokens, gain, conv_high, conv_low, gate_high, gate_low,
                 rows, normed, conv_in, gate_in, held):
    interleave_from(tokens, held, rows)
    value = rows[...]
    scaled = value * inverse_rms(value) * gain[...][None]
    normed[...] = scaled
    parts = two_parts(scaled)
    conv_in[...] = product(parts, (conv_high[...], conv_low[...]))
    gate_in[...] = product(parts, (gate_high[...], gate_low[...]))


def start_kernel(capacity, ids, segments_far, expert_ids_far, tokens_far, cotangent_far, weight_far,
                 marks, slots_own, slots_other, rows_own, rows_other,
                 rows_slice, cot_slice, own, other, conv_high, conv_low, gate_high, gate_low,
                 segments, expert_ids, tokens, cotangent, weight, rows, held, branch,
                 sems):
    pairs = (
        (segments_far, segments),
        (expert_ids_far, expert_ids),
        (tokens_far, tokens),
        (cotangent_far, cotangent),
        (weight_far, weight),
    )
    copies = [
        pltpu.make_async_copy(far, near, sems.at[i]) for i, (far, near) in enumerate(pairs)
    ]
    for copy in copies:
        copy.start()
    copies[0].wait()
    copies[1].wait()
    route_kernel(capacity, ids, segments, expert_ids, marks, slots_own, slots_other,
                 rows_own, rows_other)
    copies[2].wait()
    copies[3].wait()
    slices_kernel(ids, tokens, cotangent, slots_own, slots_other, rows_slice, cot_slice, own, other,
                  rows, held)
    copies[4].wait()
    for k, (high, low) in enumerate(((conv_high, conv_low), (gate_high, gate_low))):
        branch[k] = weight[:, k, :]
        high[...], low[...] = two_parts(branch[k])


def slices_kernel(ids, tokens, cotangent, slots_own, slots_other,
                  rows_slice, cot_slice, own, other, rows, held):
    me, core = ids[0], ids[2]
    half, part = tokens.shape[0] // 2, tokens.shape[1] // 4
    for source, out in ((tokens, rows_slice), (cotangent, cot_slice)):
        interleave_from(source, held, rows)
        for j in range(4):
            @pl.when(me == j)
            def _():
                out[:, :part] = rows[:half, part * j : part * (j + 1)]
                out[:, part:] = rows[half:, part * j : part * (j + 1)]
    send_slots(core, cot_slice[...], slots_own[...], slots_other[...], own, other)


def send_slots(core, packed, slots_own, slots_other, own, other):
    half = packed.shape[1] // 2
    rows = jnp.concatenate([packed[:, :half], packed[:, half:]])
    for slots, out in ((slots_own, own), (slots_other, other)):
        sent = select_rows(slots, rows)
        for side in range(2):
            @pl.when(core == side)
            def _():
                out[:, side * half : (side + 1) * half] = sent
                out[:, (1 - side) * half : (2 - side) * half] = jnp.zeros_like(sent)


def conv_kernel(ids, halo, gain, conv_high, conv_low, conv_in, marks, conv_weight, conv_bias,
                xproj_t, mixed, conv_out, partial, extended, halo_normed):
    taps, channels = conv_weight.shape
    length = conv_in.shape[0]
    lead = (taps - 1) * SEGMENTS
    rows = halo[...]
    scaled = rows * inverse_rms(rows) * gain[...][None]
    halo_normed[...] = scaled
    halo_conv = product(scaled, (conv_high[...], conv_low[...]))
    place = lax.broadcasted_iota(jnp.int32, (SEGMENTS, channels), 0)
    for m in range(taps - 1):
        ends = conv_in[length - lead + m * SEGMENTS : length - lead + (m + 1) * SEGMENTS, :]
        at = SEGMENTS - taps + 1 + m
        extended[m * SEGMENTS : (m + 1) * SEGMENTS, :] = jnp.where(
            place == 0, halo_conv[at : at + 1, :], pltpu.roll(ends, 1, 0)
        )
    extended[lead:, :] = conv_in[...]
    total = jnp.broadcast_to(conv_bias[...][None], (length, channels))
    for k in range(taps):
        first = (taps - 1 - k) * SEGMENTS
        total += conv_weight[k : k + 1, :] * extended[first : first + length, :] * marks[:, k : k + 1]
    mixed[...] = total
    out = total * sigmoid(total)
    conv_out[...] = out
    partial[...] = product(xproj_t[...], out, (1, 1))


def rows_at(step):
    return pl.ds(pl.multiple_of(step * SEGMENTS, SEGMENTS), SEGMENTS)


def spread(row):
    return jnp.broadcast_to(row, (SEGMENTS, row.shape[-1]))


def column_of(rows, column):
    return jnp.broadcast_to(rows[:, column : column + 1], (SEGMENTS, LANES))


def sweep(count, body, carry):
    return lax.fori_loop(0, count, body, carry, unroll=True)


def add_to(ref, first, rows, lanes, value):
    if first:
        ref[rows, lanes] = value
    else:
        ref[rows, lanes] += value


def chain_pieces(decay, value, backward):
    place = lax.broadcasted_iota(jnp.int32, decay.shape, 0)
    if backward:
        place = SEGMENTS - 1 - place

    def moved(array, distance):
        return pltpu.roll(array, (SEGMENTS - distance) if backward else distance, 0)

    distance = 1
    while distance < SEGMENTS:
        inside = place >= distance
        value = jnp.where(inside, decay * moved(value, distance) + value, value)
        decay = jnp.where(inside, decay * moved(decay, distance), decay)
        distance *= 2
    first = place == 0
    before = jnp.where(first, 0.0, moved(value, 1))
    factor = jnp.where(first, 1.0, moved(decay, 1))
    return factor, before, value


def totals_kernel(ids, p0, p1, p2, p3, dt_weight, dt_bias, decay_log, conv_out, marks,
                  coef, dt_pre, stepsize, drive, stepd, rates, entry, total, padded):
    states, channels = decay_log.shape
    rank = dt_weight.shape[0]
    length = conv_out.shape[0]
    steps = length // SEGMENTS
    projected = (p0[...] + p1[...]) + (p2[...] + p3[...])
    missing = LANES - projected.shape[0]
    coef[...] = jnp.concatenate([projected, jnp.zeros((missing, length), jnp.float32)]).T
    padded[...] = jnp.zeros_like(padded)
    padded[:rank, :] = dt_weight[...]
    pre = product(coef[...], padded[...]) + dt_bias[...][None]
    dt_pre[...] = pre
    size = softplus(pre)
    stepsize[...] = size
    drive[...] = size * conv_out[...]
    stepd[...] = jnp.where(marks[:, 1:2] > 0.5, size, NEVER)
    rates[...] = -jnp.exp(decay_log[...])
    total[...] = jnp.zeros_like(total)
    zero = jnp.zeros((SEGMENTS, LANES), jnp.float32)
    tiles = [slice(at, at + LANES) for at in range(0, channels, LANES)]
    sums = [zero] * len(tiles)
    for step in range(steps):
        rows = slice(step * SEGMENTS, (step + 1) * SEGMENTS)
        sums = [value + stepd[rows, lanes] for value, lanes in zip(sums, tiles)]
    for value, lanes in zip(sums, tiles):
        total[states : states + 1, lanes] = jnp.sum(value, axis=0, keepdims=True)
    for group in range(0, states, GROUP):
        names = range(group, group + GROUP)
        rate = [[spread(rates[n : n + 1, lanes] * LOG2E) for lanes in tiles] for n in names]

        def body(step, current):
            rows = rows_at(step)
            near = coef[rows, :]
            width = [stepd[rows, lanes] for lanes in tiles]
            push = [drive[rows, lanes] for lanes in tiles]
            later = []
            for at, n in enumerate(names):
                entering = column_of(near, rank + n)
                later.append(tuple(
                    jnp.exp2(width[t] * rate[at][t]) * current[at][t] + push[t] * entering
                    for t in range(len(tiles))
                ))
            return tuple(later)

        current = sweep(steps, body, ((zero,) * len(tiles),) * GROUP)
        for at, n in enumerate(names):
            for t, lanes in enumerate(tiles):
                decay = jnp.exp2(sums[t] * rate[at][t])
                factor, before, last = chain_pieces(decay, current[at][t], False)
                entry[0, n, :, lanes] = factor
                entry[1, n, :, lanes] = before
                total[n : n + 1, lanes] = last[SEGMENTS - 1 :, :]


def pair_kernel(ids, total, other, rates, early, late, chip):
    states = rates.shape[0]
    second = ids[2] == 1
    mine, theirs = total[...], other[...]
    first, last = jnp.where(second, theirs, mine), jnp.where(second, mine, theirs)
    early[...] = first
    late[...] = last
    chip[...] = first + last
    chip[:states, :] = (
        jnp.exp(last[states : states + 1] * rates[...]) * first[:states] + last[:states]
    )


def pair_back_kernel(ids, total, other, early, rates, late_total, chip):
    states = rates.shape[0]
    second = ids[2] == 1
    mine, theirs = total[...], other[...]
    first, last = jnp.where(second, theirs, mine), jnp.where(second, mine, theirs)
    late_total[...] = last
    chip[...] = first + jnp.exp(early[states : states + 1, :] * rates[...]) * last


def states_kernel(rank, ids, stepd, drive, coef, rates, entry, early, conv_out, gate_in, skip,
                  out_weight, *rest):
    chips = len(rest) - 8
    totals = rest[:chips]
    ssm_skip, gated, slices, kept, held, whole, kept_here, sems = rest[chips:]
    me, core, here = ids[0], ids[2], ids[3]
    states, channels = rates.shape
    length = stepd.shape[0]
    steps = length // SEGMENTS
    for key, value in enumerate(totals):
        held[key] = value[...]
    state = jnp.zeros((states, channels), jnp.float32)
    for chip in range(chips):
        value = held[here ^ chip]
        grown = jnp.exp(value[states : states + 1] * rates[...]) * state + value[:states]
        state = jnp.where(chip < here, grown, state)
    inner = jnp.exp(early[states : states + 1, :] * rates[...]) * state + early[:states, :]
    start = jnp.where(core == 1, inner, state)
    tiles = [slice(at, at + LANES) for at in range(0, channels, LANES)]
    copies = []
    for group in range(0, states, GROUP):
        names = range(group, group + GROUP)
        slab = group // GROUP
        rate = [[spread(rates[n : n + 1, lanes] * LOG2E) for lanes in tiles] for n in names]
        current = tuple(
            tuple(
                entry[0, n, :, lanes] * start[n : n + 1, lanes] + entry[1, n, :, lanes]
                for lanes in tiles
            )
            for n in names
        )
        for at in range(GROUP):
            for t, lanes in enumerate(tiles):
                kept_here[slab, 0, at, :, lanes] = current[at][t]

        def body(step, current):
            rows = rows_at(step)
            near = coef[rows, :]
            width = [stepd[rows, lanes] for lanes in tiles]
            push = [drive[rows, lanes] for lanes in tiles]
            later, total = [], [None] * len(tiles)
            for at, n in enumerate(names):
                entering, leaving = column_of(near, rank + n), column_of(near, rank + states + n)
                new = []
                for t, lanes in enumerate(tiles):
                    decay = jnp.exp2(width[t] * rate[at][t])
                    new.append(decay * current[at][t] + push[t] * entering)
                    kept_here[slab, step + 1, at, :, lanes] = new[t]
                    term = leaving * new[t]
                    total[t] = term if total[t] is None else total[t] + term
                later.append(tuple(new))
            for t, lanes in enumerate(tiles):
                add_to(ssm_skip, group == 0, rows, lanes, total[t])
            return tuple(later)

        sweep(steps, body, current)
        copies.append(pltpu.make_async_copy(kept_here.at[slab], kept.at[slab], sems.at[slab]))
        copies[-1].start()
    skipped = ssm_skip[...] + skip[...][None] * conv_out[...]
    ssm_skip[...] = skipped
    gate = gate_in[...]
    out = skipped * gate * sigmoid(gate)
    gated[...] = out
    whole[...] = product(out, out_weight[...])
    cut_slices(me, whole, slices)
    for copy in copies:
        copy.wait()


def dispatch_kernel(ids, s0, s1, s2, s3, rows_slice, slots_own, slots_other,
                    hidden, own, other):
    packed = (s0[...] + s1[...]) + (s2[...] + s3[...]) + rows_slice[...]
    hidden[...] = packed
    send_slots(ids[2], packed, slots_own[...], slots_other[...], own, other)


def raw_kernel(ids, c0, c1, c2, c3, expert_in, expert_out, raw, cot, in_high, in_low,
               out_high, out_low, held):
    join_slices(ids[0], (c0, c1, c2, c3), held, cot)
    in_high[...], in_low[...] = two_parts(expert_in[...])
    out_high[...], out_low[...] = two_parts(expert_out[...])
    raw[...] = product(cot[...], (out_high[...], out_low[...]), (1, 1))


def expert_kernel(ids, parts, raw, in_high, in_low, norm_gain, router_t,
                  slices, second, act, grad_pre, gates, grad_logits, grad_gain,
                  whole):
    me, expert = ids[0], ids[1]
    count, part = whole.shape[0] // 2, whole.shape[1] // 4
    for j in range(4):
        whole[:count, part * j : part * (j + 1)] = parts[j, :, :part]
        whole[count:, part * j : part * (j + 1)] = parts[j, :, part:]
    rows = whole[...]
    inverse = inverse_rms(rows)
    normed = rows * inverse * norm_gain[...][None]
    second[...] = normed
    normed_parts = two_parts(normed)
    router_parts = two_parts(router_t[...])
    weight = (in_high[...], in_low[...])
    logits = product(normed_parts, router_parts, (1, 1))
    logits = logits - jnp.max(logits, axis=-1, keepdims=True)
    powers = jnp.exp(logits)
    probs = powers / jnp.sum(powers, axis=-1, keepdims=True)
    chosen = jnp.where(
        lax.broadcasted_iota(jnp.int32, logits.shape, 1) == expert, 1.0, 0.0
    )
    gate = jnp.sum(probs * chosen, axis=-1, keepdims=True)
    gates[...] = gate
    hidden_act, slope = gelu_parts(product(normed_parts, weight))
    act[...] = hidden_act
    raws = raw[...]
    grad_gate = jnp.sum(hidden_act * raws, axis=-1, keepdims=True)
    grads = gate * raws * slope
    grad_pre[...] = grads
    logit_grads = grad_gate * gate * (chosen - probs)
    grad_logits[...] = logit_grads
    grad_second = product(grads, weight, (1, 1)) + product(logit_grads, router_parts)
    grad_gain[...] = jnp.sum(rows * inverse * grad_second, axis=0, keepdims=True)
    whole[...] = norm_back(rows, inverse, norm_gain[...][None], grad_second)
    cut_slices(me, whole, slices)


def expert_rest_kernel(ids, second, act, grad_pre, gates, grad_logits, cot, out_high, out_low,
                       slices, grad_in, grad_out, grad_router, whole):
    gate = gates[...]
    acts = two_parts(act[...])
    normed = two_parts(second[...])
    whole[...] = gate * product(acts, (out_high[...], out_low[...]))
    cut_slices(ids[0], whole, slices)
    grad_out[...] = product(acts, gate * cot[...], (0, 0))
    grad_in[...] = product(normed, grad_pre[...], (0, 0))
    grad_router[...] = product(grad_logits[...], normed, (0, 0))


def home_kernel(ids, own, other, base, rows_own, rows_other, out):
    half = own.shape[1] // 2
    second = ids[2] == 1

    def mine(rows):
        return jnp.where(second, rows[:, half:], rows[:, :half])

    total = select_rows(rows_own[...], mine(own[...])) + select_rows(
        rows_other[...], mine(other[...])
    )
    count = base.shape[0]
    out[:, :half] = base[:, :half] + total[:count]
    out[:, half:] = base[:, half:] + total[count:]


def whole_kernel(ids, p0, p1, p2, p3, out, held, whole, tiles):
    join_slices(ids[0], (p0, p1, p2, p3), held, whole)
    deinterleave_to(whole, tiles, out)


def leaving_kernel(rank, ids, g0, g1, g2, g3, out_weight, gate_in, ssm_skip, conv_out, stepd,
                   coef, rates, grad_hidden, grad_ssm, grad_gate_in, grad_skip, entry, total,
                   held):
    join_slices(ids[0], (g0, g1, g2, g3), held, grad_hidden)
    states, channels = rates.shape
    length = stepd.shape[0]
    steps = length // SEGMENTS
    grad_gated = product(grad_hidden[...], out_weight[...], (1, 1))
    gate = gate_in[...]
    gate_sigmoid = sigmoid(gate)
    pulled = grad_gated * gate * gate_sigmoid
    grad_ssm[...] = pulled
    grad_gate_in[...] = grad_gated * ssm_skip[...] * (
        gate_sigmoid * (1.0 + gate * (1.0 - gate_sigmoid))
    )
    grad_skip[...] = jnp.sum(pulled * conv_out[...], axis=0, keepdims=True)
    zero = jnp.zeros((SEGMENTS, LANES), jnp.float32)
    tiles = [slice(at, at + LANES) for at in range(0, channels, LANES)]
    sums = [zero] * len(tiles)
    for step in range(steps):
        rows = slice(step * SEGMENTS, (step + 1) * SEGMENTS)
        sums = [value + stepd[rows, lanes] for value, lanes in zip(sums, tiles)]
    for group in range(0, states, GROUP):
        names = range(group, group + GROUP)
        rate = [[spread(rates[n : n + 1, lanes] * LOG2E) for lanes in tiles] for n in names]

        def body(back, current):
            rows = rows_at(steps - 1 - back)
            near = coef[rows, :]
            width = [stepd[rows, lanes] for lanes in tiles]
            pull = [grad_ssm[rows, lanes] for lanes in tiles]
            later = []
            for at, n in enumerate(names):
                leaving = column_of(near, rank + states + n)
                later.append(tuple(
                    jnp.exp2(width[t] * rate[at][t]) * (current[at][t] + pull[t] * leaving)
                    for t in range(len(tiles))
                ))
            return tuple(later)

        current = sweep(steps, body, ((zero,) * len(tiles),) * GROUP)
        for at, n in enumerate(names):
            for t, lanes in enumerate(tiles):
                decay = jnp.exp2(sums[t] * rate[at][t])
                factor, before, last = chain_pieces(decay, current[at][t], True)
                entry[0, n, :, lanes] = factor
                entry[1, n, :, lanes] = before
                total[n : n + 1, lanes] = last[:1, :]


def adjoint_kernel(rank, chips, ids, stepd, drive, grad, coef, rates, entry, kept, early, late,
                   late_total, conv_out, stepsize, dt_pre, skip, dt_weight, grad_norm2, grad_router,
                   *rest):
    sums, totals = rest[:chips], rest[chips : 2 * chips]
    (partial, grad_direct, grad_dt_pre, grad_decay, grad_dt_bias, held_sums, held, kept_here,
     in_terms, out_terms, grad_push, grad_width, sems) = rest[2 * chips :]
    core, here = ids[2], ids[3]
    states, channels = rates.shape
    length = stepd.shape[0]
    steps = length // SEGMENTS
    copies = [
        pltpu.make_async_copy(kept.at[slab], kept_here.at[slab], sems.at[slab])
        for slab in range(states // GROUP)
    ]
    for copy in copies:
        copy.start()
    for key in range(chips):
        held_sums[key] = sums[key][states : states + 1, :]
        held[key] = totals[key][...]
    state = jnp.zeros((states, channels), jnp.float32)
    for chip in reversed(range(chips)):
        grown = held[here ^ chip] + jnp.exp(held_sums[here ^ chip] * rates[...]) * state
        state = jnp.where(chip > here, grown, state)
    inner = late_total[...] + jnp.exp(late[states : states + 1, :] * rates[...]) * state
    final = jnp.where(core == 1, state, inner)
    zero = jnp.zeros((SEGMENTS, LANES), jnp.float32)
    tiles = [slice(at, at + LANES) for at in range(0, channels, LANES)]
    for group in range(0, states, GROUP):
        names = range(group, group + GROUP)
        slab = group // GROUP
        rate = [[spread(rates[n : n + 1, lanes]) for lanes in tiles] for n in names]
        current = tuple(
            tuple(
                entry[0, n, :, lanes] * final[n : n + 1, lanes] + entry[1, n, :, lanes]
                for lanes in tiles
            )
            for n in names
        )
        copies[slab].wait()

        def body(back, carry):
            current, slopes = carry
            step = steps - 1 - back
            rows = rows_at(step)
            near = coef[rows, :]
            width = [stepd[rows, lanes] for lanes in tiles]
            push = [drive[rows, lanes] for lanes in tiles]
            pull = [grad[rows, lanes] for lanes in tiles]
            later, slope = [], []
            total, width_total = [None] * len(tiles), [None] * len(tiles)
            for at, n in enumerate(names):
                entering, leaving = column_of(near, rank + n), column_of(near, rank + states + n)
                new, turned, in_term, out_term = [], [], None, None
                for t, lanes in enumerate(tiles):
                    adjoint = leaving * pull[t] + current[at][t]
                    decayed = jnp.exp2(width[t] * (rate[at][t] * LOG2E)) * adjoint
                    through = decayed * kept_here[slab, step, at, :, lanes]
                    term, rated = adjoint * entering, through * rate[at][t]
                    total[t] = term if total[t] is None else total[t] + term
                    width_total[t] = rated if width_total[t] is None else width_total[t] + rated
                    new.append(decayed)
                    turned.append(slopes[at][t] + through * width[t])
                    term = adjoint * push[t]
                    in_term = term if in_term is None else in_term + term
                    term = kept_here[slab, step + 1, at, :, lanes] * pull[t]
                    out_term = term if out_term is None else out_term + term
                place = slice(n * LANES, (n + 1) * LANES)
                in_terms[rows, place] = in_term
                out_terms[rows, place] = out_term
                later.append(tuple(new))
                slope.append(tuple(turned))
            for t, lanes in enumerate(tiles):
                add_to(grad_push, group == 0, rows, lanes, total[t])
                add_to(grad_width, group == 0, rows, lanes, width_total[t])
            return tuple(later), tuple(slope)

        none = ((zero,) * len(tiles),) * GROUP
        _, slopes = sweep(steps, body, (current, none))
        for at, n in enumerate(names):
            for t, lanes in enumerate(tiles):
                grad_decay[n : n + 1, lanes] = rates[n : n + 1, lanes] * jnp.sum(
                    slopes[at][t], axis=0, keepdims=True
                )
    pushed = grad_push[...]
    grads = (pushed * conv_out[...] + grad_width[...]) * sigmoid(dt_pre[...])
    grad_dt_pre[...] = grads
    grad_dt_bias[...] = jnp.sum(grads, axis=0, keepdims=True)
    grad_direct[...] = pushed * stepsize[...] + skip[...][None] * grad[...]
    partial[:rank, :] = product(dt_weight[...], grads, (1, 1))
    shape = (2 * states, states * LANES)
    column = lax.broadcasted_iota(jnp.int32, shape, 0)
    owner = lax.broadcasted_iota(jnp.int32, shape, 1) // LANES
    total = None
    for terms, base in ((in_terms, 0), (out_terms, states)):
        ones = jnp.where(owner + base == column, 1.0, 0.0).astype(jnp.bfloat16)
        for part in two_parts(terms[...]):
            term = once(ones, part, (1, 1))
            total = term if total is None else total + term
    cols = rank + 2 * states
    partial[rank:cols, :] = total
    row = cols
    for shared in (grad_norm2, grad_router):
        for at in range(0, shared.shape[1], length):
            partial[row : row + shared.shape[0], :] = shared[:, at : at + length]
            row += shared.shape[0]
    partial[row:, :] = jnp.zeros((partial.shape[0] - row, length), jnp.float32)


def conv_back_kernel(experts, ids, p0, p1, p2, p3, xproj_t, grad_direct, mixed, conv_out, extended,
                     marks, conv_weight, coef, grad_dt_pre, grad_decay, grad_dt_bias, grad_skip,
                     normed, halo_normed, keep, send, grad_conv, grad_halo,
                     small, grad_extended, summed, weights):
    taps, channels = conv_weight.shape
    cols, states = xproj_t.shape[0], grad_decay.shape[0]
    rank = cols - 2 * states
    length = mixed.shape[0]
    lead = (taps - 1) * SEGMENTS
    summed[...] = (p0[...] + p1[...]) + (p2[...] + p3[...])
    projected = two_parts(summed[:cols, :])
    grad_out = grad_direct[...] + product(projected, xproj_t[...], (0, 0))
    value = mixed[...]
    value_sigmoid = sigmoid(value)
    grad_mixed = grad_out * (value_sigmoid * (1.0 + value * (1.0 - value_sigmoid)))
    grad_extended[...] = jnp.zeros_like(grad_extended)
    first_tap = cols + rank + states
    small[first_tap:, :] = jnp.zeros((small.shape[0] - first_tap, channels), jnp.float32)
    for k in range(taps):
        first = (taps - 1 - k) * SEGMENTS
        masked = grad_mixed * marks[:, k : k + 1]
        small[first_tap + k : first_tap + k + 1, :] = jnp.sum(
            masked * extended[first : first + length, :], axis=0, keepdims=True
        )
        grad_extended[first : first + length, :] += conv_weight[k : k + 1, :] * masked
    grad_conv[...] = grad_extended[lead:, :]
    grad_halo[...] = jnp.zeros_like(grad_halo)
    place = lax.broadcasted_iota(jnp.int32, (SEGMENTS, channels), 0)
    for m in range(taps - 1):
        rows = grad_extended[m * SEGMENTS : (m + 1) * SEGMENTS, :]
        at = SEGMENTS - taps + 1 + m
        grad_halo[at : at + 1, :] = rows[:1, :]
        inside = jnp.where(place == SEGMENTS - 1, 0.0, pltpu.roll(rows, SEGMENTS - 1, 0))
        ends = slice(length - lead + m * SEGMENTS, length - lead + (m + 1) * SEGMENTS)
        grad_conv[ends, :] += inside
    small[:cols, :] = product(projected, conv_out[...])
    low = product(coef[...], grad_dt_pre[...], (0, 0))
    small[cols : cols + rank, :] = low[:rank, :]
    small[cols + rank : first_tap, :] = grad_decay[...]
    last = first_tap + taps
    small[last : last + 1, :] = jnp.sum(grad_mixed, axis=0, keepdims=True)
    small[last + 1 : last + 2, :] = grad_dt_bias[...]
    small[last + 2 : last + 3, :] = grad_skip[...]
    first, row = last + 3, cols
    for count in (1, experts):
        for at in range(0, 2 * channels, length):
            value = summed[row : row + count, :]
            end = at + length
            for piece in range(at // channels, -(-end // channels)):
                low, high = max(at, piece * channels), min(end, (piece + 1) * channels)
                target = first + piece * count
                small[target : target + count, low - piece * channels : high - piece * channels] = (
                    value[:, low - at : high - at]
                )
            row += count
        first += 2 * count
    weights[...] = product(normed[...], grad_conv[...], (0, 0)) + product(
        halo_normed[...], grad_halo[...], (0, 0)
    )
    in_order(ids[1], (weights, small), keep, send)


def tokens_kernel(ids, grad_conv, grad_halo, conv_high, conv_low, gate_part, rows, halo_rows,
                  slices, whole):
    weight = conv_high[...], conv_low[...]
    length = grad_conv.shape[0]
    grad = product(grad_conv[...], weight, (1, 1)) + gate_part[...]
    before = product(grad_halo[...], weight, (1, 1))
    value, value_before = rows[...], halo_rows[...]
    whole[:length, :] = grad
    whole[length:, :] = jnp.zeros((whole.shape[0] - length, whole.shape[1]), jnp.float32)
    whole[length : length + SEGMENTS, :] = before
    whole[length : length + 1, :] = jnp.sum(
        value * inverse_rms(value) * grad, axis=0, keepdims=True
    ) + jnp.sum(value_before * inverse_rms(value_before) * before, axis=0, keepdims=True)
    cut_slices(ids[0], whole, slices)


def early_weights_kernel(ids, gated, grad_hidden, normed, grad_gate_in, keep, send, whole,
                         gate):
    channels = gated.shape[1]
    halves = product(gated[...], grad_hidden[...], (0, 0))
    whole[:channels, :] = halves[:, :channels]
    whole[channels:, :] = halves[:, channels:]
    gate[...] = product(normed[...], grad_gate_in[...], (0, 0))
    in_order(ids[1], (whole, gate), keep, send)


def in_order(me, wholes, keep, send):
    count = 2 * keep.shape[0]
    levels = count.bit_length() - 1
    for place in range(count):
        block = reversed_bits(place, levels) ^ me
        out, at = (keep, place) if place < count // 2 else (send, place - count // 2)
        first = 0
        for whole in wholes:
            rows = whole.shape[0] // count
            from_row = pl.multiple_of(block * rows, 8)
            out[at, first : first + rows, :] = whole[pl.ds(from_row, rows), :]
            first += rows


def gate_tokens_kernel(ids, grad_gate_in, gate_high, gate_low, out):
    out[...] = product(grad_gate_in[...], (gate_high[...], gate_low[...]), (1, 1))


def extra_kernel(ids, p0, p1, p2, p3, extra, norm1, held, whole):
    join_slices(ids[0], (p0, p1, p2, p3), held, whole)
    row = whole.shape[0] - 2 * SEGMENTS
    channels = norm1.shape[2]
    extra[...] = whole[row : row + SEGMENTS, :]
    norm1[...] = jnp.zeros_like(norm1)
    for piece in range(whole.shape[1] // channels):
        lanes = slice(piece * channels, (piece + 1) * channels)
        norm1[0, piece : piece + 1, :] = whole[row : row + 1, lanes]


def grad_tokens_kernel(taps, ids, p0, p1, p2, p3, from_next, rows, gain, grad_hidden, out,
                       held, whole, tiles):
    join_slices(ids[0], (p0, p1, p2, p3), held, whole)
    length = rows.shape[0]
    lead = (taps - 1) * SEGMENTS
    for m in range(taps - 1):
        row = length - lead + (m + 1) * SEGMENTS - 1
        at = SEGMENTS - taps + 1 + m
        whole[row : row + 1, :] += from_next[at : at + 1, :]
    value = rows[...]
    whole[:length, :] = (
        norm_back(value, inverse_rms(value), gain[...][None], whole[:length, :]) + grad_hidden[...]
    )
    deinterleave_to(whole, tiles, out)


def early_out_kernel(ids, summed, out_weight):
    count, rows, channels = summed.shape
    levels = count.bit_length() - 1
    for block in range(count):
        value = summed[reversed_bits(block ^ ids[1], levels)]
        half, row = divmod(block * rows, channels)
        out_weight[row : row + rows, half * channels : (half + 1) * channels] = value


def weights_out_kernel(counts, ids, early, late, norm1, weight, *rest):
    *outs, sum_norm1, small = rest
    count, rows = early.shape[0], early.shape[1]
    more = late.shape[1] - rows
    levels = count.bit_length() - 1
    for block in range(count):
        place = reversed_bits(block ^ ids[1], levels)
        small[block * more : (block + 1) * more, :] = late[place, rows:, :]
        weight[block * rows : (block + 1) * rows, 0, :] = late[place, :rows, :]
        weight[block * rows : (block + 1) * rows, 1, :] = early[place]
    first = 0
    channels = small.shape[1]
    for out, used in zip(outs, counts):
        per = out.shape[-1] // channels
        each = used // per
        for piece in range(per):
            lanes = slice(piece * channels, (piece + 1) * channels)
            if len(out.shape) == 1:
                out[lanes] = small[first, :]
            else:
                out[:, lanes] = small[first : first + each, :]
            first += each
    for piece in range(sum_norm1.shape[0] // channels):
        sum_norm1[piece * channels : (piece + 1) * channels] = norm1[0, piece, :]


def local(
    tokens, norm1_gain, in_weight, conv_weight, conv_bias, xproj_weight, dt_weight, dt_bias,
    decay_log, skip_gain, out_weight, norm2_gain, router_weight, expert_in, expert_out,
    segments, expert_ids, cotangent,
):
    length, width = tokens.shape
    taps, channels = conv_weight.shape
    experts = router_weight.shape[1]
    wide = experts
    capacity = 5 * length // (4 * experts)
    states, rank = decay_log.shape[0], dt_weight.shape[0]
    chips = wide // 2
    slots = chips * capacity
    steps = length // SEGMENTS
    me_wide = lax.axis_index("wide")
    ids = jnp.stack([lax.axis_index("narrow"), me_wide, me_wide & 1, me_wide // 2]).astype(jnp.int32)
    half, double = length // 2, width // 2
    bf16 = jnp.bfloat16
    rows_shape, channel_rows = shape_of(length, width), shape_of(length, channels)
    packed, packed_slots = shape_of(half, double), shape_of(slots, double)
    vmem = lambda *shape: pltpu.VMEM(shape, jnp.float32)
    xproj_t, router_t = xproj_weight.T, router_weight.T
    cols = xproj_t.shape[0]

    tiled = vmem(width // LANES, length, LANES)

    halo_rows = wide_shift(tokens[length - SEGMENTS :], 1)

    (marks, slots_own, slots_other, rows_own, rows_other, rows_slice, cot_slice, cot_own,
     cot_other, conv_high, conv_low, gate_high, gate_low) = call(
        functools.partial(start_kernel, capacity),
        [shape_of(length, SEGMENTS)]
        + [shape_of(slots, length, dtype=bf16)] * 2
        + [shape_of(length, slots, dtype=bf16)] * 2
        + [packed, packed, packed_slots, packed_slots]
        + [shape_of(width, channels, dtype=bf16)] * 4,
        ids, segments.reshape(-1, LANES), expert_ids.reshape(1, length), tokens, cotangent,
        in_weight,
        scratch=[pltpu.VMEM((segments.shape[0] // LANES, LANES), jnp.int32),
                 pltpu.VMEM((1, length), jnp.int32)] + [vmem(length, width)] * 2
        + [vmem(width, 2, channels), vmem(length, width), tiled, vmem(2, width, channels),
           pltpu.SemaphoreType.DMA((5,))],
        far_in=[0, 1, 2, 3, 4],
    )
    cot_pair = cot_own + core_swap(cot_other)
    rows, normed, conv_in, gate_in = call(
        front_kernel,
        [rows_shape, rows_shape, channel_rows, channel_rows],
        ids, tokens, norm1_gain, conv_high, conv_low, gate_high, gate_low,
        scratch=[tiled],
    )
    mixed, conv_out, partial, extended, halo_normed = call(
        conv_kernel,
        [channel_rows, channel_rows, shape_of(cols, length),
         shape_of(length + (taps - 1) * SEGMENTS, channels), shape_of(SEGMENTS, width)],
        ids, halo_rows, norm1_gain, conv_high, conv_low, conv_in, marks, conv_weight,
        conv_bias, xproj_t, after=[cot_pair],
    )
    partials = narrow_all(partial)

    partials = narrow_all(partial)

    cot_blocks = chip_each(hold(cot_pair, partial), chips)

    entry_shape = shape_of(2, states, SEGMENTS, channels)
    total_rows = -(-(states + 1) // 8) * 8
    coef, dt_pre, stepsize, drive, stepd, rates, entry, total = call(
        totals_kernel,
        [shape_of(length, LANES)] + [channel_rows] * 4
        + [shape_of(states, channels), entry_shape, shape_of(total_rows, channels)],
        ids, *partials, dt_weight, dt_bias, decay_log, conv_out, marks,
        scratch=[vmem(LANES, channels)],
    )
    total_shape = shape_of(total_rows, channels)
    early, late, chip_total = call(
        pair_kernel, [total_shape] * 3, ids, total, core_swap(total), rates, after=[cot_blocks]
    )
    chip_totals = chip_all(chip_total, chips)
    slabs = states // GROUP
    cot_held = hold(cot_blocks, chip_total)
    cot_one, cot_two = narrow_swap(cot_held, 1), narrow_swap(cot_held, 2)
    kept_shape = (slabs, steps + 1, GROUP, SEGMENTS, channels)
    ssm_skip, gated, mixer_slices, kept = call(
        functools.partial(states_kernel, rank),
        [channel_rows, channel_rows, shape_of(4, half, double), shape_of(*kept_shape)],
        ids, stepd, drive, coef, rates, entry, early, conv_out, gate_in, skip_gain,
        out_weight, *chip_totals,
        scratch=[vmem(chips, total_rows, channels), vmem(length, width), vmem(*kept_shape),
                 pltpu.SemaphoreType.DMA((slabs,))],
        out_place=[3],
    )
    mixer_slices = hold(mixer_slices, cot_one, cot_two)
    expert_rows, square = shape_of(2 * slots, width), (expert_in.shape[1], expert_in.shape[2])
    hidden_units = square[1]
    hidden_slice, hidden_own, hidden_other = call(
        dispatch_kernel,
        [packed, packed_slots, packed_slots],
        ids, *narrow_each(mixer_slices), rows_slice, slots_own, slots_other,
    )
    hidden_blocks = chip_each(hidden_own + core_swap(hidden_other), chips)
    upper, lower = hold(cot_one[: slots // 2], hidden_own), hold(cot_two[slots // 2 :], hidden_own)
    cot_three = jnp.concatenate([narrow_swap(upper, 2), narrow_swap(lower, 1)])
    raw, cot, in_high, in_low, out_high, out_low = call(
        raw_kernel,
        [shape_of(2 * slots, hidden_units), expert_rows]
        + [shape_of(*square, dtype=bf16)] * 2
        + [shape_of(square[1], square[0], dtype=bf16)] * 2,
        ids, cot_blocks, cot_one, cot_two, cot_three, expert_in[0], expert_out[0],
        scratch=[vmem(4, slots, double)],
    )
    hidden_parts = lax.all_gather(hold(hidden_blocks, raw), "narrow")
    slices_shape = shape_of(4, slots, double)
    grad_slices, second, act, grad_pre, gates, grad_logits, grad_norm2 = call(
        expert_kernel,
        [slices_shape, expert_rows] + [shape_of(2 * slots, hidden_units)] * 2
        + [shape_of(2 * slots, 1), shape_of(2 * slots, experts), shape_of(1, width)],
        ids, hidden_parts, raw, in_high, in_low, norm2_gain, router_t,
        scratch=[vmem(2 * slots, width)],
    )
    grad_mine = pair_sum(narrow_each(grad_slices))
    value_slices, grad_expert_in, grad_expert_out, grad_router_t = call(
        expert_rest_kernel,
        [slices_shape, shape_of(*square), shape_of(square[1], square[0]),
         shape_of(experts, width)],
        ids, second, act, grad_pre, gates, grad_logits, cot, out_high, out_low,
        scratch=[vmem(2 * slots, width)],
    )
    grad_back = chip_each(grad_mine, chips)
    value_mine = pair_sum(narrow_each(value_slices))
    grad_slice = call(
        home_kernel, [packed], ids, grad_back, core_swap(grad_back), cot_slice, rows_own,
        rows_other, after=[value_mine],
    )[0]
    grad_parts = narrow_all(grad_slice)
    value_back = chip_each(value_mine, chips)

    def whole_of(parts, after=()):
        return call(
            whole_kernel, [rows_shape], ids, *parts, after=after,
            scratch=[vmem(4, half, double), vmem(length, width), tiled],
        )[0]

    grad_hidden, grad_ssm, grad_gate_in, grad_skip, back_entry, back_total = call(
        functools.partial(leaving_kernel, rank),
        [rows_shape, channel_rows, channel_rows, shape_of(1, channels), entry_shape,
         shape_of(states, channels)],
        ids, *grad_parts, out_weight, gate_in, ssm_skip, conv_out, stepd, coef, rates,
        scratch=[vmem(4, half, double)], after=[value_back],
    )
    other_back = core_swap(back_total)
    block = width // wide
    half_blocks = shape_of(wide // 2, 2 * block, channels)
    early_keep, early_send = call(
        early_weights_kernel,
        [half_blocks, half_blocks],
        ids, gated, grad_hidden, normed, grad_gate_in,
        scratch=[vmem(width, channels)] * 2,
    )
    back_late, back_chip = call(
        pair_back_kernel, [shape_of(states, channels)] * 2,
        ids, back_total, other_back, early, rates, after=[early_keep],
    )
    back_totals = chip_all(back_chip, chips)
    early_arrived = core_swap(hold(early_send, back_chip))
    out_sum, gate_sum = (
        WideSum(early_keep[:, rows], early_send[:, rows])
        for rows in (slice(0, block), slice(block, None))
    )
    out_sum.arrived, gate_sum.arrived = early_arrived[:, :block], early_arrived[:, block:]
    out_sum.finish()
    gate_sum.finish()
    first_step = out_sum.start(*back_totals)

    shared_rows = (experts + 1) * (width // length)
    partial_rows = cols + shared_rows + -(cols + shared_rows) % 8
    partial_back, grad_direct, grad_dt_pre, grad_decay, grad_dt_bias = call(
        functools.partial(adjoint_kernel, rank, chips),
        [shape_of(partial_rows, length), channel_rows, channel_rows, shape_of(states, channels),
         shape_of(1, channels)],
        ids, stepd, drive, grad_ssm, coef, rates, back_entry, kept, early, late, back_late,
        conv_out, stepsize, dt_pre, skip_gain, dt_weight, grad_norm2, grad_router_t,
        *chip_totals, *back_totals,
        scratch=[vmem(chips, 1, channels), vmem(chips, states, channels), vmem(*kept_shape),
                 vmem(length, states * LANES), vmem(length, states * LANES),
                 vmem(length, channels), vmem(length, channels),
                 pltpu.SemaphoreType.DMA((slabs,))],
        in_place=[6], after=[out_sum.send, gate_sum.send],
    )
    partials_back = narrow_all(partial_back)
    gate_part = call(
        gate_tokens_kernel, [rows_shape], ids, grad_gate_in, gate_high, gate_low,
        after=[partial_back],
    )[0]
    out_sum.finish(partial_back)
    out_sum.start()
    gate_sum.start(partial_back)
    grain = 8 * wide
    small_rows = cols + rank + states + taps + 3 + (experts + 1) * (width // channels)
    small_rows += -small_rows % grain
    more = small_rows // wide
    half_blocks = shape_of(wide // 2, block + more, channels)
    token_rows = length + 2 * SEGMENTS
    conv_keep, conv_send, grad_conv, grad_halo = call(
        functools.partial(conv_back_kernel, experts),
        [half_blocks, half_blocks, channel_rows, shape_of(SEGMENTS, channels)],
        ids, *partials_back, xproj_t, grad_direct, mixed, conv_out, extended, marks,
        conv_weight, coef, grad_dt_pre, grad_decay, grad_dt_bias, grad_skip,
        normed, halo_normed,
        scratch=[vmem(small_rows, channels),
                 vmem(length + (taps - 1) * SEGMENTS, channels), vmem(partial_rows, length),
                 vmem(width, channels)],
        after=[gate_sum.arrived, out_sum.arrived],
    )
    (token_slices,) = call(
        tokens_kernel, [shape_of(4, token_rows // 2, double)],
        ids, grad_conv, grad_halo, conv_high, conv_low, gate_part, rows, halo_rows,
        scratch=[vmem(token_rows, width)],
    )
    out_sum.finish()
    gate_sum.finish()
    conv_sum = WideSum(conv_keep, conv_send)
    conv_sum.start()
    conv_sum.finish()
    (output_slice,) = call(
        home_kernel, [packed], ids, value_back, core_swap(hold(value_back, conv_keep)),
        hidden_slice, rows_own, rows_other,
    )
    levels = len(conv_sum.swaps)

    def extra_of(parts):
        return call(
            extra_kernel,
            [shape_of(SEGMENTS, width), shape_of(1, SEGMENTS, channels)],
            ids, *parts,
            scratch=[vmem(4, token_rows // 2, double), vmem(token_rows, width)],
        )

    def grad_tokens_of(parts, from_next):
        return call(
            functools.partial(grad_tokens_kernel, taps),
            [rows_shape], ids, *parts, from_next, rows, norm1_gain, grad_hidden,
            scratch=[vmem(4, token_rows // 2, double), vmem(token_rows, width), tiled],
        )[0]

    def out_weight_of(total, *others):
        return call(
            early_out_kernel, [shape_of(channels, width)], ids, total, after=others
        )[0]

    if levels == 3:
        sums = conv_sum, gate_sum, out_sum
        joint = [conv_sum.start(), *start_both(gate_sum, out_sum)]
        token_each = narrow_each(token_slices)
        for part in sums:
            part.finish(*joint, *token_each, output_slice)
        joint = [*start_both(conv_sum, gate_sum), out_sum.start()]
        token_parts = narrow_all(pair_sum(token_each))
        extra, norm1 = extra_of(token_parts)
        from_next = wide_shift(extra, -1)
        for part in sums:
            part.finish(*joint, norm1, from_next)
        arrived, norm1_other = conv_sum.start_with(norm1)
        joint = [arrived, gate_sum.start()]
        output_parts = narrow_all(hold(output_slice, norm1))
        for part in sums[:2]:
            part.finish(*joint, *output_parts)
        norm1 = norm1 + norm1_other
        arrived, norm1_other = conv_sum.start_with(norm1)
        grad_tokens = grad_tokens_of(token_parts, from_next)
        joint = [arrived, *start_both(gate_sum, out_sum, grad_tokens)]
        output = whole_of(output_parts, after=[conv_sum.send])
        for part in sums:
            part.finish(*joint, output, grad_tokens)
        norm1 = norm1 + norm1_other
        arrived, norm1_other = conv_sum.start_with(norm1)
        sum_out_weight = out_weight_of(out_sum.keep, conv_sum.send)
        conv_sum.finish(sum_out_weight)
        norm1 = norm1 + norm1_other
    else:
        token_parts = narrow_all(pair_sum(narrow_each(token_slices)))
        extra, norm1 = extra_of(token_parts)
        grad_tokens = grad_tokens_of(token_parts, wide_shift(extra, -1))
        output = whole_of(narrow_all(output_slice))
        sum_out_weight = out_weight_of(out_sum.rest())
        norm1 = norm1 + core_swap(norm1)
        norm1 = pair_sum(chip_all(norm1, chips))
    per = width // channels
    counts = (cols, rank, states, taps, 1, 1, 1, per, per * experts)
    (weight_sum, sum_xproj_t, sum_dt_weight, sum_decay, sum_taps, sum_conv_bias, sum_dt_bias,
     sum_skip, sum_norm2, sum_router_t, sum_norm1) = call(
        functools.partial(weights_out_kernel, counts),
        [shape_of(width, 2, channels)]
        + [shape_of(rows, channels) for rows in (cols, rank, states, taps)]
        + [shape_of(channels)] * 3
        + [shape_of(width), shape_of(experts, width), shape_of(width)],
        ids, gate_sum.rest(), conv_sum.rest(), norm1, scratch=[vmem(small_rows, channels)],
    )
    return (
        output,
        grad_tokens,
        sum_norm1,
        weight_sum,
        sum_taps,
        sum_conv_bias,
        sum_xproj_t.T,
        sum_dt_weight,
        sum_dt_bias,
        sum_decay,
        sum_skip,
        sum_out_weight,
        sum_norm2,
        sum_router_t.T,
        grad_expert_in[None],
        grad_expert_out[None],
    )


def solution(mesh):
    in_specs = (
        P("wide", None),
        P(),
        P(None, None, "narrow"),
        P(None, "narrow"),
        P("narrow"),
        P("narrow", None),
        P(None, "narrow"),
        P("narrow"),
        P(None, "narrow"),
        P("narrow"),
        P("narrow", None),
        P(),
        P(),
        P("wide", None, "narrow"),
        P("wide", "narrow", None),
        P(),
        P("wide", None),
        P("wide", None),
    )
    out_specs = (
        P("wide", None),
        P("wide", None),
        P(),
        P(None, None, "narrow"),
        P(None, "narrow"),
        P("narrow"),
        P("narrow", None),
        P(None, "narrow"),
        P("narrow"),
        P(None, "narrow"),
        P("narrow"),
        P("narrow", None),
        P(),
        P(),
        P("wide", None, "narrow"),
        P("wide", "narrow", None),
    )
    return jax.shard_map(local, mesh=mesh, in_specs=in_specs, out_specs=out_specs, check_vma=False)
```
